32 devices in a mesh: rep: 2 (over core), shard: 16 (over z, y, x).
Axes of the slice: x: 2, y: 2, z: 4, core: 2. Of those that a mesh axis runs over, the one named last changes fastest.
Arguments:
- streams: bfloat16 [4096, 4, 2048], P(('rep', 'shard')), may hold values from -6 to 6
- cotangent: bfloat16 [4096, 4, 2048], P(('rep', 'shard')), may hold values from -6 to 6
- deal: int32 [4096], P(('rep', 'shard')), may hold values from 0 to 127, as said below
- lengths: int32 [8, 4], replicated, may hold values from 0 to 512, as said below
- mix_attn: float32 [4, 6], replicated, may hold values from -0.9 to 1.9
- mix_mlp: float32 [4, 6], replicated, may hold values from -0.9 to 1.9
- w_qkv: bfloat16 [2048, 6144], P(('rep', 'shard')), may hold values from -0.125 to 0.125
- w_out: bfloat16 [2048, 2048], P(('rep', 'shard')), may hold values from -0.5 to 0.5
- w_gu: bfloat16 [2048, 16384], P(('rep', 'shard')), may hold values from -0.125 to 0.125
- w_down: bfloat16 [2048, 8192], P(('rep', 'shard')), may hold values from -0.0625 to 0.0625
Outputs:
- new_streams: float32 [4096, 4, 2048], P(('rep', 'shard'))
- d_streams: float32 [4096, 4, 2048], P(('rep', 'shard'))
- g_mix_attn: float32 [4, 6], replicated
- g_mix_mlp: float32 [4, 6], replicated
- g_qkv: float32 [2048, 6144], P(('rep', 'shard'))
- g_out: float32 [2048, 2048], P(('rep', 'shard'))
- g_gu: float32 [2048, 16384], P(('rep', 'shard'))
- g_down: float32 [2048, 8192], P(('rep', 'shard'))
The draws below stay inside these ranges and needn't reach their ends.
Inputs may be any that keep to these rules, and one draw needn't show every extreme that they name: `deal`: within each device's 128 entries every value appears once. `lengths`: each row sums to at most 512; in each group of 4 rows (starting at a multiple of 4) one row is 512 followed by zeros.
All inputs are finite; a program needn't handle non-finite values.
Results may differ from the reference program's by a relative error of at most 0.013.
Values may be sent and summed in bfloat16 or wider, within the bound.
A program may use at most 832 MiB of HBM per device.

```python
import math
import jax
import jax.numpy as jnp
from jax import lax

D = 2048
HEADS = 16
HEAD_DIM = 128
FF = 8192
STREAMS = 4
SEQ_SLOTS = 4
TOK_DEV = 128
TOKENS = 4096
BINS = 4
ALL_BINS = 8
CAP = 512
N_SHARD = 16


def mixing_draw(key):
    first, second, third = jax.random.split(key, 3)
    read_cols = jax.random.uniform(first, (STREAMS, 1), jnp.float32, 0.2, 0.7)
    noise = jnp.clip(jax.random.normal(second, (STREAMS, STREAMS), jnp.float32), -3.0, 3.0)
    mixing = jnp.eye(STREAMS, dtype=jnp.float32) + 0.3 * noise
    writes = jax.random.uniform(third, (STREAMS, 1), jnp.float32, 0.5, 1.5)
    return jnp.concatenate([read_cols, mixing, writes], axis=1)


def draw_mix_attn(key, part):
    key = jax.random.fold_in(key, 7)
    return mixing_draw(key)


def draw_mix_mlp(key, part):
    key = jax.random.fold_in(key, 9)
    return mixing_draw(key)


def draw_deal(key, part):
    key = jax.random.fold_in(key, 5)
    key_list = jax.random.split(key, TOKENS // TOK_DEV)
    orders = jax.vmap(lambda single: jax.random.permutation(single, TOK_DEV))(key_list)
    return orders.reshape(TOKENS).astype(jnp.int32)


def draw_lengths(key, part):
    key = jax.random.fold_in(key, 11)
    first, second = jax.random.split(key)
    ragged = jax.random.randint(first, (ALL_BINS, SEQ_SLOTS), CAP // 8, CAP // 4 + 1, dtype=jnp.int32)
    full_bin = jax.random.randint(second, (ALL_BINS // BINS,), 0, BINS, dtype=jnp.int32)
    bin_index = jnp.arange(ALL_BINS, dtype=jnp.int32)
    is_full = bin_index % BINS == full_bin[bin_index // BINS]
    full_row = jnp.where(jnp.arange(SEQ_SLOTS, dtype=jnp.int32) == 0, CAP, 0).astype(jnp.int32)
    return jnp.where(is_full[:, None], full_row[None, :], ragged).astype(jnp.int32)


def levels(key, shape, cuts, least, high):
    level, own = 1.0, jax.random.fold_in(key, 6)
    for dim, blocks in cuts:
        steps = jnp.exp(jax.random.uniform(jax.random.fold_in(own, dim), (blocks,), jnp.float32, least / len(cuts), high / len(cuts)))
        level = level * jnp.repeat(steps, shape[dim] // blocks).reshape([-1 if axis == dim else 1 for axis in range(len(shape))])
    return level


def normal_values(stream_key, extent, width, limit, cuts=(), kind=jnp.bfloat16):
    values = width * jax.random.normal(stream_key, extent, jnp.float32)
    if cuts:
        values = values * levels(stream_key, extent, cuts, -0.22, 0.18)
    return jnp.clip(values, -limit, limit).astype(kind)


def setup_inputs(seed: int = 0) -> dict:
    key_of = jax.random.split(jax.random.key(seed), 11)
    streams = normal_values(key_of[0], (TOKENS, STREAMS, D), 1.0, 6.0, ((0, 32),))
    cotangent = normal_values(key_of[1], (TOKENS, STREAMS, D), 1.0, 6.0, ((0, 32),))
    deal = draw_deal(jax.random.fold_in(key_of[10], 71), 0)
    lengths = draw_lengths(jax.random.fold_in(key_of[10], 71), 0)
    mix_attn = draw_mix_attn(jax.random.fold_in(key_of[10], 71), 0)
    mix_mlp = draw_mix_mlp(jax.random.fold_in(key_of[10], 71), 0)
    w_qkv = normal_values(key_of[6], (D, 3 * D), D ** -0.5, 0.125, ((0, 32),))
    w_out = normal_values(key_of[7], (D, D), (D // 16) ** -0.5, 0.5, ((0, 32),))
    w_gu = normal_values(key_of[8], (D, 2 * FF), D ** -0.5, 0.125, ((0, 32),))
    w_down = normal_values(key_of[9], (D, FF), FF ** -0.5, 0.0625, ((0, 32),))
    return {"streams": streams, "cotangent": cotangent, "deal": deal, "lengths": lengths, "mix_attn": mix_attn, "mix_mlp": mix_mlp, "w_qkv": w_qkv, "w_out": w_out, "w_gu": w_gu, "w_down": w_down}


EPSILON = 1e-05
HIGHEST = lax.Precision.HIGHEST

@jax.custom_vjp
def low(v):
    return lax.optimization_barrier(v.astype(jnp.bfloat16)).astype(jnp.float32)

@jax.custom_vjp
def low_back(v):
    return v

def low_keep(v):
    return (low(v), None)

def low_pass(kept, grad):
    return (grad,)

def back_keep(v):
    return (v, None)

def back_low(kept, grad):
    return (low(grad),)
low.defvjp(low_keep, low_pass)
low_back.defvjp(back_keep, back_low)

def normalize(inputs):
    centred = inputs - lax.optimization_barrier(jnp.mean(inputs, -1, keepdims=True))
    inverse = lax.rsqrt(lax.optimization_barrier(jnp.mean(centred * centred, -1, keepdims=True)) + EPSILON)
    return centred * inverse

def read_streams(streams, weights):
    return lax.optimization_barrier(jnp.sum(streams * weights[None, :, None], axis=1))

def write_streams(streams, mixing, branch, out_weights):
    result = branch[:, None, :] * out_weights[None, :, None]
    for source in range(streams.shape[1]):
        result = result + streams[:, source, None, :] * mixing[source][None, :, None]
    return result

def slot_layout(lengths_row, capacity):
    seq_count = lengths_row.shape[-1]
    seq_ends = jnp.cumsum(lengths_row, axis=-1).astype(jnp.int32)
    slot_index = jnp.arange(capacity, dtype=jnp.int32)
    segment = lax.optimization_barrier(jnp.sum((slot_index[:, None] >= seq_ends[..., None, :]).astype(jnp.int32), axis=-1))
    seq_starts = (seq_ends - lengths_row).astype(jnp.int32)
    chosen = (segment[..., None] == jnp.arange(seq_count, dtype=jnp.int32)).astype(jnp.int32)
    start_of = lax.optimization_barrier(jnp.sum(chosen * seq_starts[..., None, :], axis=-1))
    is_live = segment < seq_count
    segment = jnp.where(is_live, segment, seq_count + slot_index).astype(jnp.int32)
    position = jnp.where(is_live, slot_index - start_of, 0).astype(jnp.int32)
    return (segment, position)

def rope_tables(position, head_width):
    half_width = head_width // 2
    frequency = jnp.exp(jnp.arange(half_width, dtype=jnp.float32) * (-2.0 * math.log(10000.0) / head_width))
    angles = position.astype(jnp.float32)[..., None] * frequency
    return (jnp.cos(angles), jnp.sin(angles))

def rotate(inputs, cosine, sine_table):
    half_width = inputs.shape[-1] // 2
    first = inputs[..., :half_width]
    second = inputs[..., half_width:]
    return jnp.concatenate([first * cosine - second * sine_table, second * cosine + first * sine_table], axis=-1)

def visible(seg_query, pos_query, seg_key, pos_key):
    return (seg_query[:, None] == seg_key[None, :]) & (pos_key[None, :] <= pos_query[:, None])

def routing(deal):
    token_index = jnp.arange(TOKENS, dtype=jnp.int32)
    device = token_index // TOK_DEV
    group_index = device // N_SHARD
    member = device % N_SHARD
    slot_rows = TOK_DEV // BINS
    bin_row = ((group_index * BINS + deal // slot_rows) * CAP + member * slot_rows + deal % slot_rows).astype(jnp.int32)
    gather_order = jnp.zeros((TOKENS,), jnp.int32).at[bin_row].set(token_index)
    return (bin_row, gather_order)

def attend_bin(inputs):
    qkv_rows, segment, position = inputs
    pieces = qkv_rows.reshape(CAP, 3, HEADS, HEAD_DIM)
    cosine, sine_table = rope_tables(position, HEAD_DIM)
    cosine = cosine[:, None, :]
    sine_table = sine_table[:, None, :]
    queries = low(rotate(pieces[:, 0], cosine, sine_table))
    key_rows = low(rotate(pieces[:, 1], cosine, sine_table))
    value_rows = pieces[:, 2]
    scores = jnp.einsum('qhd,khd->hqk', queries, key_rows, precision=HIGHEST) * (1.0 / math.sqrt(HEAD_DIM))
    scores = low_back(scores)
    scores = jnp.where(visible(segment, position, segment, position)[None], scores, -1e+30)
    row_peak = lax.optimization_barrier(jnp.max(scores, -1, keepdims=True))
    exp_scores = jnp.exp(scores - row_peak)
    probability = low(exp_scores / lax.optimization_barrier(jnp.sum(exp_scores, -1, keepdims=True)))
    attended = jnp.einsum('hqk,khd->qhd', probability, value_rows, precision=HIGHEST)
    return low_back(low(attended)).reshape(CAP, D)

def hyper_layer(streams, attn_mixing, mlp_mixing, qkv_weight, out_weight, gu_weight, down_weight, bin_row, gather_order, segment, position):
    read_attn = read_streams(streams, attn_mixing[:, 0])
    normed_attn = low(normalize(read_attn))
    qkv_rows = low_back(low(jnp.dot(normed_attn, qkv_weight, preferred_element_type=jnp.float32, precision=HIGHEST)))
    binned = qkv_rows[gather_order].reshape(ALL_BINS, CAP, 3 * D)
    attended = lax.map(jax.checkpoint(attend_bin), (binned, segment, position))
    attn_rows = attended.reshape(TOKENS, D)[bin_row]
    branch_attn = low_back(jnp.dot(attn_rows, out_weight, preferred_element_type=jnp.float32, precision=HIGHEST))
    middle_streams = write_streams(streams, attn_mixing[:, 1:1 + STREAMS], branch_attn, attn_mixing[:, STREAMS + 1])
    read_mlp = read_streams(middle_streams, mlp_mixing[:, 0])
    normed_mlp = low(normalize(read_mlp))
    gate_up = low_back(jnp.dot(normed_mlp, gu_weight, preferred_element_type=jnp.float32, precision=HIGHEST))
    hidden = low(jax.nn.silu(gate_up[:, FF:]) * gate_up[:, :FF])
    branch_mlp = low_back(jnp.dot(hidden, down_weight.T, preferred_element_type=jnp.float32, precision=HIGHEST))
    return write_streams(middle_streams, mlp_mixing[:, 1:1 + STREAMS], branch_mlp, mlp_mixing[:, STREAMS + 1])

def reference(streams, cotangent, deal, lengths, mix_attn, mix_mlp, w_qkv, w_out, w_gu, w_down):
    bin_row, gather_order = routing(deal)
    segment, position = slot_layout(lengths, CAP)

    def forward(streams_in, attn_mixing, mlp_mixing, qkv_weight, out_weight, gu_weight, down_weight):
        return hyper_layer(streams_in, attn_mixing, mlp_mixing, qkv_weight, out_weight, gu_weight, down_weight, bin_row, gather_order, segment, position)
    new_streams, pullback = jax.vjp(forward, streams.astype(jnp.float32), mix_attn, mix_mlp, w_qkv.astype(jnp.float32), w_out.astype(jnp.float32), w_gu.astype(jnp.float32), w_down.astype(jnp.float32))
    gradients = pullback(cotangent.astype(jnp.float32))
    return (new_streams, gradients[0], gradients[1], gradients[2], gradients[3], gradients[4], gradients[5], gradients[6])
```

```python
import functools
import math

import jax
import jax.numpy as jnp
from jax import lax
from jax.experimental import pallas as pl
from jax.experimental.pallas import tpu as pltpu
from jax.sharding import PartitionSpec as P

HEADS = 16
HEAD_DIM = 128
GROUP = 16
EPSILON = 1e-05
MESH = pl.DeviceIdType.MESH
CONTRACT_LAST = (((1,), (1,)), ((), ()))
CONTRACT_FIRST = (((0,), (0,)), ((), ()))
MIB = 1 << 20
BF = jnp.bfloat16
F32 = jnp.float32


class Here:
    def __init__(self):
        self.rep = lax.axis_index("rep")
        shard = lax.axis_index("shard")
        self.lo = shard % GROUP
        self.base = shard - self.lo
        self.bits = [(self.lo // (1 << i)) % 2 for i in range(4)]

    def flip(self, mask):
        out = self.lo
        for i in range(4):
            if mask & (1 << i):
                out = out + (1 << i) * (1 - 2 * self.bits[i])
        return out

    def dev(self, mask):
        return (self.rep, self.base + self.flip(mask))

    def partner(self):
        return (1 - self.rep, self.base + self.lo)


def barrier(here, masks, partner):
    sem = pltpu.get_barrier_semaphore()
    targets = [here.dev(m) for m in masks]
    if partner:
        targets.append(here.partner())
    for t in targets:
        pl.semaphore_signal(sem, inc=1, device_id=t, device_id_type=MESH)
    pl.semaphore_wait(sem, len(targets))


TREE = (1, 2, 4, 8, 12)
ALL = tuple(range(1, GROUP))


def rcopy(src, dst, send, recv, dev):
    return pltpu.make_async_remote_copy(
        src_ref=src, dst_ref=dst, send_sem=send, recv_sem=recv, device_id=dev, device_id_type=MESH
    )


class Gather:
    sems = (4, 7)

    def __init__(self, here, x, out, send, recv):
        self.here, self.x, self.out, self.send, self.recv = here, x, out, send, recv
        self.half = x.shape[0] // 2
        self.sent = []

    def _go(self, block, part, j, slot, mask):
        ref = self.out.at[block, pl.ds(part * self.half, self.half)]
        c = rcopy(ref, ref, self.send.at[j, slot], self.recv.at[j, slot], self.here.dev(mask))
        c.start()
        self.sent.append(c)

    def _wait(self, j, slot, block, part):
        ref = self.out.at[block, pl.ds(part * self.half, self.half)]
        rcopy(ref, ref, self.send.at[j, slot], self.recv.at[j, slot], self.here.dev(1)).wait_recv()

    def begin(self, own_sem):
        own = pltpu.make_async_copy(self.x, self.out.at[self.here.lo], own_sem)
        own.start()
        for j in (1, 3, 2):
            c = rcopy(self.x, self.out.at[self.here.lo], self.send.at[j, 6], self.recv.at[j, 6], self.here.dev(4 * j))
            c.start()
            self.sent.append(c)
        own.wait()
        self.spread(0)

    def spread(self, j):
        b = self.here.flip(4 * j)
        if j:
            ref = self.out.at[b]
            rcopy(ref, ref, self.send.at[j, 6], self.recv.at[j, 6], self.here.dev(4)).wait_recv()
        self._go(b, 0, j, 0, 1)
        self._go(b, 1, j, 1, 2)
        self._go(b, 0, j, 2, 2)
        self._go(b, 1, j, 3, 1)

    def forward(self, j):
        m = 4 * j
        self._wait(j, 0, self.here.flip(m ^ 1), 0)
        self._go(self.here.flip(m ^ 1), 0, j, 4, 2)
        self._wait(j, 1, self.here.flip(m ^ 2), 1)
        self._go(self.here.flip(m ^ 2), 1, j, 5, 1)

    def settle(self, j):
        m = 4 * j
        self._wait(j, 2, self.here.flip(m ^ 2), 0)
        self._wait(j, 3, self.here.flip(m ^ 1), 1)
        self._wait(j, 4, self.here.flip(m ^ 3), 0)
        self._wait(j, 5, self.here.flip(m ^ 3), 1)

    def end(self):
        for c in self.sent:
            c.wait_send()

    ORDER = (0, 1, 3, 2)


def run_gathers(gathers, own_sems):
    for i, g in enumerate(gathers):
        if i == 0:
            g.begin(own_sems.at[0])
        order = g.ORDER
        g.spread(order[1])
        g.forward(order[0])
        g.spread(order[2])
        g.forward(order[1])
        g.spread(order[3])
        g.forward(order[2])
        if i + 1 < len(gathers):
            gathers[i + 1].begin(own_sems.at[i + 1])
        g.forward(order[3])
    for g in gathers:
        for j in range(4):
            g.settle(j)


def rowwise(n, step, body):
    def at(i, carry):
        body(pl.ds(pl.multiple_of(i * step, step), step))
        return carry

    lax.fori_loop(0, n // step, at, 0)


class Scatter:
    sems = (4, 7)

    @staticmethod
    def scratch(rows, d):
        h = rows // 2
        return [
            pltpu.VMEM((4, 4, h, d), BF),
            pltpu.VMEM((4, 2, h, d), BF),
            pltpu.VMEM((4, 2, h, d), BF),
            pltpu.VMEM((4, rows, d), BF),
            pltpu.VMEM((4, rows, d), BF),
            pltpu.SemaphoreType.DMA(Scatter.sems),
            pltpu.SemaphoreType.DMA(Scatter.sems),
        ]

    def __init__(self, here, part, scratch):
        self.here, self.part = here, part
        self.first, self.second, self.mid, self.zin, self.zout, self.send, self.recv = scratch
        self.rows = part.shape[1]
        self.half = self.rows // 2
        self.sent = []

    def _copy(self, j, slot, src, dst, mask):
        return rcopy(src, dst, self.send.at[j, slot], self.recv.at[j, slot], self.here.dev(mask))

    def _go(self, *a):
        c = self._copy(*a)
        c.start()
        self.sent.append(c)

    def _piece(self, mask, part):
        return self.part.at[self.here.flip(mask), pl.ds(part * self.half, self.half)]

    def start(self, j):
        m = 4 * j
        self._go(j, 1, self._piece(m ^ 3, 0), self.first.at[j, 1], 2)
        self._go(j, 3, self._piece(m ^ 3, 1), self.first.at[j, 3], 1)
        self._go(j, 0, self._piece(m ^ 2, 0), self.first.at[j, 0], 2)
        self._go(j, 2, self._piece(m ^ 1, 1), self.first.at[j, 2], 1)

    def cross(self, j):
        m = 4 * j
        h = self.half
        for slot, mask, part, to in ((1, 1, 0, 1), (3, 2, 1, 2)):
            self._copy(j, slot, self.first.at[j, slot], self.first.at[j, slot], 1).wait_recv()
            own = self._piece(m ^ mask, part)

            def body(r, own=own, slot=slot, part=part):
                self.mid[j, part, r] = (own[r].astype(F32) + self.first[j, slot, r].astype(F32)).astype(BF)

            rowwise(h, 16, body)
            self._go(j, 4 + part, self.mid.at[j, part], self.second.at[j, part], to)

    def finish(self, j, out=None):
        m = 4 * j
        h = self.half
        for part, slot in ((0, 0), (1, 2)):
            self._copy(j, slot, self.first.at[j, slot], self.first.at[j, slot], 1).wait_recv()
            self._copy(j, 4 + part, self.second.at[j, part], self.second.at[j, part], 1).wait_recv()
        if out is not None:
            for k in (1, 2, 3):
                self._copy(k, 6, self.zin.at[k], self.zin.at[k], 4).wait_recv()
        for part, slot in ((0, 0), (1, 2)):
            own = self._piece(m, part)

            def body(r, own=own, part=part, slot=slot):
                total = own[r].astype(F32) + self.first[j, slot, r].astype(F32) + self.second[j, part, r].astype(F32)
                at = pl.ds(part * h + r.start, r.size)
                if out is None:
                    self.zout[j, at] = total.astype(BF)
                else:
                    for k in (1, 2, 3):
                        total = total + self.zin[k, at].astype(F32)
                    out[at] = total.astype(out.dtype)

            rowwise(h, 16, body)
        if out is None:
            self._go(j, 6, self.zout.at[j], self.zin.at[j], m)

    def end(self):
        for c in self.sent:
            c.wait_send()

    ORDER = (2, 3, 1, 0)


def run_scatters(scatters, outs):
    for i, (s, out) in enumerate(zip(scatters, outs)):
        order = s.ORDER
        if i == 0:
            s.start(order[0])
        s.start(order[1])
        s.cross(order[0])
        s.start(order[2])
        s.cross(order[1])
        s.finish(order[0])
        s.start(order[3])
        s.cross(order[2])
        s.finish(order[1])
        if i + 1 < len(scatters):
            scatters[i + 1].start(order[0])
        s.cross(order[3])
        s.finish(order[2])
        s.finish(order[3], out)
    for s in scatters:
        s.end()


def any_spec(n):
    return [pl.BlockSpec(memory_space=pl.ANY)] * n


def vmem_spec(n):
    return [pl.BlockSpec(memory_space=pltpu.VMEM)] * n


def params(cid, mib=60):
    return pltpu.CompilerParams(collective_id=cid, has_side_effects=True, vmem_limit_bytes=mib * MIB)


def exchange_columns(here, src, dst, width, cols, send, recv, own_sem):
    copies = []
    own = []
    for i, c in enumerate(cols):
        for m in range(GROUP):
            peer = here.flip(m)
            at = src.at[:, :, pl.ds(pl.multiple_of(c + peer * width, 128), width)]
            to = dst.at[here.rep, :, here.lo, :, pl.ds(i * width, width)]
            if m == 0:
                cp = pltpu.make_async_copy(at, to, own_sem.at[i])
                cp.start()
                own.append(cp)
            else:
                cp = rcopy(at, to, send.at[i, m], recv.at[i, m], here.dev(m))
                cp.start()
                copies.append(cp)

    def arrive():
        for cp in own:
            cp.wait()
        for i, c in enumerate(cols):
            for m in ALL:
                to = dst.at[here.rep, :, here.flip(m), :, pl.ds(i * width, width)]
                rcopy(to, to, send.at[i, m], recv.at[i, m], here.dev(m)).wait_recv()

    def end():
        for cp in copies:
            cp.wait_send()

    return arrive, end


def front_kernel(
    n1, dy2, wqkv, wout, wgu, wdn,
    n1g, dy2g, qkvs, outs, gus, dns,
    gsend, grecv, own, csend, crecv, cown, psend, precv,
):
    here = Here()
    barrier(here, ALL, True)
    q = exchange_columns(here, wqkv, qkvs, 128, (0, 2048, 4096), csend.at[0], crecv.at[0], cown.at[0])
    half = wgu.shape[2] // 2
    ga = Gather(here, n1, n1g, gsend.at[0], grecv.at[0])
    gb = Gather(here, dy2, dy2g, gsend.at[1], grecv.at[1])
    gc = Gather(here, wout, outs.at[here.rep], gsend.at[2], grecv.at[2])
    ga.begin(own.at[0])
    u = exchange_columns(here, wgu, gus, half // GROUP, (0, half), csend.at[1], crecv.at[1], cown.at[1])
    d = exchange_columns(here, wdn, dns, half // GROUP, (0,), csend.at[2], crecv.at[2], cown.at[2])
    gathers = [ga, gb, gc]
    for i, g in enumerate(gathers):
        order = g.ORDER
        g.spread(order[1])
        g.forward(order[0])
        g.spread(order[2])
        g.forward(order[1])
        g.spread(order[3])
        g.forward(order[2])
        if i + 1 < len(gathers):
            gathers[i + 1].begin(own.at[i + 1])
        g.forward(order[3])
    passes = []
    for i, ((arrive, _), dst) in enumerate(zip((q, u, d), (qkvs, gus, dns))):
        arrive()
        cp = rcopy(dst.at[here.rep], dst.at[here.rep], psend.at[i], precv.at[i], here.partner())
        cp.start()
        passes.append((cp, dst))
    for g in gathers:
        for j in range(4):
            g.settle(j)
    cp = rcopy(outs.at[here.rep], outs.at[here.rep], psend.at[3], precv.at[3], here.partner())
    cp.start()
    passes.append((cp, outs))
    for i, (cp, dst) in enumerate(passes):
        cp.wait_send()
        other = dst.at[1 - here.rep]
        rcopy(other, other, psend.at[i], precv.at[i], here.partner()).wait_recv()
    for g in gathers:
        g.end()
    for _, end in (q, u, d):
        end()


def front(n1, dy2, wqkv, wout, wgu, wdn, cid):
    hi, rows, _ = wqkv.shape
    d = n1.shape[1]
    ff = wdn.shape[2]
    shape = lambda *s: jax.ShapeDtypeStruct(s, BF)
    out_rows = wout.shape[0]
    return pl.pallas_call(
        front_kernel,
        out_shape=(
            shape(GROUP, *n1.shape),
            shape(GROUP, *dy2.shape),
            shape(2, hi, GROUP, rows, 3 * HEAD_DIM),
            shape(2, GROUP, out_rows, wout.shape[1]),
            shape(2, hi, GROUP, rows, 2 * ff // GROUP),
            shape(2, hi, GROUP, rows, ff // GROUP),
        ),
        in_specs=any_spec(6),
        out_specs=any_spec(6),
        scratch_shapes=[
            pltpu.SemaphoreType.DMA((3,) + Gather.sems),
            pltpu.SemaphoreType.DMA((3,) + Gather.sems),
            pltpu.SemaphoreType.DMA((3,)),
            pltpu.SemaphoreType.DMA((3, 3, GROUP)),
            pltpu.SemaphoreType.DMA((3, 3, GROUP)),
            pltpu.SemaphoreType.DMA((3, 3)),
            pltpu.SemaphoreType.DMA((4,)),
            pltpu.SemaphoreType.DMA((4,)),
        ],
        compiler_params=params(cid, 16),
    )(n1, dy2, wqkv, wout, wgu, wdn)


def gather_kernel(x, out, send, recv, own):
    here = Here()
    barrier(here, TREE, False)
    g = Gather(here, x, out, send, recv)
    run_gathers([g], own)
    g.end()


def gather(x, cid):
    return pl.pallas_call(
        gather_kernel,
        out_shape=jax.ShapeDtypeStruct((GROUP,) + x.shape, x.dtype),
        in_specs=any_spec(1),
        out_specs=pl.BlockSpec(memory_space=pl.ANY),
        scratch_shapes=[
            pltpu.SemaphoreType.DMA(Gather.sems),
            pltpu.SemaphoreType.DMA(Gather.sems),
            pltpu.SemaphoreType.DMA((1,)),
        ],
        compiler_params=params(cid, 16),
    )(x)


def swap_kernel(x, out, send, recv, own):
    here = Here()
    barrier(here, ALL, False)
    cps = []
    for m in ALL:
        c = rcopy(x.at[here.flip(m)], out.at[here.lo], send.at[m], recv.at[m], here.dev(m))
        c.start()
        cps.append(c)
    c = pltpu.make_async_copy(x.at[here.lo], out.at[here.lo], own)
    c.start()
    c.wait()
    for m in ALL:
        ref = out.at[here.flip(m)]
        rcopy(ref, ref, send.at[m], recv.at[m], here.dev(m)).wait_recv()
    for c in cps:
        c.wait_send()


def swap(x, cid):
    return pl.pallas_call(
        swap_kernel,
        out_shape=jax.ShapeDtypeStruct(x.shape, x.dtype),
        in_specs=any_spec(1),
        out_specs=pl.BlockSpec(memory_space=pl.ANY),
        scratch_shapes=[
            pltpu.SemaphoreType.DMA((GROUP,)),
            pltpu.SemaphoreType.DMA((GROUP,)),
            pltpu.SemaphoreType.DMA,
        ],
        compiler_params=params(cid, 16),
    )(x)


def pair_add(here, g, inbox, total, send, recv):
    cp = rcopy(g.at[1 - here.rep], inbox, send, recv, here.partner())
    cp.start()
    cp.wait()

    def body(r):
        total[r] = (g[here.rep, r].astype(F32) + inbox[r].astype(F32)).astype(BF)

    rowwise(inbox.shape[0], 16, body)


def send_home(here, total, out, send, recv, own):
    rows = out.shape[1]
    cps = []
    for m in ALL:
        at = total.at[pl.ds(pl.multiple_of(here.flip(m) * rows, rows), rows)]
        c = rcopy(at, out.at[here.lo], send.at[m], recv.at[m], here.dev(m))
        c.start()
        cps.append(c)
    at = total.at[pl.ds(pl.multiple_of(here.lo * rows, rows), rows)]
    c = pltpu.make_async_copy(at, out.at[here.lo], own)
    c.start()
    c.wait()

    def end():
        for m in ALL:
            ref = out.at[here.flip(m)]
            rcopy(ref, ref, send.at[m], recv.at[m], here.dev(m)).wait_recv()
        for c in cps:
            c.wait_send()

    return end


def mlp_home_kernel(g, out, inbox, total, psend, precv, send, recv, own):
    here = Here()
    barrier(here, ALL, True)
    pair_add(here, g, inbox, total, psend, precv)
    send_home(here, total, out, send, recv, own)()


def home_scratch(n, w):
    return [
        pltpu.VMEM((n, w), BF),
        pltpu.VMEM((n, w), BF),
        pltpu.SemaphoreType.DMA,
        pltpu.SemaphoreType.DMA,
        pltpu.SemaphoreType.DMA((GROUP,)),
        pltpu.SemaphoreType.DMA((GROUP,)),
        pltpu.SemaphoreType.DMA,
    ]


def mlp_home(g, cid):
    _, n, w = g.shape
    return pl.pallas_call(
        mlp_home_kernel,
        out_shape=jax.ShapeDtypeStruct((GROUP, n // GROUP, w), BF),
        in_specs=vmem_spec(1),
        out_specs=pl.BlockSpec(memory_space=pl.ANY),
        scratch_shapes=home_scratch(n, w),
        compiler_params=params(cid),
    )(g)


def scatter_kernel(a, b, aout, bout, *scratch):
    here = Here()
    barrier(here, TREE, False)
    n = len(scratch) // 2
    run_scatters([Scatter(here, a, scratch[:n]), Scatter(here, b, scratch[n:])], [aout, bout])


def scatter_two(a, b, cid):
    _, rows, d = a.shape
    return pl.pallas_call(
        scatter_kernel,
        out_shape=(jax.ShapeDtypeStruct((rows, d), F32),) * 2,
        in_specs=vmem_spec(2),
        out_specs=tuple(vmem_spec(2)),
        scratch_shapes=Scatter.scratch(rows, d) * 2,
        compiler_params=params(cid),
    )(a, b)


def back_kernel(dn, gout, gqkv, dn_out, gout_out, gqkv_out, *scratch):
    here = Here()
    barrier(here, ALL, True)
    n = len(Scatter.scratch(16, 128))
    s1, scratch = scratch[:n], scratch[n:]
    s2, scratch = scratch[:n], scratch[n:]
    (obox, osum, osend, orecv), scratch = scratch[:4], scratch[4:]
    pair_add(here, gqkv, *scratch[:4])
    end = send_home(here, scratch[1], gqkv_out, *scratch[4:])
    pair_add(here, gout, obox, osum, osend, orecv)
    sums = osum.reshape(GROUP, gout.shape[1] // GROUP, gout.shape[2])
    run_scatters([Scatter(here, dn, s1), Scatter(here, sums, s2)], [dn_out, gout_out])
    end()


def back(dn, gout, gqkv, cid):
    _, rows, d = dn.shape
    n, w = gqkv.shape[1:]
    on, od = gout.shape[1:]
    return pl.pallas_call(
        back_kernel,
        out_shape=(
            jax.ShapeDtypeStruct((rows, d), F32),
            jax.ShapeDtypeStruct((on // GROUP, od), F32),
            jax.ShapeDtypeStruct((GROUP, n // GROUP, w), BF),
        ),
        in_specs=vmem_spec(3),
        out_specs=(*vmem_spec(2), *any_spec(1)),
        scratch_shapes=[
            *Scatter.scratch(rows, d),
            *Scatter.scratch(on // GROUP, od),
            pltpu.VMEM((on, od), BF),
            pltpu.VMEM((on, od), BF),
            pltpu.SemaphoreType.DMA,
            pltpu.SemaphoreType.DMA,
            *home_scratch(n, w),
        ],
        compiler_params=params(cid),
    )(dn, gout, gqkv)


def normalize(inputs):
    centred = inputs - jnp.mean(inputs, -1, keepdims=True)
    inverse = lax.rsqrt(jnp.mean(centred * centred, -1, keepdims=True) + EPSILON)
    return (centred * inverse, inverse)


def normalize_back(grad_out, normed, inverse):
    return inverse * (
        grad_out
        - jnp.mean(grad_out, -1, keepdims=True)
        - normed * jnp.mean(grad_out * normed, -1, keepdims=True)
    )


def write_streams(streams, mixing, branch, out_weights):
    result = branch[:, None, :] * out_weights[None, :, None]
    for source in range(streams.shape[1]):
        result = result + streams[:, source, None, :] * mixing[source][None, :, None]
    return result


def write_back(grad_out, mixing):
    result = jnp.zeros_like(grad_out)
    for target in range(grad_out.shape[1]):
        result = result + grad_out[:, target, None, :] * mixing[:, target][None, :, None]
    return result


def mixing_grad(streams, grad_out, branch, grad_read):
    highest = lax.Precision.HIGHEST
    first = jnp.einsum("tjd,td->j", streams, grad_read, precision=highest)
    middle = jnp.einsum("tjd,tid->ji", streams, grad_out, precision=highest)
    final_cols = jnp.einsum("td,tid->i", branch, grad_out, precision=highest)
    return jnp.concatenate([first[:, None], middle, final_cols[:, None]], axis=1)


def slot_layout(lengths_row, capacity):
    seq_count = lengths_row.shape[-1]
    seq_ends = jnp.cumsum(lengths_row, axis=-1)
    slot_index = jnp.arange(capacity, dtype=jnp.int32)
    segment = jnp.sum((slot_index[:, None] >= seq_ends[..., None, :]).astype(jnp.int32), axis=-1)
    seq_starts = seq_ends - lengths_row
    chosen = (segment[..., None] == jnp.arange(seq_count, dtype=jnp.int32)).astype(jnp.int32)
    start_of = jnp.sum(chosen * seq_starts[..., None, :], axis=-1)
    is_live = segment < seq_count
    segment = jnp.where(is_live, segment, seq_count + slot_index)
    position = jnp.where(is_live, slot_index - start_of, 0)
    return (segment, position)


def rope_tables(position, head_width):
    half_width = head_width // 2
    frequency = jnp.exp(
        jnp.arange(half_width, dtype=jnp.float32) * (-2.0 * math.log(10000.0) / head_width)
    )
    angles = position.astype(jnp.float32)[..., None] * frequency
    return (jnp.cos(angles), jnp.sin(angles))


def rotate(inputs, cosine, sine_table):
    half_width = inputs.shape[-1] // 2
    first = inputs[..., :half_width]
    second = inputs[..., half_width:]
    return jnp.concatenate(
        [first * cosine - second * sine_table, second * cosine + first * sine_table], axis=-1
    )


def dot(a, b):
    return jnp.dot(a, b, preferred_element_type=F32)


def dot_t(a, b):
    return lax.dot_general(a, b, CONTRACT_LAST, preferred_element_type=F32)


def t_dot(a, b):
    return lax.dot_general(a, b, CONTRACT_FIRST, preferred_element_type=F32)


def shards(streams, cotangent, deal, lengths, mix_attn, mix_mlp, w_qkv, w_out, w_gu, w_down):
    tokens, stream_count, width = streams.shape
    shard_size = lax.axis_size("shard")
    hi = shard_size // GROUP
    hi_groups = [[h * GROUP + l for h in range(hi)] for l in range(GROUP)]
    shard = lax.axis_index("shard")
    my_hi = shard // GROUP
    bin_count = shard_size // 4
    my_bins = bin_count // hi
    per_bin = tokens // bin_count
    capacity = per_bin * shard_size
    ff = w_down.shape[1]

    def swap_hi(rows):
        if hi == 1:
            return rows
        return lax.all_to_all(rows, "shard", 0, 0, axis_index_groups=hi_groups, tiled=True)

    def to_bins(rows):
        return swap_hi(rows).reshape(hi, my_bins, per_bin, -1).swapaxes(0, 1).reshape(tokens, -1)

    def from_bins(rows):
        return swap_hi(rows.reshape(my_bins, hi, per_bin, -1).swapaxes(0, 1).reshape(tokens, -1))

    def gather_hi(rows):
        if hi == 1:
            return rows[None]
        return lax.all_gather(rows, "shard", axis_index_groups=hi_groups)

    def sum_hi(rows):
        if hi == 1:
            return rows[0]
        return lax.psum_scatter(rows, "shard", axis_index_groups=hi_groups)

    sorter = (jnp.arange(tokens, dtype=jnp.int32)[:, None] == deal[None, :]).astype(BF)

    streams_in = streams.astype(F32)
    grad_new = cotangent.astype(F32)
    read_attn = jnp.sum(streams_in * mix_attn[:, 0][None, :, None], axis=1)
    normed_attn, inverse_attn = normalize(read_attn)
    low_attn = to_bins(dot(sorter, normed_attn.astype(BF)).astype(BF))
    low_grad_mlp = jnp.sum(grad_new * mix_mlp[:, stream_count + 1][None, :, None], axis=1).astype(BF)

    n1g, dy2g, qkvs, outs, gus, dns = front(
        low_attn, low_grad_mlp, gather_hi(w_qkv), gather_hi(w_out).reshape(-1, width), gather_hi(w_gu), gather_hi(w_down), 1
    )
    rows = w_qkv.shape[0]
    n1g = n1g.reshape(GROUP * tokens, width)
    dy2g = dy2g.reshape(GROUP * tokens, width)
    qkvs = qkvs.reshape(width, 3 * HEAD_DIM)
    outs = outs.reshape(2, GROUP, hi, rows, width).swapaxes(1, 2).reshape(width, width)
    gus = gus.reshape(width, 2 * ff // GROUP)
    dns = dns.reshape(width, ff // GROUP)

    bins = lax.axis_index("rep") * bin_count + my_hi * my_bins
    lengths_here = lax.dynamic_slice_in_dim(lengths, bins, my_bins, 0)
    segment, position = slot_layout(lengths_here, capacity)

    def local_order(x):
        return x.reshape(my_bins, hi, GROUP, per_bin).swapaxes(1, 2).reshape(my_bins, capacity)

    segment, position = local_order(segment), local_order(position)
    cosine, sine = rope_tables(position, HEAD_DIM)
    slots = GROUP * tokens // my_bins // GROUP

    def by_bin(x):
        return x.reshape(GROUP, my_bins, slots, -1).swapaxes(0, 1).reshape(my_bins, capacity, -1)

    def by_token(x):
        return x.reshape(my_bins, GROUP, slots, -1).swapaxes(0, 1).reshape(GROUP, tokens, -1)

    scale = 1.0 / math.sqrt(HEAD_DIM)
    qkv = by_bin(dot(n1g, qkvs).astype(BF))
    queries = rotate(qkv[..., :HEAD_DIM].astype(F32), cosine, sine).astype(BF)
    keys = rotate(qkv[..., HEAD_DIM : 2 * HEAD_DIM].astype(F32), cosine, sine).astype(BF)
    values = qkv[..., 2 * HEAD_DIM :]
    seen = (segment[:, :, None] == segment[:, None, :]) & (position[:, None, :] <= position[:, :, None])
    scores = jnp.einsum("bqd,bkd->bqk", queries, keys, preferred_element_type=F32) * scale
    scores = jnp.where(seen, scores, -1e30)
    peak = jnp.max(scores, -1, keepdims=True)
    weights = jnp.exp(scores - peak)
    probability = weights / jnp.sum(weights, -1, keepdims=True)
    low_probability = probability.astype(BF)
    attended = jnp.einsum("bqk,bkd->bqd", low_probability, values, preferred_element_type=F32).astype(BF)
    home = swap(by_token(attended), 2)
    attn_sorted = from_bins(home.swapaxes(0, 1).reshape(tokens, width))
    attn_rows = t_dot(sorter, attn_sorted).astype(BF)

    branch_attn = dot(attn_rows, outs)
    middle_streams = write_streams(
        streams_in, mix_attn[:, 1 : 1 + stream_count], branch_attn, mix_attn[:, stream_count + 1]
    )
    read_mlp = jnp.sum(middle_streams * mix_mlp[:, 0][None, :, None], axis=1)
    normed_mlp, inverse_mlp = normalize(read_mlp)
    n2g = gather(normed_mlp.astype(BF), 3).reshape(GROUP * tokens, width)
    gate_up = dot(n2g, gus)
    up_part = gate_up[:, : ff // GROUP]
    gate_part = gate_up[:, ff // GROUP :]
    sigmoid = jax.nn.sigmoid(gate_part)
    silu_value = gate_part * sigmoid
    hidden = (silu_value * up_part).astype(BF)
    y2_part = dot_t(hidden, dns).astype(BF).reshape(GROUP, tokens, width)
    grad_hidden = dot(dy2g, dns)
    grad_up = grad_hidden * silu_value
    grad_gate = grad_hidden * up_part * sigmoid * (1.0 + gate_part * (1.0 - sigmoid))
    grad_gate_up = jnp.concatenate([grad_up, grad_gate], axis=1).astype(BF)
    dn2_part = dot_t(grad_gate_up, gus).astype(BF).reshape(GROUP, tokens, width)
    branch_mlp, grad_normed_mlp = scatter_two(y2_part, dn2_part, 4)
    grad_read_mlp = normalize_back(grad_normed_mlp, normed_mlp, inverse_mlp)
    new_streams = write_streams(
        middle_streams, mix_mlp[:, 1 : 1 + stream_count], branch_mlp, mix_mlp[:, stream_count + 1]
    )
    mix_grad_mlp = mixing_grad(middle_streams, grad_new, branch_mlp, grad_read_mlp)
    grad_middle = (
        write_back(grad_new, mix_mlp[:, 1 : 1 + stream_count])
        + grad_read_mlp[:, None, :] * mix_mlp[:, 0][None, :, None]
    )
    g_mlp = jnp.concatenate([t_dot(n2g, grad_gate_up), t_dot(dy2g, hidden)], axis=1).astype(BF)

    def row_order(x):
        return x.reshape(2, hi, GROUP, rows, -1).swapaxes(1, 2).reshape(2, GROUP * hi * rows, -1)

    def own_rows(x):
        x = x.astype(F32).reshape(GROUP, hi, rows, -1).transpose(1, 2, 0, 3)
        return sum_hi(x.reshape(hi, rows, -1)).reshape(rows, GROUP, -1)

    g_mlp = own_rows(mlp_home(row_order(g_mlp), 5))
    low_grad_attn = jnp.sum(grad_middle * mix_attn[:, stream_count + 1][None, :, None], axis=1).astype(BF)
    grad_attn = dot_t(low_grad_attn, outs).astype(BF)
    grad_sorted = to_bins(dot(sorter, grad_attn).astype(BF))
    d_out = by_bin(swap(grad_sorted.reshape(tokens, GROUP, HEAD_DIM).swapaxes(0, 1), 6))
    grad_values = jnp.einsum("bqk,bqd->bkd", low_probability, d_out, preferred_element_type=F32)
    grad_probs = jnp.einsum("bqd,bkd->bqk", d_out, values, preferred_element_type=F32)
    shared = jnp.sum(grad_probs * probability, -1, keepdims=True)
    grad_scores = (probability * (grad_probs - shared)).astype(BF)
    grad_query = jnp.einsum("bqk,bkd->bqd", grad_scores, keys, preferred_element_type=F32) * scale
    grad_keys = jnp.einsum("bqk,bqd->bkd", grad_scores, queries, preferred_element_type=F32) * scale
    grad_qkv = by_token(
        jnp.concatenate(
            [rotate(grad_query, cosine, -sine), rotate(grad_keys, cosine, -sine), grad_values], axis=-1
        ).astype(BF)
    ).reshape(GROUP * tokens, 3 * HEAD_DIM)
    dn1_part = dot_t(grad_qkv, qkvs).astype(BF).reshape(GROUP, tokens, width)
    g_qkv = row_order(t_dot(n1g, grad_qkv).astype(BF))
    g_out = row_order(t_dot(attn_rows, low_grad_attn).astype(BF))
    dn1, g_out, g_qkv = back(dn1_part, g_out, g_qkv, 7)
    g_out = sum_hi(g_out.reshape(hi, rows, width))
    g_qkv = own_rows(g_qkv)
    dn1 = lax.dot_general(
        sorter.astype(F32), from_bins(dn1), CONTRACT_FIRST, precision=lax.Precision.HIGHEST, preferred_element_type=F32
    )
    grad_read_attn = normalize_back(dn1, normed_attn, inverse_attn)
    mix_grad_attn = mixing_grad(streams_in, grad_middle, branch_attn, grad_read_attn)
    d_streams = (
        write_back(grad_middle, mix_attn[:, 1 : 1 + stream_count])
        + grad_read_attn[:, None, :] * mix_attn[:, 0][None, :, None]
    )
    g_mix_attn, g_mix_mlp = lax.psum((mix_grad_attn, mix_grad_mlp), ("rep", "shard"))
    block = ff // GROUP
    return (
        new_streams,
        d_streams,
        g_mix_attn,
        g_mix_mlp,
        g_qkv.reshape(rows, GROUP, 3, HEAD_DIM).swapaxes(1, 2).reshape(rows, -1),
        g_out,
        jnp.concatenate([g_mlp[:, :, :block].reshape(rows, ff), g_mlp[:, :, block : 2 * block].reshape(rows, ff)], axis=1),
        g_mlp[:, :, 2 * block :].reshape(rows, ff),
    )


def solution(mesh):
    both = ("rep", "shard")
    return jax.shard_map(
        shards,
        mesh=mesh,
        in_specs=(
            P(both, None, None),
            P(both, None, None),
            P(both),
            P(),
            P(),
            P(),
            P(both, None),
            P(both, None),
            P(both, None),
            P(both, None),
        ),
        out_specs=(
            P(both, None, None),
            P(both, None, None),
            P(),
            P(),
            P(both, None),
            P(both, None),
            P(both, None),
            P(both, None),
        ),
        check_vma=False,
    )
```

```python
import functools
import math

import jax
import jax.numpy as jnp
from jax import lax
from jax.experimental import pallas as pl
from jax.experimental.pallas import tpu as pltpu
from jax.sharding import PartitionSpec as P

HEADS = 16
HEAD_DIM = 128
GROUP = 16
EPSILON = 1e-05
MESH = pl.DeviceIdType.MESH
CONTRACT_LAST = (((1,), (1,)), ((), ()))
CONTRACT_FIRST = (((0,), (0,)), ((), ()))
MIB = 1 << 20
BF = jnp.bfloat16
F32 = jnp.float32


class Here:
    def __init__(self):
        self.rep = lax.axis_index("rep")
        shard = lax.axis_index("shard")
        self.lo = shard % GROUP
        self.base = shard - self.lo
        self.bits = [(self.lo // (1 << i)) % 2 for i in range(4)]

    def flip(self, mask):
        out = self.lo
        for i in range(4):
            if mask & (1 << i):
                out = out + (1 << i) * (1 - 2 * self.bits[i])
        return out

    def dev(self, mask):
        return (self.rep, self.base + self.flip(mask))

    def partner(self):
        return (1 - self.rep, self.base + self.lo)


def barrier(here, masks, partner):
    sem = pltpu.get_barrier_semaphore()
    targets = [here.dev(m) for m in masks]
    if partner:
        targets.append(here.partner())
    for t in targets:
        pl.semaphore_signal(sem, inc=1, device_id=t, device_id_type=MESH)
    pl.semaphore_wait(sem, len(targets))


TREE = (1, 2, 4, 8, 12)
ALL = tuple(range(1, GROUP))


def rcopy(src, dst, send, recv, dev):
    return pltpu.make_async_remote_copy(
        src_ref=src, dst_ref=dst, send_sem=send, recv_sem=recv, device_id=dev, device_id_type=MESH
    )


class Gather:
    sems = (4, 7)

    def __init__(self, here, x, out, send, recv):
        self.here, self.x, self.out, self.send, self.recv = here, x, out, send, recv
        self.half = x.shape[0] // 2
        self.sent = []

    def _go(self, block, part, j, slot, mask):
        ref = self.out.at[block, pl.ds(part * self.half, self.half)]
        c = rcopy(ref, ref, self.send.at[j, slot], self.recv.at[j, slot], self.here.dev(mask))
        c.start()
        self.sent.append(c)

    def _wait(self, j, slot, block, part):
        ref = self.out.at[block, pl.ds(part * self.half, self.half)]
        rcopy(ref, ref, self.send.at[j, slot], self.recv.at[j, slot], self.here.dev(1)).wait_recv()

    def begin(self, own_sem):
        own = pltpu.make_async_copy(self.x, self.out.at[self.here.lo], own_sem)
        own.start()
        for j in (1, 3, 2):
            c = rcopy(self.x, self.out.at[self.here.lo], self.send.at[j, 6], self.recv.at[j, 6], self.here.dev(4 * j))
            c.start()
            self.sent.append(c)
        own.wait()
        self.spread(0)

    def spread(self, j):
        b = self.here.flip(4 * j)
        if j:
            ref = self.out.at[b]
            rcopy(ref, ref, self.send.at[j, 6], self.recv.at[j, 6], self.here.dev(4)).wait_recv()
        self._go(b, 0, j, 0, 1)
        self._go(b, 1, j, 1, 2)
        self._go(b, 0, j, 2, 2)
        self._go(b, 1, j, 3, 1)

    def forward(self, j):
        m = 4 * j
        self._wait(j, 0, self.here.flip(m ^ 1), 0)
        self._go(self.here.flip(m ^ 1), 0, j, 4, 2)
        self._wait(j, 1, self.here.flip(m ^ 2), 1)
        self._go(self.here.flip(m ^ 2), 1, j, 5, 1)

    def settle(self, j):
        m = 4 * j
        self._wait(j, 2, self.here.flip(m ^ 2), 0)
        self._wait(j, 3, self.here.flip(m ^ 1), 1)
        self._wait(j, 4, self.here.flip(m ^ 3), 0)
        self._wait(j, 5, self.here.flip(m ^ 3), 1)

    def end(self):
        for c in self.sent:
            c.wait_send()

    ORDER = (0, 1, 3, 2)


def rowwise(n, step, body):
    def at(i, carry):
        body(pl.ds(pl.multiple_of(i * step, step), step))
        return carry

    lax.fori_loop(0, n // step, at, 0)


class Scatter:
    sems = (4, 7)

    @staticmethod
    def scratch(rows, d):
        h = rows // 2
        return [
            pltpu.VMEM((4, 4, h, d), BF),
            pltpu.VMEM((4, 2, h, d), BF),
            pltpu.VMEM((3, rows, d), BF),
            pltpu.SemaphoreType.DMA(Scatter.sems),
            pltpu.SemaphoreType.DMA(Scatter.sems),
        ]

    def __init__(self, here, part, scratch):
        self.here, self.part = here, part
        self.first, self.second, self.zin, self.send, self.recv = scratch
        self.rows = part.shape[1]
        self.half = self.rows // 2
        self.sent = []

    def _copy(self, j, slot, src, dst, mask):
        return rcopy(src, dst, self.send.at[j, slot], self.recv.at[j, slot], self.here.dev(mask))

    def _go(self, *a):
        c = self._copy(*a)
        c.start()
        self.sent.append(c)

    def _piece(self, mask, part):
        return self.part.at[self.here.flip(mask), pl.ds(part * self.half, self.half)]

    def start(self, j):
        m = 4 * j
        self._go(j, 1, self._piece(m ^ 3, 0), self.first.at[j, 1], 2)
        self._go(j, 3, self._piece(m ^ 3, 1), self.first.at[j, 3], 1)
        self._go(j, 0, self._piece(m ^ 2, 0), self.first.at[j, 0], 2)
        self._go(j, 2, self._piece(m ^ 1, 1), self.first.at[j, 2], 1)

    def cross(self, j):
        m = 4 * j
        h = self.half
        for slot, mask, part, to in ((1, 1, 0, 1), (3, 2, 1, 2)):
            self._copy(j, slot, self.first.at[j, slot], self.first.at[j, slot], 1).wait_recv()
            own = self._piece(m ^ mask, part)

            def body(r, own=own, slot=slot):
                own[r] = (own[r].astype(F32) + self.first[j, slot, r].astype(F32)).astype(BF)

            rowwise(h, 16, body)
            self._go(j, 4 + part, own, self.second.at[j, part], to)

    def finish(self, j, out=None):
        m = 4 * j
        h = self.half
        for part, slot in ((0, 0), (1, 2)):
            self._copy(j, slot, self.first.at[j, slot], self.first.at[j, slot], 1).wait_recv()
            self._copy(j, 4 + part, self.second.at[j, part], self.second.at[j, part], 1).wait_recv()
        if out is not None:
            for k in (1, 2, 3):
                self._copy(k, 6, self.zin.at[k - 1], self.zin.at[k - 1], 4).wait_recv()
        for part, slot in ((0, 0), (1, 2)):
            own = self._piece(m, part)

            def body(r, own=own, part=part, slot=slot):
                total = own[r].astype(F32) + self.first[j, slot, r].astype(F32) + self.second[j, part, r].astype(F32)
                at = pl.ds(part * h + r.start, r.size)
                if out is None:
                    own[r] = total.astype(BF)
                else:
                    for k in (1, 2, 3):
                        total = total + self.zin[k - 1, at].astype(F32)
                    out[at] = total.astype(out.dtype)

            rowwise(h, 16, body)
        if out is None:
            self._go(j, 6, self.part.at[self.here.flip(m)], self.zin.at[j - 1], m)

    def end(self):
        for c in self.sent:
            c.wait_send()

    ORDER = (2, 3, 1, 0)


def run_scatters(scatters, outs):
    for i, (s, out) in enumerate(zip(scatters, outs)):
        order = s.ORDER
        if i == 0:
            s.start(order[0])
        s.start(order[1])
        s.cross(order[0])
        s.start(order[2])
        s.cross(order[1])
        s.finish(order[0])
        s.start(order[3])
        s.cross(order[2])
        s.finish(order[1])
        if i + 1 < len(scatters):
            scatters[i + 1].start(order[0])
        s.cross(order[3])
        s.finish(order[2])
        s.finish(order[3], out)
    for s in scatters:
        s.end()


def any_spec(n):
    return [pl.BlockSpec(memory_space=pl.ANY)] * n


def vmem_spec(n):
    return [pl.BlockSpec(memory_space=pltpu.VMEM)] * n


def params(cid, mib=60):
    return pltpu.CompilerParams(collective_id=cid, has_side_effects=True, vmem_limit_bytes=mib * MIB)


def exchange_columns(here, src, dst, width, cols, send, recv, own_sem):
    copies = []
    own = []
    for i, c in enumerate(cols):
        for m in range(GROUP):
            peer = here.flip(m)
            at = src.at[:, :, pl.ds(pl.multiple_of(c + peer * width, 128), width)]
            to = dst.at[here.rep, :, here.lo, :, pl.ds(i * width, width)]
            if m == 0:
                cp = pltpu.make_async_copy(at, to, own_sem.at[i])
                cp.start()
                own.append(cp)
            else:
                cp = rcopy(at, to, send.at[i, m], recv.at[i, m], here.dev(m))
                cp.start()
                copies.append(cp)

    def arrive():
        for cp in own:
            cp.wait()
        for i, c in enumerate(cols):
            for m in ALL:
                to = dst.at[here.rep, :, here.flip(m), :, pl.ds(i * width, width)]
                rcopy(to, to, send.at[i, m], recv.at[i, m], here.dev(m)).wait_recv()

    def end():
        for cp in copies:
            cp.wait_send()

    return arrive, end


def front_kernel(
    n1, dy2, wqkv, wout, wgu, wdn,
    n1g, dy2g, qkvs, outs, gus, dns,
    gsend, grecv, own, csend, crecv, cown, psend, precv,
):
    here = Here()
    barrier(here, ALL, True)
    q = exchange_columns(here, wqkv, qkvs, 128, (0, 2048, 4096), csend.at[0], crecv.at[0], cown.at[0])
    half = wgu.shape[2] // 2
    ga = Gather(here, n1, n1g, gsend.at[0], grecv.at[0])
    gb = Gather(here, dy2, dy2g, gsend.at[1], grecv.at[1])
    gc = Gather(here, wout, outs.at[here.rep], gsend.at[2], grecv.at[2])
    ga.begin(own.at[0])
    u = exchange_columns(here, wgu, gus, half // GROUP, (0, half), csend.at[1], crecv.at[1], cown.at[1])
    d = exchange_columns(here, wdn, dns, half // GROUP, (0,), csend.at[2], crecv.at[2], cown.at[2])
    gathers = [ga, gb, gc]
    for i, g in enumerate(gathers):
        order = g.ORDER
        g.spread(order[1])
        g.forward(order[0])
        g.spread(order[2])
        g.forward(order[1])
        g.spread(order[3])
        g.forward(order[2])
        if i + 1 < len(gathers):
            gathers[i + 1].begin(own.at[i + 1])
        g.forward(order[3])
    passes = []
    for i, ((arrive, _), dst) in enumerate(zip((q, u, d), (qkvs, gus, dns))):
        arrive()
        cp = rcopy(dst.at[here.rep], dst.at[here.rep], psend.at[i], precv.at[i], here.partner())
        cp.start()
        passes.append((cp, dst))
    for g in gathers:
        for j in range(4):
            g.settle(j)
    cp = rcopy(outs.at[here.rep], outs.at[here.rep], psend.at[3], precv.at[3], here.partner())
    cp.start()
    passes.append((cp, outs))
    for i, (cp, dst) in enumerate(passes):
        cp.wait_send()
        other = dst.at[1 - here.rep]
        rcopy(other, other, psend.at[i], precv.at[i], here.partner()).wait_recv()
    for g in gathers:
        g.end()
    for _, end in (q, u, d):
        end()


def front(n1, dy2, wqkv, wout, wgu, wdn, cid):
    hi, rows, _ = wqkv.shape
    d = n1.shape[1]
    ff = wdn.shape[2]
    shape = lambda *s: jax.ShapeDtypeStruct(s, BF)
    out_rows = wout.shape[0]
    return pl.pallas_call(
        front_kernel,
        out_shape=(
            shape(GROUP, *n1.shape),
            shape(GROUP, *dy2.shape),
            shape(2, hi, GROUP, rows, 3 * HEAD_DIM),
            shape(2, GROUP, out_rows, wout.shape[1]),
            shape(2, hi, GROUP, rows, 2 * ff // GROUP),
            shape(2, hi, GROUP, rows, ff // GROUP),
        ),
        in_specs=any_spec(6),
        out_specs=any_spec(6),
        scratch_shapes=[
            pltpu.SemaphoreType.DMA((3,) + Gather.sems),
            pltpu.SemaphoreType.DMA((3,) + Gather.sems),
            pltpu.SemaphoreType.DMA((3,)),
            pltpu.SemaphoreType.DMA((3, 3, GROUP)),
            pltpu.SemaphoreType.DMA((3, 3, GROUP)),
            pltpu.SemaphoreType.DMA((3, 3)),
            pltpu.SemaphoreType.DMA((4,)),
            pltpu.SemaphoreType.DMA((4,)),
        ],
        compiler_params=params(cid, 16),
    )(n1, dy2, wqkv, wout, wgu, wdn)


def swap_kernel(x, out, send, recv, own):
    here = Here()
    barrier(here, ALL, False)

    def block(ref, l):
        if len(ref.shape) == 3:
            return ref.at[l]
        return ref.at[:, pl.ds(pl.multiple_of(l * HEAD_DIM, HEAD_DIM), HEAD_DIM)]

    cps = []
    for m in ALL:
        c = rcopy(block(x, here.flip(m)), block(out, here.lo), send.at[m], recv.at[m], here.dev(m))
        c.start()
        cps.append(c)
    c = pltpu.make_async_copy(block(x, here.lo), block(out, here.lo), own)
    c.start()
    c.wait()
    for m in ALL:
        ref = block(out, here.flip(m))
        rcopy(ref, ref, send.at[m], recv.at[m], here.dev(m)).wait_recv()
    for c in cps:
        c.wait_send()


def swap(x, cid):
    if x.ndim == 3:
        shape = (x.shape[1], GROUP * HEAD_DIM)
    else:
        shape = (GROUP, x.shape[0], HEAD_DIM)
    return pl.pallas_call(
        swap_kernel,
        out_shape=jax.ShapeDtypeStruct(shape, x.dtype),
        in_specs=any_spec(1),
        out_specs=pl.BlockSpec(memory_space=pl.ANY),
        scratch_shapes=[
            pltpu.SemaphoreType.DMA((GROUP,)),
            pltpu.SemaphoreType.DMA((GROUP,)),
            pltpu.SemaphoreType.DMA,
        ],
        compiler_params=params(cid, 16),
    )(x)


def pair_add(here, g, inbox, send, recv):
    cp = rcopy(g.at[1 - here.rep], inbox, send, recv, here.partner())
    cp.start()
    cp.wait()

    def body(r):
        g[here.rep, r] = (g[here.rep, r].astype(F32) + inbox[r].astype(F32)).astype(BF)

    rowwise(inbox.shape[0], 16, body)


def send_home(here, total, out, send, recv, own):
    _, hi, rows, _ = out.shape

    def block(h, m):
        at = (h * GROUP + here.flip(m)) * rows
        return total.at[pl.ds(pl.multiple_of(at, rows), rows)]

    cps = []
    owns = []
    for h in range(hi):
        for m in ALL:
            c = rcopy(block(h, m), out.at[here.lo, h], send.at[h, m], recv.at[h, m], here.dev(m))
            c.start()
            cps.append(c)
        c = pltpu.make_async_copy(block(h, 0), out.at[here.lo, h], own.at[h])
        c.start()
        owns.append(c)

    def end():
        for c in owns:
            c.wait()
        for h in range(hi):
            for m in ALL:
                ref = out.at[here.flip(m), h]
                rcopy(ref, ref, send.at[h, m], recv.at[h, m], here.dev(m)).wait_recv()
        for c in cps:
            c.wait_send()

    return end


def home_sems(hi):
    return [
        pltpu.SemaphoreType.DMA((hi, GROUP)),
        pltpu.SemaphoreType.DMA((hi, GROUP)),
        pltpu.SemaphoreType.DMA((hi,)),
    ]


def mlp_kernel(
    n2, dy2g_in, wgu_in, wdn_in, dn2, y2p, home,
    n2g, dy2g, wgu, wdn, part, hidden, dgu, y2s, grads, inbox,
    gsend, grecv, own, load, y2sem, psend, precv, hsend, hrecv, hown, *scratch,
):
    here = Here()
    barrier(here, ALL, True)
    g = Gather(here, n2, n2g, gsend, grecv)
    rs = Scatter(here, part, scratch)
    g.begin(own)
    loads = []
    for i, (src, dst) in enumerate(((wgu_in, wgu), (wdn_in, wdn), (dy2g_in, dy2g))):
        c = pltpu.make_async_copy(src, dst, load.at[i])
        c.start()
        loads.append(c)
    width, ff = wdn.shape
    tokens = n2.shape[0]
    group_rows = 4 * tokens
    step = 256
    y2copies = []

    def compute(j):
        first = here.flip(4 * j) - here.lo % 4
        blocks = pl.ds(first, 4)
        if not y2copies:
            for c in loads:
                c.wait()

        def gates(k, carry):
            up_at = pl.ds(pl.multiple_of(k * step, step), step)
            gate_at = pl.ds(pl.multiple_of(ff + k * step, step), step)
            x = n2g[blocks].reshape(group_rows, width)
            up = dot(x, wgu[:, up_at])
            gate = dot(x, wgu[:, gate_at])
            dh = dot(dy2g[blocks].reshape(group_rows, width), wdn[:, up_at])
            sigmoid = 1.0 / (1.0 + jnp.exp(-gate))
            silu = gate * sigmoid
            hidden[blocks, :, up_at] = (silu * up).astype(BF).reshape(4, tokens, step)
            dgu[blocks, :, up_at] = (dh * silu).astype(BF).reshape(4, tokens, step)
            dgu[blocks, :, gate_at] = (
                (dh * up * sigmoid * (1.0 + gate * (1.0 - sigmoid))).astype(BF).reshape(4, tokens, step)
            )
            return carry

        lax.fori_loop(0, ff // step, gates, 0)
        if y2copies:
            y2copies[-1].wait()

        def outputs(k, carry):
            at = pl.ds(pl.multiple_of(k * step, step), step)
            h = hidden[blocks].reshape(group_rows, ff)
            y2s[:, :, at] = dot_t(h, wdn[at, :]).astype(BF).reshape(4, tokens, step)
            d = dgu[blocks].reshape(group_rows, 2 * ff)
            part[blocks, :, at] = dot_t(d, wgu[at, :]).astype(BF).reshape(4, tokens, step)
            return carry

        lax.fori_loop(0, width // step, outputs, 0)
        c = pltpu.make_async_copy(y2s, y2p.at[blocks], y2sem.at[len(y2copies)])
        c.start()
        y2copies.append(c)

    half = width // 2
    chunks = half // step

    def weight_grads(which, k):
        cols = pl.ds(pl.multiple_of(which * half + k * step, step), step)
        rows = pl.ds(pl.multiple_of(k * step, step), step)
        x = n2g[:, :, cols].reshape(GROUP * tokens, step)
        grads[which, rows, : 2 * ff] = t_dot(x, dgu[...].reshape(GROUP * tokens, 2 * ff)).astype(BF)
        x = dy2g[:, :, cols].reshape(GROUP * tokens, step)
        grads[which, rows, 2 * ff :] = t_dot(x, hidden[...].reshape(GROUP * tokens, ff)).astype(BF)

    def pass_chunk(k):
        rows = pl.ds(pl.multiple_of(k * step, step), step)
        return rcopy(grads.at[1 - here.rep, rows], inbox.at[rows], psend.at[k], precv.at[k], here.partner())

    o = g.ORDER
    g.spread(o[1])
    g.forward(o[0])
    g.settle(o[0])
    compute(o[0])
    rs.start(o[0])
    g.spread(o[2])
    g.forward(o[1])
    g.settle(o[1])
    compute(o[1])
    rs.start(o[1])
    g.spread(o[3])
    g.forward(o[2])
    rs.cross(o[0])
    g.settle(o[2])
    compute(o[2])
    rs.start(o[2])
    g.forward(o[3])
    rs.cross(o[1])
    g.settle(o[3])
    rs.finish(o[1])
    compute(o[3])
    rs.start(o[3])
    rs.cross(o[2])
    rs.finish(o[2])

    def other_half(k, carry):
        weight_grads(1 - here.rep, k)
        pass_chunk(k).start()
        return carry

    lax.fori_loop(0, chunks, other_half, 0)
    rs.cross(o[3])
    rs.finish(o[3])

    def own_half(k, carry):
        weight_grads(here.rep, k)
        return carry

    lax.fori_loop(0, chunks, own_half, 0)

    def add(k, carry):
        pass_chunk(k).wait()

        def rows_add(i, carry):
            r = pl.ds(pl.multiple_of(k * step + i * 16, 16), 16)
            grads[here.rep, r] = (grads[here.rep, r].astype(F32) + inbox[r].astype(F32)).astype(BF)
            return carry

        return lax.fori_loop(0, step // 16, rows_add, carry)

    lax.fori_loop(0, chunks, add, 0)
    finish = send_home(here, grads.at[here.rep], home, hsend, hrecv, hown)
    rs.finish(0, dn2)
    y2copies[-1].wait()
    finish()
    g.end()
    rs.end()


def mlp(n2, dy2g, wgu, wdn, hi, cid):
    tokens, width = n2.shape
    ff = wdn.shape[1]
    half = width // 2
    blocks = (GROUP, tokens)
    return pl.pallas_call(
        mlp_kernel,
        out_shape=(
            jax.ShapeDtypeStruct((tokens, width), F32),
            jax.ShapeDtypeStruct((*blocks, width), BF),
            jax.ShapeDtypeStruct((GROUP, hi, half // (hi * GROUP), 3 * ff), BF),
        ),
        in_specs=[*vmem_spec(1), *any_spec(3)],
        out_specs=(*vmem_spec(1), *any_spec(2)),
        scratch_shapes=[
            pltpu.VMEM((*blocks, width), BF),
            pltpu.VMEM((*blocks, width), BF),
            pltpu.VMEM(wgu.shape, BF),
            pltpu.VMEM(wdn.shape, BF),
            pltpu.VMEM((*blocks, width), BF),
            pltpu.VMEM((*blocks, ff), BF),
            pltpu.VMEM((*blocks, 2 * ff), BF),
            pltpu.VMEM((4, tokens, width), BF),
            pltpu.VMEM((2, half, 3 * ff), BF),
            pltpu.VMEM((half, 3 * ff), BF),
            pltpu.SemaphoreType.DMA(Gather.sems),
            pltpu.SemaphoreType.DMA(Gather.sems),
            pltpu.SemaphoreType.DMA,
            pltpu.SemaphoreType.DMA((3,)),
            pltpu.SemaphoreType.DMA((4,)),
            pltpu.SemaphoreType.DMA((half // 256,)),
            pltpu.SemaphoreType.DMA((half // 256,)),
            *home_sems(hi),
            *Scatter.scratch(tokens, width),
        ],
        compiler_params=params(cid, 63),
        cost_estimate=pl.CostEstimate(
            flops=2 * GROUP * tokens * width * ff * 9, bytes_accessed=60 * MIB, transcendentals=0
        ),
    )(n2, dy2g, wgu, wdn)


def back_kernel(dn_in, y2_in, gout_in, gqkv, dn_out, y2_out, gout_out, gqkv_out, dn, y2, gout, load, *scratch):
    here = Here()
    barrier(here, ALL, True)
    loads = []
    for i, (src, dst) in enumerate(((gout_in, gout), (dn_in, dn), (y2_in, y2))):
        c = pltpu.make_async_copy(src, dst, load.at[i])
        c.start()
        loads.append(c)
    n = len(Scatter.scratch(16, 128))
    s1, scratch = scratch[:n], scratch[n:]
    s2, scratch = scratch[:n], scratch[n:]
    s3, scratch = scratch[:n], scratch[n:]
    (obox, osend, orecv), scratch = scratch[:3], scratch[3:]
    pair_add(here, gqkv, *scratch[:3])
    end = send_home(here, gqkv.at[here.rep], gqkv_out, *scratch[3:])
    for c in loads:
        c.wait()
    pair_add(here, gout, obox, osend, orecv)
    sums = gout.reshape(2, GROUP, gout.shape[1] // GROUP, gout.shape[2]).at[here.rep]
    run_scatters(
        [Scatter(here, dn, s1), Scatter(here, y2, s2), Scatter(here, sums, s3)], [dn_out, y2_out, gout_out]
    )
    end()


def back(dn, y2, gout, gqkv, hi, cid):
    _, rows, d = dn.shape
    n, w = gqkv.shape[1:]
    on, od = gout.shape[1:]
    return pl.pallas_call(
        back_kernel,
        out_shape=(
            jax.ShapeDtypeStruct((rows, d), F32),
            jax.ShapeDtypeStruct((rows, d), F32),
            jax.ShapeDtypeStruct((on // GROUP, od), F32),
            jax.ShapeDtypeStruct((GROUP, hi, n // (hi * GROUP), w), BF),
        ),
        in_specs=[*any_spec(3), *vmem_spec(1)],
        out_specs=(*vmem_spec(3), *any_spec(1)),
        scratch_shapes=[
            pltpu.VMEM(dn.shape, BF),
            pltpu.VMEM(y2.shape, BF),
            pltpu.VMEM(gout.shape, BF),
            pltpu.SemaphoreType.DMA((3,)),
            *Scatter.scratch(rows, d),
            *Scatter.scratch(rows, d),
            *Scatter.scratch(on // GROUP, od),
            pltpu.VMEM((on, od), BF),
            pltpu.SemaphoreType.DMA,
            pltpu.SemaphoreType.DMA,
            pltpu.VMEM((n, w), BF),
            pltpu.SemaphoreType.DMA,
            pltpu.SemaphoreType.DMA,
            *home_sems(hi),
        ],
        compiler_params=params(cid, 63),
    )(dn, y2, gout, gqkv)


def read_mix(ref):
    return [[ref[i, k] for k in range(6)] for i in range(4)]


def mixed(weights, planes):
    total = weights[0] * planes[0]
    for w, p in zip(weights[1:], planes[1:]):
        total = total + w * p
    return total


def moments(x):
    centred = x - jnp.mean(x, -1, keepdims=True)
    inverse = lax.rsqrt(jnp.mean(centred * centred, -1, keepdims=True) + EPSILON)
    return centred * inverse, inverse


def normalize_back(grad_out, normed, inverse):
    return inverse * (
        grad_out
        - jnp.mean(grad_out, -1, keepdims=True)
        - normed * jnp.mean(grad_out * normed, -1, keepdims=True)
    )


def lane_sums(x):
    total = x[:, :128]
    for c in range(128, x.shape[1], 128):
        total = total + x[:, c : c + 128]
    return total


def read_x2(m, p, h, y1):
    fold = [sum(p[s][0] * m[j][1 + s] for s in range(4)) for j in range(4)]
    return mixed(fold + [sum(p[s][0] * m[s][5] for s in range(4))], [*h, y1])


TILE = 512


def open_kernel(mixa, mixm, sorter, x, g, hs, gs, n1, dy2, plane):
    m, p = read_mix(mixa), read_mix(mixm)
    tokens, streams, width = x.shape
    for src, dst in ((x, hs), (g, gs)):

        def split(r, src=src):
            v = src[r].astype(F32)
            for i in range(streams):
                plane[i, r] = v[:, i, :].astype(BF)

        rowwise(tokens, 16, split)
        for i in range(streams):
            for c in range(0, width, TILE):
                at = slice(c, c + TILE)
                dst[i, :, at] = dot(sorter[...], plane[i, :, at]).astype(BF)

    def norm(r):
        x1 = mixed([m[j][0] for j in range(4)], [hs[j, r].astype(F32) for j in range(4)])
        n1[r] = moments(x1)[0].astype(BF)
        dy2[r] = mixed([p[j][5] for j in range(4)], [gs[j, r].astype(F32) for j in range(4)]).astype(BF)

    rowwise(tokens, 16, norm)


def smem_spec(n):
    return [pl.BlockSpec(memory_space=pltpu.SMEM)] * n


def local_params(mib=60):
    return pltpu.CompilerParams(vmem_limit_bytes=mib * MIB)


def open_streams(mixa, mixm, sorter, x, g):
    tokens, streams, width = x.shape
    return pl.pallas_call(
        open_kernel,
        out_shape=(
            jax.ShapeDtypeStruct((streams, tokens, width), BF),
            jax.ShapeDtypeStruct((streams, tokens, width), BF),
            jax.ShapeDtypeStruct((tokens, width), BF),
            jax.ShapeDtypeStruct((tokens, width), BF),
        ),
        in_specs=[*smem_spec(2), *vmem_spec(3)],
        out_specs=tuple(vmem_spec(4)),
        scratch_shapes=[pltpu.VMEM((streams, tokens, width), BF)],
        compiler_params=local_params(),
    )(mixa, mixm, sorter, x, g)


def middle_kernel(mixa, mixm, hs, attn, wout, y1, n2):
    m, p = read_mix(mixa), read_mix(mixm)
    tokens, width = attn.shape

    def tile(i, carry):
        at = pl.ds(pl.multiple_of(i * TILE, TILE), TILE)
        y1[:, at] = dot(attn[...], wout[:, at])
        return carry

    lax.fori_loop(0, width // TILE, tile, 0)

    def norm(r):
        x2 = read_x2(m, p, [hs[j, r].astype(F32) for j in range(4)], y1[r])
        n2[r] = moments(x2)[0].astype(BF)

    rowwise(tokens, 16, norm)


def middle(mixa, mixm, hs, attn, wout):
    tokens, width = attn.shape
    return pl.pallas_call(
        middle_kernel,
        out_shape=(
            jax.ShapeDtypeStruct((tokens, width), F32),
            jax.ShapeDtypeStruct((tokens, width), BF),
        ),
        in_specs=[*smem_spec(2), *vmem_spec(3)],
        out_specs=tuple(vmem_spec(2)),
        compiler_params=local_params(),
    )(mixa, mixm, hs, attn, wout)


def unsort(sorter, planes, out):
    streams, tokens, width = planes.shape
    for i in range(streams):

        def tile(k, carry, i=i):
            at = pl.ds(pl.multiple_of(k * TILE, TILE), TILE)
            v = planes[i, :, at]
            high = v.astype(BF)
            low = (v - high.astype(F32)).astype(BF)
            out[:, i, at] = t_dot(sorter[...], high) + t_dot(sorter[...], low)
            return carry

        lax.fori_loop(0, width // TILE, tile, 0)


def turn_kernel(mixa, mixm, hs, gs, y1, dn2, wout, dx2, dy1, d_out, sums):
    m, p = read_mix(mixa), read_mix(mixm)
    tokens, width = y1.shape
    sums[...] = jnp.zeros_like(sums)

    def body(r):
        x2 = read_x2(m, p, [hs[j, r].astype(F32) for j in range(4)], y1[r])
        normed, inverse = moments(x2)
        dx2[r] = normalize_back(dn2[r], normed, inverse)
        for c in range(0, width, TILE):
            at = slice(c, c + TILE)
            h = [hs[j, r, at].astype(F32) for j in range(4)]
            y = y1[r, at]
            h1 = [mixed([*(m[j][1 + i] for j in range(4)), m[i][5]], [*h, y]) for i in range(4)]
            g = [gs[j, r, at].astype(F32) for j in range(4)]
            dx = dx2[r, at]
            g1 = [mixed([*(p[j][1 + i] for i in range(4)), p[j][0]], [*g, dx]) for j in range(4)]
            dy1[r, at] = mixed([m[j][5] for j in range(4)], g1).astype(BF)
            for j in range(4):
                sums[j * 6] += lane_sums(h1[j] * dx)
                for i in range(4):
                    sums[j * 6 + 1 + i] += lane_sums(h1[j] * g[i])

    rowwise(tokens, 16, body)

    def tile(i, carry):
        at = pl.ds(pl.multiple_of(i * TILE, TILE), TILE)
        d_out[:, at] = dot_t(dy1[...], wout[at, :]).astype(BF)
        return carry

    lax.fori_loop(0, width // TILE, tile, 0)


def turn(mixa, mixm, hs, gs, y1, dn2, wout):
    streams, tokens, width = hs.shape
    return pl.pallas_call(
        turn_kernel,
        out_shape=(
            jax.ShapeDtypeStruct((tokens, width), F32),
            jax.ShapeDtypeStruct((tokens, width), BF),
            jax.ShapeDtypeStruct((tokens, width), BF),
            jax.ShapeDtypeStruct((24, 16, 128), F32),
        ),
        in_specs=[*smem_spec(2), *vmem_spec(5)],
        out_specs=tuple(vmem_spec(4)),
        compiler_params=local_params(),
    )(mixa, mixm, hs, gs, y1, dn2, wout)


def close_kernel(
    mixa, mixm, sorter, hs, gs, dx2, y1, y2, dn1, other, new, d_streams, total,
    sums, planes, fresh, mine, inbox, send, recv,
):
    here = Here()
    barrier(here, ALL, True)
    m, p = read_mix(mixa), read_mix(mixm)
    tokens, width = y1.shape
    sums[:24] = jnp.zeros((24, *sums.shape[1:]), F32)
    sums[24:] = other[...]

    def body(r):
        x1 = mixed([m[j][0] for j in range(4)], [hs[j, r].astype(F32) for j in range(4)])
        normed, inverse = moments(x1)
        planes[0, r] = normalize_back(dn1[r], normed, inverse)
        for c in range(0, width, TILE):
            at = slice(c, c + TILE)
            h = [hs[j, r, at].astype(F32) for j in range(4)]
            g = [gs[j, r, at].astype(F32) for j in range(4)]
            y = y1[r, at]
            dx = planes[0, r, at]
            dm = dx2[r, at]
            g1 = [mixed([*(p[j][1 + i] for i in range(4)), p[j][0]], [*g, dm]) for j in range(4)]
            for j in range(4):
                planes[j, r, at] = mixed([*(m[j][1 + i] for i in range(4)), m[j][0]], [*g1, dx])
                sums[j * 6] += lane_sums(h[j] * dx)
                for i in range(4):
                    sums[j * 6 + 1 + i] += lane_sums(h[j] * g1[i])
                sums[j * 6 + 5] += lane_sums(y * g1[j])
            h1 = [mixed([*(m[j][1 + i] for j in range(4)), m[i][5]], [*h, y]) for i in range(4)]
            y = y2[r, at]
            for i in range(4):
                fresh[i, r, at] = mixed([*(p[j][1 + i] for j in range(4)), p[i][5]], [*h1, y])
                sums[24 + i * 6 + 5] += lane_sums(y * g[i])

    rowwise(tokens, 16, body)
    mine[0] = jnp.sum(sums[...], axis=1)
    pair = rcopy(mine.at[0], inbox.at[0], send.at[0], recv.at[0], here.partner())
    pair.start()
    pair.wait()
    mine[1] = mine[0] + inbox[0]
    cps = []
    for k in ALL:
        c = rcopy(mine.at[1], inbox.at[k], send.at[k], recv.at[k], here.dev(k))
        c.start()
        cps.append(c)
    unsort(sorter, fresh, new)
    unsort(sorter, planes, d_streams)
    everyone = mine[1]
    for c in cps:
        c.wait()
    for k in ALL:
        everyone = everyone + inbox[k]
    total[...] = everyone


def close(mixa, mixm, sorter, hs, gs, dx2, y1, y2, dn1, other, cid):
    streams, tokens, width = hs.shape
    return pl.pallas_call(
        close_kernel,
        out_shape=(
            jax.ShapeDtypeStruct((tokens, streams, width), F32),
            jax.ShapeDtypeStruct((tokens, streams, width), F32),
            jax.ShapeDtypeStruct((48, 128), F32),
        ),
        in_specs=[*smem_spec(2), *vmem_spec(8)],
        out_specs=tuple(vmem_spec(3)),
        scratch_shapes=[
            pltpu.VMEM((48, 16, 128), F32),
            pltpu.VMEM((streams, tokens, width), F32),
            pltpu.VMEM((streams, tokens, width), F32),
            pltpu.VMEM((2, 48, 128), F32),
            pltpu.VMEM((GROUP, 48, 128), F32),
            pltpu.SemaphoreType.DMA((GROUP,)),
            pltpu.SemaphoreType.DMA((GROUP,)),
        ],
        compiler_params=params(cid),
    )(mixa, mixm, sorter, hs, gs, dx2, y1, y2, dn1, other)


def slot_layout(lengths_row, capacity):
    seq_count = lengths_row.shape[-1]
    seq_ends = jnp.cumsum(lengths_row, axis=-1)
    slot_index = jnp.arange(capacity, dtype=jnp.int32)
    segment = jnp.sum((slot_index[:, None] >= seq_ends[..., None, :]).astype(jnp.int32), axis=-1)
    seq_starts = seq_ends - lengths_row
    chosen = (segment[..., None] == jnp.arange(seq_count, dtype=jnp.int32)).astype(jnp.int32)
    start_of = jnp.sum(chosen * seq_starts[..., None, :], axis=-1)
    is_live = segment < seq_count
    segment = jnp.where(is_live, segment, seq_count + slot_index)
    position = jnp.where(is_live, slot_index - start_of, 0)
    return (segment, position)


def rope_tables(position, head_width):
    half_width = head_width // 2
    frequency = jnp.exp(
        jnp.arange(half_width, dtype=jnp.float32) * (-2.0 * math.log(10000.0) / head_width)
    )
    angles = position.astype(jnp.float32)[..., None] * frequency
    return (jnp.cos(angles), jnp.sin(angles))


def rotate(inputs, cosine, sine_table):
    half_width = inputs.shape[-1] // 2
    first = inputs[..., :half_width]
    second = inputs[..., half_width:]
    return jnp.concatenate(
        [first * cosine - second * sine_table, second * cosine + first * sine_table], axis=-1
    )


def dot(a, b):
    return jnp.dot(a, b, preferred_element_type=F32)


def dot_t(a, b):
    return lax.dot_general(a, b, CONTRACT_LAST, preferred_element_type=F32)


def t_dot(a, b):
    return lax.dot_general(a, b, CONTRACT_FIRST, preferred_element_type=F32)


def shards(streams, cotangent, deal, lengths, mix_attn, mix_mlp, w_qkv, w_out, w_gu, w_down):
    tokens, stream_count, width = streams.shape
    shard_size = lax.axis_size("shard")
    hi = shard_size // GROUP
    hi_groups = [[h * GROUP + l for h in range(hi)] for l in range(GROUP)]
    shard = lax.axis_index("shard")
    my_hi = shard // GROUP
    bin_count = shard_size // 4
    my_bins = bin_count // hi
    per_bin = tokens // bin_count
    capacity = per_bin * shard_size
    ff = w_down.shape[1]

    def swap_hi(rows):
        if hi == 1:
            return rows
        return lax.all_to_all(rows, "shard", 0, 0, axis_index_groups=hi_groups, tiled=True)

    def to_bins(rows):
        return swap_hi(rows).reshape(hi, my_bins, per_bin, -1).swapaxes(0, 1).reshape(tokens, -1)

    def from_bins(rows):
        return swap_hi(rows.reshape(my_bins, hi, per_bin, -1).swapaxes(0, 1).reshape(tokens, -1))

    def gather_hi(rows):
        if hi == 1:
            return rows[None]
        return lax.all_gather(rows, "shard", axis_index_groups=hi_groups)

    def sum_hi(rows):
        if hi == 1:
            return rows[0]
        return lax.psum_scatter(rows, "shard", axis_index_groups=hi_groups)

    sorter = (jnp.arange(tokens, dtype=jnp.int32)[:, None] == deal[None, :]).astype(BF)

    hs, gs, n1, low_grad_mlp = open_streams(mix_attn, mix_mlp, sorter, streams, cotangent)
    low_attn = to_bins(n1)

    n1g, dy2g, qkvs, outs, gus, dns = front(
        low_attn, low_grad_mlp, gather_hi(w_qkv), gather_hi(w_out).reshape(-1, width), gather_hi(w_gu), gather_hi(w_down), 1
    )
    rows = w_qkv.shape[0]
    n1g = n1g.reshape(GROUP * tokens, width)
    qkvs = qkvs.reshape(width, 3 * HEAD_DIM)
    outs = outs.reshape(2, GROUP, hi, rows, width).swapaxes(1, 2).reshape(width, width)
    gus = gus.reshape(width, 2 * ff // GROUP)
    dns = dns.reshape(width, ff // GROUP)

    bins = lax.axis_index("rep") * bin_count + my_hi * my_bins
    lengths_here = lax.dynamic_slice_in_dim(lengths, bins, my_bins, 0)
    segment, position = slot_layout(lengths_here, capacity)

    def local_order(x):
        return x.reshape(my_bins, hi, GROUP, per_bin).swapaxes(1, 2).reshape(my_bins, capacity)

    segment, position = local_order(segment), local_order(position)
    cosine, sine = rope_tables(position, HEAD_DIM)
    slots = GROUP * tokens // my_bins // GROUP

    def by_bin(x):
        return x.reshape(GROUP, my_bins, slots, -1).swapaxes(0, 1).reshape(my_bins, capacity, -1)

    def by_token(x):
        return x.reshape(my_bins, GROUP, slots, -1).swapaxes(0, 1).reshape(GROUP, tokens, -1)

    scale = 1.0 / math.sqrt(HEAD_DIM)
    qkv = by_bin(dot(n1g, qkvs).astype(BF))
    queries = rotate(qkv[..., :HEAD_DIM].astype(F32), cosine, sine).astype(BF)
    keys = rotate(qkv[..., HEAD_DIM : 2 * HEAD_DIM].astype(F32), cosine, sine).astype(BF)
    values = qkv[..., 2 * HEAD_DIM :]
    seen = (segment[:, :, None] == segment[:, None, :]) & (position[:, None, :] <= position[:, :, None])
    scores = jnp.einsum("bqd,bkd->bqk", queries, keys, preferred_element_type=F32) * scale
    scores = jnp.where(seen, scores, -1e30)
    peak = jnp.max(scores, -1, keepdims=True)
    weights = jnp.exp(scores - peak)
    probability = weights / jnp.sum(weights, -1, keepdims=True)
    low_probability = probability.astype(BF)
    attended = jnp.einsum("bqk,bkd->bqd", low_probability, values, preferred_element_type=F32).astype(BF)
    attn_rows = from_bins(swap(by_token(attended), 2))
    y1, n2 = middle(mix_attn, mix_mlp, hs, attn_rows, outs)
    dn2, y2_part, g_mlp = mlp(n2, dy2g, gus, dns, hi, 4)
    dx2, low_grad_attn, grad_attn, mlp_sums = turn(mix_attn, mix_mlp, hs, gs, y1, dn2, outs)

    def own_rows(x):
        x = x.astype(F32).transpose(1, 2, 0, 3)
        return sum_hi(x.reshape(hi, rows, -1)).reshape(rows, GROUP, -1)

    g_mlp = own_rows(g_mlp)
    d_out = by_bin(swap(to_bins(grad_attn), 6))
    grad_values = jnp.einsum("bqk,bqd->bkd", low_probability, d_out, preferred_element_type=F32)
    grad_probs = jnp.einsum("bqd,bkd->bqk", d_out, values, preferred_element_type=F32)
    shared = jnp.sum(grad_probs * probability, -1, keepdims=True)
    grad_scores = (probability * (grad_probs - shared)).astype(BF)
    grad_query = jnp.einsum("bqk,bkd->bqd", grad_scores, keys, preferred_element_type=F32) * scale
    grad_keys = jnp.einsum("bqk,bqd->bkd", grad_scores, queries, preferred_element_type=F32) * scale
    grad_qkv = by_token(
        jnp.concatenate(
            [rotate(grad_query, cosine, -sine), rotate(grad_keys, cosine, -sine), grad_values], axis=-1
        ).astype(BF)
    ).reshape(GROUP * tokens, 3 * HEAD_DIM)
    dn1_part = dot_t(grad_qkv, qkvs).astype(BF).reshape(GROUP, tokens, width)
    g_qkv = t_dot(n1g, grad_qkv).astype(BF).reshape(2, width // 2, -1)
    g_out = t_dot(attn_rows, low_grad_attn).astype(BF)
    g_out = g_out.reshape(2, hi, GROUP, rows, width).swapaxes(1, 2).reshape(2, width // 2, width)
    dn1, y2, g_out, g_qkv = back(dn1_part, y2_part, g_out, g_qkv, hi, 7)
    g_out = sum_hi(g_out.reshape(hi, rows, width))
    g_qkv = own_rows(g_qkv)
    new_streams, d_streams, sums = close(
        mix_attn, mix_mlp, sorter, hs, gs, dx2, y1, y2, from_bins(dn1), mlp_sums, 8
    )
    if hi > 1:
        sums = lax.psum(sums, "shard", axis_index_groups=hi_groups)
    sums = jnp.sum(sums, axis=-1).reshape(2, 4, 6)
    g_mix_attn, g_mix_mlp = sums[0], sums[1]
    block = ff // GROUP
    return (
        new_streams,
        d_streams,
        g_mix_attn,
        g_mix_mlp,
        g_qkv.reshape(rows, GROUP, 3, HEAD_DIM).swapaxes(1, 2).reshape(rows, -1),
        g_out,
        jnp.concatenate([g_mlp[:, :, :block].reshape(rows, ff), g_mlp[:, :, block : 2 * block].reshape(rows, ff)], axis=1),
        g_mlp[:, :, 2 * block :].reshape(rows, ff),
    )


def solution(mesh):
    both = ("rep", "shard")
    return jax.shard_map(
        shards,
        mesh=mesh,
        in_specs=(
            P(both, None, None),
            P(both, None, None),
            P(both),
            P(),
            P(),
            P(),
            P(both, None),
            P(both, None),
            P(both, None),
            P(both, None),
        ),
        out_specs=(
            P(both, None, None),
            P(both, None, None),
            P(),
            P(),
            P(both, None),
            P(both, None),
            P(both, None),
            P(both, None),
        ),
        check_vma=False,
    )
```

```python
import functools
import math

import jax
import jax.numpy as jnp
from jax import lax
from jax.experimental import pallas as pl
from jax.experimental.pallas import tpu as pltpu
from jax.sharding import PartitionSpec as P

HEADS = 16
HEAD_DIM = 128
GROUP = 16
EPSILON = 1e-05
MESH = pl.DeviceIdType.MESH
CONTRACT_LAST = (((1,), (1,)), ((), ()))
CONTRACT_FIRST = (((0,), (0,)), ((), ()))
MIB = 1 << 20
BF = jnp.bfloat16
F32 = jnp.float32


class Here:
    def __init__(self):
        self.rep = lax.axis_index("rep")
        shard = lax.axis_index("shard")
        self.lo = shard % GROUP
        self.base = shard - self.lo
        self.bits = [(self.lo // (1 << i)) % 2 for i in range(4)]

    def flip(self, mask):
        out = self.lo
        for i in range(4):
            if mask & (1 << i):
                out = out + (1 << i) * (1 - 2 * self.bits[i])
        return out

    def dev(self, mask):
        return (self.rep, self.base + self.flip(mask))

    def partner(self):
        return (1 - self.rep, self.base + self.lo)


def barrier(here, masks, partner):
    sem = pltpu.get_barrier_semaphore()
    targets = [here.dev(m) for m in masks]
    if partner:
        targets.append(here.partner())
    for t in targets:
        pl.semaphore_signal(sem, inc=1, device_id=t, device_id_type=MESH)
    pl.semaphore_wait(sem, len(targets))


TREE = (1, 2, 4, 8, 12)
ALL = tuple(range(1, GROUP))


def rcopy(src, dst, send, recv, dev):
    return pltpu.make_async_remote_copy(
        src_ref=src, dst_ref=dst, send_sem=send, recv_sem=recv, device_id=dev, device_id_type=MESH
    )


class Gather:
    sems = (4, 7)

    def __init__(self, here, x, out, send, recv):
        self.here, self.x, self.out, self.send, self.recv = here, x, out, send, recv
        self.half = x.shape[0] // 2
        self.sent = []

    def _go(self, block, part, j, slot, mask):
        ref = self.out.at[block, pl.ds(part * self.half, self.half)]
        c = rcopy(ref, ref, self.send.at[j, slot], self.recv.at[j, slot], self.here.dev(mask))
        c.start()
        self.sent.append(c)

    def _wait(self, j, slot, block, part):
        ref = self.out.at[block, pl.ds(part * self.half, self.half)]
        rcopy(ref, ref, self.send.at[j, slot], self.recv.at[j, slot], self.here.dev(1)).wait_recv()

    def begin(self, own_sem):
        own = pltpu.make_async_copy(self.x, self.out.at[self.here.lo], own_sem)
        own.start()
        for j in (1, 3, 2):
            c = rcopy(self.x, self.out.at[self.here.lo], self.send.at[j, 6], self.recv.at[j, 6], self.here.dev(4 * j))
            c.start()
            self.sent.append(c)
        own.wait()
        self.spread(0)

    def spread(self, j):
        b = self.here.flip(4 * j)
        if j:
            ref = self.out.at[b]
            rcopy(ref, ref, self.send.at[j, 6], self.recv.at[j, 6], self.here.dev(4)).wait_recv()
        self._go(b, 0, j, 0, 1)
        self._go(b, 1, j, 1, 2)
        self._go(b, 0, j, 2, 2)
        self._go(b, 1, j, 3, 1)

    def forward(self, j):
        m = 4 * j
        self._wait(j, 0, self.here.flip(m ^ 1), 0)
        self._go(self.here.flip(m ^ 1), 0, j, 4, 2)
        self._wait(j, 1, self.here.flip(m ^ 2), 1)
        self._go(self.here.flip(m ^ 2), 1, j, 5, 1)

    def settle(self, j):
        m = 4 * j
        self._wait(j, 2, self.here.flip(m ^ 2), 0)
        self._wait(j, 3, self.here.flip(m ^ 1), 1)
        self._wait(j, 4, self.here.flip(m ^ 3), 0)
        self._wait(j, 5, self.here.flip(m ^ 3), 1)

    def end(self):
        for c in self.sent:
            c.wait_send()

    ORDER = (0, 1, 3, 2)


def rowwise(n, step, body):
    def at(i, carry):
        body(pl.ds(pl.multiple_of(i * step, step), step))
        return carry

    lax.fori_loop(0, n // step, at, 0)


class Scatter:
    sems = (4, 7)

    @staticmethod
    def scratch(rows, d):
        h = rows // 2
        return [
            pltpu.VMEM((4, 4, h, d), BF),
            pltpu.VMEM((4, 2, h, d), BF),
            pltpu.VMEM((3, rows, d), BF),
            pltpu.SemaphoreType.DMA(Scatter.sems),
            pltpu.SemaphoreType.DMA(Scatter.sems),
        ]

    def __init__(self, here, part, scratch):
        self.here, self.part = here, part
        self.first, self.second, self.zin, self.send, self.recv = scratch
        self.rows = part.shape[1]
        self.half = self.rows // 2
        self.sent = []

    def _copy(self, j, slot, src, dst, mask):
        return rcopy(src, dst, self.send.at[j, slot], self.recv.at[j, slot], self.here.dev(mask))

    def _go(self, *a):
        c = self._copy(*a)
        c.start()
        self.sent.append(c)

    def _piece(self, mask, part):
        return self.part.at[self.here.flip(mask), pl.ds(part * self.half, self.half)]

    def start(self, j):
        m = 4 * j
        self._go(j, 1, self._piece(m ^ 3, 0), self.first.at[j, 1], 2)
        self._go(j, 3, self._piece(m ^ 3, 1), self.first.at[j, 3], 1)
        self._go(j, 0, self._piece(m ^ 2, 0), self.first.at[j, 0], 2)
        self._go(j, 2, self._piece(m ^ 1, 1), self.first.at[j, 2], 1)

    def cross(self, j):
        m = 4 * j
        h = self.half
        for slot, mask, part, to in ((1, 1, 0, 1), (3, 2, 1, 2)):
            self._copy(j, slot, self.first.at[j, slot], self.first.at[j, slot], 1).wait_recv()
            own = self._piece(m ^ mask, part)

            def body(r, own=own, slot=slot):
                own[r] = (own[r].astype(F32) + self.first[j, slot, r].astype(F32)).astype(BF)

            rowwise(h, 16, body)
            self._go(j, 4 + part, own, self.second.at[j, part], to)

    def finish(self, j, out=None):
        m = 4 * j
        h = self.half
        for part, slot in ((0, 0), (1, 2)):
            self._copy(j, slot, self.first.at[j, slot], self.first.at[j, slot], 1).wait_recv()
            self._copy(j, 4 + part, self.second.at[j, part], self.second.at[j, part], 1).wait_recv()
        if out is not None:
            for k in (1, 2, 3):
                self._copy(k, 6, self.zin.at[k - 1], self.zin.at[k - 1], 4).wait_recv()
        for part, slot in ((0, 0), (1, 2)):
            own = self._piece(m, part)

            def body(r, own=own, part=part, slot=slot):
                total = own[r].astype(F32) + self.first[j, slot, r].astype(F32) + self.second[j, part, r].astype(F32)
                at = pl.ds(part * h + r.start, r.size)
                if out is None:
                    own[r] = total.astype(BF)
                else:
                    for k in (1, 2, 3):
                        total = total + self.zin[k - 1, at].astype(F32)
                    out[at] = total.astype(out.dtype)

            rowwise(h, 16, body)
        if out is None:
            self._go(j, 6, self.part.at[self.here.flip(m)], self.zin.at[j - 1], m)

    def end(self):
        for c in self.sent:
            c.wait_send()

    ORDER = (2, 3, 1, 0)


def run_scatters(scatters, outs):
    for i, (s, out) in enumerate(zip(scatters, outs)):
        order = s.ORDER
        if i == 0:
            s.start(order[0])
        s.start(order[1])
        s.cross(order[0])
        s.start(order[2])
        s.cross(order[1])
        s.finish(order[0])
        s.start(order[3])
        s.cross(order[2])
        s.finish(order[1])
        if i + 1 < len(scatters):
            scatters[i + 1].start(order[0])
        s.cross(order[3])
        s.finish(order[2])
        s.finish(order[3], out)
    for s in scatters:
        s.end()


def any_spec(n):
    return [pl.BlockSpec(memory_space=pl.ANY)] * n


def vmem_spec(n):
    return [pl.BlockSpec(memory_space=pltpu.VMEM)] * n


def params(cid, mib=60):
    return pltpu.CompilerParams(collective_id=cid, has_side_effects=True, vmem_limit_bytes=mib * MIB)


def exchange_columns(here, src, dst, width, cols, send, recv, own_sem):
    copies = []
    own = []
    for i, c in enumerate(cols):
        for m in range(GROUP):
            peer = here.flip(m)
            at = src.at[:, :, pl.ds(pl.multiple_of(c + peer * width, 128), width)]
            to = dst.at[here.rep, :, here.lo, :, pl.ds(i * width, width)]
            if m == 0:
                cp = pltpu.make_async_copy(at, to, own_sem.at[i])
                cp.start()
                own.append(cp)
            else:
                cp = rcopy(at, to, send.at[i, m], recv.at[i, m], here.dev(m))
                cp.start()
                copies.append(cp)

    def arrive():
        for cp in own:
            cp.wait()
        for i, c in enumerate(cols):
            for m in ALL:
                to = dst.at[here.rep, :, here.flip(m), :, pl.ds(i * width, width)]
                rcopy(to, to, send.at[i, m], recv.at[i, m], here.dev(m)).wait_recv()

    def end():
        for cp in copies:
            cp.wait_send()

    return arrive, end


def front_kernel(
    n1, dy2, wqkv, wout, wgu, wdn,
    n1g, dy2g, qkvs, outs, gus, dns,
    gsend, grecv, own, csend, crecv, cown, psend, precv,
):
    here = Here()
    barrier(here, ALL, True)
    q = exchange_columns(here, wqkv, qkvs, 128, (0, 2048, 4096), csend.at[0], crecv.at[0], cown.at[0])
    half = wgu.shape[2] // 2
    ga = Gather(here, n1, n1g, gsend.at[0], grecv.at[0])
    gb = Gather(here, dy2, dy2g, gsend.at[1], grecv.at[1])
    gc = Gather(here, wout, outs.at[here.rep], gsend.at[2], grecv.at[2])
    ga.begin(own.at[0])
    u = exchange_columns(here, wgu, gus, half // GROUP, (0, half), csend.at[1], crecv.at[1], cown.at[1])
    d = exchange_columns(here, wdn, dns, half // GROUP, (0,), csend.at[2], crecv.at[2], cown.at[2])
    gathers = [ga, gb, gc]
    for i, g in enumerate(gathers):
        order = g.ORDER
        g.spread(order[1])
        g.forward(order[0])
        g.spread(order[2])
        g.forward(order[1])
        g.spread(order[3])
        g.forward(order[2])
        if i + 1 < len(gathers):
            gathers[i + 1].begin(own.at[i + 1])
        g.forward(order[3])
    passes = []
    for i, ((arrive, _), dst) in enumerate(zip((q, u, d), (qkvs, gus, dns))):
        arrive()
        cp = rcopy(dst.at[here.rep], dst.at[here.rep], psend.at[i], precv.at[i], here.partner())
        cp.start()
        passes.append((cp, dst))
    for g in gathers:
        for j in range(4):
            g.settle(j)
    cp = rcopy(outs.at[here.rep], outs.at[here.rep], psend.at[3], precv.at[3], here.partner())
    cp.start()
    passes.append((cp, outs))
    for i, (cp, dst) in enumerate(passes):
        cp.wait_send()
        other = dst.at[1 - here.rep]
        rcopy(other, other, psend.at[i], precv.at[i], here.partner()).wait_recv()
    for g in gathers:
        g.end()
    for _, end in (q, u, d):
        end()


def front(n1, dy2, wqkv, wout, wgu, wdn, cid):
    hi, rows, _ = wqkv.shape
    d = n1.shape[1]
    ff = wdn.shape[2]
    shape = lambda *s: jax.ShapeDtypeStruct(s, BF)
    out_rows = wout.shape[0]
    return pl.pallas_call(
        front_kernel,
        out_shape=(
            shape(GROUP, *n1.shape),
            shape(GROUP, *dy2.shape),
            shape(2, hi, GROUP, rows, 3 * HEAD_DIM),
            shape(2, GROUP, out_rows, wout.shape[1]),
            shape(2, hi, GROUP, rows, 2 * ff // GROUP),
            shape(2, hi, GROUP, rows, ff // GROUP),
        ),
        in_specs=any_spec(6),
        out_specs=any_spec(6),
        scratch_shapes=[
            pltpu.SemaphoreType.DMA((3,) + Gather.sems),
            pltpu.SemaphoreType.DMA((3,) + Gather.sems),
            pltpu.SemaphoreType.DMA((3,)),
            pltpu.SemaphoreType.DMA((3, 3, GROUP)),
            pltpu.SemaphoreType.DMA((3, 3, GROUP)),
            pltpu.SemaphoreType.DMA((3, 3)),
            pltpu.SemaphoreType.DMA((4,)),
            pltpu.SemaphoreType.DMA((4,)),
        ],
        compiler_params=params(cid, 16),
    )(n1, dy2, wqkv, wout, wgu, wdn)


def swap_kernel(x, out, send, recv, own):
    here = Here()
    barrier(here, ALL, False)

    def block(ref, l):
        if len(ref.shape) == 3:
            return ref.at[l]
        return ref.at[:, pl.ds(pl.multiple_of(l * HEAD_DIM, HEAD_DIM), HEAD_DIM)]

    cps = []
    for m in ALL:
        c = rcopy(block(x, here.flip(m)), block(out, here.lo), send.at[m], recv.at[m], here.dev(m))
        c.start()
        cps.append(c)
    c = pltpu.make_async_copy(block(x, here.lo), block(out, here.lo), own)
    c.start()
    c.wait()
    for m in ALL:
        ref = block(out, here.flip(m))
        rcopy(ref, ref, send.at[m], recv.at[m], here.dev(m)).wait_recv()
    for c in cps:
        c.wait_send()


def swap(x, cid):
    if x.ndim == 3:
        shape = (x.shape[1], GROUP * HEAD_DIM)
    else:
        shape = (GROUP, x.shape[0], HEAD_DIM)
    return pl.pallas_call(
        swap_kernel,
        out_shape=jax.ShapeDtypeStruct(shape, x.dtype),
        in_specs=any_spec(1),
        out_specs=pl.BlockSpec(memory_space=pl.ANY),
        scratch_shapes=[
            pltpu.SemaphoreType.DMA((GROUP,)),
            pltpu.SemaphoreType.DMA((GROUP,)),
            pltpu.SemaphoreType.DMA,
        ],
        compiler_params=params(cid, 16),
    )(x)


def pair_add(here, g, inbox, send, recv):
    cp = rcopy(g.at[1 - here.rep], inbox, send, recv, here.partner())
    cp.start()
    cp.wait()

    def body(r):
        g[here.rep, r] = (g[here.rep, r].astype(F32) + inbox[r].astype(F32)).astype(BF)

    rowwise(inbox.shape[0], 16, body)


def send_home(here, total, out, send, recv, own):
    _, hi, rows, _ = out.shape

    def block(h, m):
        at = (h * GROUP + here.flip(m)) * rows
        return total.at[pl.ds(pl.multiple_of(at, rows), rows)]

    cps = []
    owns = []
    for h in range(hi):
        for m in ALL:
            c = rcopy(block(h, m), out.at[here.lo, h], send.at[h, m], recv.at[h, m], here.dev(m))
            c.start()
            cps.append(c)
        c = pltpu.make_async_copy(block(h, 0), out.at[here.lo, h], own.at[h])
        c.start()
        owns.append(c)

    def end():
        for c in owns:
            c.wait()
        for h in range(hi):
            for m in ALL:
                ref = out.at[here.flip(m), h]
                rcopy(ref, ref, send.at[h, m], recv.at[h, m], here.dev(m)).wait_recv()
        for c in cps:
            c.wait_send()

    return end


def home_sems(hi):
    return [
        pltpu.SemaphoreType.DMA((hi, GROUP)),
        pltpu.SemaphoreType.DMA((hi, GROUP)),
        pltpu.SemaphoreType.DMA((hi,)),
    ]


def mlp_kernel(
    mixa, mixm, n2, dy2g_in, wgu_in, wdn_in, hs, gs, wout, y1, y2p, grads_out, dx2, dy1, d_out, sums,
    n2g, dy2g, wgu, wdn, part, hidden, dgu, y2s, grads, inbox, dn2,
    gsend, grecv, own, load, y2sem, psend, precv, late, *scratch,
):
    here = Here()
    barrier(here, TREE, True)
    g = Gather(here, n2, n2g, gsend, grecv)
    rs = Scatter(here, part, scratch)
    g.begin(own)
    loads = []
    for i, (src, dst) in enumerate(((wgu_in, wgu), (wdn_in, wdn), (dy2g_in, dy2g))):
        c = pltpu.make_async_copy(src, dst, load.at[i])
        c.start()
        loads.append(c)
    width, ff = wdn.shape
    tokens = n2.shape[0]
    group_rows = 4 * tokens
    step = 256
    y2copies = []

    def compute(j):
        first = here.flip(4 * j) - here.lo % 4
        blocks = pl.ds(first, 4)
        if not y2copies:
            for c in loads:
                c.wait()

        def gates(k, carry):
            up_at = pl.ds(pl.multiple_of(k * step, step), step)
            gate_at = pl.ds(pl.multiple_of(ff + k * step, step), step)
            x = n2g[blocks].reshape(group_rows, width)
            up = dot(x, wgu[:, up_at])
            gate = dot(x, wgu[:, gate_at])
            dh = dot(dy2g[blocks].reshape(group_rows, width), wdn[:, up_at])
            sigmoid = 1.0 / (1.0 + jnp.exp(-gate))
            silu = gate * sigmoid
            hidden[blocks, :, up_at] = (silu * up).astype(BF).reshape(4, tokens, step)
            dgu[blocks, :, up_at] = (dh * silu).astype(BF).reshape(4, tokens, step)
            dgu[blocks, :, gate_at] = (
                (dh * up * sigmoid * (1.0 + gate * (1.0 - sigmoid))).astype(BF).reshape(4, tokens, step)
            )
            return carry

        lax.fori_loop(0, ff // step, gates, 0)
        if y2copies:
            y2copies[-1].wait()

        def outputs(k, carry):
            at = pl.ds(pl.multiple_of(k * step, step), step)
            h = hidden[blocks].reshape(group_rows, ff)
            y2s[:, :, at] = dot_t(h, wdn[at, :]).astype(BF).reshape(4, tokens, step)
            d = dgu[blocks].reshape(group_rows, 2 * ff)
            part[blocks, :, at] = dot_t(d, wgu[at, :]).astype(BF).reshape(4, tokens, step)
            return carry

        lax.fori_loop(0, width // step, outputs, 0)
        c = pltpu.make_async_copy(y2s, y2p.at[blocks], y2sem.at[len(y2copies)])
        c.start()
        y2copies.append(c)

    half = width // 2
    chunks = half // step

    def weight_grads(which, k):
        cols = pl.ds(pl.multiple_of(which * half + k * step, step), step)
        rows = pl.ds(pl.multiple_of(k * step, step), step)
        x = n2g[:, :, cols].reshape(GROUP * tokens, step)
        grads[which, rows, : 2 * ff] = t_dot(x, dgu[...].reshape(GROUP * tokens, 2 * ff)).astype(BF)
        x = dy2g[:, :, cols].reshape(GROUP * tokens, step)
        grads[which, rows, 2 * ff :] = t_dot(x, hidden[...].reshape(GROUP * tokens, ff)).astype(BF)

    def pass_chunk(k):
        rows = pl.ds(pl.multiple_of(k * step, step), step)
        return rcopy(grads.at[1 - here.rep, rows], inbox.at[rows], psend.at[k], precv.at[k], here.partner())

    o = g.ORDER
    g.spread(o[1])
    g.forward(o[0])
    g.settle(o[0])
    compute(o[0])
    rs.start(o[0])
    g.spread(o[2])
    g.forward(o[1])
    g.settle(o[1])
    compute(o[1])
    rs.start(o[1])
    g.spread(o[3])
    g.forward(o[2])
    rs.cross(o[0])
    g.settle(o[2])
    compute(o[2])
    rs.start(o[2])
    g.forward(o[3])
    rs.cross(o[1])
    g.settle(o[3])
    rs.finish(o[1])
    compute(o[3])
    rs.start(o[3])
    rs.cross(o[2])
    rs.finish(o[2])

    def other_half(k, carry):
        weight_grads(1 - here.rep, k)
        pass_chunk(k).start()
        return carry

    lax.fori_loop(0, chunks, other_half, 0)
    rs.cross(o[3])
    rs.finish(o[3])

    def own_half(k, carry):
        weight_grads(here.rep, k)
        return carry

    lax.fori_loop(0, chunks, own_half, 0)
    g.end()
    streams = hs.shape[0]
    loads = []
    for i, (src, dst) in enumerate(((hs, n2g.at[:streams]), (gs, n2g.at[streams : 2 * streams]), (wout, dy2g))):
        c = pltpu.make_async_copy(src, dst, late.at[i])
        c.start()
        loads.append(c)

    def add(k, carry):
        pass_chunk(k).wait()

        def rows_add(i, carry):
            r = pl.ds(pl.multiple_of(k * step + i * 16, 16), 16)
            grads[here.rep, r] = (grads[here.rep, r].astype(F32) + inbox[r].astype(F32)).astype(BF)
            return carry

        return lax.fori_loop(0, step // 16, rows_add, carry)

    lax.fori_loop(0, chunks, add, 0)
    out = pltpu.make_async_copy(grads.at[here.rep], grads_out, late.at[3])
    out.start()
    rs.finish(0, dn2)
    for c in loads:
        c.wait()
    turn(read_mix(mixa), read_mix(mixm), n2g, y1, dn2, dy2g, dx2, dy1, d_out, sums)
    out.wait()
    y2copies[-1].wait()
    rs.end()


def mlp(mixa, mixm, n2, dy2g, wgu, wdn, hs, gs, wout, y1, cid):
    tokens, width = n2.shape
    ff = wdn.shape[1]
    half = width // 2
    blocks = (GROUP, tokens)
    return pl.pallas_call(
        mlp_kernel,
        out_shape=(
            jax.ShapeDtypeStruct((*blocks, width), BF),
            jax.ShapeDtypeStruct((half, 3 * ff), BF),
            jax.ShapeDtypeStruct((tokens, width), F32),
            jax.ShapeDtypeStruct((tokens, width), BF),
            jax.ShapeDtypeStruct((tokens, width), BF),
            jax.ShapeDtypeStruct((24, 16, 128), F32),
        ),
        in_specs=[*smem_spec(2), *vmem_spec(1), *any_spec(6), *vmem_spec(1)],
        out_specs=(*any_spec(2), *vmem_spec(4)),
        scratch_shapes=[
            pltpu.VMEM((*blocks, width), BF),
            pltpu.VMEM((*blocks, width), BF),
            pltpu.VMEM(wgu.shape, BF),
            pltpu.VMEM(wdn.shape, BF),
            pltpu.VMEM((*blocks, width), BF),
            pltpu.VMEM((*blocks, ff), BF),
            pltpu.VMEM((*blocks, 2 * ff), BF),
            pltpu.VMEM((4, tokens, width), BF),
            pltpu.VMEM((2, half, 3 * ff), BF),
            pltpu.VMEM((half, 3 * ff), BF),
            pltpu.VMEM((tokens, width), F32),
            pltpu.SemaphoreType.DMA(Gather.sems),
            pltpu.SemaphoreType.DMA(Gather.sems),
            pltpu.SemaphoreType.DMA,
            pltpu.SemaphoreType.DMA((3,)),
            pltpu.SemaphoreType.DMA((4,)),
            pltpu.SemaphoreType.DMA((half // 256,)),
            pltpu.SemaphoreType.DMA((half // 256,)),
            pltpu.SemaphoreType.DMA((4,)),
            *Scatter.scratch(tokens, width),
        ],
        compiler_params=params(cid, 63),
        cost_estimate=pl.CostEstimate(
            flops=2 * GROUP * tokens * width * ff * 9, bytes_accessed=60 * MIB, transcendentals=0
        ),
    )(mixa, mixm, n2, dy2g, wgu, wdn, hs, gs, wout.reshape(GROUP, tokens, width), y1)


def rope_parts(rope):
    other = pltpu.roll(rope, HEAD_DIM // 2, 1)
    first = lax.broadcasted_iota(jnp.int32, rope.shape, 1) < HEAD_DIM // 2
    return jnp.where(first, rope, other), jnp.where(first, -other, rope)


def turned(x, cosine, sine):
    return x * cosine + pltpu.roll(x, HEAD_DIM // 2, 1) * sine


CODE = 4096


def head_of_bin(qkv, tables, b):
    rope, code_row, code_col = tables
    slots = qkv.shape[1] // rope.shape[0]
    rows = pl.ds(b * slots, slots)
    n = GROUP * slots

    def piece(i):
        return qkv[:, rows, i * HEAD_DIM : (i + 1) * HEAD_DIM].reshape(n, HEAD_DIM)

    cos, sin = rope_parts(rope[b])
    queries = turned(piece(0).astype(F32), cos, sin).astype(BF)
    keys = turned(piece(1).astype(F32), cos, sin).astype(BF)
    query_code, key_code = code_row[b], code_col[b]
    segment_code = query_code - jnp.bitwise_and(query_code, CODE - 1)
    seen = (key_code <= query_code) & (key_code >= segment_code)
    scores = jnp.where(seen, dot_t(queries, keys) * (1.0 / math.sqrt(HEAD_DIM)), -1e30)
    weights = jnp.exp(scores - jnp.max(scores, -1, keepdims=True))
    probability = weights / jnp.sum(weights, -1, keepdims=True)
    return queries, keys, piece(2), probability, rows, cos, sin


def attend_back(qkv, d_out, dqkv, tables, b):
    queries, keys, values, probability, rows, cos, sin = head_of_bin(qkv, tables, b)
    n, slots = queries.shape[0], rows.size
    scale = 1.0 / math.sqrt(HEAD_DIM)
    grad = d_out[:, rows].reshape(n, HEAD_DIM)
    grad_values = t_dot(probability.astype(BF), grad)
    grad_probs = dot_t(grad, values)
    shared = jnp.sum(grad_probs * probability, -1, keepdims=True)
    grad_scores = (probability * (grad_probs - shared)).astype(BF)
    grad_query = dot(grad_scores, keys) * scale
    grad_keys = t_dot(grad_scores, queries) * scale
    for i, v in enumerate((turned(grad_query, cos, -sin), turned(grad_keys, cos, -sin), grad_values)):
        dqkv[:, rows, i * HEAD_DIM : (i + 1) * HEAD_DIM] = v.astype(BF).reshape(GROUP, slots, HEAD_DIM)


def back_kernel(
    d_rows, qkv, qkvs, dy1, attn, rope, code_row, code_col, n1g, y2_in, gmlp,
    dn_out, y2_out, gout_out, gqkv_out, gmlp_out,
    d_out, dqkv, dn, y2, gout, stage, gqkv, tiles, obox, qbox,
    dsend, drecv, down, load, tile_sem, osend, orecv, qsend, qrecv, *scratch,
):
    here = Here()
    barrier(here, ALL, True)
    tables = (rope, code_row, code_col)
    bins = rope.shape[0]
    swaps = []
    for m in ALL:
        at = pl.ds(pl.multiple_of(here.flip(m) * HEAD_DIM, HEAD_DIM), HEAD_DIM)
        c = rcopy(d_rows.at[:, at], d_out.at[here.lo], dsend.at[m], drecv.at[m], here.dev(m))
        c.start()
        swaps.append(c)
    at = pl.ds(pl.multiple_of(here.lo * HEAD_DIM, HEAD_DIM), HEAD_DIM)
    mine = pltpu.make_async_copy(d_rows.at[:, at], d_out.at[here.lo], down)
    mine.start()
    y2_load = pltpu.make_async_copy(y2_in, y2, load)
    y2_load.start()
    _, tokens, width = dn.shape
    k = len(Scatter.scratch(16, 128))
    rs_dn = Scatter(here, dn, scratch[:k])
    rs_y2 = Scatter(here, y2, scratch[k : 2 * k])
    rs_go = Scatter(here, gout.reshape(GROUP, gout.shape[0] // GROUP, width), scratch[2 * k : 3 * k])
    qhome, mhome = scratch[3 * k : 3 * k + 3], scratch[3 * k + 3 :]
    order = rs_y2.ORDER
    y2_load.wait()
    for j in order:
        rs_y2.start(j)
    end_mlp = send_home(here, gmlp, gmlp_out, *mhome)
    mine.wait()
    for m in ALL:
        ref = d_out.at[here.flip(m)]
        rcopy(ref, ref, dsend.at[m], drecv.at[m], here.dev(m)).wait_recv()

    half = width // 2
    step = 256
    chunks = half // step

    def out_grads(which, k):
        cols = pl.ds(pl.multiple_of(which * half + k * step, step), step)
        return t_dot(attn[:, cols], dy1[...]).astype(BF)

    def gout_pass(k):
        at = pl.ds(k * step, step)
        return rcopy(stage.at[k % 2], obox.at[at], osend.at[k], orecv.at[k], here.partner())

    gqkv_pair = rcopy(gqkv.at[1 - here.rep], qbox, qsend, qrecv, here.partner())

    for b in range(bins):
        attend_back(qkv, d_out, dqkv, tables, b)
        if b == 0:
            rs_y2.cross(order[0])
        elif b < 3:
            rs_y2.cross(order[b])
            rs_y2.finish(order[b - 1])
    rs_y2.cross(order[3])
    rs_y2.finish(order[2])

    narrow = tiles.shape[3]

    def qkv_tile(k):
        cols = pl.ds(k * narrow, narrow)
        return pltpu.make_async_copy(n1g.at[:, :, cols], tiles.at[k % 2], tile_sem.at[k % 2])

    qkv_tile(0).start()
    for j in order:
        blocks = pl.ds(here.flip(4 * j) - here.lo % 4, 4)

        def part(k, carry, blocks=blocks):
            at = pl.ds(pl.multiple_of(k * TILE, TILE), TILE)
            d = dqkv[blocks].reshape(4 * tokens, 3 * HEAD_DIM)
            dn[blocks, :, at] = dot_t(d, qkvs[at, :]).astype(BF).reshape(4, tokens, TILE)
            return carry

        lax.fori_loop(0, width // TILE, part, 0)
        rs_dn.start(j)
    count = width // narrow
    for k in range(count):
        if k + 1 < count:
            qkv_tile(k + 1).start()
        qkv_tile(k).wait()
        x = tiles[k % 2].reshape(GROUP * tokens, narrow)
        rows = pl.ds((k % (count // 2)) * narrow, narrow)
        gqkv[k // (count // 2), rows, :] = t_dot(x, dqkv[...].reshape(GROUP * tokens, 3 * HEAD_DIM)).astype(BF)
    gqkv_pair.start()
    rs_y2.finish(0, y2_out)
    rs_dn.cross(order[0])
    for k in range(chunks):
        if k >= 2:
            gout_pass(k - 2).wait_send()
        stage[k % 2] = out_grads(1 - here.rep, k)
        gout_pass(k).start()
    rs_dn.cross(order[1])
    rs_dn.finish(order[0])
    for k in range(chunks):
        gout[k * step : (k + 1) * step, :] = out_grads(here.rep, k)

    def add(ref, box):
        def body(r):
            ref[r] = (ref[r].astype(F32) + box[r].astype(F32)).astype(BF)

        rowwise(box.shape[0], 16, body)

    gqkv_pair.wait()
    add(gqkv.at[here.rep], qbox)
    end_qkv = send_home(here, gqkv.at[here.rep], gqkv_out, *qhome)
    rs_dn.cross(order[2])
    rs_dn.finish(order[1])
    for k in range(chunks):
        gout_pass(k).wait_recv()
        if k >= chunks - 2:
            gout_pass(k).wait_send()
    add(gout, obox)
    for j in order:
        rs_go.start(j)
    rs_dn.cross(order[3])
    rs_dn.finish(order[2])
    rs_go.cross(order[0])
    rs_go.cross(order[1])
    rs_go.finish(order[0])
    rs_go.cross(order[2])
    rs_go.finish(order[1])
    rs_go.cross(order[3])
    rs_go.finish(order[2])
    rs_dn.finish(0, dn_out)
    rs_go.finish(0, gout_out)
    end_mlp()
    end_qkv()
    for c in swaps:
        c.wait_send()
    for rs in (rs_dn, rs_y2, rs_go):
        rs.end()


def back(d_rows, qkv, qkvs, dy1, attn, tables, n1g, y2, gmlp, hi, cid):
    tokens, width = d_rows.shape
    half = width // 2
    w = qkv.shape[2]
    blocks = (GROUP, tokens, width)
    return pl.pallas_call(
        back_kernel,
        out_shape=(
            jax.ShapeDtypeStruct((tokens, width), F32),
            jax.ShapeDtypeStruct((tokens, width), F32),
            jax.ShapeDtypeStruct((half // GROUP, width), F32),
            jax.ShapeDtypeStruct((GROUP, hi, half // (hi * GROUP), w), BF),
            jax.ShapeDtypeStruct((GROUP, hi, half // (hi * GROUP), gmlp.shape[1]), BF),
        ),
        in_specs=[*vmem_spec(8), *any_spec(3)],
        out_specs=(*vmem_spec(3), *any_spec(2)),
        scratch_shapes=[
            pltpu.VMEM((GROUP, tokens, HEAD_DIM), BF),
            pltpu.VMEM((GROUP, tokens, w), BF),
            pltpu.VMEM(blocks, BF),
            pltpu.VMEM(blocks, BF),
            pltpu.VMEM((half, width), BF),
            pltpu.VMEM((2, 256, width), BF),
            pltpu.VMEM((2, half, w), BF),
            pltpu.VMEM((2, GROUP, tokens, TILE // 4), BF),
            pltpu.VMEM((half, width), BF),
            pltpu.VMEM((half, w), BF),
            pltpu.SemaphoreType.DMA((GROUP,)),
            pltpu.SemaphoreType.DMA((GROUP,)),
            pltpu.SemaphoreType.DMA,
            pltpu.SemaphoreType.DMA,
            pltpu.SemaphoreType.DMA((2,)),
            pltpu.SemaphoreType.DMA((half // 256,)),
            pltpu.SemaphoreType.DMA((half // 256,)),
            pltpu.SemaphoreType.DMA,
            pltpu.SemaphoreType.DMA,
            *Scatter.scratch(tokens, width),
            *Scatter.scratch(tokens, width),
            *Scatter.scratch(half // GROUP, width),
            *home_sems(hi),
            *home_sems(hi),
        ],
        compiler_params=params(cid, 63),
    )(d_rows, qkv, qkvs, dy1, attn, *tables, n1g, y2, gmlp)


def read_mix(ref):
    return [[ref[i, k] for k in range(6)] for i in range(4)]


def mixed(weights, planes):
    total = weights[0] * planes[0]
    for w, p in zip(weights[1:], planes[1:]):
        total = total + w * p
    return total


def moments(x):
    centred = x - jnp.mean(x, -1, keepdims=True)
    inverse = lax.rsqrt(jnp.mean(centred * centred, -1, keepdims=True) + EPSILON)
    return centred * inverse, inverse


def normalize_back(grad_out, normed, inverse):
    return inverse * (
        grad_out
        - jnp.mean(grad_out, -1, keepdims=True)
        - normed * jnp.mean(grad_out * normed, -1, keepdims=True)
    )


def lane_sums(x):
    total = x[:, :128]
    for c in range(128, x.shape[1], 128):
        total = total + x[:, c : c + 128]
    return total


def read_x2(m, p, h, y1):
    fold = [sum(p[s][0] * m[j][1 + s] for s in range(4)) for j in range(4)]
    return mixed(fold + [sum(p[s][0] * m[s][5] for s in range(4))], [*h, y1])


TILE = 512


def open_kernel(mixa, mixm, sorter, x, g, hs, gs, n1, dy2, plane):
    m, p = read_mix(mixa), read_mix(mixm)
    tokens, streams, width = x.shape
    for src, dst in ((x, hs), (g, gs)):

        def split(r, src=src):
            v = src[r].astype(F32)
            for i in range(streams):
                plane[i, r] = v[:, i, :].astype(BF)

        rowwise(tokens, 16, split)
        for i in range(streams):
            for c in range(0, width, TILE):
                at = slice(c, c + TILE)
                dst[i, :, at] = dot(sorter[...], plane[i, :, at]).astype(BF)

    def norm(r):
        x1 = mixed([m[j][0] for j in range(4)], [hs[j, r].astype(F32) for j in range(4)])
        n1[r] = moments(x1)[0].astype(BF)
        dy2[r] = mixed([p[j][5] for j in range(4)], [gs[j, r].astype(F32) for j in range(4)]).astype(BF)

    rowwise(tokens, 16, norm)


def smem_spec(n):
    return [pl.BlockSpec(memory_space=pltpu.SMEM)] * n


def local_params(mib=60):
    return pltpu.CompilerParams(vmem_limit_bytes=mib * MIB)


def open_streams(mixa, mixm, sorter, x, g):
    tokens, streams, width = x.shape
    return pl.pallas_call(
        open_kernel,
        out_shape=(
            jax.ShapeDtypeStruct((streams, tokens, width), BF),
            jax.ShapeDtypeStruct((streams, tokens, width), BF),
            jax.ShapeDtypeStruct((tokens, width), BF),
            jax.ShapeDtypeStruct((tokens, width), BF),
        ),
        in_specs=[*smem_spec(2), *vmem_spec(3)],
        out_specs=tuple(vmem_spec(4)),
        scratch_shapes=[pltpu.VMEM((streams, tokens, width), BF)],
        compiler_params=local_params(),
    )(mixa, mixm, sorter, x, g)


def middle_kernel(mixa, mixm, hs, attn, wout, y1, n2):
    m, p = read_mix(mixa), read_mix(mixm)
    tokens, width = attn.shape

    def tile(i, carry):
        at = pl.ds(pl.multiple_of(i * TILE, TILE), TILE)
        y1[:, at] = dot(attn[...], wout[:, at])
        return carry

    lax.fori_loop(0, width // TILE, tile, 0)

    def norm(r):
        x2 = read_x2(m, p, [hs[j, r].astype(F32) for j in range(4)], y1[r])
        n2[r] = moments(x2)[0].astype(BF)

    rowwise(tokens, 16, norm)


def middle(mixa, mixm, hs, attn, wout):
    tokens, width = attn.shape
    return pl.pallas_call(
        middle_kernel,
        out_shape=(
            jax.ShapeDtypeStruct((tokens, width), F32),
            jax.ShapeDtypeStruct((tokens, width), BF),
        ),
        in_specs=[*smem_spec(2), *vmem_spec(3)],
        out_specs=tuple(vmem_spec(2)),
        compiler_params=local_params(),
    )(mixa, mixm, hs, attn, wout)


def unsort(sorter, planes, out):
    streams, tokens, width = planes.shape
    for i in range(streams):

        def tile(k, carry, i=i):
            at = pl.ds(pl.multiple_of(k * TILE, TILE), TILE)
            v = planes[i, :, at]
            high = v.astype(BF)
            low = (v - high.astype(F32)).astype(BF)
            out[:, i, at] = t_dot(sorter[...], high) + t_dot(sorter[...], low)
            return carry

        lax.fori_loop(0, width // TILE, tile, 0)


def turn(m, p, planes, y1, dn2, wout, dx2, dy1, d_out, sums):
    tokens, width = y1.shape
    sums[...] = jnp.zeros_like(sums)

    def body(r):
        x2 = read_x2(m, p, [planes[j, r].astype(F32) for j in range(4)], y1[r])
        normed, inverse = moments(x2)
        dx2[r] = normalize_back(dn2[r], normed, inverse)
        for c in range(0, width, TILE):
            at = slice(c, c + TILE)
            h = [planes[j, r, at].astype(F32) for j in range(4)]
            y = y1[r, at]
            h1 = [mixed([*(m[j][1 + i] for j in range(4)), m[i][5]], [*h, y]) for i in range(4)]
            g = [planes[4 + j, r, at].astype(F32) for j in range(4)]
            dx = dx2[r, at]
            g1 = [mixed([*(p[j][1 + i] for i in range(4)), p[j][0]], [*g, dx]) for j in range(4)]
            dy1[r, at] = mixed([m[j][5] for j in range(4)], g1).astype(BF)
            for j in range(4):
                sums[j * 6] += lane_sums(h1[j] * dx)
                for i in range(4):
                    sums[j * 6 + 1 + i] += lane_sums(h1[j] * g[i])

    rowwise(tokens, 16, body)
    blocks = TILE // wout.shape[1]

    def tile(i, carry):
        at = pl.ds(pl.multiple_of(i * TILE, TILE), TILE)
        rows = wout[pl.ds(i * blocks, blocks)].reshape(TILE, width)
        d_out[:, at] = dot_t(dy1[...], rows).astype(BF)
        return carry

    lax.fori_loop(0, width // TILE, tile, 0)


def close_kernel(
    mixa, mixm, sorter, hs, gs, dx2, y1, y2, dn1, other, new, d_streams, total,
    sums, planes, fresh, mine, inbox, send, recv,
):
    here = Here()
    barrier(here, ALL, True)
    m, p = read_mix(mixa), read_mix(mixm)
    tokens, width = y1.shape
    sums[:24] = jnp.zeros((24, *sums.shape[1:]), F32)
    sums[24:] = other[...]

    def body(r):
        x1 = mixed([m[j][0] for j in range(4)], [hs[j, r].astype(F32) for j in range(4)])
        normed, inverse = moments(x1)
        planes[0, r] = normalize_back(dn1[r], normed, inverse)
        for c in range(0, width, TILE):
            at = slice(c, c + TILE)
            h = [hs[j, r, at].astype(F32) for j in range(4)]
            g = [gs[j, r, at].astype(F32) for j in range(4)]
            y = y1[r, at]
            dx = planes[0, r, at]
            dm = dx2[r, at]
            g1 = [mixed([*(p[j][1 + i] for i in range(4)), p[j][0]], [*g, dm]) for j in range(4)]
            for j in range(4):
                planes[j, r, at] = mixed([*(m[j][1 + i] for i in range(4)), m[j][0]], [*g1, dx])
                sums[j * 6] += lane_sums(h[j] * dx)
                for i in range(4):
                    sums[j * 6 + 1 + i] += lane_sums(h[j] * g1[i])
                sums[j * 6 + 5] += lane_sums(y * g1[j])
            h1 = [mixed([*(m[j][1 + i] for j in range(4)), m[i][5]], [*h, y]) for i in range(4)]
            y = y2[r, at]
            for i in range(4):
                fresh[i, r, at] = mixed([*(p[j][1 + i] for j in range(4)), p[i][5]], [*h1, y])
                sums[24 + i * 6 + 5] += lane_sums(y * g[i])

    rowwise(tokens, 16, body)
    mine[0] = jnp.sum(sums[...], axis=1)
    pair = rcopy(mine.at[0], inbox.at[0], send.at[0], recv.at[0], here.partner())
    pair.start()
    pair.wait()
    mine[1] = mine[0] + inbox[0]
    cps = []
    for k in ALL:
        c = rcopy(mine.at[1], inbox.at[k], send.at[k], recv.at[k], here.dev(k))
        c.start()
        cps.append(c)
    unsort(sorter, fresh, new)
    unsort(sorter, planes, d_streams)
    everyone = mine[1]
    for c in cps:
        c.wait()
    for k in ALL:
        everyone = everyone + inbox[k]
    total[...] = everyone


def close(mixa, mixm, sorter, hs, gs, dx2, y1, y2, dn1, other, cid):
    streams, tokens, width = hs.shape
    return pl.pallas_call(
        close_kernel,
        out_shape=(
            jax.ShapeDtypeStruct((tokens, streams, width), F32),
            jax.ShapeDtypeStruct((tokens, streams, width), F32),
            jax.ShapeDtypeStruct((48, 128), F32),
        ),
        in_specs=[*smem_spec(2), *vmem_spec(8)],
        out_specs=tuple(vmem_spec(3)),
        scratch_shapes=[
            pltpu.VMEM((48, 16, 128), F32),
            pltpu.VMEM((streams, tokens, width), F32),
            pltpu.VMEM((streams, tokens, width), F32),
            pltpu.VMEM((2, 48, 128), F32),
            pltpu.VMEM((GROUP, 48, 128), F32),
            pltpu.SemaphoreType.DMA((GROUP,)),
            pltpu.SemaphoreType.DMA((GROUP,)),
        ],
        compiler_params=params(cid),
    )(mixa, mixm, sorter, hs, gs, dx2, y1, y2, dn1, other)


def slot_layout(lengths_row, capacity):
    seq_count = lengths_row.shape[-1]
    seq_ends = jnp.cumsum(lengths_row, axis=-1)
    slot_index = jnp.arange(capacity, dtype=jnp.int32)
    segment = jnp.sum((slot_index[:, None] >= seq_ends[..., None, :]).astype(jnp.int32), axis=-1)
    seq_starts = seq_ends - lengths_row
    chosen = (segment[..., None] == jnp.arange(seq_count, dtype=jnp.int32)).astype(jnp.int32)
    start_of = jnp.sum(chosen * seq_starts[..., None, :], axis=-1)
    is_live = segment < seq_count
    segment = jnp.where(is_live, segment, seq_count + slot_index)
    position = jnp.where(is_live, slot_index - start_of, 0)
    return (segment, position)


def rope_tables(position, head_width):
    half_width = head_width // 2
    frequency = jnp.exp(
        jnp.arange(half_width, dtype=jnp.float32) * (-2.0 * math.log(10000.0) / head_width)
    )
    angles = position.astype(jnp.float32)[..., None] * frequency
    return (jnp.cos(angles), jnp.sin(angles))


def rotate(inputs, cosine, sine_table):
    half_width = inputs.shape[-1] // 2
    first = inputs[..., :half_width]
    second = inputs[..., half_width:]
    return jnp.concatenate(
        [first * cosine - second * sine_table, second * cosine + first * sine_table], axis=-1
    )


def dot(a, b):
    return jnp.dot(a, b, preferred_element_type=F32)


def dot_t(a, b):
    return lax.dot_general(a, b, CONTRACT_LAST, preferred_element_type=F32)


def t_dot(a, b):
    return lax.dot_general(a, b, CONTRACT_FIRST, preferred_element_type=F32)


def shards(streams, cotangent, deal, lengths, mix_attn, mix_mlp, w_qkv, w_out, w_gu, w_down):
    tokens, stream_count, width = streams.shape
    shard_size = lax.axis_size("shard")
    hi = shard_size // GROUP
    hi_groups = [[h * GROUP + l for h in range(hi)] for l in range(GROUP)]
    shard = lax.axis_index("shard")
    my_hi = shard // GROUP
    bin_count = shard_size // 4
    my_bins = bin_count // hi
    per_bin = tokens // bin_count
    capacity = per_bin * shard_size
    ff = w_down.shape[1]

    def swap_hi(rows):
        if hi == 1:
            return rows
        return lax.all_to_all(rows, "shard", 0, 0, axis_index_groups=hi_groups, tiled=True)

    def to_bins(rows):
        return swap_hi(rows).reshape(hi, my_bins, per_bin, -1).swapaxes(0, 1).reshape(tokens, -1)

    def from_bins(rows):
        return swap_hi(rows.reshape(my_bins, hi, per_bin, -1).swapaxes(0, 1).reshape(tokens, -1))

    def gather_hi(rows):
        if hi == 1:
            return rows[None]
        return lax.all_gather(rows, "shard", axis_index_groups=hi_groups)

    def sum_hi(rows):
        if hi == 1:
            return rows[0]
        return lax.psum_scatter(rows, "shard", axis_index_groups=hi_groups)

    sorter = (jnp.arange(tokens, dtype=jnp.int32)[:, None] == deal[None, :]).astype(BF)

    hs, gs, n1, low_grad_mlp = open_streams(mix_attn, mix_mlp, sorter, streams, cotangent)
    low_attn = to_bins(n1)

    n1g, dy2g, qkvs, outs, gus, dns = front(
        low_attn, low_grad_mlp, gather_hi(w_qkv), gather_hi(w_out).reshape(-1, width), gather_hi(w_gu), gather_hi(w_down), 1
    )
    rows = w_qkv.shape[0]
    qkvs = qkvs.reshape(width, 3 * HEAD_DIM)
    outs = outs.reshape(2, GROUP, hi, rows, width).swapaxes(1, 2).reshape(width, width)
    gus = gus.reshape(width, 2 * ff // GROUP)
    dns = dns.reshape(width, ff // GROUP)

    bins = lax.axis_index("rep") * bin_count + my_hi * my_bins
    lengths_here = lax.dynamic_slice_in_dim(lengths, bins, my_bins, 0)
    segment, position = slot_layout(lengths_here, capacity)

    def local_order(x):
        return x.reshape(my_bins, hi, GROUP, per_bin).swapaxes(1, 2).reshape(my_bins, capacity)

    segment, position = local_order(segment), local_order(position)
    cosine, sine = rope_tables(position, HEAD_DIM)
    slots = GROUP * tokens // my_bins // GROUP

    def by_bin(x):
        return x.reshape(GROUP, my_bins, slots, -1).swapaxes(0, 1).reshape(my_bins, capacity, -1)

    def by_token(x):
        return x.reshape(my_bins, GROUP, slots, -1).swapaxes(0, 1).reshape(GROUP, tokens, -1)

    scale = 1.0 / math.sqrt(HEAD_DIM)
    raw_qkv = dot(n1g.reshape(GROUP * tokens, width), qkvs).astype(BF)
    qkv = by_bin(raw_qkv)
    queries = rotate(qkv[..., :HEAD_DIM].astype(F32), cosine, sine).astype(BF)
    keys = rotate(qkv[..., HEAD_DIM : 2 * HEAD_DIM].astype(F32), cosine, sine).astype(BF)
    values = qkv[..., 2 * HEAD_DIM :]
    seen = (segment[:, :, None] == segment[:, None, :]) & (position[:, None, :] <= position[:, :, None])
    scores = jnp.einsum("bqd,bkd->bqk", queries, keys, preferred_element_type=F32) * scale
    scores = jnp.where(seen, scores, -1e30)
    peak = jnp.max(scores, -1, keepdims=True)
    weights = jnp.exp(scores - peak)
    probability = weights / jnp.sum(weights, -1, keepdims=True)
    low_probability = probability.astype(BF)
    attended = jnp.einsum("bqk,bkd->bqd", low_probability, values, preferred_element_type=F32).astype(BF)
    attn_rows = from_bins(swap(by_token(attended), 2))
    y1, n2 = middle(mix_attn, mix_mlp, hs, attn_rows, outs)
    y2_part, g_mlp, dx2, low_grad_attn, grad_attn, mlp_sums = mlp(
        mix_attn, mix_mlp, n2, dy2g, gus, dns, hs, gs, outs, y1, 4
    )

    def own_rows(x):
        x = x.astype(F32).transpose(1, 2, 0, 3)
        return sum_hi(x.reshape(hi, rows, -1)).reshape(rows, GROUP, -1)

    code = segment * CODE + position
    tables = (jnp.concatenate([cosine, sine], -1), code[:, :, None], code[:, None, :])
    attn_cols = attn_rows.reshape(tokens, 2, hi, GROUP, rows).swapaxes(2, 3).reshape(tokens, width)
    dn1, y2, g_out, g_qkv, g_mlp = back(
        to_bins(grad_attn), raw_qkv.reshape(GROUP, tokens, -1), qkvs, low_grad_attn, attn_cols, tables,
        n1g, y2_part, g_mlp, hi, 7,
    )
    g_mlp = own_rows(g_mlp)
    g_out = sum_hi(g_out.reshape(hi, rows, width))
    g_qkv = own_rows(g_qkv)
    new_streams, d_streams, sums = close(
        mix_attn, mix_mlp, sorter, hs, gs, dx2, y1, y2, from_bins(dn1), mlp_sums, 8
    )
    if hi > 1:
        sums = lax.psum(sums, "shard", axis_index_groups=hi_groups)
    sums = jnp.sum(sums, axis=-1).reshape(2, 4, 6)
    g_mix_attn, g_mix_mlp = sums[0], sums[1]
    block = ff // GROUP
    return (
        new_streams,
        d_streams,
        g_mix_attn,
        g_mix_mlp,
        g_qkv.reshape(rows, GROUP, 3, HEAD_DIM).swapaxes(1, 2).reshape(rows, -1),
        g_out,
        jnp.concatenate([g_mlp[:, :, :block].reshape(rows, ff), g_mlp[:, :, block : 2 * block].reshape(rows, ff)], axis=1),
        g_mlp[:, :, 2 * block :].reshape(rows, ff),
    )


def solution(mesh):
    both = ("rep", "shard")
    return jax.shard_map(
        shards,
        mesh=mesh,
        in_specs=(
            P(both, None, None),
            P(both, None, None),
            P(both),
            P(),
            P(),
            P(),
            P(both, None),
            P(both, None),
            P(both, None),
            P(both, None),
        ),
        out_specs=(
            P(both, None, None),
            P(both, None, None),
            P(),
            P(),
            P(both, None),
            P(both, None),
            P(both, None),
            P(both, None),
        ),
        check_vma=False,
    )
```

```python
import functools
import math

import jax
import jax.numpy as jnp
from jax import lax
from jax.experimental import pallas as pl
from jax.experimental.pallas import tpu as pltpu
from jax.sharding import PartitionSpec as P

HEADS = 16
HEAD_DIM = 128
GROUP = 16
CUBE = 8
EPSILON = 1e-05
MESH = pl.DeviceIdType.MESH
CONTRACT_LAST = (((1,), (1,)), ((), ()))
CONTRACT_FIRST = (((0,), (0,)), ((), ()))
MIB = 1 << 20
BF = jnp.bfloat16
F32 = jnp.float32


class Here:
    def __init__(self):
        self.rep = lax.axis_index("rep")
        shard = lax.axis_index("shard")
        self.lo = shard % GROUP
        self.base = shard - self.lo
        self.bits = [(self.lo // (1 << i)) % 2 for i in range(4)]

    def flip(self, mask):
        out = self.lo
        for i in range(4):
            if mask & (1 << i):
                out = out + (1 << i) * (1 - 2 * self.bits[i])
        return out

    def dev(self, mask):
        return (self.rep, self.base + self.flip(mask))

    def partner(self):
        return (1 - self.rep, self.base + self.lo)


def barrier(here, masks, partner):
    sem = pltpu.get_barrier_semaphore()
    targets = [here.dev(m) for m in masks]
    if partner:
        targets.append(here.partner())
    for t in targets:
        pl.semaphore_signal(sem, inc=1, device_id=t, device_id_type=MESH)
    pl.semaphore_wait(sem, len(targets))


TREE = (1, 2, 4, 8, 12)
ALL = tuple(range(1, GROUP))


def rcopy(src, dst, send, recv, dev):
    return pltpu.make_async_remote_copy(
        src_ref=src, dst_ref=dst, send_sem=send, recv_sem=recv, device_id=dev, device_id_type=MESH
    )


class Gather:
    sems = (4, 7)

    def __init__(self, here, x, out, send, recv):
        self.here, self.x, self.out, self.send, self.recv = here, x, out, send, recv
        self.half = x.shape[0] // 2
        self.off = here.lo - here.lo % out.shape[0]
        self.far = (1, 3, 2) if out.shape[0] == GROUP else (1,)
        self.sent = []

    def block(self, mask):
        return self.here.flip(mask) - self.off

    def _go(self, block, part, j, slot, mask):
        ref = self.out.at[block, pl.ds(part * self.half, self.half)]
        c = rcopy(ref, ref, self.send.at[j, slot], self.recv.at[j, slot], self.here.dev(mask))
        c.start()
        self.sent.append(c)

    def _wait(self, j, slot, block, part):
        ref = self.out.at[block, pl.ds(part * self.half, self.half)]
        rcopy(ref, ref, self.send.at[j, slot], self.recv.at[j, slot], self.here.dev(1)).wait_recv()

    def begin(self, own_sem):
        own = pltpu.make_async_copy(self.x, self.out.at[self.block(0)], own_sem)
        own.start()
        for j in self.far:
            c = rcopy(self.x, self.out.at[self.block(0)], self.send.at[j, 6], self.recv.at[j, 6], self.here.dev(4 * j))
            c.start()
            self.sent.append(c)
        own.wait()
        self.spread(0)

    def spread(self, j):
        b = self.block(4 * j)
        if j:
            ref = self.out.at[b]
            rcopy(ref, ref, self.send.at[j, 6], self.recv.at[j, 6], self.here.dev(4)).wait_recv()
        self._go(b, 0, j, 0, 1)
        self._go(b, 1, j, 1, 2)
        self._go(b, 0, j, 2, 2)
        self._go(b, 1, j, 3, 1)

    def forward(self, j):
        m = 4 * j
        self._wait(j, 0, self.block(m ^ 1), 0)
        self._go(self.block(m ^ 1), 0, j, 4, 2)
        self._wait(j, 1, self.block(m ^ 2), 1)
        self._go(self.block(m ^ 2), 1, j, 5, 1)

    def settle(self, j):
        m = 4 * j
        self._wait(j, 2, self.block(m ^ 2), 0)
        self._wait(j, 3, self.block(m ^ 1), 1)
        self._wait(j, 4, self.block(m ^ 3), 0)
        self._wait(j, 5, self.block(m ^ 3), 1)

    def end(self):
        for c in self.sent:
            c.wait_send()


def rowwise(n, step, body):
    def at(i, carry):
        body(pl.ds(pl.multiple_of(i * step, step), step))
        return carry

    lax.fori_loop(0, n // step, at, 0)


class Scatter:
    sems = (4, 7)

    @staticmethod
    def scratch(rows, d, span=GROUP):
        h = rows // 2
        zs = span // 4
        return [
            pltpu.VMEM((zs, 4, h, d), BF),
            pltpu.VMEM((zs, 2, h, d), BF),
            pltpu.VMEM((zs - 1, rows, d), BF),
            pltpu.SemaphoreType.DMA(Scatter.sems),
            pltpu.SemaphoreType.DMA(Scatter.sems),
        ]

    def __init__(self, here, part, scratch):
        self.here, self.part = here, part
        self.first, self.second, self.zin, self.send, self.recv = scratch
        self.rows = part.shape[1]
        self.off = here.lo - here.lo % part.shape[0]
        self.far = tuple(range(1, part.shape[0] // 4))
        self.half = self.rows // 2
        self.sent = []

    def _copy(self, j, slot, src, dst, mask):
        return rcopy(src, dst, self.send.at[j, slot], self.recv.at[j, slot], self.here.dev(mask))

    def _go(self, *a):
        c = self._copy(*a)
        c.start()
        self.sent.append(c)

    def _piece(self, mask, part):
        return self.part.at[self.here.flip(mask) - self.off, pl.ds(part * self.half, self.half)]

    def start(self, j):
        m = 4 * j
        self._go(j, 1, self._piece(m ^ 3, 0), self.first.at[j, 1], 2)
        self._go(j, 3, self._piece(m ^ 3, 1), self.first.at[j, 3], 1)
        self._go(j, 0, self._piece(m ^ 2, 0), self.first.at[j, 0], 2)
        self._go(j, 2, self._piece(m ^ 1, 1), self.first.at[j, 2], 1)

    def cross(self, j):
        m = 4 * j
        h = self.half
        for slot, mask, part, to in ((1, 1, 0, 1), (3, 2, 1, 2)):
            self._copy(j, slot, self.first.at[j, slot], self.first.at[j, slot], 1).wait_recv()
            own = self._piece(m ^ mask, part)

            def body(r, own=own, slot=slot):
                own[r] = (own[r].astype(F32) + self.first[j, slot, r].astype(F32)).astype(BF)

            rowwise(h, 16, body)
            self._go(j, 4 + part, own, self.second.at[j, part], to)

    def finish(self, j, out=None):
        m = 4 * j
        h = self.half
        for part, slot in ((0, 0), (1, 2)):
            self._copy(j, slot, self.first.at[j, slot], self.first.at[j, slot], 1).wait_recv()
            self._copy(j, 4 + part, self.second.at[j, part], self.second.at[j, part], 1).wait_recv()
        if out is not None:
            for k in self.far:
                self._copy(k, 6, self.zin.at[k - 1], self.zin.at[k - 1], 4).wait_recv()
        for part, slot in ((0, 0), (1, 2)):
            own = self._piece(m, part)

            def body(r, own=own, part=part, slot=slot):
                total = own[r].astype(F32) + self.first[j, slot, r].astype(F32) + self.second[j, part, r].astype(F32)
                at = pl.ds(part * h + r.start, r.size)
                if out is None:
                    own[r] = total.astype(BF)
                else:
                    for k in self.far:
                        total = total + self.zin[k - 1, at].astype(F32)
                    out[at] = total.astype(out.dtype)

            rowwise(h, 16, body)
        if out is None:
            self._go(j, 6, self.part.at[self.here.flip(m) - self.off], self.zin.at[j - 1], m)

    def end(self):
        for c in self.sent:
            c.wait_send()


def any_spec(n):
    return [pl.BlockSpec(memory_space=pl.ANY)] * n


def vmem_spec(n):
    return [pl.BlockSpec(memory_space=pltpu.VMEM)] * n


def params(cid, mib=60):
    return pltpu.CompilerParams(collective_id=cid, has_side_effects=True, vmem_limit_bytes=mib * MIB)


def exchange_columns(here, src, dst, width, cols, span, send, recv, own_sem):
    copies = []
    own = []
    for i, c in enumerate(cols):
        for m in range(GROUP):
            peer = here.flip(m)
            at = src.at[:, :, pl.ds(pl.multiple_of(c + (peer % span) * width, 128), width)]
            to = dst.at[here.rep, :, here.lo, :, pl.ds(i * width, width)]
            if m == 0:
                cp = pltpu.make_async_copy(at, to, own_sem.at[i])
                cp.start()
                own.append(cp)
            else:
                cp = rcopy(at, to, send.at[i, m], recv.at[i, m], here.dev(m))
                cp.start()
                copies.append(cp)

    def arrive():
        for cp in own:
            cp.wait()
        for i, c in enumerate(cols):
            for m in ALL:
                to = dst.at[here.rep, :, here.flip(m), :, pl.ds(i * width, width)]
                rcopy(to, to, send.at[i, m], recv.at[i, m], here.dev(m)).wait_recv()

    def end():
        for cp in copies:
            cp.wait_send()

    return arrive, end


def rope_parts(rope):
    other = pltpu.roll(rope, HEAD_DIM // 2, 1)
    first = lax.broadcasted_iota(jnp.int32, rope.shape, 1) < HEAD_DIM // 2
    return jnp.where(first, rope, other), jnp.where(first, -other, rope)


def turned(x, cosine, sine):
    return x * cosine + pltpu.roll(x, HEAD_DIM // 2, 1) * sine


CODE = 4096


def head_of_bin(qkv, tables, b):
    rope, code_row, code_col = tables
    slots = qkv.shape[1] // rope.shape[0]
    rows = pl.ds(b * slots, slots)
    n = GROUP * slots

    def piece(i):
        return qkv[:, rows, i * HEAD_DIM : (i + 1) * HEAD_DIM].reshape(n, HEAD_DIM)

    cos, sin = rope_parts(rope[b])
    queries = turned(piece(0).astype(F32), cos, sin).astype(BF)
    keys = turned(piece(1).astype(F32), cos, sin).astype(BF)
    query_code, key_code = code_row[b], code_col[b]
    segment_code = query_code - jnp.bitwise_and(query_code, CODE - 1)
    seen = (key_code <= query_code) & (key_code >= segment_code)
    scores = jnp.where(seen, dot_t(queries, keys) * (1.0 / math.sqrt(HEAD_DIM)), -1e30)
    weights = jnp.exp(scores - jnp.max(scores, -1, keepdims=True))
    probability = weights / jnp.sum(weights, -1, keepdims=True)
    return queries, keys, piece(2), probability, rows, cos, sin


def attend(qkv, out, tables, b):
    _, _, values, probability, rows, _, _ = head_of_bin(qkv, tables, b)
    attended = dot(probability.astype(BF), values).astype(BF)
    out[:, rows] = attended.reshape(GROUP, rows.size, HEAD_DIM)


def front_kernel(
    n1, rope, code_row, code_col, dy2, wqkv, wout, wgu, wdn,
    raw, n1g_out, dy2g, qkvs, outs, gus, dns, attn,
    n1g, wq, attended,
    gsend, grecv, own, csend, crecv, cown, psend, precv, late, group_out, ssend, srecv, sown,
):
    here = Here()
    barrier(here, ALL, True)
    tables = (rope, code_row, code_col)
    tokens, width = n1.shape
    q = exchange_columns(here, wqkv, qkvs, 128, (0, 2048, 4096), GROUP, csend.at[0], crecv.at[0], cown.at[0])
    half = wgu.shape[2] // 2
    ga = Gather(here, n1, n1g, gsend.at[0], grecv.at[0])
    gb = Gather(here, dy2, dy2g, gsend.at[1], grecv.at[1])
    gc = Gather(here, wout, outs.at[here.rep], gsend.at[2], grecv.at[2])
    o = (0, 1, 3, 2)

    def hand_over(i, dst):
        cp = rcopy(dst.at[here.rep], dst.at[here.rep], psend.at[i], precv.at[i], here.partner())
        cp.start()
        return cp

    def other_core(i, dst):
        other = dst.at[1 - here.rep]
        rcopy(other, other, psend.at[i], precv.at[i], here.partner()).wait_recv()

    ga.begin(own.at[0])
    ga.spread(o[1])
    ga.forward(o[0])
    q[0]()
    q_pass = hand_over(0, qkvs)
    ga.spread(o[2])
    ga.forward(o[1])
    ga.spread(o[3])
    ga.forward(o[2])
    gc.begin(own.at[2])
    u = exchange_columns(here, wgu, gus, half // CUBE, (0, half), CUBE, csend.at[1], crecv.at[1], cown.at[1])
    d = exchange_columns(here, wdn, dns, half // CUBE, (0,), CUBE, csend.at[2], crecv.at[2], cown.at[2])
    ga.forward(o[3])
    other_core(0, qkvs)
    get = pltpu.make_async_copy(qkvs, wq, late)
    get.start()
    get.wait()
    copies = []
    for k, j in enumerate(o):
        ga.settle(j)
        blocks = pl.ds(here.flip(4 * j) - here.lo % 4, 4)
        x = n1g[blocks].reshape(4 * tokens, width)
        raw[blocks] = dot(x, wq[...].reshape(width, wq.shape[-1])).astype(BF).reshape(4, tokens, wq.shape[-1])
        c = pltpu.make_async_copy(n1g.at[blocks], n1g_out.at[blocks], group_out.at[k])
        c.start()
        copies.append(c)
    bins = rope.shape[0]
    for b in range(bins):
        attend(raw, attended, tables, b)
        if b < 3:
            gc.spread(o[b + 1])
            gc.forward(o[b])
    swaps = []
    at = pl.ds(pl.multiple_of(here.lo * HEAD_DIM, HEAD_DIM), HEAD_DIM)
    for m in ALL:
        c = rcopy(attended.at[here.flip(m)], attn.at[:, at], ssend.at[m], srecv.at[m], here.dev(m))
        c.start()
        swaps.append(c)
    mine = pltpu.make_async_copy(attended.at[here.lo], attn.at[:, at], sown)
    mine.start()
    gb.begin(own.at[1])
    gc.forward(o[3])
    gb.spread(1)
    gb.forward(0)
    for j in o:
        gc.settle(j)
    out_pass = hand_over(3, outs)
    gb.forward(1)
    u[0]()
    u_pass = hand_over(1, gus)
    d[0]()
    d_pass = hand_over(2, dns)
    gb.settle(0)
    gb.settle(1)
    mine.wait()
    for m in ALL:
        ref = attn.at[:, pl.ds(pl.multiple_of(here.flip(m) * HEAD_DIM, HEAD_DIM), HEAD_DIM)]
        rcopy(ref, ref, ssend.at[m], srecv.at[m], here.dev(m)).wait_recv()
    for i, dst in ((1, gus), (2, dns), (3, outs)):
        other_core(i, dst)
    for c in (q_pass, u_pass, d_pass, out_pass, *swaps):
        c.wait_send()
    for c in copies:
        c.wait()
    for g in (ga, gb, gc):
        g.end()
    for _, end in (q, u, d):
        end()


def front(n1, tables, dy2, wqkv, wout, wgu, wdn, cid):
    hi, rows, _ = wqkv.shape
    ff = wdn.shape[2]
    tokens = n1.shape[0]
    shape = lambda *s: jax.ShapeDtypeStruct(s, BF)
    out_rows = wout.shape[0]
    head = 3 * HEAD_DIM
    return pl.pallas_call(
        front_kernel,
        out_shape=(
            shape(GROUP, tokens, head),
            shape(GROUP, *n1.shape),
            shape(CUBE, *dy2.shape),
            shape(2, hi, GROUP, rows, head),
            shape(2, GROUP, out_rows, wout.shape[1]),
            shape(2, hi, GROUP, rows, 2 * ff // CUBE),
            shape(2, hi, GROUP, rows, ff // CUBE),
            shape(tokens, GROUP * HEAD_DIM),
        ),
        in_specs=[*vmem_spec(4), *any_spec(5)],
        out_specs=(*vmem_spec(1), *any_spec(7)),
        scratch_shapes=[
            pltpu.VMEM((GROUP, *n1.shape), BF),
            pltpu.VMEM((2, hi, GROUP, rows, head), BF),
            pltpu.VMEM((GROUP, tokens, HEAD_DIM), BF),
            pltpu.SemaphoreType.DMA((3,) + Gather.sems),
            pltpu.SemaphoreType.DMA((3,) + Gather.sems),
            pltpu.SemaphoreType.DMA((3,)),
            pltpu.SemaphoreType.DMA((3, 3, GROUP)),
            pltpu.SemaphoreType.DMA((3, 3, GROUP)),
            pltpu.SemaphoreType.DMA((3, 3)),
            pltpu.SemaphoreType.DMA((4,)),
            pltpu.SemaphoreType.DMA((4,)),
            pltpu.SemaphoreType.DMA,
            pltpu.SemaphoreType.DMA((4,)),
            pltpu.SemaphoreType.DMA((GROUP,)),
            pltpu.SemaphoreType.DMA((GROUP,)),
            pltpu.SemaphoreType.DMA,
        ],
        compiler_params=params(cid, 40),
    )(n1, *tables, dy2, wqkv, wout, wgu, wdn)


def pair_add(here, g, inbox, send, recv):
    cp = rcopy(g.at[1 - here.rep], inbox, send, recv, here.partner())
    cp.start()
    cp.wait()

    def body(r):
        g[here.rep, r] = (g[here.rep, r].astype(F32) + inbox[r].astype(F32)).astype(BF)

    rowwise(inbox.shape[0], 16, body)


def send_home(here, total, out, send, recv, own):
    _, hi, rows, _ = out.shape

    def block(h, m):
        at = (h * GROUP + here.flip(m)) * rows
        return total.at[pl.ds(pl.multiple_of(at, rows), rows)]

    cps = []
    owns = []
    for h in range(hi):
        for m in ALL:
            c = rcopy(block(h, m), out.at[here.lo, h], send.at[h, m], recv.at[h, m], here.dev(m))
            c.start()
            cps.append(c)
        c = pltpu.make_async_copy(block(h, 0), out.at[here.lo, h], own.at[h])
        c.start()
        owns.append(c)

    def end():
        for c in owns:
            c.wait()
        for h in range(hi):
            for m in ALL:
                ref = out.at[here.flip(m), h]
                rcopy(ref, ref, send.at[h, m], recv.at[h, m], here.dev(m)).wait_recv()
        for c in cps:
            c.wait_send()

    return end


def home_sems(hi):
    return [
        pltpu.SemaphoreType.DMA((hi, GROUP)),
        pltpu.SemaphoreType.DMA((hi, GROUP)),
        pltpu.SemaphoreType.DMA((hi,)),
    ]


def mlp_kernel(
    mixa, mixm, n2, dy2g_in, wgu_in, wdn_in, hs, gs, wout, y1, y2p, grads_out, dx2, dy1, d_out, sums,
    n2g, dy2g, wgu, wdn, part, hidden, dgu, y2s, grads, inbox, dn2,
    gsend, grecv, own, load, y2sem, psend, precv, late, *scratch,
):
    here = Here()
    barrier(here, (1, 2, 4), True)
    g = Gather(here, n2, n2g, gsend, grecv)
    rs = Scatter(here, part, scratch)
    g.begin(own)
    loads = []
    for i, (src, dst) in enumerate(((wgu_in, wgu), (wdn_in, wdn), (dy2g_in, dy2g))):
        c = pltpu.make_async_copy(src, dst, load.at[i])
        c.start()
        loads.append(c)
    width, ff = wdn.shape
    tokens = n2.shape[0]
    group_rows = 4 * tokens
    step = 256
    y2copies = []

    def compute(j):
        first = here.flip(4 * j) - here.lo % 4 - g.off
        blocks = pl.ds(first, 4)
        if not y2copies:
            for c in loads:
                c.wait()

        def gates(k, carry):
            up_at = pl.ds(pl.multiple_of(k * step, step), step)
            gate_at = pl.ds(pl.multiple_of(ff + k * step, step), step)
            x = n2g[blocks].reshape(group_rows, width)
            up = dot(x, wgu[:, up_at])
            gate = dot(x, wgu[:, gate_at])
            dh = dot(dy2g[blocks].reshape(group_rows, width), wdn[:, up_at])
            sigmoid = 1.0 / (1.0 + jnp.exp(-gate))
            silu = gate * sigmoid
            hidden[blocks, :, up_at] = (silu * up).astype(BF).reshape(4, tokens, step)
            dgu[blocks, :, up_at] = (dh * silu).astype(BF).reshape(4, tokens, step)
            dgu[blocks, :, gate_at] = (
                (dh * up * sigmoid * (1.0 + gate * (1.0 - sigmoid))).astype(BF).reshape(4, tokens, step)
            )
            return carry

        lax.fori_loop(0, ff // step, gates, 0)
        if y2copies:
            y2copies[-1].wait()

        def outputs(k, carry):
            at = pl.ds(pl.multiple_of(k * step, step), step)
            h = hidden[blocks].reshape(group_rows, ff)
            y2s[:, :, at] = dot_t(h, wdn[at, :]).astype(BF).reshape(4, tokens, step)
            d = dgu[blocks].reshape(group_rows, 2 * ff)
            part[blocks, :, at] = dot_t(d, wgu[at, :]).astype(BF).reshape(4, tokens, step)
            return carry

        lax.fori_loop(0, width // step, outputs, 0)
        c = pltpu.make_async_copy(y2s, y2p.at[blocks], y2sem.at[len(y2copies)])
        c.start()
        y2copies.append(c)

    half = width // 2
    chunks = half // step

    def weight_grads(which, k):
        cols = pl.ds(pl.multiple_of(which * half + k * step, step), step)
        rows = pl.ds(pl.multiple_of(k * step, step), step)
        x = n2g[:, :, cols].reshape(CUBE * tokens, step)
        grads[which, rows, : 2 * ff] = t_dot(x, dgu[...].reshape(CUBE * tokens, 2 * ff)).astype(BF)
        x = dy2g[:, :, cols].reshape(CUBE * tokens, step)
        grads[which, rows, 2 * ff :] = t_dot(x, hidden[...].reshape(CUBE * tokens, ff)).astype(BF)

    def pass_chunk(k):
        rows = pl.ds(pl.multiple_of(k * step, step), step)
        return rcopy(grads.at[1 - here.rep, rows], inbox.at[rows], psend.at[k], precv.at[k], here.partner())

    g.spread(1)
    g.forward(0)
    g.settle(0)
    compute(0)
    rs.start(0)
    g.forward(1)
    rs.cross(0)
    g.settle(1)
    compute(1)
    rs.start(1)

    def other_half(k, carry):
        weight_grads(1 - here.rep, k)
        pass_chunk(k).start()
        return carry

    lax.fori_loop(0, chunks, other_half, 0)
    rs.cross(1)
    rs.finish(1)

    def own_half(k, carry):
        weight_grads(here.rep, k)
        return carry

    lax.fori_loop(0, chunks, own_half, 0)
    g.end()
    streams = hs.shape[0]
    loads = []
    for i, (src, dst) in enumerate(((hs, n2g.at[:streams]), (gs, n2g.at[streams : 2 * streams]), (wout, wgu))):
        c = pltpu.make_async_copy(src, dst, late.at[i])
        c.start()
        loads.append(c)

    def add(k, carry):
        pass_chunk(k).wait()

        def rows_add(i, carry):
            r = pl.ds(pl.multiple_of(k * step + i * 16, 16), 16)
            grads[here.rep, r] = (grads[here.rep, r].astype(F32) + inbox[r].astype(F32)).astype(BF)
            return carry

        return lax.fori_loop(0, step // 16, rows_add, carry)

    lax.fori_loop(0, chunks, add, 0)
    out = pltpu.make_async_copy(grads.at[here.rep], grads_out, late.at[3])
    out.start()
    rs.finish(0, dn2)
    for c in loads:
        c.wait()
    turn(read_mix(mixa), read_mix(mixm), n2g, y1, dn2, wgu, dx2, dy1, d_out, sums)
    out.wait()
    y2copies[-1].wait()
    rs.end()


def mlp(mixa, mixm, n2, dy2g, wgu, wdn, hs, gs, wout, y1, cid):
    tokens, width = n2.shape
    ff = wdn.shape[1]
    half = width // 2
    blocks = (CUBE, tokens)
    return pl.pallas_call(
        mlp_kernel,
        out_shape=(
            jax.ShapeDtypeStruct((*blocks, width), BF),
            jax.ShapeDtypeStruct((half, 3 * ff), BF),
            jax.ShapeDtypeStruct((tokens, width), F32),
            jax.ShapeDtypeStruct((tokens, width), BF),
            jax.ShapeDtypeStruct((tokens, width), BF),
            jax.ShapeDtypeStruct((24, 16, 128), F32),
        ),
        in_specs=[*smem_spec(2), *vmem_spec(1), *any_spec(6), *vmem_spec(1)],
        out_specs=(*any_spec(2), *vmem_spec(4)),
        scratch_shapes=[
            pltpu.VMEM((*blocks, width), BF),
            pltpu.VMEM((*blocks, width), BF),
            pltpu.VMEM(wgu.shape, BF),
            pltpu.VMEM(wdn.shape, BF),
            pltpu.VMEM((*blocks, width), BF),
            pltpu.VMEM((*blocks, ff), BF),
            pltpu.VMEM((*blocks, 2 * ff), BF),
            pltpu.VMEM((4, tokens, width), BF),
            pltpu.VMEM((2, half, 3 * ff), BF),
            pltpu.VMEM((half, 3 * ff), BF),
            pltpu.VMEM((tokens, width), F32),
            pltpu.SemaphoreType.DMA(Gather.sems),
            pltpu.SemaphoreType.DMA(Gather.sems),
            pltpu.SemaphoreType.DMA,
            pltpu.SemaphoreType.DMA((3,)),
            pltpu.SemaphoreType.DMA((4,)),
            pltpu.SemaphoreType.DMA((half // 256,)),
            pltpu.SemaphoreType.DMA((half // 256,)),
            pltpu.SemaphoreType.DMA((4,)),
            *Scatter.scratch(tokens, width, CUBE),
        ],
        compiler_params=params(cid, 63),
        cost_estimate=pl.CostEstimate(
            flops=2 * CUBE * tokens * width * ff * 9, bytes_accessed=60 * MIB, transcendentals=0
        ),
    )(mixa, mixm, n2, dy2g, wgu, wdn, hs, gs, wout, y1)


def attend_back(qkv, d_out, dqkv, tables, b):
    queries, keys, values, probability, rows, cos, sin = head_of_bin(qkv, tables, b)
    n, slots = queries.shape[0], rows.size
    scale = 1.0 / math.sqrt(HEAD_DIM)
    grad = d_out[:, rows].reshape(n, HEAD_DIM)
    grad_values = t_dot(probability.astype(BF), grad)
    grad_probs = dot_t(grad, values)
    shared = jnp.sum(grad_probs * probability, -1, keepdims=True)
    grad_scores = (probability * (grad_probs - shared)).astype(BF)
    grad_query = dot(grad_scores, keys) * scale
    grad_keys = t_dot(grad_scores, queries) * scale
    for i, v in enumerate((turned(grad_query, cos, -sin), turned(grad_keys, cos, -sin), grad_values)):
        dqkv[:, rows, i * HEAD_DIM : (i + 1) * HEAD_DIM] = v.astype(BF).reshape(GROUP, slots, HEAD_DIM)


def back_kernel(
    d_rows, qkv, qkvs, dy1, attn, rope, code_row, code_col, n1g, y2_in, gmlp,
    dn_out, y2_out, gout_out, gqkv_out, gmlp_out,
    d_out, dqkv, dn, y2, gout, stage, gqkv, tiles, obox, qbox,
    dsend, drecv, down, load, tile_sem, osend, orecv, qsend, qrecv, *scratch,
):
    here = Here()
    barrier(here, ALL, True)
    tables = (rope, code_row, code_col)
    bins = rope.shape[0]
    swaps = []
    for m in ALL:
        at = pl.ds(pl.multiple_of(here.flip(m) * HEAD_DIM, HEAD_DIM), HEAD_DIM)
        c = rcopy(d_rows.at[:, at], d_out.at[here.lo], dsend.at[m], drecv.at[m], here.dev(m))
        c.start()
        swaps.append(c)
    at = pl.ds(pl.multiple_of(here.lo * HEAD_DIM, HEAD_DIM), HEAD_DIM)
    mine = pltpu.make_async_copy(d_rows.at[:, at], d_out.at[here.lo], down)
    mine.start()
    y2_load = pltpu.make_async_copy(y2_in, y2, load)
    y2_load.start()
    _, tokens, width = dn.shape
    k = len(Scatter.scratch(16, 128))
    rs_dn = Scatter(here, dn, scratch[:k])
    rs_y2 = Scatter(here, y2, scratch[k : 2 * k])
    rs_go = Scatter(here, gout.reshape(GROUP, gout.shape[0] // GROUP, width), scratch[2 * k : 3 * k])
    qhome, mhome = scratch[3 * k : 3 * k + 3], scratch[3 * k + 3 :]
    order = (2, 3, 1, 0)
    y2_load.wait()
    rs_y2.start(1)
    rs_y2.start(0)
    end_mlp = send_home(here, gmlp, gmlp_out, *mhome)
    mine.wait()
    for m in ALL:
        ref = d_out.at[here.flip(m)]
        rcopy(ref, ref, dsend.at[m], drecv.at[m], here.dev(m)).wait_recv()

    half = width // 2
    step = 256
    chunks = half // step

    def out_grads(which, k):
        cols = pl.ds(pl.multiple_of(which * half + k * step, step), step)
        return t_dot(attn[:, cols], dy1[...]).astype(BF)

    def gout_pass(k):
        at = pl.ds(k * step, step)
        return rcopy(stage.at[k % 2], obox.at[at], osend.at[k], orecv.at[k], here.partner())

    gqkv_pair = rcopy(gqkv.at[1 - here.rep], qbox, qsend, qrecv, here.partner())

    for b in range(bins):
        attend_back(qkv, d_out, dqkv, tables, b)
        if b == 1:
            rs_y2.cross(1)
        elif b == 2:
            rs_y2.cross(0)
            rs_y2.finish(1)

    narrow = tiles.shape[3]

    def qkv_tile(k):
        cols = pl.ds(k * narrow, narrow)
        return pltpu.make_async_copy(n1g.at[:, :, cols], tiles.at[k % 2], tile_sem.at[k % 2])

    qkv_tile(0).start()
    for j in order:
        blocks = pl.ds(here.flip(4 * j) - here.lo % 4, 4)

        def part(k, carry, blocks=blocks):
            at = pl.ds(pl.multiple_of(k * TILE, TILE), TILE)
            d = dqkv[blocks].reshape(4 * tokens, 3 * HEAD_DIM)
            dn[blocks, :, at] = dot_t(d, qkvs[at, :]).astype(BF).reshape(4, tokens, TILE)
            return carry

        lax.fori_loop(0, width // TILE, part, 0)
        rs_dn.start(j)
    count = width // narrow
    for k in range(count):
        if k + 1 < count:
            qkv_tile(k + 1).start()
        qkv_tile(k).wait()
        x = tiles[k % 2].reshape(GROUP * tokens, narrow)
        rows = pl.ds((k % (count // 2)) * narrow, narrow)
        gqkv[k // (count // 2), rows, :] = t_dot(x, dqkv[...].reshape(GROUP * tokens, 3 * HEAD_DIM)).astype(BF)
    gqkv_pair.start()
    rs_y2.finish(0, y2_out)
    rs_dn.cross(order[0])
    for k in range(chunks):
        if k >= 2:
            gout_pass(k - 2).wait_send()
        stage[k % 2] = out_grads(1 - here.rep, k)
        gout_pass(k).start()
    rs_dn.cross(order[1])
    rs_dn.finish(order[0])
    for k in range(chunks):
        gout[k * step : (k + 1) * step, :] = out_grads(here.rep, k)

    def add(ref, box):
        def body(r):
            ref[r] = (ref[r].astype(F32) + box[r].astype(F32)).astype(BF)

        rowwise(box.shape[0], 16, body)

    gqkv_pair.wait()
    add(gqkv.at[here.rep], qbox)
    end_qkv = send_home(here, gqkv.at[here.rep], gqkv_out, *qhome)
    rs_dn.cross(order[2])
    rs_dn.finish(order[1])
    for k in range(chunks):
        gout_pass(k).wait_recv()
        if k >= chunks - 2:
            gout_pass(k).wait_send()
    add(gout, obox)
    for j in order:
        rs_go.start(j)
    rs_dn.cross(order[3])
    rs_dn.finish(order[2])
    rs_go.cross(order[0])
    rs_go.cross(order[1])
    rs_go.finish(order[0])
    rs_go.cross(order[2])
    rs_go.finish(order[1])
    rs_go.cross(order[3])
    rs_go.finish(order[2])
    rs_dn.finish(0, dn_out)
    rs_go.finish(0, gout_out)
    end_mlp()
    end_qkv()
    for c in swaps:
        c.wait_send()
    for rs in (rs_dn, rs_y2, rs_go):
        rs.end()


def back(d_rows, qkv, qkvs, dy1, attn, tables, n1g, y2, gmlp, hi, cid):
    tokens, width = d_rows.shape
    half = width // 2
    w = qkv.shape[2]
    return pl.pallas_call(
        back_kernel,
        out_shape=(
            jax.ShapeDtypeStruct((tokens, width), F32),
            jax.ShapeDtypeStruct((tokens, width), F32),
            jax.ShapeDtypeStruct((half // GROUP, width), F32),
            jax.ShapeDtypeStruct((GROUP, hi, half // (hi * GROUP), w), BF),
            jax.ShapeDtypeStruct((GROUP, hi, half // (hi * GROUP), gmlp.shape[1]), BF),
        ),
        in_specs=[*vmem_spec(8), *any_spec(3)],
        out_specs=(*vmem_spec(3), *any_spec(2)),
        scratch_shapes=[
            pltpu.VMEM((GROUP, tokens, HEAD_DIM), BF),
            pltpu.VMEM((GROUP, tokens, w), BF),
            pltpu.VMEM((GROUP, tokens, width), BF),
            pltpu.VMEM((CUBE, tokens, width), BF),
            pltpu.VMEM((half, width), BF),
            pltpu.VMEM((2, 256, width), BF),
            pltpu.VMEM((2, half, w), BF),
            pltpu.VMEM((2, GROUP, tokens, TILE // 4), BF),
            pltpu.VMEM((half, width), BF),
            pltpu.VMEM((half, w), BF),
            pltpu.SemaphoreType.DMA((GROUP,)),
            pltpu.SemaphoreType.DMA((GROUP,)),
            pltpu.SemaphoreType.DMA,
            pltpu.SemaphoreType.DMA,
            pltpu.SemaphoreType.DMA((2,)),
            pltpu.SemaphoreType.DMA((half // 256,)),
            pltpu.SemaphoreType.DMA((half // 256,)),
            pltpu.SemaphoreType.DMA,
            pltpu.SemaphoreType.DMA,
            *Scatter.scratch(tokens, width),
            *Scatter.scratch(tokens, width, CUBE),
            *Scatter.scratch(half // GROUP, width),
            *home_sems(hi),
            *home_sems(hi),
        ],
        compiler_params=params(cid, 63),
    )(d_rows, qkv, qkvs, dy1, attn, *tables, n1g, y2, gmlp)


def read_mix(ref):
    return [[ref[i, k] for k in range(6)] for i in range(4)]


def mixed(weights, planes):
    total = weights[0] * planes[0]
    for w, p in zip(weights[1:], planes[1:]):
        total = total + w * p
    return total


def moments(x):
    centred = x - jnp.mean(x, -1, keepdims=True)
    inverse = lax.rsqrt(jnp.mean(centred * centred, -1, keepdims=True) + EPSILON)
    return centred * inverse, inverse


def normalize_back(grad_out, normed, inverse):
    return inverse * (
        grad_out
        - jnp.mean(grad_out, -1, keepdims=True)
        - normed * jnp.mean(grad_out * normed, -1, keepdims=True)
    )


def lane_sums(x):
    total = x[:, :128]
    for c in range(128, x.shape[1], 128):
        total = total + x[:, c : c + 128]
    return total


def read_x2(m, p, h, y1):
    fold = [sum(p[s][0] * m[j][1 + s] for s in range(4)) for j in range(4)]
    return mixed(fold + [sum(p[s][0] * m[s][5] for s in range(4))], [*h, y1])


TILE = 512


def open_kernel(mixa, mixm, sorter, x, g, hs, gs, n1, dy2, plane):
    m, p = read_mix(mixa), read_mix(mixm)
    tokens, streams, width = x.shape
    for src, dst in ((x, hs), (g, gs)):

        def split(r, src=src):
            v = src[r].astype(F32)
            for i in range(streams):
                plane[i, r] = v[:, i, :].astype(BF)

        rowwise(tokens, 16, split)
        for i in range(streams):
            for c in range(0, width, TILE):
                at = slice(c, c + TILE)
                dst[i, :, at] = dot(sorter[...], plane[i, :, at]).astype(BF)

    def norm(r):
        x1 = mixed([m[j][0] for j in range(4)], [hs[j, r].astype(F32) for j in range(4)])
        n1[r] = moments(x1)[0].astype(BF)
        dy2[r] = mixed([p[j][5] for j in range(4)], [gs[j, r].astype(F32) for j in range(4)]).astype(BF)

    rowwise(tokens, 16, norm)


def smem_spec(n):
    return [pl.BlockSpec(memory_space=pltpu.SMEM)] * n


def local_params(mib=60):
    return pltpu.CompilerParams(vmem_limit_bytes=mib * MIB)


def open_streams(mixa, mixm, sorter, x, g):
    tokens, streams, width = x.shape
    return pl.pallas_call(
        open_kernel,
        out_shape=(
            jax.ShapeDtypeStruct((streams, tokens, width), BF),
            jax.ShapeDtypeStruct((streams, tokens, width), BF),
            jax.ShapeDtypeStruct((tokens, width), BF),
            jax.ShapeDtypeStruct((tokens, width), BF),
        ),
        in_specs=[*smem_spec(2), *vmem_spec(3)],
        out_specs=tuple(vmem_spec(4)),
        scratch_shapes=[pltpu.VMEM((streams, tokens, width), BF)],
        compiler_params=local_params(),
    )(mixa, mixm, sorter, x, g)


def middle_kernel(mixa, mixm, hs, attn, wout, y1, n2):
    m, p = read_mix(mixa), read_mix(mixm)
    tokens, width = attn.shape

    def tile(i, carry):
        at = pl.ds(pl.multiple_of(i * TILE, TILE), TILE)
        y1[:, at] = dot(attn[...], wout[:, at])
        return carry

    lax.fori_loop(0, width // TILE, tile, 0)

    def norm(r):
        x2 = read_x2(m, p, [hs[j, r].astype(F32) for j in range(4)], y1[r])
        n2[r] = moments(x2)[0].astype(BF)

    rowwise(tokens, 16, norm)


def middle(mixa, mixm, hs, attn, wout):
    tokens, width = attn.shape
    return pl.pallas_call(
        middle_kernel,
        out_shape=(
            jax.ShapeDtypeStruct((tokens, width), F32),
            jax.ShapeDtypeStruct((tokens, width), BF),
        ),
        in_specs=[*smem_spec(2), *vmem_spec(3)],
        out_specs=tuple(vmem_spec(2)),
        compiler_params=local_params(),
    )(mixa, mixm, hs, attn, wout)


def unsort(sorter, planes, out):
    streams, tokens, width = planes.shape
    for i in range(streams):

        def tile(k, carry, i=i):
            at = pl.ds(pl.multiple_of(k * TILE, TILE), TILE)
            v = planes[i, :, at]
            high = v.astype(BF)
            low = (v - high.astype(F32)).astype(BF)
            out[:, i, at] = t_dot(sorter[...], high) + t_dot(sorter[...], low)
            return carry

        lax.fori_loop(0, width // TILE, tile, 0)


def turn(m, p, planes, y1, dn2, wout, dx2, dy1, d_out, sums):
    tokens, width = y1.shape
    sums[...] = jnp.zeros_like(sums)

    def body(r):
        x2 = read_x2(m, p, [planes[j, r].astype(F32) for j in range(4)], y1[r])
        normed, inverse = moments(x2)
        dx2[r] = normalize_back(dn2[r], normed, inverse)
        for c in range(0, width, TILE):
            at = slice(c, c + TILE)
            h = [planes[j, r, at].astype(F32) for j in range(4)]
            y = y1[r, at]
            h1 = [mixed([*(m[j][1 + i] for j in range(4)), m[i][5]], [*h, y]) for i in range(4)]
            g = [planes[4 + j, r, at].astype(F32) for j in range(4)]
            dx = dx2[r, at]
            g1 = [mixed([*(p[j][1 + i] for i in range(4)), p[j][0]], [*g, dx]) for j in range(4)]
            dy1[r, at] = mixed([m[j][5] for j in range(4)], g1).astype(BF)
            for j in range(4):
                sums[j * 6] += lane_sums(h1[j] * dx)
                for i in range(4):
                    sums[j * 6 + 1 + i] += lane_sums(h1[j] * g[i])

    rowwise(tokens, 16, body)
    def tile(i, carry):
        at = pl.ds(pl.multiple_of(i * TILE, TILE), TILE)
        d_out[:, at] = dot_t(dy1[...], wout[at, :]).astype(BF)
        return carry

    lax.fori_loop(0, width // TILE, tile, 0)


def close_kernel(
    mixa, mixm, sorter, hs, gs, dx2, y1, y2, dn1, other, new, d_streams, total,
    sums, planes, fresh, mine, inbox, send, recv,
):
    here = Here()
    barrier(here, ALL, True)
    m, p = read_mix(mixa), read_mix(mixm)
    tokens, width = y1.shape
    sums[:24] = jnp.zeros((24, *sums.shape[1:]), F32)
    sums[24:] = other[...]

    def body(r):
        x1 = mixed([m[j][0] for j in range(4)], [hs[j, r].astype(F32) for j in range(4)])
        normed, inverse = moments(x1)
        planes[0, r] = normalize_back(dn1[r], normed, inverse)
        for c in range(0, width, TILE):
            at = slice(c, c + TILE)
            h = [hs[j, r, at].astype(F32) for j in range(4)]
            g = [gs[j, r, at].astype(F32) for j in range(4)]
            y = y1[r, at]
            dx = planes[0, r, at]
            dm = dx2[r, at]
            g1 = [mixed([*(p[j][1 + i] for i in range(4)), p[j][0]], [*g, dm]) for j in range(4)]
            for j in range(4):
                planes[j, r, at] = mixed([*(m[j][1 + i] for i in range(4)), m[j][0]], [*g1, dx])
                sums[j * 6] += lane_sums(h[j] * dx)
                for i in range(4):
                    sums[j * 6 + 1 + i] += lane_sums(h[j] * g1[i])
                sums[j * 6 + 5] += lane_sums(y * g1[j])
            h1 = [mixed([*(m[j][1 + i] for j in range(4)), m[i][5]], [*h, y]) for i in range(4)]
            y = y2[r, at]
            for i in range(4):
                fresh[i, r, at] = mixed([*(p[j][1 + i] for j in range(4)), p[i][5]], [*h1, y])
                sums[24 + i * 6 + 5] += lane_sums(y * g[i])

    rowwise(tokens, 16, body)
    mine[0] = jnp.sum(sums[...], axis=1)
    pair = rcopy(mine.at[0], inbox.at[0], send.at[0], recv.at[0], here.partner())
    pair.start()
    pair.wait()
    mine[1] = mine[0] + inbox[0]
    cps = []
    for k in ALL:
        c = rcopy(mine.at[1], inbox.at[k], send.at[k], recv.at[k], here.dev(k))
        c.start()
        cps.append(c)
    unsort(sorter, fresh, new)
    unsort(sorter, planes, d_streams)
    everyone = mine[1]
    for c in cps:
        c.wait()
    for k in ALL:
        everyone = everyone + inbox[k]
    total[...] = everyone


def close(mixa, mixm, sorter, hs, gs, dx2, y1, y2, dn1, other, cid):
    streams, tokens, width = hs.shape
    return pl.pallas_call(
        close_kernel,
        out_shape=(
            jax.ShapeDtypeStruct((tokens, streams, width), F32),
            jax.ShapeDtypeStruct((tokens, streams, width), F32),
            jax.ShapeDtypeStruct((48, 128), F32),
        ),
        in_specs=[*smem_spec(2), *vmem_spec(8)],
        out_specs=tuple(vmem_spec(3)),
        scratch_shapes=[
            pltpu.VMEM((48, 16, 128), F32),
            pltpu.VMEM((streams, tokens, width), F32),
            pltpu.VMEM((streams, tokens, width), F32),
            pltpu.VMEM((2, 48, 128), F32),
            pltpu.VMEM((GROUP, 48, 128), F32),
            pltpu.SemaphoreType.DMA((GROUP,)),
            pltpu.SemaphoreType.DMA((GROUP,)),
        ],
        compiler_params=params(cid),
    )(mixa, mixm, sorter, hs, gs, dx2, y1, y2, dn1, other)


def slot_layout(lengths_row, capacity):
    seq_count = lengths_row.shape[-1]
    seq_ends = jnp.cumsum(lengths_row, axis=-1)
    slot_index = jnp.arange(capacity, dtype=jnp.int32)
    segment = jnp.sum((slot_index[:, None] >= seq_ends[..., None, :]).astype(jnp.int32), axis=-1)
    seq_starts = seq_ends - lengths_row
    chosen = (segment[..., None] == jnp.arange(seq_count, dtype=jnp.int32)).astype(jnp.int32)
    start_of = jnp.sum(chosen * seq_starts[..., None, :], axis=-1)
    is_live = segment < seq_count
    segment = jnp.where(is_live, segment, seq_count + slot_index)
    position = jnp.where(is_live, slot_index - start_of, 0)
    return (segment, position)


def rope_tables(position, head_width):
    half_width = head_width // 2
    frequency = jnp.exp(
        jnp.arange(half_width, dtype=jnp.float32) * (-2.0 * math.log(10000.0) / head_width)
    )
    angles = position.astype(jnp.float32)[..., None] * frequency
    return (jnp.cos(angles), jnp.sin(angles))


def dot(a, b):
    return jnp.dot(a, b, preferred_element_type=F32)


def dot_t(a, b):
    return lax.dot_general(a, b, CONTRACT_LAST, preferred_element_type=F32)


def t_dot(a, b):
    return lax.dot_general(a, b, CONTRACT_FIRST, preferred_element_type=F32)


def shards(streams, cotangent, deal, lengths, mix_attn, mix_mlp, w_qkv, w_out, w_gu, w_down):
    tokens, stream_count, width = streams.shape
    shard_size = lax.axis_size("shard")
    hi = shard_size // GROUP
    hi_groups = [[h * GROUP + l for h in range(hi)] for l in range(GROUP)]
    shard = lax.axis_index("shard")
    my_hi = shard // GROUP
    bin_count = shard_size // 4
    my_bins = bin_count // hi
    per_bin = tokens // bin_count
    capacity = per_bin * shard_size
    ff = w_down.shape[1]

    def swap_hi(rows):
        if hi == 1:
            return rows
        return lax.all_to_all(rows, "shard", 0, 0, axis_index_groups=hi_groups, tiled=True)

    def to_bins(rows):
        return swap_hi(rows).reshape(hi, my_bins, per_bin, -1).swapaxes(0, 1).reshape(tokens, -1)

    def from_bins(rows):
        return swap_hi(rows.reshape(my_bins, hi, per_bin, -1).swapaxes(0, 1).reshape(tokens, -1))

    def gather_hi(rows):
        if hi == 1:
            return rows[None]
        return lax.all_gather(rows, "shard", axis_index_groups=hi_groups)

    def sum_hi(rows):
        if hi == 1:
            return rows[0]
        return lax.psum_scatter(rows, "shard", axis_index_groups=hi_groups)

    sorter = (jnp.arange(tokens, dtype=jnp.int32)[:, None] == deal[None, :]).astype(BF)

    hs, gs, n1, low_grad_mlp = open_streams(mix_attn, mix_mlp, sorter, streams, cotangent)
    low_attn = to_bins(n1)

    bins = lax.axis_index("rep") * bin_count + my_hi * my_bins
    lengths_here = lax.dynamic_slice_in_dim(lengths, bins, my_bins, 0)
    segment, position = slot_layout(lengths_here, capacity)

    def local_order(x):
        return x.reshape(my_bins, hi, GROUP, per_bin).swapaxes(1, 2).reshape(my_bins, capacity)

    segment, position = local_order(segment), local_order(position)
    cosine, sine = rope_tables(position, HEAD_DIM)
    code = segment * CODE + position
    tables = (jnp.concatenate([cosine, sine], -1), code[:, :, None], code[:, None, :])

    raw_qkv, n1g, dy2g, qkvs, outs, gus, dns, attn_rows = front(
        low_attn, tables, low_grad_mlp,
        gather_hi(w_qkv), gather_hi(w_out).reshape(-1, width), gather_hi(w_gu), gather_hi(w_down), 1,
    )
    rows = w_qkv.shape[0]
    qkvs = qkvs.reshape(width, 3 * HEAD_DIM)
    outs = outs.reshape(2, GROUP, hi, rows, width).swapaxes(1, 2).reshape(width, width)
    gus = gus.reshape(width, 2 * ff // CUBE)
    dns = dns.reshape(width, ff // CUBE)
    attn_rows = from_bins(attn_rows)
    y1, n2 = middle(mix_attn, mix_mlp, hs, attn_rows, outs)
    y2_part, g_mlp, dx2, low_grad_attn, grad_attn, mlp_sums = mlp(
        mix_attn, mix_mlp, n2, dy2g, gus, dns, hs, gs, outs, y1, 4
    )

    def own_rows(x):
        x = x.astype(F32).transpose(1, 2, 0, 3)
        return sum_hi(x.reshape(hi, rows, -1)).reshape(rows, x.shape[2], -1)

    attn_cols = attn_rows.reshape(tokens, 2, hi, GROUP, rows).swapaxes(2, 3).reshape(tokens, width)
    dn1, y2, g_out, g_qkv, g_mlp = back(
        to_bins(grad_attn), raw_qkv, qkvs, low_grad_attn, attn_cols, tables,
        n1g, y2_part, g_mlp, hi, 7,
    )
    g_mlp = g_mlp.astype(F32).reshape(2, CUBE, *g_mlp.shape[1:]).sum(0)
    g_mlp = own_rows(g_mlp)
    g_out = sum_hi(g_out.reshape(hi, rows, width))
    g_qkv = own_rows(g_qkv)
    new_streams, d_streams, sums = close(
        mix_attn, mix_mlp, sorter, hs, gs, dx2, y1, y2, from_bins(dn1), mlp_sums, 8
    )
    if hi > 1:
        sums = lax.psum(sums, "shard", axis_index_groups=hi_groups)
    sums = jnp.sum(sums, axis=-1).reshape(2, 4, 6)
    g_mix_attn, g_mix_mlp = sums[0], sums[1]
    block = ff // CUBE
    return (
        new_streams,
        d_streams,
        g_mix_attn,
        g_mix_mlp,
        g_qkv.reshape(rows, GROUP, 3, HEAD_DIM).swapaxes(1, 2).reshape(rows, -1),
        g_out,
        jnp.concatenate([g_mlp[:, :, :block].reshape(rows, ff), g_mlp[:, :, block : 2 * block].reshape(rows, ff)], axis=1),
        g_mlp[:, :, 2 * block :].reshape(rows, ff),
    )


def solution(mesh):
    both = ("rep", "shard")
    return jax.shard_map(
        shards,
        mesh=mesh,
        in_specs=(
            P(both, None, None),
            P(both, None, None),
            P(both),
            P(),
            P(),
            P(),
            P(both, None),
            P(both, None),
            P(both, None),
            P(both, None),
        ),
        out_specs=(
            P(both, None, None),
            P(both, None, None),
            P(),
            P(),
            P(both, None),
            P(both, None),
            P(both, None),
            P(both, None),
        ),
        check_vma=False,
    )
```

```python
import functools
import math

import jax
import jax.numpy as jnp
from jax import lax
from jax.experimental import pallas as pl
from jax.experimental.pallas import tpu as pltpu
from jax.sharding import PartitionSpec as P

HEADS = 16
HEAD_DIM = 128
GROUP = 16
CUBE = 8
EPSILON = 1e-05
MESH = pl.DeviceIdType.MESH
CONTRACT_LAST = (((1,), (1,)), ((), ()))
CONTRACT_FIRST = (((0,), (0,)), ((), ()))
MIB = 1 << 20
BF = jnp.bfloat16
F32 = jnp.float32


class Here:
    def __init__(self):
        self.rep = lax.axis_index("rep")
        shard = lax.axis_index("shard")
        self.lo = shard % GROUP
        self.base = shard - self.lo
        self.bits = [(self.lo // (1 << i)) % 2 for i in range(4)]
        one, two, three = (self.flip(m) - self.lo for m in (4, 8, 12))
        self.inner = self.bits[2] + self.bits[3] - 2 * self.bits[2] * self.bits[3]
        self.away = (
            0,
            one,
            self.inner * three + (1 - self.inner) * two,
            self.inner * two + (1 - self.inner) * three,
        )

    def flip(self, mask):
        out = self.lo
        for i in range(4):
            if mask & (1 << i):
                out = out + (1 << i) * (1 - 2 * self.bits[i])
        return out

    def dev(self, mask):
        return (self.rep, self.base + self.flip(mask))

    def partner(self):
        return (1 - self.rep, self.base + self.lo)


def barrier(here, masks, partner):
    sem = pltpu.get_barrier_semaphore()
    targets = [here.dev(m) for m in masks]
    if partner:
        targets.append(here.partner())
    for t in targets:
        pl.semaphore_signal(sem, inc=1, device_id=t, device_id_type=MESH)
    pl.semaphore_wait(sem, len(targets))


TREE = (1, 2, 4, 8, 12)
ALL = tuple(range(1, GROUP))


def rcopy(src, dst, send, recv, dev):
    return pltpu.make_async_remote_copy(
        src_ref=src, dst_ref=dst, send_sem=send, recv_sem=recv, device_id=dev, device_id_type=MESH
    )


class Gather:
    sems = (4, 7)

    def __init__(self, here, x, out, send, recv):
        self.here, self.x, self.out, self.send, self.recv = here, x, out, send, recv
        self.half = x.shape[0] // 2
        self.off = here.lo - here.lo % out.shape[0]
        self.far = (1, 3, 2) if out.shape[0] == GROUP else (1,)
        self.sent = []

    def block(self, mask):
        return self.here.flip(mask) - self.off

    def _go(self, block, part, j, slot, mask):
        ref = self.out.at[block, pl.ds(part * self.half, self.half)]
        c = rcopy(ref, ref, self.send.at[j, slot], self.recv.at[j, slot], self.here.dev(mask))
        c.start()
        self.sent.append(c)

    def _wait(self, j, slot, block, part):
        ref = self.out.at[block, pl.ds(part * self.half, self.half)]
        rcopy(ref, ref, self.send.at[j, slot], self.recv.at[j, slot], self.here.dev(1)).wait_recv()

    def begin(self, own_sem):
        own = pltpu.make_async_copy(self.x, self.out.at[self.block(0)], own_sem)
        own.start()
        for j in self.far:
            c = rcopy(self.x, self.out.at[self.block(0)], self.send.at[j, 6], self.recv.at[j, 6], self.here.dev(4 * j))
            c.start()
            self.sent.append(c)
        own.wait()
        self.spread(0)

    def spread(self, j):
        b = self.block(4 * j)
        if j:
            ref = self.out.at[b]
            rcopy(ref, ref, self.send.at[j, 6], self.recv.at[j, 6], self.here.dev(4)).wait_recv()
        self._go(b, 0, j, 0, 1)
        self._go(b, 1, j, 1, 2)
        self._go(b, 0, j, 2, 2)
        self._go(b, 1, j, 3, 1)

    def forward(self, j):
        m = 4 * j
        self._wait(j, 0, self.block(m ^ 1), 0)
        self._go(self.block(m ^ 1), 0, j, 4, 2)
        self._wait(j, 1, self.block(m ^ 2), 1)
        self._go(self.block(m ^ 2), 1, j, 5, 1)

    def settle(self, j):
        m = 4 * j
        self._wait(j, 2, self.block(m ^ 2), 0)
        self._wait(j, 3, self.block(m ^ 1), 1)
        self._wait(j, 4, self.block(m ^ 3), 0)
        self._wait(j, 5, self.block(m ^ 3), 1)

    def end(self):
        for c in self.sent:
            c.wait_send()


def rowwise(n, step, body):
    def at(i, carry):
        body(pl.ds(pl.multiple_of(i * step, step), step))
        return carry

    lax.fori_loop(0, n // step, at, 0)


class Scatter:
    sems = (5, 7)

    @staticmethod
    def scratch(rows, d, span=GROUP):
        h = rows // 2
        zs = span // 4
        return [
            pltpu.VMEM((zs, 4, h, d), BF),
            pltpu.VMEM((zs, 2, h, d), BF),
            pltpu.VMEM((5 if span == GROUP else 1, rows, d), BF),
            pltpu.SemaphoreType.DMA(Scatter.sems),
            pltpu.SemaphoreType.DMA(Scatter.sems),
        ]

    def __init__(self, here, part, scratch):
        self.here, self.part = here, part
        self.first, self.second, self.zin, self.send, self.recv = scratch
        self.rows = part.shape[1]
        self.half = self.rows // 2
        self.off = here.lo - here.lo % part.shape[0]
        self.line = part.shape[0] == GROUP
        self.sent = []

    def _copy(self, k, slot, src, dst, mask):
        return rcopy(src, dst, self.send.at[k, slot], self.recv.at[k, slot], self.here.dev(mask))

    def _go(self, *a):
        c = self._copy(*a)
        c.start()
        self.sent.append(c)

    def _block(self, k, q):
        return self.here.flip(q) + self.here.away[k] - self.off

    def _piece(self, k, q, part):
        return self.part.at[self._block(k, q), pl.ds(part * self.half, self.half)]

    def start(self, k):
        self._go(k, 1, self._piece(k, 3, 0), self.first.at[k, 1], 2)
        self._go(k, 3, self._piece(k, 3, 1), self.first.at[k, 3], 1)
        self._go(k, 0, self._piece(k, 2, 0), self.first.at[k, 0], 2)
        self._go(k, 2, self._piece(k, 1, 1), self.first.at[k, 2], 1)

    def cross(self, k):
        h = self.half
        for slot, q, part, to in ((1, 1, 0, 1), (3, 2, 1, 2)):
            self._copy(k, slot, self.first.at[k, slot], self.first.at[k, slot], 1).wait_recv()
            own = self._piece(k, q, part)

            def body(r, own=own, slot=slot):
                own[r] = (own[r].astype(F32) + self.first[k, slot, r].astype(F32)).astype(BF)

            rowwise(h, 16, body)
            self._go(k, 4 + part, own, self.second.at[k, part], to)

    def _reduce(self, k, boxes, out):
        h = self.half
        for part, slot in ((0, 0), (1, 2)):
            own = self._piece(k, 0, part)

            def body(r, own=own, part=part, slot=slot):
                total = own[r].astype(F32) + self.first[k, slot, r].astype(F32) + self.second[k, part, r].astype(F32)
                at = pl.ds(part * h + r.start, r.size)
                for b in boxes:
                    total = total + self.zin[b, at].astype(F32)
                if out is None:
                    own[r] = total.astype(BF)
                else:
                    out[at] = total.astype(out.dtype)

            rowwise(h, 16, body)

    def _box(self, b):
        return self.zin.at[b], self.recv.at[(1, 2, 3, 0, 4)[b], 6]

    def _pass(self, k, b, mask):
        box, full = self._box(b)
        return rcopy(self.part.at[self._block(k, 0)], box, self.send.at[k, 6], full, self.here.dev(mask))

    def _full(self, b):
        box, full = self._box(b)
        rcopy(box, box, self.send.at[0, 6], full, self.here.dev(4)).wait_recv()

    def finish(self, k, out=None):
        for part, slot in ((0, 0), (1, 2)):
            self._copy(k, slot, self.first.at[k, slot], self.first.at[k, slot], 1).wait_recv()
            self._copy(k, 4 + part, self.second.at[k, part], self.second.at[k, part], 1).wait_recv()
        if k == 0:
            self._full(0)
        if not self.line:
            self._reduce(k, () if k else (0,), out)
            if k:
                self._pass(k, 0, 4).start()
                self.sent.append(self._pass(k, 0, 4))
            return
        inner = self.here.inner

        @pl.when(inner == 0)
        def _():
            self._reduce(k, () if k else (0,), out)
            if k:
                self._pass(k, k - 1, 4).start()

        @pl.when(inner == 1)
        def _():
            boxes = ((0, 3), (4,), (1,), (2,))[k]
            for b in boxes:
                if b:
                    self._full(b)
            self._reduce(k, boxes, out)
            if k == 1:
                self._pass(k, 0, 4).start()
            elif k:
                self._pass(k, k + 1, 12).start()

        if k:
            self.sent.append(self._pass(k, 0, 4))

    def end(self):
        for c in self.sent:
            c.wait_send()


def any_spec(n):
    return [pl.BlockSpec(memory_space=pl.ANY)] * n


def vmem_spec(n):
    return [pl.BlockSpec(memory_space=pltpu.VMEM)] * n


def params(cid, mib=60):
    return pltpu.CompilerParams(collective_id=cid, has_side_effects=True, vmem_limit_bytes=mib * MIB)


def exchange_columns(here, src, dst, width, cols, span, send, recv, own_sem):
    copies = []
    own = []
    for i, c in enumerate(cols):
        for m in range(GROUP):
            peer = here.flip(m)
            at = src.at[:, :, pl.ds(pl.multiple_of(c + (peer % span) * width, 128), width)]
            to = dst.at[here.rep, :, here.lo, :, pl.ds(i * width, width)]
            if m == 0:
                cp = pltpu.make_async_copy(at, to, own_sem.at[i])
                cp.start()
                own.append(cp)
            else:
                cp = rcopy(at, to, send.at[i, m], recv.at[i, m], here.dev(m))
                cp.start()
                copies.append(cp)

    def arrive():
        for cp in own:
            cp.wait()
        for i, c in enumerate(cols):
            for m in ALL:
                to = dst.at[here.rep, :, here.flip(m), :, pl.ds(i * width, width)]
                rcopy(to, to, send.at[i, m], recv.at[i, m], here.dev(m)).wait_recv()

    def end():
        for cp in copies:
            cp.wait_send()

    return arrive, end


def rope_parts(rope):
    other = pltpu.roll(rope, HEAD_DIM // 2, 1)
    first = lax.broadcasted_iota(jnp.int32, rope.shape, 1) < HEAD_DIM // 2
    return jnp.where(first, rope, other), jnp.where(first, -other, rope)


def turned(x, cosine, sine):
    return x * cosine + pltpu.roll(x, HEAD_DIM // 2, 1) * sine


CODE = 4096


def head_of_bin(qkv, tables, b):
    rope, code_row, code_col = tables
    slots = qkv.shape[1] // rope.shape[0]
    rows = pl.ds(b * slots, slots)
    n = GROUP * slots

    def piece(i):
        return qkv[:, rows, i * HEAD_DIM : (i + 1) * HEAD_DIM].reshape(n, HEAD_DIM)

    cos, sin = rope_parts(rope[b])
    queries = turned(piece(0).astype(F32), cos, sin).astype(BF)
    keys = turned(piece(1).astype(F32), cos, sin).astype(BF)
    query_code, key_code = code_row[b], code_col[b]
    segment_code = query_code - jnp.bitwise_and(query_code, CODE - 1)
    seen = (key_code <= query_code) & (key_code >= segment_code)
    scores = jnp.where(seen, dot_t(queries, keys) * (1.0 / math.sqrt(HEAD_DIM)), -1e30)
    weights = jnp.exp(scores - jnp.max(scores, -1, keepdims=True))
    probability = weights / jnp.sum(weights, -1, keepdims=True)
    return queries, keys, piece(2), probability, rows, cos, sin


def attend(qkv, out, tables, b):
    _, _, values, probability, rows, _, _ = head_of_bin(qkv, tables, b)
    attended = dot(probability.astype(BF), values).astype(BF)
    out[:, rows] = attended.reshape(GROUP, rows.size, HEAD_DIM)


def front_kernel(
    mixm, n1, rope, code_row, code_col, sorter, g, wqkv, wout, wgu, wdn,
    raw, gs, n1g_out, dy2g, qkvs, outs, gus, dns, attn,
    n1g, wq, attended, plane, dy2,
    gsend, grecv, own, csend, crecv, cown, psend, precv, late, group_out, ssend, srecv, sown,
):
    here = Here()
    barrier(here, ALL, True)
    tables = (rope, code_row, code_col)
    tokens, width = n1.shape
    q = exchange_columns(here, wqkv, qkvs, 128, (0, 2048, 4096), GROUP, csend.at[0], crecv.at[0], cown.at[0])
    half = wgu.shape[2] // 2
    ga = Gather(here, n1, n1g, gsend.at[0], grecv.at[0])
    gb = Gather(here, dy2, dy2g, gsend.at[1], grecv.at[1])
    gc = Gather(here, wout, outs.at[here.rep], gsend.at[2], grecv.at[2])
    o = (0, 1, 3, 2)

    def hand_over(i, dst):
        cp = rcopy(dst.at[here.rep], dst.at[here.rep], psend.at[i], precv.at[i], here.partner())
        cp.start()
        return cp

    def other_core(i, dst):
        other = dst.at[1 - here.rep]
        rcopy(other, other, psend.at[i], precv.at[i], here.partner()).wait_recv()

    ga.begin(own.at[0])
    ga.spread(o[1])
    ga.forward(o[0])
    q[0]()
    q_pass = hand_over(0, qkvs)
    ga.spread(o[2])
    ga.forward(o[1])
    ga.spread(o[3])
    ga.forward(o[2])
    gc.begin(own.at[2])
    u = exchange_columns(here, wgu, gus, half // CUBE, (0, half), CUBE, csend.at[1], crecv.at[1], cown.at[1])
    d = exchange_columns(here, wdn, dns, half // CUBE, (0,), CUBE, csend.at[2], crecv.at[2], cown.at[2])
    ga.forward(o[3])
    sort_planes(sorter, g, gs, plane)
    p = read_mix(mixm)

    def to_branch(r):
        dy2[r] = mixed([p[j][5] for j in range(4)], [gs[j, r].astype(F32) for j in range(4)]).astype(BF)

    rowwise(tokens, 16, to_branch)
    other_core(0, qkvs)
    get = pltpu.make_async_copy(qkvs, wq, late)
    get.start()
    get.wait()
    copies = []
    for k, j in enumerate(o):
        ga.settle(j)
        blocks = pl.ds(here.flip(4 * j) - here.lo % 4, 4)
        x = n1g[blocks].reshape(4 * tokens, width)
        raw[blocks] = dot(x, wq[...].reshape(width, wq.shape[-1])).astype(BF).reshape(4, tokens, wq.shape[-1])
        c = pltpu.make_async_copy(n1g.at[blocks], n1g_out.at[blocks], group_out.at[k])
        c.start()
        copies.append(c)
    bins = rope.shape[0]
    for b in range(bins):
        attend(raw, attended, tables, b)
        if b < 3:
            gc.spread(o[b + 1])
            gc.forward(o[b])
    swaps = []
    at = pl.ds(pl.multiple_of(here.lo * HEAD_DIM, HEAD_DIM), HEAD_DIM)
    for m in ALL:
        c = rcopy(attended.at[here.flip(m)], attn.at[:, at], ssend.at[m], srecv.at[m], here.dev(m))
        c.start()
        swaps.append(c)
    mine = pltpu.make_async_copy(attended.at[here.lo], attn.at[:, at], sown)
    mine.start()
    gb.begin(own.at[1])
    gc.forward(o[3])
    gb.spread(1)
    gb.forward(0)
    for j in o:
        gc.settle(j)
    out_pass = hand_over(3, outs)
    gb.forward(1)
    u[0]()
    u_pass = hand_over(1, gus)
    d[0]()
    d_pass = hand_over(2, dns)
    gb.settle(0)
    gb.settle(1)
    mine.wait()
    for m in ALL:
        ref = attn.at[:, pl.ds(pl.multiple_of(here.flip(m) * HEAD_DIM, HEAD_DIM), HEAD_DIM)]
        rcopy(ref, ref, ssend.at[m], srecv.at[m], here.dev(m)).wait_recv()
    for i, dst in ((1, gus), (2, dns), (3, outs)):
        other_core(i, dst)
    for c in (q_pass, u_pass, d_pass, out_pass, *swaps):
        c.wait_send()
    for c in copies:
        c.wait()
    for g in (ga, gb, gc):
        g.end()
    for _, end in (q, u, d):
        end()


def front(mixm, n1, tables, sorter, g, wqkv, wout, wgu, wdn, cid):
    hi, rows, _ = wqkv.shape
    ff = wdn.shape[2]
    tokens = n1.shape[0]
    shape = lambda *s: jax.ShapeDtypeStruct(s, BF)
    out_rows = wout.shape[0]
    head = 3 * HEAD_DIM
    return pl.pallas_call(
        front_kernel,
        out_shape=(
            shape(GROUP, tokens, head),
            shape(g.shape[1], tokens, g.shape[2]),
            shape(GROUP, *n1.shape),
            shape(CUBE, *n1.shape),
            shape(2, hi, GROUP, rows, head),
            shape(2, GROUP, out_rows, wout.shape[1]),
            shape(2, hi, GROUP, rows, 2 * ff // CUBE),
            shape(2, hi, GROUP, rows, ff // CUBE),
            shape(tokens, GROUP * HEAD_DIM),
        ),
        in_specs=[*smem_spec(1), *vmem_spec(6), *any_spec(4)],
        out_specs=(*vmem_spec(2), *any_spec(7)),
        scratch_shapes=[
            pltpu.VMEM((GROUP, *n1.shape), BF),
            pltpu.VMEM((2, hi, GROUP, rows, head), BF),
            pltpu.VMEM((GROUP, tokens, HEAD_DIM), BF),
            pltpu.VMEM((g.shape[1], tokens, g.shape[2]), BF),
            pltpu.VMEM(n1.shape, BF),
            pltpu.SemaphoreType.DMA((3,) + Gather.sems),
            pltpu.SemaphoreType.DMA((3,) + Gather.sems),
            pltpu.SemaphoreType.DMA((3,)),
            pltpu.SemaphoreType.DMA((3, 3, GROUP)),
            pltpu.SemaphoreType.DMA((3, 3, GROUP)),
            pltpu.SemaphoreType.DMA((3, 3)),
            pltpu.SemaphoreType.DMA((4,)),
            pltpu.SemaphoreType.DMA((4,)),
            pltpu.SemaphoreType.DMA,
            pltpu.SemaphoreType.DMA((4,)),
            pltpu.SemaphoreType.DMA((GROUP,)),
            pltpu.SemaphoreType.DMA((GROUP,)),
            pltpu.SemaphoreType.DMA,
        ],
        compiler_params=params(cid, 62),
    )(mixm, n1, *tables, sorter, g, wqkv, wout, wgu, wdn)


def pair_add(here, g, inbox, send, recv):
    cp = rcopy(g.at[1 - here.rep], inbox, send, recv, here.partner())
    cp.start()
    cp.wait()

    def body(r):
        g[here.rep, r] = (g[here.rep, r].astype(F32) + inbox[r].astype(F32)).astype(BF)

    rowwise(inbox.shape[0], 16, body)


def send_home(here, total, out, send, recv, own):
    _, hi, rows, _ = out.shape

    def block(h, m):
        at = (h * GROUP + here.flip(m)) * rows
        return total.at[pl.ds(pl.multiple_of(at, rows), rows)]

    cps = []
    owns = []
    for h in range(hi):
        for m in ALL:
            c = rcopy(block(h, m), out.at[here.lo, h], send.at[h, m], recv.at[h, m], here.dev(m))
            c.start()
            cps.append(c)
        c = pltpu.make_async_copy(block(h, 0), out.at[here.lo, h], own.at[h])
        c.start()
        owns.append(c)

    def end():
        for c in owns:
            c.wait()
        for h in range(hi):
            for m in ALL:
                ref = out.at[here.flip(m), h]
                rcopy(ref, ref, send.at[h, m], recv.at[h, m], here.dev(m)).wait_recv()
        for c in cps:
            c.wait_send()

    return end


def home_sems(hi):
    return [
        pltpu.SemaphoreType.DMA((hi, GROUP)),
        pltpu.SemaphoreType.DMA((hi, GROUP)),
        pltpu.SemaphoreType.DMA((hi,)),
    ]


def mlp_kernel(
    mixa, mixm, n2, dy2g_in, wgu_in, wdn_in, hs, gs, wout, y1, y2p, grads_out, dx2, dy1, d_out, sums,
    n2g, dy2g, wgu, wdn, part, hidden, dgu, y2s, grads, inbox, dn2,
    gsend, grecv, own, load, y2sem, psend, precv, late, *scratch,
):
    here = Here()
    barrier(here, (1, 2, 4), True)
    g = Gather(here, n2, n2g, gsend, grecv)
    rs = Scatter(here, part, scratch)
    g.begin(own)
    loads = []
    for i, (src, dst) in enumerate(((wgu_in, wgu), (wdn_in, wdn), (dy2g_in, dy2g))):
        c = pltpu.make_async_copy(src, dst, load.at[i])
        c.start()
        loads.append(c)
    width, ff = wdn.shape
    tokens = n2.shape[0]
    group_rows = 4 * tokens
    step = 256
    y2copies = []

    def compute(j):
        first = here.flip(4 * j) - here.lo % 4 - g.off
        blocks = pl.ds(first, 4)
        if not y2copies:
            for c in loads:
                c.wait()

        def gates(k, carry):
            up_at = pl.ds(pl.multiple_of(k * step, step), step)
            gate_at = pl.ds(pl.multiple_of(ff + k * step, step), step)
            x = n2g[blocks].reshape(group_rows, width)
            up = dot(x, wgu[:, up_at])
            gate = dot(x, wgu[:, gate_at])
            dh = dot(dy2g[blocks].reshape(group_rows, width), wdn[:, up_at])
            sigmoid = 1.0 / (1.0 + jnp.exp(-gate))
            silu = gate * sigmoid
            hidden[blocks, :, up_at] = (silu * up).astype(BF).reshape(4, tokens, step)
            dgu[blocks, :, up_at] = (dh * silu).astype(BF).reshape(4, tokens, step)
            dgu[blocks, :, gate_at] = (
                (dh * up * sigmoid * (1.0 + gate * (1.0 - sigmoid))).astype(BF).reshape(4, tokens, step)
            )
            return carry

        lax.fori_loop(0, ff // step, gates, 0)
        if y2copies:
            y2copies[-1].wait()

        def outputs(k, carry):
            at = pl.ds(pl.multiple_of(k * step, step), step)
            h = hidden[blocks].reshape(group_rows, ff)
            y2s[:, :, at] = dot_t(h, wdn[at, :]).astype(BF).reshape(4, tokens, step)
            d = dgu[blocks].reshape(group_rows, 2 * ff)
            part[blocks, :, at] = dot_t(d, wgu[at, :]).astype(BF).reshape(4, tokens, step)
            return carry

        lax.fori_loop(0, width // step, outputs, 0)
        c = pltpu.make_async_copy(y2s, y2p.at[blocks], y2sem.at[len(y2copies)])
        c.start()
        y2copies.append(c)

    half = width // 2
    chunks = half // step

    def weight_grads(which, k):
        cols = pl.ds(pl.multiple_of(which * half + k * step, step), step)
        rows = pl.ds(pl.multiple_of(k * step, step), step)
        x = n2g[:, :, cols].reshape(CUBE * tokens, step)
        grads[which, rows, : 2 * ff] = t_dot(x, dgu[...].reshape(CUBE * tokens, 2 * ff)).astype(BF)
        x = dy2g[:, :, cols].reshape(CUBE * tokens, step)
        grads[which, rows, 2 * ff :] = t_dot(x, hidden[...].reshape(CUBE * tokens, ff)).astype(BF)

    def pass_chunk(k):
        rows = pl.ds(pl.multiple_of(k * step, step), step)
        return rcopy(grads.at[1 - here.rep, rows], inbox.at[rows], psend.at[k], precv.at[k], here.partner())

    g.spread(1)
    g.forward(0)
    g.settle(0)
    compute(0)
    rs.start(0)
    g.forward(1)
    rs.cross(0)
    g.settle(1)
    compute(1)
    rs.start(1)

    def other_half(k, carry):
        weight_grads(1 - here.rep, k)
        pass_chunk(k).start()
        return carry

    lax.fori_loop(0, chunks, other_half, 0)
    rs.cross(1)
    rs.finish(1)

    def own_half(k, carry):
        weight_grads(here.rep, k)
        return carry

    lax.fori_loop(0, chunks, own_half, 0)
    g.end()
    streams = hs.shape[0]
    loads = []
    for i, (src, dst) in enumerate(((hs, n2g.at[:streams]), (gs, n2g.at[streams : 2 * streams]), (wout, wgu))):
        c = pltpu.make_async_copy(src, dst, late.at[i])
        c.start()
        loads.append(c)

    def add(k, carry):
        pass_chunk(k).wait()

        def rows_add(i, carry):
            r = pl.ds(pl.multiple_of(k * step + i * 16, 16), 16)
            grads[here.rep, r] = (grads[here.rep, r].astype(F32) + inbox[r].astype(F32)).astype(BF)
            return carry

        return lax.fori_loop(0, step // 16, rows_add, carry)

    lax.fori_loop(0, chunks, add, 0)
    out = pltpu.make_async_copy(grads.at[here.rep], grads_out, late.at[3])
    out.start()
    rs.finish(0, dn2)
    for c in loads:
        c.wait()
    turn(read_mix(mixa), read_mix(mixm), n2g, y1, dn2, wgu, dx2, dy1, d_out, sums)
    out.wait()
    y2copies[-1].wait()
    rs.end()


def mlp(mixa, mixm, n2, dy2g, wgu, wdn, hs, gs, wout, y1, cid):
    tokens, width = n2.shape
    ff = wdn.shape[1]
    half = width // 2
    blocks = (CUBE, tokens)
    return pl.pallas_call(
        mlp_kernel,
        out_shape=(
            jax.ShapeDtypeStruct((*blocks, width), BF),
            jax.ShapeDtypeStruct((half, 3 * ff), BF),
            jax.ShapeDtypeStruct((tokens, width), F32),
            jax.ShapeDtypeStruct((tokens, width), BF),
            jax.ShapeDtypeStruct((tokens, width), BF),
            jax.ShapeDtypeStruct((24, 16, 128), F32),
        ),
        in_specs=[*smem_spec(2), *vmem_spec(1), *any_spec(6), *vmem_spec(1)],
        out_specs=(*any_spec(2), *vmem_spec(4)),
        scratch_shapes=[
            pltpu.VMEM((*blocks, width), BF),
            pltpu.VMEM((*blocks, width), BF),
            pltpu.VMEM(wgu.shape, BF),
            pltpu.VMEM(wdn.shape, BF),
            pltpu.VMEM((*blocks, width), BF),
            pltpu.VMEM((*blocks, ff), BF),
            pltpu.VMEM((*blocks, 2 * ff), BF),
            pltpu.VMEM((4, tokens, width), BF),
            pltpu.VMEM((2, half, 3 * ff), BF),
            pltpu.VMEM((half, 3 * ff), BF),
            pltpu.VMEM((tokens, width), F32),
            pltpu.SemaphoreType.DMA(Gather.sems),
            pltpu.SemaphoreType.DMA(Gather.sems),
            pltpu.SemaphoreType.DMA,
            pltpu.SemaphoreType.DMA((3,)),
            pltpu.SemaphoreType.DMA((4,)),
            pltpu.SemaphoreType.DMA((half // 256,)),
            pltpu.SemaphoreType.DMA((half // 256,)),
            pltpu.SemaphoreType.DMA((4,)),
            *Scatter.scratch(tokens, width, CUBE),
        ],
        compiler_params=params(cid, 63),
        cost_estimate=pl.CostEstimate(
            flops=2 * CUBE * tokens * width * ff * 9, bytes_accessed=60 * MIB, transcendentals=0
        ),
    )(mixa, mixm, n2, dy2g, wgu, wdn, hs, gs, wout, y1)


def attend_back(qkv, d_out, dqkv, tables, b):
    queries, keys, values, probability, rows, cos, sin = head_of_bin(qkv, tables, b)
    n, slots = queries.shape[0], rows.size
    scale = 1.0 / math.sqrt(HEAD_DIM)
    grad = d_out[:, rows].reshape(n, HEAD_DIM)
    grad_values = t_dot(probability.astype(BF), grad)
    grad_probs = dot_t(grad, values)
    shared = jnp.sum(grad_probs * probability, -1, keepdims=True)
    grad_scores = (probability * (grad_probs - shared)).astype(BF)
    grad_query = dot(grad_scores, keys) * scale
    grad_keys = t_dot(grad_scores, queries) * scale
    for i, v in enumerate((turned(grad_query, cos, -sin), turned(grad_keys, cos, -sin), grad_values)):
        dqkv[:, rows, i * HEAD_DIM : (i + 1) * HEAD_DIM] = v.astype(BF).reshape(GROUP, slots, HEAD_DIM)


class GradsHome:
    @staticmethod
    def scratch(hi, rows, w):
        return [
            pltpu.VMEM((hi, CUBE, rows, w), BF),
            pltpu.VMEM((hi, CUBE, rows, w), BF),
            *[pltpu.SemaphoreType.DMA((hi, CUBE))] * 6,
        ]

    def __init__(self, here, gmlp, out, scratch):
        self.here, self.out = here, out
        self.mine, self.box, self.zsend, self.zrecv, self.load, self.send, self.recv, self.own = scratch
        self.hi, _, self.rows, _ = self.mine.shape
        self.sent = []
        self.loads = {}
        self.gmlp = gmlp

    def begin(self, wave):
        here = self.here
        for h in range(self.hi):
            for m in wave:

                def block(mask, h=h):
                    at = (h * GROUP + here.flip(mask)) * self.rows
                    return self.gmlp.at[pl.ds(pl.multiple_of(at, self.rows), self.rows)]

                c = rcopy(block(m ^ 8), self.box.at[h, m], self.zsend.at[h, m], self.zrecv.at[h, m], here.dev(8))
                c.start()
                self.sent.append(c)
                c = pltpu.make_async_copy(block(m), self.mine.at[h, m], self.load.at[h, m])
                c.start()
                self.loads[h, m] = c

    def relay(self, m):
        here = self.here
        for h in range(self.hi):
            box, mine = self.box.at[h, m], self.mine.at[h, m]
            self.loads[h, m].wait()
            rcopy(box, box, self.zsend.at[h, m], self.zrecv.at[h, m], here.dev(8)).wait_recv()

            def body(r, box=box, mine=mine):
                mine[r] = (mine[r].astype(F32) + box[r].astype(F32)).astype(BF)

            rowwise(self.rows, 16, body)
            to = self.out.at[here.lo % CUBE, h]
            if m:
                c = rcopy(mine, to, self.send.at[h, m], self.recv.at[h, m], here.dev(m))
                self.sent.append(c)
            else:
                c = pltpu.make_async_copy(mine, to, self.own.at[h, 0])
                self.loads[h, 0] = c
            c.start()

    def end(self):
        here = self.here
        for h in range(self.hi):
            self.loads[h, 0].wait()
            for m in range(1, CUBE):
                ref = self.out.at[here.flip(m) % CUBE, h]
                rcopy(ref, ref, self.send.at[h, m], self.recv.at[h, m], here.dev(m)).wait_recv()
        for c in self.sent:
            c.wait_send()


def back_kernel(
    d_rows, qkv, qkvs, dy1, attn, rope, code_row, code_col, n1g, y2_in, gmlp,
    dn_out, y2_out, gout_out, gqkv_out, gmlp_out,
    d_out, dqkv, dn, y2, gout, stage, gqkv, tiles, obox, qbox,
    dsend, drecv, down, load, tile_sem, osend, orecv, qsend, qrecv, *scratch,
):
    here = Here()
    barrier(here, ALL, True)
    tables = (rope, code_row, code_col)
    bins = rope.shape[0]
    swaps = []
    for m in ALL:
        at = pl.ds(pl.multiple_of(here.flip(m) * HEAD_DIM, HEAD_DIM), HEAD_DIM)
        c = rcopy(d_rows.at[:, at], d_out.at[here.lo], dsend.at[m], drecv.at[m], here.dev(m))
        c.start()
        swaps.append(c)
    at = pl.ds(pl.multiple_of(here.lo * HEAD_DIM, HEAD_DIM), HEAD_DIM)
    mine = pltpu.make_async_copy(d_rows.at[:, at], d_out.at[here.lo], down)
    mine.start()
    y2_load = pltpu.make_async_copy(y2_in, y2, load)
    y2_load.start()
    _, tokens, width = dn.shape
    k = len(Scatter.scratch(16, 128))
    rs_dn = Scatter(here, dn, scratch[:k])
    rs_y2 = Scatter(here, y2, scratch[k : 2 * k])
    rs_go = Scatter(here, gout.reshape(GROUP, gout.shape[0] // GROUP, width), scratch[2 * k : 3 * k])
    qhome = scratch[3 * k : 3 * k + 3]
    gm = GradsHome(here, gmlp, gmlp_out, scratch[3 * k + 3 :])
    gm.begin((0, 1))
    order = (3, 2, 1, 0)
    y2_load.wait()
    rs_y2.start(1)
    rs_y2.start(0)
    gm.begin((2,))
    mine.wait()
    for m in ALL:
        ref = d_out.at[here.flip(m)]
        rcopy(ref, ref, dsend.at[m], drecv.at[m], here.dev(m)).wait_recv()

    half = width // 2
    step = 256
    chunks = half // step

    def out_grads(which, k):
        cols = pl.ds(pl.multiple_of(which * half + k * step, step), step)
        return t_dot(attn[:, cols], dy1[...]).astype(BF)

    def gout_pass(k):
        at = pl.ds(k * step, step)
        return rcopy(stage.at[k % 2], obox.at[at], osend.at[k], orecv.at[k], here.partner())

    gqkv_pair = rcopy(gqkv.at[1 - here.rep], qbox, qsend, qrecv, here.partner())

    for b in range(bins):
        attend_back(qkv, d_out, dqkv, tables, b)
        if b == 1:
            rs_y2.cross(1)
        elif b == 2:
            rs_y2.cross(0)
            rs_y2.finish(1)

    narrow = tiles.shape[3]

    def qkv_tile(k):
        cols = pl.ds(k * narrow, narrow)
        return pltpu.make_async_copy(n1g.at[:, :, cols], tiles.at[k % 2], tile_sem.at[k % 2])

    qkv_tile(0).start()
    gm.relay(0)
    gm.begin((3,))
    for j in order:
        blocks = pl.ds(here.lo + here.away[j] - here.lo % 4, 4)

        def part(k, carry, blocks=blocks):
            at = pl.ds(pl.multiple_of(k * TILE, TILE), TILE)
            d = dqkv[blocks].reshape(4 * tokens, 3 * HEAD_DIM)
            dn[blocks, :, at] = dot_t(d, qkvs[at, :]).astype(BF).reshape(4, tokens, TILE)
            return carry

        lax.fori_loop(0, width // TILE, part, 0)
        rs_dn.start(j)
    count = width // narrow
    for k in range(count):
        if k + 1 < count:
            qkv_tile(k + 1).start()
        qkv_tile(k).wait()
        x = tiles[k % 2].reshape(GROUP * tokens, narrow)
        rows = pl.ds((k % (count // 2)) * narrow, narrow)
        gqkv[k // (count // 2), rows, :] = t_dot(x, dqkv[...].reshape(GROUP * tokens, 3 * HEAD_DIM)).astype(BF)
    gqkv_pair.start()
    gm.relay(1)
    gm.begin((4,))
    rs_y2.finish(0, y2_out)
    rs_dn.cross(order[0])
    for k in range(chunks):
        if k >= 2:
            gout_pass(k - 2).wait_send()
        stage[k % 2] = out_grads(1 - here.rep, k)
        gout_pass(k).start()
    rs_dn.cross(order[1])
    rs_dn.finish(order[0])
    for k in range(chunks):
        gout[k * step : (k + 1) * step, :] = out_grads(here.rep, k)

    def add(ref, box):
        def body(r):
            ref[r] = (ref[r].astype(F32) + box[r].astype(F32)).astype(BF)

        rowwise(box.shape[0], 16, body)

    gqkv_pair.wait()
    add(gqkv.at[here.rep], qbox)
    gm.relay(2)
    gm.begin((5,))
    end_qkv = send_home(here, gqkv.at[here.rep], gqkv_out, *qhome)
    rs_dn.cross(order[2])
    rs_dn.finish(order[1])
    for k in range(chunks):
        gout_pass(k).wait_recv()
        if k >= chunks - 2:
            gout_pass(k).wait_send()
    add(gout, obox)
    for j in order:
        rs_go.start(j)
    rs_dn.cross(order[3])
    rs_dn.finish(order[2])
    rs_go.cross(order[0])
    gm.relay(3)
    gm.begin((6,))
    rs_go.cross(order[1])
    rs_go.finish(order[0])
    gm.relay(4)
    gm.begin((7,))
    rs_go.cross(order[2])
    rs_go.finish(order[1])
    gm.relay(5)
    rs_go.cross(order[3])
    rs_go.finish(order[2])
    rs_dn.finish(0, dn_out)
    gm.relay(6)
    rs_go.finish(0, gout_out)
    gm.relay(7)
    gm.end()
    end_qkv()
    for c in swaps:
        c.wait_send()
    for rs in (rs_dn, rs_y2, rs_go):
        rs.end()


def back(d_rows, qkv, qkvs, dy1, attn, tables, n1g, y2, gmlp, hi, cid):
    tokens, width = d_rows.shape
    half = width // 2
    w = qkv.shape[2]
    return pl.pallas_call(
        back_kernel,
        out_shape=(
            jax.ShapeDtypeStruct((tokens, width), F32),
            jax.ShapeDtypeStruct((tokens, width), F32),
            jax.ShapeDtypeStruct((half // GROUP, width), F32),
            jax.ShapeDtypeStruct((GROUP, hi, half // (hi * GROUP), w), BF),
            jax.ShapeDtypeStruct((CUBE, hi, half // (hi * GROUP), gmlp.shape[1]), BF),
        ),
        in_specs=[*vmem_spec(8), *any_spec(3)],
        out_specs=(*vmem_spec(3), *any_spec(2)),
        scratch_shapes=[
            pltpu.VMEM((GROUP, tokens, HEAD_DIM), BF),
            pltpu.VMEM((GROUP, tokens, w), BF),
            pltpu.VMEM((GROUP, tokens, width), BF),
            pltpu.VMEM((CUBE, tokens, width), BF),
            pltpu.VMEM((half, width), BF),
            pltpu.VMEM((2, 256, width), BF),
            pltpu.VMEM((2, half, w), BF),
            pltpu.VMEM((2, GROUP, tokens, TILE // 4), BF),
            pltpu.VMEM((half, width), BF),
            pltpu.VMEM((half, w), BF),
            pltpu.SemaphoreType.DMA((GROUP,)),
            pltpu.SemaphoreType.DMA((GROUP,)),
            pltpu.SemaphoreType.DMA,
            pltpu.SemaphoreType.DMA,
            pltpu.SemaphoreType.DMA((2,)),
            pltpu.SemaphoreType.DMA((half // 256,)),
            pltpu.SemaphoreType.DMA((half // 256,)),
            pltpu.SemaphoreType.DMA,
            pltpu.SemaphoreType.DMA,
            *Scatter.scratch(tokens, width),
            *Scatter.scratch(tokens, width, CUBE),
            *Scatter.scratch(half // GROUP, width),
            *home_sems(hi),
            *GradsHome.scratch(hi, half // (hi * GROUP), gmlp.shape[1]),
        ],
        compiler_params=params(cid, 63),
    )(d_rows, qkv, qkvs, dy1, attn, *tables, n1g, y2, gmlp)


def read_mix(ref):
    return [[ref[i, k] for k in range(6)] for i in range(4)]


def mixed(weights, planes):
    total = weights[0] * planes[0]
    for w, p in zip(weights[1:], planes[1:]):
        total = total + w * p
    return total


def moments(x):
    centred = x - jnp.mean(x, -1, keepdims=True)
    inverse = lax.rsqrt(jnp.mean(centred * centred, -1, keepdims=True) + EPSILON)
    return centred * inverse, inverse


def normalize_back(grad_out, normed, inverse):
    return inverse * (
        grad_out
        - jnp.mean(grad_out, -1, keepdims=True)
        - normed * jnp.mean(grad_out * normed, -1, keepdims=True)
    )


def lane_sums(x):
    total = x[:, :128]
    for c in range(128, x.shape[1], 128):
        total = total + x[:, c : c + 128]
    return total


def read_x2(m, p, h, y1):
    fold = [sum(p[s][0] * m[j][1 + s] for s in range(4)) for j in range(4)]
    return mixed(fold + [sum(p[s][0] * m[s][5] for s in range(4))], [*h, y1])


TILE = 512


def sort_planes(sorter, x, planes, plane):
    tokens, streams, width = x.shape

    def split(r):
        v = x[r].astype(F32)
        for i in range(streams):
            plane[i, r] = v[:, i, :].astype(BF)

    rowwise(tokens, 16, split)
    for i in range(streams):
        for c in range(0, width, TILE):
            at = slice(c, c + TILE)
            planes[i, :, at] = dot(sorter[...], plane[i, :, at]).astype(BF)


def open_kernel(mixa, sorter, x, hs, n1, plane):
    m = read_mix(mixa)
    sort_planes(sorter, x, hs, plane)

    def norm(r):
        x1 = mixed([m[j][0] for j in range(4)], [hs[j, r].astype(F32) for j in range(4)])
        n1[r] = moments(x1)[0].astype(BF)

    rowwise(x.shape[0], 16, norm)


def smem_spec(n):
    return [pl.BlockSpec(memory_space=pltpu.SMEM)] * n


def local_params(mib=60):
    return pltpu.CompilerParams(vmem_limit_bytes=mib * MIB)


def open_streams(mixa, sorter, x):
    tokens, streams, width = x.shape
    return pl.pallas_call(
        open_kernel,
        out_shape=(
            jax.ShapeDtypeStruct((streams, tokens, width), BF),
            jax.ShapeDtypeStruct((tokens, width), BF),
        ),
        in_specs=[*smem_spec(1), *vmem_spec(2)],
        out_specs=tuple(vmem_spec(2)),
        scratch_shapes=[pltpu.VMEM((streams, tokens, width), BF)],
        compiler_params=local_params(),
    )(mixa, sorter, x)


def middle_kernel(mixa, mixm, hs, attn, wout, y1, n2):
    m, p = read_mix(mixa), read_mix(mixm)
    tokens, width = attn.shape

    def tile(i, carry):
        at = pl.ds(pl.multiple_of(i * TILE, TILE), TILE)
        y1[:, at] = dot(attn[...], wout[:, at])
        return carry

    lax.fori_loop(0, width // TILE, tile, 0)

    def norm(r):
        x2 = read_x2(m, p, [hs[j, r].astype(F32) for j in range(4)], y1[r])
        n2[r] = moments(x2)[0].astype(BF)

    rowwise(tokens, 16, norm)


def middle(mixa, mixm, hs, attn, wout):
    tokens, width = attn.shape
    return pl.pallas_call(
        middle_kernel,
        out_shape=(
            jax.ShapeDtypeStruct((tokens, width), F32),
            jax.ShapeDtypeStruct((tokens, width), BF),
        ),
        in_specs=[*smem_spec(2), *vmem_spec(3)],
        out_specs=tuple(vmem_spec(2)),
        compiler_params=local_params(),
    )(mixa, mixm, hs, attn, wout)


def unsort(sorter, planes, out):
    streams, tokens, width = planes.shape
    for i in range(streams):

        def tile(k, carry, i=i):
            at = pl.ds(pl.multiple_of(k * TILE, TILE), TILE)
            v = planes[i, :, at]
            high = v.astype(BF)
            low = (v - high.astype(F32)).astype(BF)
            out[:, i, at] = t_dot(sorter[...], high) + t_dot(sorter[...], low)
            return carry

        lax.fori_loop(0, width // TILE, tile, 0)


def turn(m, p, planes, y1, dn2, wout, dx2, dy1, d_out, sums):
    tokens, width = y1.shape
    sums[...] = jnp.zeros_like(sums)

    def body(r):
        x2 = read_x2(m, p, [planes[j, r].astype(F32) for j in range(4)], y1[r])
        normed, inverse = moments(x2)
        dx2[r] = normalize_back(dn2[r], normed, inverse)
        for c in range(0, width, TILE):
            at = slice(c, c + TILE)
            h = [planes[j, r, at].astype(F32) for j in range(4)]
            y = y1[r, at]
            h1 = [mixed([*(m[j][1 + i] for j in range(4)), m[i][5]], [*h, y]) for i in range(4)]
            g = [planes[4 + j, r, at].astype(F32) for j in range(4)]
            dx = dx2[r, at]
            g1 = [mixed([*(p[j][1 + i] for i in range(4)), p[j][0]], [*g, dx]) for j in range(4)]
            dy1[r, at] = mixed([m[j][5] for j in range(4)], g1).astype(BF)
            for j in range(4):
                sums[j * 6] += lane_sums(h1[j] * dx)
                for i in range(4):
                    sums[j * 6 + 1 + i] += lane_sums(h1[j] * g[i])

    rowwise(tokens, 16, body)
    def tile(i, carry):
        at = pl.ds(pl.multiple_of(i * TILE, TILE), TILE)
        d_out[:, at] = dot_t(dy1[...], wout[at, :]).astype(BF)
        return carry

    lax.fori_loop(0, width // TILE, tile, 0)


def close_kernel(
    mixa, mixm, sorter, hs, gs, dx2, y1, y2, dn1, other, new, d_streams, mix_a, mix_m,
    sums, planes, fresh, mine, inbox, send, recv,
):
    here = Here()
    barrier(here, ALL, True)
    m, p = read_mix(mixa), read_mix(mixm)
    tokens, width = y1.shape
    sums[:24] = jnp.zeros((24, *sums.shape[1:]), F32)
    sums[24:] = other[...]

    def body(r):
        x1 = mixed([m[j][0] for j in range(4)], [hs[j, r].astype(F32) for j in range(4)])
        normed, inverse = moments(x1)
        planes[0, r] = normalize_back(dn1[r], normed, inverse)
        for c in range(0, width, TILE):
            at = slice(c, c + TILE)
            h = [hs[j, r, at].astype(F32) for j in range(4)]
            g = [gs[j, r, at].astype(F32) for j in range(4)]
            y = y1[r, at]
            dx = planes[0, r, at]
            dm = dx2[r, at]
            g1 = [mixed([*(p[j][1 + i] for i in range(4)), p[j][0]], [*g, dm]) for j in range(4)]
            for j in range(4):
                planes[j, r, at] = mixed([*(m[j][1 + i] for i in range(4)), m[j][0]], [*g1, dx])
                sums[j * 6] += lane_sums(h[j] * dx)
                for i in range(4):
                    sums[j * 6 + 1 + i] += lane_sums(h[j] * g1[i])
                sums[j * 6 + 5] += lane_sums(y * g1[j])
            h1 = [mixed([*(m[j][1 + i] for j in range(4)), m[i][5]], [*h, y]) for i in range(4)]
            y = y2[r, at]
            for i in range(4):
                fresh[i, r, at] = mixed([*(p[j][1 + i] for j in range(4)), p[i][5]], [*h1, y])
                sums[24 + i * 6 + 5] += lane_sums(y * g[i])

    rowwise(tokens, 16, body)
    mine[0] = jnp.sum(sums[...], axis=1)
    pair = rcopy(mine.at[0], inbox.at[0], send.at[0], recv.at[0], here.partner())
    pair.start()
    pair.wait()
    mine[1] = mine[0] + inbox[0]
    cps = []
    for k in ALL:
        c = rcopy(mine.at[1], inbox.at[k], send.at[k], recv.at[k], here.dev(k))
        c.start()
        cps.append(c)
    unsort(sorter, fresh, new)
    unsort(sorter, planes, d_streams)
    everyone = mine[1]
    for c in cps:
        c.wait()
    for k in ALL:
        everyone = everyone + inbox[k]
    everyone = jnp.sum(everyone, axis=1, keepdims=True)
    for n, out in enumerate((mix_a, mix_m)):
        row = lax.broadcasted_iota(jnp.int32, out.shape, 0)
        col = lax.broadcasted_iota(jnp.int32, out.shape, 1)
        value = jnp.zeros(out.shape, F32)
        for j in range(4):
            for c in range(6):
                k = n * 24 + j * 6 + c
                value = jnp.where((row == j) & (col == c), everyone[k : k + 1], value)
        out[...] = value


def close(mixa, mixm, sorter, hs, gs, dx2, y1, y2, dn1, other, cid):
    streams, tokens, width = hs.shape
    return pl.pallas_call(
        close_kernel,
        out_shape=(
            jax.ShapeDtypeStruct((tokens, streams, width), F32),
            jax.ShapeDtypeStruct((tokens, streams, width), F32),
            jax.ShapeDtypeStruct(mixa.shape, F32),
            jax.ShapeDtypeStruct(mixm.shape, F32),
        ),
        in_specs=[*smem_spec(2), *vmem_spec(8)],
        out_specs=tuple(vmem_spec(4)),
        scratch_shapes=[
            pltpu.VMEM((48, 16, 128), F32),
            pltpu.VMEM((streams, tokens, width), F32),
            pltpu.VMEM((streams, tokens, width), F32),
            pltpu.VMEM((2, 48, 128), F32),
            pltpu.VMEM((GROUP, 48, 128), F32),
            pltpu.SemaphoreType.DMA((GROUP,)),
            pltpu.SemaphoreType.DMA((GROUP,)),
        ],
        compiler_params=params(cid),
    )(mixa, mixm, sorter, hs, gs, dx2, y1, y2, dn1, other)


def lay_out_kernel(qkv, out, mlp, gqkv, gout, ggu, gdown):
    head = HEAD_DIM
    for l in range(qkv.shape[0]):
        for i in range(3):
            at = i * GROUP * head + l * head
            gqkv[:, :, at : at + head] = qkv[l, :, :, i * head : (i + 1) * head].astype(F32)
    block = mlp.shape[3] // 3
    for l in range(CUBE):
        for i in range(2):
            at = (i * CUBE + l) * block
            ggu[:, :, at : at + block] = mlp[l, :, :, i * block : (i + 1) * block].astype(F32)
        gdown[:, :, l * block : (l + 1) * block] = mlp[l, :, :, 2 * block :].astype(F32)
    gout[...] = out[...]


def lay_out(qkv, out, mlp):
    _, hi, rows, w = mlp.shape
    ff = w // 3 * CUBE
    shapes = [(hi, rows, GROUP * qkv.shape[3]), out.shape, (hi, rows, 2 * ff), (hi, rows, ff)]
    return pl.pallas_call(
        lay_out_kernel,
        out_shape=tuple(jax.ShapeDtypeStruct(s, F32) for s in shapes),
        in_specs=vmem_spec(3),
        out_specs=tuple(vmem_spec(4)),
        compiler_params=local_params(),
    )(qkv, out, mlp)


def slot_layout(lengths_row, capacity):
    seq_count = lengths_row.shape[-1]
    seq_ends = jnp.cumsum(lengths_row, axis=-1)
    slot_index = jnp.arange(capacity, dtype=jnp.int32)
    segment = jnp.sum((slot_index[:, None] >= seq_ends[..., None, :]).astype(jnp.int32), axis=-1)
    seq_starts = seq_ends - lengths_row
    chosen = (segment[..., None] == jnp.arange(seq_count, dtype=jnp.int32)).astype(jnp.int32)
    start_of = jnp.sum(chosen * seq_starts[..., None, :], axis=-1)
    is_live = segment < seq_count
    segment = jnp.where(is_live, segment, seq_count + slot_index)
    position = jnp.where(is_live, slot_index - start_of, 0)
    return (segment, position)


def rope_tables(position, head_width):
    half_width = head_width // 2
    frequency = jnp.exp(
        jnp.arange(half_width, dtype=jnp.float32) * (-2.0 * math.log(10000.0) / head_width)
    )
    angles = position.astype(jnp.float32)[..., None] * frequency
    return (jnp.cos(angles), jnp.sin(angles))


def dot(a, b):
    return jnp.dot(a, b, preferred_element_type=F32)


def dot_t(a, b):
    return lax.dot_general(a, b, CONTRACT_LAST, preferred_element_type=F32)


def t_dot(a, b):
    return lax.dot_general(a, b, CONTRACT_FIRST, preferred_element_type=F32)


def shards(streams, cotangent, deal, lengths, mix_attn, mix_mlp, w_qkv, w_out, w_gu, w_down):
    tokens, stream_count, width = streams.shape
    shard_size = lax.axis_size("shard")
    hi = shard_size // GROUP
    hi_groups = [[h * GROUP + l for h in range(hi)] for l in range(GROUP)]
    shard = lax.axis_index("shard")
    my_hi = shard // GROUP
    bin_count = shard_size // 4
    my_bins = bin_count // hi
    per_bin = tokens // bin_count
    capacity = per_bin * shard_size
    ff = w_down.shape[1]

    def swap_hi(rows):
        if hi == 1:
            return rows
        return lax.all_to_all(rows, "shard", 0, 0, axis_index_groups=hi_groups, tiled=True)

    def to_bins(rows):
        return swap_hi(rows).reshape(hi, my_bins, per_bin, -1).swapaxes(0, 1).reshape(tokens, -1)

    def from_bins(rows):
        return swap_hi(rows.reshape(my_bins, hi, per_bin, -1).swapaxes(0, 1).reshape(tokens, -1))

    def gather_hi(rows):
        if hi == 1:
            return rows[None]
        return lax.all_gather(rows, "shard", axis_index_groups=hi_groups)

    def sum_hi(rows):
        if hi == 1:
            return rows[0]
        return lax.psum_scatter(rows, "shard", axis_index_groups=hi_groups)

    sorter = (jnp.arange(tokens, dtype=jnp.int32)[:, None] == deal[None, :]).astype(BF)

    hs, n1 = open_streams(mix_attn, sorter, streams)
    low_attn = to_bins(n1)

    bins = lax.axis_index("rep") * bin_count + my_hi * my_bins
    lengths_here = lax.dynamic_slice_in_dim(lengths, bins, my_bins, 0)
    segment, position = slot_layout(lengths_here, capacity)

    def local_order(x):
        return x.reshape(my_bins, hi, GROUP, per_bin).swapaxes(1, 2).reshape(my_bins, capacity)

    segment, position = local_order(segment), local_order(position)
    cosine, sine = rope_tables(position, HEAD_DIM)
    code = segment * CODE + position
    tables = (jnp.concatenate([cosine, sine], -1), code[:, :, None], code[:, None, :])

    raw_qkv, gs, n1g, dy2g, qkvs, outs, gus, dns, attn_rows = front(
        mix_mlp, low_attn, tables, sorter, cotangent,
        gather_hi(w_qkv), gather_hi(w_out).reshape(-1, width), gather_hi(w_gu), gather_hi(w_down), 1,
    )
    rows = w_qkv.shape[0]
    qkvs = qkvs.reshape(width, 3 * HEAD_DIM)
    outs = outs.reshape(2, GROUP, hi, rows, width).swapaxes(1, 2).reshape(width, width)
    gus = gus.reshape(width, 2 * ff // CUBE)
    dns = dns.reshape(width, ff // CUBE)
    attn_rows = from_bins(attn_rows)
    y1, n2 = middle(mix_attn, mix_mlp, hs, attn_rows, outs)
    y2_part, g_mlp, dx2, low_grad_attn, grad_attn, mlp_sums = mlp(
        mix_attn, mix_mlp, n2, dy2g, gus, dns, hs, gs, outs, y1, 4
    )

    attn_cols = attn_rows.reshape(tokens, 2, hi, GROUP, rows).swapaxes(2, 3).reshape(tokens, width)
    dn1, y2, g_out, g_qkv, g_mlp = back(
        to_bins(grad_attn), raw_qkv, qkvs, low_grad_attn, attn_cols, tables,
        n1g, y2_part, g_mlp, hi, 7,
    )
    weight_grads = lay_out(g_qkv, g_out.reshape(hi, rows, width), g_mlp)
    new_streams, d_streams, g_mix_attn, g_mix_mlp = close(
        mix_attn, mix_mlp, sorter, hs, gs, dx2, y1, y2, from_bins(dn1), mlp_sums, 8
    )
    if hi > 1:
        g_mix_attn, g_mix_mlp = lax.psum((g_mix_attn, g_mix_mlp), "shard", axis_index_groups=hi_groups)
    return (new_streams, d_streams, g_mix_attn, g_mix_mlp, *(sum_hi(g) for g in weight_grads))


def solution(mesh):
    both = ("rep", "shard")
    return jax.shard_map(
        shards,
        mesh=mesh,
        in_specs=(
            P(both, None, None),
            P(both, None, None),
            P(both),
            P(),
            P(),
            P(),
            P(both, None),
            P(both, None),
            P(both, None),
            P(both, None),
        ),
        out_specs=(
            P(both, None, None),
            P(both, None, None),
            P(),
            P(),
            P(both, None),
            P(both, None),
            P(both, None),
            P(both, None),
        ),
        check_vma=False,
    )
```

```python
import functools
import math

import jax
import jax.numpy as jnp
from jax import lax
from jax.experimental import pallas as pl
from jax.experimental.pallas import tpu as pltpu
from jax.sharding import PartitionSpec as P

HEADS = 16
HEAD_DIM = 128
GROUP = 16
CUBE = 8
EPSILON = 1e-05
MESH = pl.DeviceIdType.MESH
CONTRACT_LAST = (((1,), (1,)), ((), ()))
CONTRACT_FIRST = (((0,), (0,)), ((), ()))
MIB = 1 << 20
BF = jnp.bfloat16
F32 = jnp.float32


class Here:
    def __init__(self):
        self.rep = lax.axis_index("rep")
        shard = lax.axis_index("shard")
        self.lo = shard % GROUP
        self.base = shard - self.lo
        self.bits = [(self.lo // (1 << i)) % 2 for i in range(4)]
        one, two, three = (self.flip(m) - self.lo for m in (4, 8, 12))
        self.inner = self.bits[2] + self.bits[3] - 2 * self.bits[2] * self.bits[3]
        self.away = (
            0,
            one,
            self.inner * three + (1 - self.inner) * two,
            self.inner * two + (1 - self.inner) * three,
        )

    def flip(self, mask):
        out = self.lo
        for i in range(4):
            if mask & (1 << i):
                out = out + (1 << i) * (1 - 2 * self.bits[i])
        return out

    def dev(self, mask):
        return (self.rep, self.base + self.flip(mask))

    def partner(self):
        return (1 - self.rep, self.base + self.lo)


def barrier(here, masks, partner):
    sem = pltpu.get_barrier_semaphore()
    targets = [here.dev(m) for m in masks]
    if partner:
        targets.append(here.partner())
    for t in targets:
        pl.semaphore_signal(sem, inc=1, device_id=t, device_id_type=MESH)
    pl.semaphore_wait(sem, len(targets))


TREE = (1, 2, 4, 8, 12)
ALL = tuple(range(1, GROUP))


def rcopy(src, dst, send, recv, dev):
    return pltpu.make_async_remote_copy(
        src_ref=src, dst_ref=dst, send_sem=send, recv_sem=recv, device_id=dev, device_id_type=MESH
    )


class Gather:
    sems = (4, 7)

    def __init__(self, here, x, out, send, recv):
        self.here, self.x, self.out, self.send, self.recv = here, x, out, send, recv
        self.half = x.shape[0] // 2
        self.off = here.lo - here.lo % out.shape[0]
        self.far = (1, 3, 2) if out.shape[0] == GROUP else (1,)
        self.sent = []

    def block(self, mask):
        return self.here.flip(mask) - self.off

    def _go(self, block, part, j, slot, mask):
        ref = self.out.at[block, pl.ds(part * self.half, self.half)]
        c = rcopy(ref, ref, self.send.at[j, slot], self.recv.at[j, slot], self.here.dev(mask))
        c.start()
        self.sent.append(c)

    def _wait(self, j, slot, block, part):
        ref = self.out.at[block, pl.ds(part * self.half, self.half)]
        rcopy(ref, ref, self.send.at[j, slot], self.recv.at[j, slot], self.here.dev(1)).wait_recv()

    def begin(self, own_sem):
        own = pltpu.make_async_copy(self.x, self.out.at[self.block(0)], own_sem)
        own.start()
        for j in self.far:
            c = rcopy(self.x, self.out.at[self.block(0)], self.send.at[j, 6], self.recv.at[j, 6], self.here.dev(4 * j))
            c.start()
            self.sent.append(c)
        own.wait()
        self.spread(0)

    def spread(self, j):
        b = self.block(4 * j)
        if j:
            ref = self.out.at[b]
            rcopy(ref, ref, self.send.at[j, 6], self.recv.at[j, 6], self.here.dev(4)).wait_recv()
        self._go(b, 0, j, 0, 1)
        self._go(b, 1, j, 1, 2)
        self._go(b, 0, j, 2, 2)
        self._go(b, 1, j, 3, 1)

    def forward(self, j):
        m = 4 * j
        self._wait(j, 0, self.block(m ^ 1), 0)
        self._go(self.block(m ^ 1), 0, j, 4, 2)
        self._wait(j, 1, self.block(m ^ 2), 1)
        self._go(self.block(m ^ 2), 1, j, 5, 1)

    def settle(self, j):
        m = 4 * j
        self._wait(j, 2, self.block(m ^ 2), 0)
        self._wait(j, 3, self.block(m ^ 1), 1)
        self._wait(j, 4, self.block(m ^ 3), 0)
        self._wait(j, 5, self.block(m ^ 3), 1)

    def end(self):
        for c in self.sent:
            c.wait_send()


def rowwise(n, step, body):
    def at(i, carry):
        body(pl.ds(pl.multiple_of(i * step, step), step))
        return carry

    lax.fori_loop(0, n // step, at, 0)


class Scatter:
    sems = (5, 7)

    @staticmethod
    def scratch(rows, d, span=GROUP):
        h = rows // 2
        zs = span // 4
        return [
            pltpu.VMEM((zs, 4, h, d), BF),
            pltpu.VMEM((zs, 2, h, d), BF),
            pltpu.VMEM((5 if span == GROUP else 1, rows, d), BF),
            pltpu.SemaphoreType.DMA(Scatter.sems),
            pltpu.SemaphoreType.DMA(Scatter.sems),
        ]

    def __init__(self, here, part, scratch):
        self.here, self.part = here, part
        self.first, self.second, self.zin, self.send, self.recv = scratch
        self.rows = part.shape[1]
        self.half = self.rows // 2
        self.off = here.lo - here.lo % part.shape[0]
        self.line = part.shape[0] == GROUP
        self.sent = []

    def _copy(self, k, slot, src, dst, mask):
        return rcopy(src, dst, self.send.at[k, slot], self.recv.at[k, slot], self.here.dev(mask))

    def _go(self, *a):
        c = self._copy(*a)
        c.start()
        self.sent.append(c)

    def _block(self, k, q):
        return self.here.flip(q) + self.here.away[k] - self.off

    def _piece(self, k, q, part):
        return self.part.at[self._block(k, q), pl.ds(part * self.half, self.half)]

    def start(self, k):
        self._go(k, 1, self._piece(k, 3, 0), self.first.at[k, 1], 2)
        self._go(k, 3, self._piece(k, 3, 1), self.first.at[k, 3], 1)
        self._go(k, 0, self._piece(k, 2, 0), self.first.at[k, 0], 2)
        self._go(k, 2, self._piece(k, 1, 1), self.first.at[k, 2], 1)

    def cross(self, k):
        h = self.half
        for slot, q, part, to in ((1, 1, 0, 1), (3, 2, 1, 2)):
            self._copy(k, slot, self.first.at[k, slot], self.first.at[k, slot], 1).wait_recv()
            own = self._piece(k, q, part)

            def body(r, own=own, slot=slot):
                own[r] = (own[r].astype(F32) + self.first[k, slot, r].astype(F32)).astype(BF)

            rowwise(h, 16, body)
            self._go(k, 4 + part, own, self.second.at[k, part], to)

    def _reduce(self, k, boxes, out):
        h = self.half
        for part, slot in ((0, 0), (1, 2)):
            own = self._piece(k, 0, part)

            def body(r, own=own, part=part, slot=slot):
                total = own[r].astype(F32) + self.first[k, slot, r].astype(F32) + self.second[k, part, r].astype(F32)
                at = pl.ds(part * h + r.start, r.size)
                for b in boxes:
                    total = total + self.zin[b, at].astype(F32)
                if out is None:
                    own[r] = total.astype(BF)
                else:
                    out[at] = total.astype(out.dtype)

            rowwise(h, 16, body)

    def _box(self, b):
        return self.zin.at[b], self.recv.at[(1, 2, 3, 0, 4)[b], 6]

    def _pass(self, k, b, mask):
        box, full = self._box(b)
        return rcopy(self.part.at[self._block(k, 0)], box, self.send.at[k, 6], full, self.here.dev(mask))

    def _full(self, b):
        box, full = self._box(b)
        rcopy(box, box, self.send.at[0, 6], full, self.here.dev(4)).wait_recv()

    def finish(self, k, out=None):
        for part, slot in ((0, 0), (1, 2)):
            self._copy(k, slot, self.first.at[k, slot], self.first.at[k, slot], 1).wait_recv()
            self._copy(k, 4 + part, self.second.at[k, part], self.second.at[k, part], 1).wait_recv()
        if k == 0:
            self._full(0)
        if not self.line:
            self._reduce(k, () if k else (0,), out)
            if k:
                self._pass(k, 0, 4).start()
                self.sent.append(self._pass(k, 0, 4))
            return
        inner = self.here.inner

        @pl.when(inner == 0)
        def _():
            self._reduce(k, () if k else (0,), out)
            if k:
                self._pass(k, k - 1, 4).start()

        @pl.when(inner == 1)
        def _():
            boxes = ((0, 3), (4,), (1,), (2,))[k]
            for b in boxes:
                if b:
                    self._full(b)
            self._reduce(k, boxes, out)
            if k == 1:
                self._pass(k, 0, 4).start()
            elif k:
                self._pass(k, k + 1, 12).start()

        if k:
            self.sent.append(self._pass(k, 0, 4))

    def end(self):
        for c in self.sent:
            c.wait_send()


def any_spec(n):
    return [pl.BlockSpec(memory_space=pl.ANY)] * n


def vmem_spec(n):
    return [pl.BlockSpec(memory_space=pltpu.VMEM)] * n


def params(cid, mib=60):
    return pltpu.CompilerParams(collective_id=cid, has_side_effects=True, vmem_limit_bytes=mib * MIB)


def exchange_columns(here, src, dst, width, cols, span, send, recv, own_sem):
    copies = []
    own = []
    for i, c in enumerate(cols):
        for m in range(GROUP):
            peer = here.flip(m)
            at = src.at[:, :, pl.ds(pl.multiple_of(c + (peer % span) * width, 128), width)]
            to = dst.at[here.rep, :, here.lo, :, pl.ds(i * width, width)]
            if m == 0:
                cp = pltpu.make_async_copy(at, to, own_sem.at[i])
                cp.start()
                own.append(cp)
            else:
                cp = rcopy(at, to, send.at[i, m], recv.at[i, m], here.dev(m))
                cp.start()
                copies.append(cp)

    def arrive():
        for cp in own:
            cp.wait()
        for i, c in enumerate(cols):
            for m in ALL:
                to = dst.at[here.rep, :, here.flip(m), :, pl.ds(i * width, width)]
                rcopy(to, to, send.at[i, m], recv.at[i, m], here.dev(m)).wait_recv()

    def end():
        for cp in copies:
            cp.wait_send()

    return arrive, end


def rope_parts(rope):
    other = pltpu.roll(rope, HEAD_DIM // 2, 1)
    first = lax.broadcasted_iota(jnp.int32, rope.shape, 1) < HEAD_DIM // 2
    return jnp.where(first, rope, other), jnp.where(first, -other, rope)


def turned(x, cosine, sine):
    return x * cosine + pltpu.roll(x, HEAD_DIM // 2, 1) * sine


CODE = 4096


def head_of_bin(qkv, tables, b):
    rope, code_row, code_col = tables
    slots = qkv.shape[1] // rope.shape[0]
    rows = pl.ds(b * slots, slots)
    n = GROUP * slots

    def piece(i):
        return qkv[:, rows, i * HEAD_DIM : (i + 1) * HEAD_DIM].reshape(n, HEAD_DIM)

    cos, sin = rope_parts(rope[b])
    queries = turned(piece(0).astype(F32), cos, sin).astype(BF)
    keys = turned(piece(1).astype(F32), cos, sin).astype(BF)
    query_code, key_code = code_row[b], code_col[b]
    segment_code = query_code - jnp.bitwise_and(query_code, CODE - 1)
    seen = (key_code <= query_code) & (key_code >= segment_code)
    scores = jnp.where(seen, dot_t(queries, keys) * (1.0 / math.sqrt(HEAD_DIM)), -1e30)
    weights = jnp.exp(scores - jnp.max(scores, -1, keepdims=True))
    probability = weights / jnp.sum(weights, -1, keepdims=True)
    return queries, keys, piece(2), probability, rows, cos, sin


def attend(qkv, out, tables, b):
    _, _, values, probability, rows, _, _ = head_of_bin(qkv, tables, b)
    attended = dot(probability.astype(BF), values).astype(BF)
    out[:, rows] = attended.reshape(GROUP, rows.size, HEAD_DIM)


def front_kernel(
    mixm, n1, rope, code_row, code_col, sorter, g, wqkv, wout, wgu, wdn,
    raw, gs, n1g_out, dy2g, qkvs, outs, gus, dns, attn,
    n1g, wq, attended, plane, dy2,
    gsend, grecv, own, csend, crecv, cown, psend, precv, late, group_out, ssend, srecv, sown,
):
    here = Here()
    barrier(here, ALL, True)
    tables = (rope, code_row, code_col)
    tokens, width = n1.shape
    q = exchange_columns(here, wqkv, qkvs, 128, (0, 2048, 4096), GROUP, csend.at[0], crecv.at[0], cown.at[0])
    half = wgu.shape[2] // 2
    ga = Gather(here, n1, n1g, gsend.at[0], grecv.at[0])
    gb = Gather(here, dy2, dy2g, gsend.at[1], grecv.at[1])
    gc = Gather(here, wout, outs.at[here.rep], gsend.at[2], grecv.at[2])
    o = (0, 1, 3, 2)

    def hand_over(i, dst):
        cp = rcopy(dst.at[here.rep], dst.at[here.rep], psend.at[i], precv.at[i], here.partner())
        cp.start()
        return cp

    def other_core(i, dst):
        other = dst.at[1 - here.rep]
        rcopy(other, other, psend.at[i], precv.at[i], here.partner()).wait_recv()

    ga.begin(own.at[0])
    ga.spread(o[1])
    ga.forward(o[0])
    q[0]()
    q_pass = hand_over(0, qkvs)
    ga.spread(o[2])
    ga.forward(o[1])
    ga.spread(o[3])
    ga.forward(o[2])
    gc.begin(own.at[2])
    u = exchange_columns(here, wgu, gus, half // CUBE, (0, half), CUBE, csend.at[1], crecv.at[1], cown.at[1])
    d = exchange_columns(here, wdn, dns, half // CUBE, (0,), CUBE, csend.at[2], crecv.at[2], cown.at[2])
    ga.forward(o[3])
    sort_planes(sorter, g, gs, plane)
    p = read_mix(mixm)

    def to_branch(r):
        dy2[r] = mixed([p[j][5] for j in range(4)], [gs[j, r].astype(F32) for j in range(4)]).astype(BF)

    rowwise(tokens, 16, to_branch)
    other_core(0, qkvs)
    get = pltpu.make_async_copy(qkvs, wq, late)
    get.start()
    get.wait()
    copies = []
    for k, j in enumerate(o):
        ga.settle(j)
        blocks = pl.ds(here.flip(4 * j) - here.lo % 4, 4)
        x = n1g[blocks].reshape(4 * tokens, width)
        raw[blocks] = dot(x, wq[...].reshape(width, wq.shape[-1])).astype(BF).reshape(4, tokens, wq.shape[-1])
        c = pltpu.make_async_copy(n1g.at[blocks], n1g_out.at[blocks], group_out.at[k])
        c.start()
        copies.append(c)
    bins = rope.shape[0]
    for b in range(bins):
        attend(raw, attended, tables, b)
        if b < 3:
            gc.spread(o[b + 1])
            gc.forward(o[b])
    swaps = []
    at = pl.ds(pl.multiple_of(here.lo * HEAD_DIM, HEAD_DIM), HEAD_DIM)
    for m in ALL:
        c = rcopy(attended.at[here.flip(m)], attn.at[:, at], ssend.at[m], srecv.at[m], here.dev(m))
        c.start()
        swaps.append(c)
    mine = pltpu.make_async_copy(attended.at[here.lo], attn.at[:, at], sown)
    mine.start()
    gb.begin(own.at[1])
    gc.forward(o[3])
    gb.spread(1)
    gb.forward(0)
    for j in o:
        gc.settle(j)
    out_pass = hand_over(3, outs)
    gb.forward(1)
    u[0]()
    u_pass = hand_over(1, gus)
    d[0]()
    d_pass = hand_over(2, dns)
    gb.settle(0)
    gb.settle(1)
    mine.wait()
    for m in ALL:
        ref = attn.at[:, pl.ds(pl.multiple_of(here.flip(m) * HEAD_DIM, HEAD_DIM), HEAD_DIM)]
        rcopy(ref, ref, ssend.at[m], srecv.at[m], here.dev(m)).wait_recv()
    for i, dst in ((1, gus), (2, dns), (3, outs)):
        other_core(i, dst)
    for c in (q_pass, u_pass, d_pass, out_pass, *swaps):
        c.wait_send()
    for c in copies:
        c.wait()
    for g in (ga, gb, gc):
        g.end()
    for _, end in (q, u, d):
        end()


def front(mixm, n1, tables, sorter, g, wqkv, wout, wgu, wdn, cid):
    hi, rows, _ = wqkv.shape
    ff = wdn.shape[2]
    tokens = n1.shape[0]
    shape = lambda *s: jax.ShapeDtypeStruct(s, BF)
    out_rows = wout.shape[0]
    head = 3 * HEAD_DIM
    return pl.pallas_call(
        front_kernel,
        out_shape=(
            shape(GROUP, tokens, head),
            shape(g.shape[1], tokens, g.shape[2]),
            shape(GROUP, *n1.shape),
            shape(CUBE, *n1.shape),
            shape(2, hi, GROUP, rows, head),
            shape(2, GROUP, out_rows, wout.shape[1]),
            shape(2, hi, GROUP, rows, 2 * ff // CUBE),
            shape(2, hi, GROUP, rows, ff // CUBE),
            shape(tokens, GROUP * HEAD_DIM),
        ),
        in_specs=[*smem_spec(1), *vmem_spec(6), *any_spec(4)],
        out_specs=(*vmem_spec(2), *any_spec(7)),
        scratch_shapes=[
            pltpu.VMEM((GROUP, *n1.shape), BF),
            pltpu.VMEM((2, hi, GROUP, rows, head), BF),
            pltpu.VMEM((GROUP, tokens, HEAD_DIM), BF),
            pltpu.VMEM((g.shape[1], tokens, g.shape[2]), BF),
            pltpu.VMEM(n1.shape, BF),
            pltpu.SemaphoreType.DMA((3,) + Gather.sems),
            pltpu.SemaphoreType.DMA((3,) + Gather.sems),
            pltpu.SemaphoreType.DMA((3,)),
            pltpu.SemaphoreType.DMA((3, 3, GROUP)),
            pltpu.SemaphoreType.DMA((3, 3, GROUP)),
            pltpu.SemaphoreType.DMA((3, 3)),
            pltpu.SemaphoreType.DMA((4,)),
            pltpu.SemaphoreType.DMA((4,)),
            pltpu.SemaphoreType.DMA,
            pltpu.SemaphoreType.DMA((4,)),
            pltpu.SemaphoreType.DMA((GROUP,)),
            pltpu.SemaphoreType.DMA((GROUP,)),
            pltpu.SemaphoreType.DMA,
        ],
        compiler_params=params(cid, 62),
    )(mixm, n1, *tables, sorter, g, wqkv, wout, wgu, wdn)


def pair_add(here, g, inbox, send, recv):
    cp = rcopy(g.at[1 - here.rep], inbox, send, recv, here.partner())
    cp.start()
    cp.wait()

    def body(r):
        g[here.rep, r] = (g[here.rep, r].astype(F32) + inbox[r].astype(F32)).astype(BF)

    rowwise(inbox.shape[0], 16, body)


def send_home(here, total, out, send, recv, own):
    _, hi, rows, _ = out.shape

    def block(h, m):
        at = (h * GROUP + here.flip(m)) * rows
        return total.at[pl.ds(pl.multiple_of(at, rows), rows)]

    cps = []
    owns = []
    for h in range(hi):
        for m in ALL:
            c = rcopy(block(h, m), out.at[here.lo, h], send.at[h, m], recv.at[h, m], here.dev(m))
            c.start()
            cps.append(c)
        c = pltpu.make_async_copy(block(h, 0), out.at[here.lo, h], own.at[h])
        c.start()
        owns.append(c)

    def end():
        for c in owns:
            c.wait()
        for h in range(hi):
            for m in ALL:
                ref = out.at[here.flip(m), h]
                rcopy(ref, ref, send.at[h, m], recv.at[h, m], here.dev(m)).wait_recv()
        for c in cps:
            c.wait_send()

    return end


def home_sems(hi):
    return [
        pltpu.SemaphoreType.DMA((hi, GROUP)),
        pltpu.SemaphoreType.DMA((hi, GROUP)),
        pltpu.SemaphoreType.DMA((hi,)),
    ]


def mlp_kernel(
    mixa, mixm, n2, dy2g_in, wgu_in, wdn_in, hs, gs, wout, y1, y2p, grads_out, dx2, dy1, d_out, sums,
    n2g, dy2g, wgu, wdn, part, hidden, dgu, y2s, grads, inbox, dn2,
    gsend, grecv, own, load, y2sem, psend, precv, late, *scratch,
):
    here = Here()
    barrier(here, (1, 2, 4), True)
    g = Gather(here, n2, n2g, gsend, grecv)
    rs = Scatter(here, part, scratch)
    g.begin(own)
    loads = []
    for i, (src, dst) in enumerate(((wgu_in, wgu), (wdn_in, wdn), (dy2g_in, dy2g))):
        c = pltpu.make_async_copy(src, dst, load.at[i])
        c.start()
        loads.append(c)
    width, ff = wdn.shape
    tokens = n2.shape[0]
    group_rows = 4 * tokens
    step = 256
    y2copies = []

    def compute(j):
        first = here.flip(4 * j) - here.lo % 4 - g.off
        blocks = pl.ds(first, 4)
        if not y2copies:
            for c in loads:
                c.wait()

        def gates(k, carry):
            up_at = pl.ds(pl.multiple_of(k * step, step), step)
            gate_at = pl.ds(pl.multiple_of(ff + k * step, step), step)
            x = n2g[blocks].reshape(group_rows, width)
            up = dot(x, wgu[:, up_at])
            gate = dot(x, wgu[:, gate_at])
            dh = dot(dy2g[blocks].reshape(group_rows, width), wdn[:, up_at])
            sigmoid = 1.0 / (1.0 + jnp.exp(-gate))
            silu = gate * sigmoid
            hidden[blocks, :, up_at] = (silu * up).astype(BF).reshape(4, tokens, step)
            dgu[blocks, :, up_at] = (dh * silu).astype(BF).reshape(4, tokens, step)
            dgu[blocks, :, gate_at] = (
                (dh * up * sigmoid * (1.0 + gate * (1.0 - sigmoid))).astype(BF).reshape(4, tokens, step)
            )
            return carry

        lax.fori_loop(0, ff // step, gates, 0)
        if y2copies:
            y2copies[-1].wait()

        def outputs(k, carry):
            at = pl.ds(pl.multiple_of(k * step, step), step)
            h = hidden[blocks].reshape(group_rows, ff)
            y2s[:, :, at] = dot_t(h, wdn[at, :]).astype(BF).reshape(4, tokens, step)
            d = dgu[blocks].reshape(group_rows, 2 * ff)
            part[blocks, :, at] = dot_t(d, wgu[at, :]).astype(BF).reshape(4, tokens, step)
            return carry

        lax.fori_loop(0, width // step, outputs, 0)
        c = pltpu.make_async_copy(y2s, y2p.at[blocks], y2sem.at[len(y2copies)])
        c.start()
        y2copies.append(c)

    half = width // 2
    chunks = half // step

    def weight_grads(which, k):
        cols = pl.ds(pl.multiple_of(which * half + k * step, step), step)
        rows = pl.ds(pl.multiple_of(k * step, step), step)
        x = n2g[:, :, cols].reshape(CUBE * tokens, step)
        grads[which, rows, : 2 * ff] = t_dot(x, dgu[...].reshape(CUBE * tokens, 2 * ff)).astype(BF)
        x = dy2g[:, :, cols].reshape(CUBE * tokens, step)
        grads[which, rows, 2 * ff :] = t_dot(x, hidden[...].reshape(CUBE * tokens, ff)).astype(BF)

    def pass_chunk(k):
        rows = pl.ds(pl.multiple_of(k * step, step), step)
        return rcopy(grads.at[1 - here.rep, rows], inbox.at[rows], psend.at[k], precv.at[k], here.partner())

    g.spread(1)
    g.forward(0)
    g.settle(0)
    compute(0)
    rs.start(0)
    g.forward(1)
    rs.cross(0)
    g.settle(1)
    compute(1)
    rs.start(1)

    def other_half(k, carry):
        weight_grads(1 - here.rep, k)
        pass_chunk(k).start()
        return carry

    lax.fori_loop(0, chunks, other_half, 0)
    rs.cross(1)
    rs.finish(1)

    def own_half(k, carry):
        weight_grads(here.rep, k)
        return carry

    lax.fori_loop(0, chunks, own_half, 0)
    g.end()
    streams = hs.shape[0]
    loads = []
    for i, (src, dst) in enumerate(((hs, n2g.at[:streams]), (gs, n2g.at[streams : 2 * streams]), (wout, wgu))):
        c = pltpu.make_async_copy(src, dst, late.at[i])
        c.start()
        loads.append(c)

    def add(k, carry):
        pass_chunk(k).wait()

        def rows_add(i, carry):
            r = pl.ds(pl.multiple_of(k * step + i * 16, 16), 16)
            grads[here.rep, r] = (grads[here.rep, r].astype(F32) + inbox[r].astype(F32)).astype(BF)
            return carry

        return lax.fori_loop(0, step // 16, rows_add, carry)

    lax.fori_loop(0, chunks, add, 0)
    out = pltpu.make_async_copy(grads.at[here.rep], grads_out, late.at[3])
    out.start()
    rs.finish(0, dn2)
    for c in loads:
        c.wait()
    turn(read_mix(mixa), read_mix(mixm), n2g, y1, dn2, wgu, dx2, dy1, d_out, sums)
    out.wait()
    y2copies[-1].wait()
    rs.end()


def mlp(mixa, mixm, n2, dy2g, wgu, wdn, hs, gs, wout, y1, cid):
    tokens, width = n2.shape
    ff = wdn.shape[1]
    half = width // 2
    blocks = (CUBE, tokens)
    return pl.pallas_call(
        mlp_kernel,
        out_shape=(
            jax.ShapeDtypeStruct((*blocks, width), BF),
            jax.ShapeDtypeStruct((half, 3 * ff), BF),
            jax.ShapeDtypeStruct((tokens, width), F32),
            jax.ShapeDtypeStruct((tokens, width), BF),
            jax.ShapeDtypeStruct((tokens, width), BF),
            jax.ShapeDtypeStruct((24, 16, 128), F32),
        ),
        in_specs=[*smem_spec(2), *vmem_spec(1), *any_spec(6), *vmem_spec(1)],
        out_specs=(*any_spec(2), *vmem_spec(4)),
        scratch_shapes=[
            pltpu.VMEM((*blocks, width), BF),
            pltpu.VMEM((*blocks, width), BF),
            pltpu.VMEM(wgu.shape, BF),
            pltpu.VMEM(wdn.shape, BF),
            pltpu.VMEM((*blocks, width), BF),
            pltpu.VMEM((*blocks, ff), BF),
            pltpu.VMEM((*blocks, 2 * ff), BF),
            pltpu.VMEM((4, tokens, width), BF),
            pltpu.VMEM((2, half, 3 * ff), BF),
            pltpu.VMEM((half, 3 * ff), BF),
            pltpu.VMEM((tokens, width), F32),
            pltpu.SemaphoreType.DMA(Gather.sems),
            pltpu.SemaphoreType.DMA(Gather.sems),
            pltpu.SemaphoreType.DMA,
            pltpu.SemaphoreType.DMA((3,)),
            pltpu.SemaphoreType.DMA((4,)),
            pltpu.SemaphoreType.DMA((half // 256,)),
            pltpu.SemaphoreType.DMA((half // 256,)),
            pltpu.SemaphoreType.DMA((4,)),
            *Scatter.scratch(tokens, width, CUBE),
        ],
        compiler_params=params(cid, 63),
        cost_estimate=pl.CostEstimate(
            flops=2 * CUBE * tokens * width * ff * 9, bytes_accessed=60 * MIB, transcendentals=0
        ),
    )(mixa, mixm, n2, dy2g, wgu, wdn, hs, gs, wout, y1)


def attend_back(qkv, d_out, dqkv, tables, b):
    queries, keys, values, probability, rows, cos, sin = head_of_bin(qkv, tables, b)
    n, slots = queries.shape[0], rows.size
    scale = 1.0 / math.sqrt(HEAD_DIM)
    grad = d_out[:, rows].reshape(n, HEAD_DIM)
    grad_values = t_dot(probability.astype(BF), grad)
    grad_probs = dot_t(grad, values)
    shared = jnp.sum(grad_probs * probability, -1, keepdims=True)
    grad_scores = (probability * (grad_probs - shared)).astype(BF)
    grad_query = dot(grad_scores, keys) * scale
    grad_keys = t_dot(grad_scores, queries) * scale
    for i, v in enumerate((turned(grad_query, cos, -sin), turned(grad_keys, cos, -sin), grad_values)):
        dqkv[:, rows, i * HEAD_DIM : (i + 1) * HEAD_DIM] = v.astype(BF).reshape(GROUP, slots, HEAD_DIM)


class GradsHome:
    @staticmethod
    def scratch(hi, rows, w):
        return [
            pltpu.VMEM((hi, CUBE, rows, w), BF),
            pltpu.VMEM((hi, CUBE, rows, w), BF),
            *[pltpu.SemaphoreType.DMA((hi, CUBE))] * 6,
        ]

    def __init__(self, here, gmlp, out, scratch):
        self.here, self.out = here, out
        self.mine, self.box, self.zsend, self.zrecv, self.load, self.send, self.recv, self.own = scratch
        self.hi, _, self.rows, _ = self.mine.shape
        self.sent = []
        self.loads = {}
        self.gmlp = gmlp

    def begin(self, wave):
        here = self.here
        for h in range(self.hi):
            for m in wave:

                def block(mask, h=h):
                    at = (h * GROUP + here.flip(mask)) * self.rows
                    return self.gmlp.at[pl.ds(pl.multiple_of(at, self.rows), self.rows)]

                c = rcopy(block(m ^ 8), self.box.at[h, m], self.zsend.at[h, m], self.zrecv.at[h, m], here.dev(8))
                c.start()
                self.sent.append(c)
                c = pltpu.make_async_copy(block(m), self.mine.at[h, m], self.load.at[h, m])
                c.start()
                self.loads[h, m] = c

    def relay(self, m):
        here = self.here
        for h in range(self.hi):
            box, mine = self.box.at[h, m], self.mine.at[h, m]
            self.loads[h, m].wait()
            rcopy(box, box, self.zsend.at[h, m], self.zrecv.at[h, m], here.dev(8)).wait_recv()

            def body(r, box=box, mine=mine):
                mine[r] = (mine[r].astype(F32) + box[r].astype(F32)).astype(BF)

            rowwise(self.rows, 16, body)
            to = self.out.at[here.lo % CUBE, h]
            if m:
                c = rcopy(mine, to, self.send.at[h, m], self.recv.at[h, m], here.dev(m))
                self.sent.append(c)
            else:
                c = pltpu.make_async_copy(mine, to, self.own.at[h, 0])
                self.loads[h, 0] = c
            c.start()

    def end(self):
        here = self.here
        for h in range(self.hi):
            self.loads[h, 0].wait()
            for m in range(1, CUBE):
                ref = self.out.at[here.flip(m) % CUBE, h]
                rcopy(ref, ref, self.send.at[h, m], self.recv.at[h, m], here.dev(m)).wait_recv()
        for c in self.sent:
            c.wait_send()


def back_kernel(
    d_rows, qkv, qkvs, dy1, attn, rope, code_row, code_col, n1g, y2_in, gmlp,
    dn_out, y2_out, gout_out, gqkv_out, gmlp_out,
    d_out, dqkv, dn, y2, gout, stage, gqkv, tiles, obox, qbox,
    dsend, drecv, down, load, tile_sem, osend, orecv, qsend, qrecv, *scratch,
):
    here = Here()
    barrier(here, ALL, True)
    tables = (rope, code_row, code_col)
    bins = rope.shape[0]
    swaps = []
    for m in ALL:
        at = pl.ds(pl.multiple_of(here.flip(m) * HEAD_DIM, HEAD_DIM), HEAD_DIM)
        c = rcopy(d_rows.at[:, at], d_out.at[here.lo], dsend.at[m], drecv.at[m], here.dev(m))
        c.start()
        swaps.append(c)
    at = pl.ds(pl.multiple_of(here.lo * HEAD_DIM, HEAD_DIM), HEAD_DIM)
    mine = pltpu.make_async_copy(d_rows.at[:, at], d_out.at[here.lo], down)
    mine.start()
    y2_load = pltpu.make_async_copy(y2_in, y2, load)
    y2_load.start()
    _, tokens, width = dn.shape
    k = len(Scatter.scratch(16, 128))
    rs_dn = Scatter(here, dn, scratch[:k])
    rs_y2 = Scatter(here, y2, scratch[k : 2 * k])
    rs_go = Scatter(here, gout.reshape(GROUP, gout.shape[0] // GROUP, width), scratch[2 * k : 3 * k])
    qhome = scratch[3 * k : 3 * k + 3]
    gm = GradsHome(here, gmlp, gmlp_out, scratch[3 * k + 3 :])
    gm.begin((0, 1))
    order = (3, 2, 1, 0)
    y2_load.wait()
    rs_y2.start(1)
    rs_y2.start(0)
    gm.begin((2, 3))
    mine.wait()
    for m in ALL:
        ref = d_out.at[here.flip(m)]
        rcopy(ref, ref, dsend.at[m], drecv.at[m], here.dev(m)).wait_recv()

    half = width // 2
    step = 256
    chunks = half // step

    def out_grads(which, k):
        cols = pl.ds(pl.multiple_of(which * half + k * step, step), step)
        return t_dot(attn[:, cols], dy1[...]).astype(BF)

    def gout_pass(k):
        at = pl.ds(k * step, step)
        return rcopy(stage.at[k % 2], obox.at[at], osend.at[k], orecv.at[k], here.partner())

    gqkv_pair = rcopy(gqkv.at[1 - here.rep], qbox, qsend, qrecv, here.partner())

    for b in range(bins):
        attend_back(qkv, d_out, dqkv, tables, b)
        if b == 1:
            rs_y2.cross(1)
        elif b == 2:
            rs_y2.cross(0)
            rs_y2.finish(1)

    narrow = tiles.shape[3]

    def qkv_tile(k):
        cols = pl.ds(k * narrow, narrow)
        return pltpu.make_async_copy(n1g.at[:, :, cols], tiles.at[k % 2], tile_sem.at[k % 2])

    qkv_tile(0).start()
    for j in order:
        blocks = pl.ds(here.lo + here.away[j] - here.lo % 4, 4)

        def part(k, carry, blocks=blocks):
            at = pl.ds(pl.multiple_of(k * TILE, TILE), TILE)
            d = dqkv[blocks].reshape(4 * tokens, 3 * HEAD_DIM)
            dn[blocks, :, at] = dot_t(d, qkvs[at, :]).astype(BF).reshape(4, tokens, TILE)
            return carry

        lax.fori_loop(0, width // TILE, part, 0)
        rs_dn.start(j)
    count = width // narrow
    for k in range(count):
        if k + 1 < count:
            qkv_tile(k + 1).start()
        qkv_tile(k).wait()
        x = tiles[k % 2].reshape(GROUP * tokens, narrow)
        rows = pl.ds((k % (count // 2)) * narrow, narrow)
        gqkv[k // (count // 2), rows, :] = t_dot(x, dqkv[...].reshape(GROUP * tokens, 3 * HEAD_DIM)).astype(BF)
    gqkv_pair.start()
    gm.relay(0)
    gm.relay(1)
    gm.begin((4, 5))
    rs_y2.finish(0, y2_out)
    rs_dn.cross(order[0])
    for k in range(chunks):
        if k >= 2:
            gout_pass(k - 2).wait_send()
        stage[k % 2] = out_grads(1 - here.rep, k)
        gout_pass(k).start()
    rs_dn.cross(order[1])
    rs_dn.finish(order[0])
    for k in range(chunks):
        gout[k * step : (k + 1) * step, :] = out_grads(here.rep, k)

    def add(ref, box):
        def body(r):
            ref[r] = (ref[r].astype(F32) + box[r].astype(F32)).astype(BF)

        rowwise(box.shape[0], 16, body)

    gqkv_pair.wait()
    add(gqkv.at[here.rep], qbox)
    gm.relay(2)
    gm.begin((6,))
    end_qkv = send_home(here, gqkv.at[here.rep], gqkv_out, *qhome)
    rs_dn.cross(order[2])
    rs_dn.finish(order[1])
    gm.relay(3)
    gm.begin((7,))
    for k in range(chunks):
        gout_pass(k).wait_recv()
        if k >= chunks - 2:
            gout_pass(k).wait_send()
    add(gout, obox)
    for j in order:
        rs_go.start(j)
    rs_dn.cross(order[3])
    rs_dn.finish(order[2])
    rs_go.cross(order[0])
    gm.relay(4)
    rs_go.cross(order[1])
    rs_go.finish(order[0])
    gm.relay(5)
    rs_go.cross(order[2])
    rs_go.finish(order[1])
    gm.relay(6)
    rs_go.cross(order[3])
    rs_go.finish(order[2])
    rs_dn.finish(0, dn_out)
    rs_go.finish(0, gout_out)
    gm.relay(7)
    gm.end()
    end_qkv()
    for c in swaps:
        c.wait_send()
    for rs in (rs_dn, rs_y2, rs_go):
        rs.end()


def back(d_rows, qkv, qkvs, dy1, attn, tables, n1g, y2, gmlp, hi, cid):
    tokens, width = d_rows.shape
    half = width // 2
    w = qkv.shape[2]
    return pl.pallas_call(
        back_kernel,
        out_shape=(
            jax.ShapeDtypeStruct((tokens, width), F32),
            jax.ShapeDtypeStruct((tokens, width), F32),
            jax.ShapeDtypeStruct((half // GROUP, width), F32),
            jax.ShapeDtypeStruct((GROUP, hi, half // (hi * GROUP), w), BF),
            jax.ShapeDtypeStruct((CUBE, hi, half // (hi * GROUP), gmlp.shape[1]), BF),
        ),
        in_specs=[*vmem_spec(8), *any_spec(3)],
        out_specs=(*vmem_spec(3), *any_spec(2)),
        scratch_shapes=[
            pltpu.VMEM((GROUP, tokens, HEAD_DIM), BF),
            pltpu.VMEM((GROUP, tokens, w), BF),
            pltpu.VMEM((GROUP, tokens, width), BF),
            pltpu.VMEM((CUBE, tokens, width), BF),
            pltpu.VMEM((half, width), BF),
            pltpu.VMEM((2, 256, width), BF),
            pltpu.VMEM((2, half, w), BF),
            pltpu.VMEM((2, GROUP, tokens, TILE // 4), BF),
            pltpu.VMEM((half, width), BF),
            pltpu.VMEM((half, w), BF),
            pltpu.SemaphoreType.DMA((GROUP,)),
            pltpu.SemaphoreType.DMA((GROUP,)),
            pltpu.SemaphoreType.DMA,
            pltpu.SemaphoreType.DMA,
            pltpu.SemaphoreType.DMA((2,)),
            pltpu.SemaphoreType.DMA((half // 256,)),
            pltpu.SemaphoreType.DMA((half // 256,)),
            pltpu.SemaphoreType.DMA,
            pltpu.SemaphoreType.DMA,
            *Scatter.scratch(tokens, width),
            *Scatter.scratch(tokens, width, CUBE),
            *Scatter.scratch(half // GROUP, width),
            *home_sems(hi),
            *GradsHome.scratch(hi, half // (hi * GROUP), gmlp.shape[1]),
        ],
        compiler_params=params(cid, 63),
    )(d_rows, qkv, qkvs, dy1, attn, *tables, n1g, y2, gmlp)


def read_mix(ref):
    return [[ref[i, k] for k in range(6)] for i in range(4)]


def mixed(weights, planes):
    total = weights[0] * planes[0]
    for w, p in zip(weights[1:], planes[1:]):
        total = total + w * p
    return total


def moments(x):
    centred = x - jnp.mean(x, -1, keepdims=True)
    inverse = lax.rsqrt(jnp.mean(centred * centred, -1, keepdims=True) + EPSILON)
    return centred * inverse, inverse


def normalize_back(grad_out, normed, inverse):
    return inverse * (
        grad_out
        - jnp.mean(grad_out, -1, keepdims=True)
        - normed * jnp.mean(grad_out * normed, -1, keepdims=True)
    )


def lane_sums(x):
    total = x[:, :128]
    for c in range(128, x.shape[1], 128):
        total = total + x[:, c : c + 128]
    return total


def read_x2(m, p, h, y1):
    fold = [sum(p[s][0] * m[j][1 + s] for s in range(4)) for j in range(4)]
    return mixed(fold + [sum(p[s][0] * m[s][5] for s in range(4))], [*h, y1])


TILE = 512


def sort_planes(sorter, x, planes, plane):
    tokens, streams, width = x.shape

    def split(r):
        v = x[r].astype(F32)
        for i in range(streams):
            plane[i, r] = v[:, i, :].astype(BF)

    rowwise(tokens, 16, split)
    for i in range(streams):
        for c in range(0, width, TILE):
            at = slice(c, c + TILE)
            planes[i, :, at] = dot(sorter[...], plane[i, :, at]).astype(BF)


def open_kernel(mixa, sorter, x, hs, n1, plane):
    m = read_mix(mixa)
    sort_planes(sorter, x, hs, plane)

    def norm(r):
        x1 = mixed([m[j][0] for j in range(4)], [hs[j, r].astype(F32) for j in range(4)])
        n1[r] = moments(x1)[0].astype(BF)

    rowwise(x.shape[0], 16, norm)


def smem_spec(n):
    return [pl.BlockSpec(memory_space=pltpu.SMEM)] * n


def local_params(mib=60):
    return pltpu.CompilerParams(vmem_limit_bytes=mib * MIB)


def open_streams(mixa, sorter, x):
    tokens, streams, width = x.shape
    return pl.pallas_call(
        open_kernel,
        out_shape=(
            jax.ShapeDtypeStruct((streams, tokens, width), BF),
            jax.ShapeDtypeStruct((tokens, width), BF),
        ),
        in_specs=[*smem_spec(1), *vmem_spec(2)],
        out_specs=tuple(vmem_spec(2)),
        scratch_shapes=[pltpu.VMEM((streams, tokens, width), BF)],
        compiler_params=local_params(),
    )(mixa, sorter, x)


def middle_kernel(mixa, mixm, hs, attn, wout, y1, n2):
    m, p = read_mix(mixa), read_mix(mixm)
    tokens, width = attn.shape

    def tile(i, carry):
        at = pl.ds(pl.multiple_of(i * TILE, TILE), TILE)
        y1[:, at] = dot(attn[...], wout[:, at])
        return carry

    lax.fori_loop(0, width // TILE, tile, 0)

    def norm(r):
        x2 = read_x2(m, p, [hs[j, r].astype(F32) for j in range(4)], y1[r])
        n2[r] = moments(x2)[0].astype(BF)

    rowwise(tokens, 16, norm)


def middle(mixa, mixm, hs, attn, wout):
    tokens, width = attn.shape
    return pl.pallas_call(
        middle_kernel,
        out_shape=(
            jax.ShapeDtypeStruct((tokens, width), F32),
            jax.ShapeDtypeStruct((tokens, width), BF),
        ),
        in_specs=[*smem_spec(2), *vmem_spec(3)],
        out_specs=tuple(vmem_spec(2)),
        compiler_params=local_params(),
    )(mixa, mixm, hs, attn, wout)


def unsort(sorter, planes, out):
    streams, tokens, width = planes.shape
    for i in range(streams):

        def tile(k, carry, i=i):
            at = pl.ds(pl.multiple_of(k * TILE, TILE), TILE)
            v = planes[i, :, at]
            high = v.astype(BF)
            low = (v - high.astype(F32)).astype(BF)
            out[:, i, at] = t_dot(sorter[...], high) + t_dot(sorter[...], low)
            return carry

        lax.fori_loop(0, width // TILE, tile, 0)


def turn(m, p, planes, y1, dn2, wout, dx2, dy1, d_out, sums):
    tokens, width = y1.shape
    sums[...] = jnp.zeros_like(sums)

    def body(r):
        x2 = read_x2(m, p, [planes[j, r].astype(F32) for j in range(4)], y1[r])
        normed, inverse = moments(x2)
        dx2[r] = normalize_back(dn2[r], normed, inverse)
        for c in range(0, width, TILE):
            at = slice(c, c + TILE)
            h = [planes[j, r, at].astype(F32) for j in range(4)]
            y = y1[r, at]
            h1 = [mixed([*(m[j][1 + i] for j in range(4)), m[i][5]], [*h, y]) for i in range(4)]
            g = [planes[4 + j, r, at].astype(F32) for j in range(4)]
            dx = dx2[r, at]
            g1 = [mixed([*(p[j][1 + i] for i in range(4)), p[j][0]], [*g, dx]) for j in range(4)]
            dy1[r, at] = mixed([m[j][5] for j in range(4)], g1).astype(BF)
            for j in range(4):
                sums[j * 6] += lane_sums(h1[j] * dx)
                for i in range(4):
                    sums[j * 6 + 1 + i] += lane_sums(h1[j] * g[i])

    rowwise(tokens, 16, body)
    def tile(i, carry):
        at = pl.ds(pl.multiple_of(i * TILE, TILE), TILE)
        d_out[:, at] = dot_t(dy1[...], wout[at, :]).astype(BF)
        return carry

    lax.fori_loop(0, width // TILE, tile, 0)


def close_kernel(
    mixa, mixm, sorter, hs, gs, dx2, y1, y2, dn1, other, new, d_streams, mix_a, mix_m,
    sums, planes, fresh, mine, inbox, send, recv,
):
    here = Here()
    barrier(here, ALL, True)
    m, p = read_mix(mixa), read_mix(mixm)
    tokens, width = y1.shape
    sums[:24] = jnp.zeros((24, *sums.shape[1:]), F32)
    sums[24:] = other[...]

    def body(r):
        x1 = mixed([m[j][0] for j in range(4)], [hs[j, r].astype(F32) for j in range(4)])
        normed, inverse = moments(x1)
        planes[0, r] = normalize_back(dn1[r], normed, inverse)
        for c in range(0, width, TILE):
            at = slice(c, c + TILE)
            h = [hs[j, r, at].astype(F32) for j in range(4)]
            g = [gs[j, r, at].astype(F32) for j in range(4)]
            y = y1[r, at]
            dx = planes[0, r, at]
            dm = dx2[r, at]
            g1 = [mixed([*(p[j][1 + i] for i in range(4)), p[j][0]], [*g, dm]) for j in range(4)]
            for j in range(4):
                planes[j, r, at] = mixed([*(m[j][1 + i] for i in range(4)), m[j][0]], [*g1, dx])
                sums[j * 6] += lane_sums(h[j] * dx)
                for i in range(4):
                    sums[j * 6 + 1 + i] += lane_sums(h[j] * g1[i])
                sums[j * 6 + 5] += lane_sums(y * g1[j])
            h1 = [mixed([*(m[j][1 + i] for j in range(4)), m[i][5]], [*h, y]) for i in range(4)]
            y = y2[r, at]
            for i in range(4):
                fresh[i, r, at] = mixed([*(p[j][1 + i] for j in range(4)), p[i][5]], [*h1, y])
                sums[24 + i * 6 + 5] += lane_sums(y * g[i])

    rowwise(tokens, 16, body)
    mine[0] = jnp.sum(sums[...], axis=1)
    pair = rcopy(mine.at[0], inbox.at[0], send.at[0], recv.at[0], here.partner())
    pair.start()
    pair.wait()
    mine[1] = mine[0] + inbox[0]
    cps = []
    for k in ALL:
        c = rcopy(mine.at[1], inbox.at[k], send.at[k], recv.at[k], here.dev(k))
        c.start()
        cps.append(c)
    unsort(sorter, fresh, new)
    unsort(sorter, planes, d_streams)
    everyone = mine[1]
    for c in cps:
        c.wait()
    for k in ALL:
        everyone = everyone + inbox[k]
    everyone = jnp.sum(everyone, axis=1, keepdims=True)
    for n, out in enumerate((mix_a, mix_m)):
        row = lax.broadcasted_iota(jnp.int32, out.shape, 0)
        col = lax.broadcasted_iota(jnp.int32, out.shape, 1)
        value = jnp.zeros(out.shape, F32)
        for j in range(4):
            for c in range(6):
                k = n * 24 + j * 6 + c
                value = jnp.where((row == j) & (col == c), everyone[k : k + 1], value)
        out[...] = value


def close(mixa, mixm, sorter, hs, gs, dx2, y1, y2, dn1, other, cid):
    streams, tokens, width = hs.shape
    return pl.pallas_call(
        close_kernel,
        out_shape=(
            jax.ShapeDtypeStruct((tokens, streams, width), F32),
            jax.ShapeDtypeStruct((tokens, streams, width), F32),
            jax.ShapeDtypeStruct(mixa.shape, F32),
            jax.ShapeDtypeStruct(mixm.shape, F32),
        ),
        in_specs=[*smem_spec(2), *vmem_spec(8)],
        out_specs=tuple(vmem_spec(4)),
        scratch_shapes=[
            pltpu.VMEM((48, 16, 128), F32),
            pltpu.VMEM((streams, tokens, width), F32),
            pltpu.VMEM((streams, tokens, width), F32),
            pltpu.VMEM((2, 48, 128), F32),
            pltpu.VMEM((GROUP, 48, 128), F32),
            pltpu.SemaphoreType.DMA((GROUP,)),
            pltpu.SemaphoreType.DMA((GROUP,)),
        ],
        compiler_params=params(cid),
    )(mixa, mixm, sorter, hs, gs, dx2, y1, y2, dn1, other)


def lay_out_kernel(qkv, out, mlp, gqkv, gout, ggu, gdown):
    head = HEAD_DIM
    for l in range(qkv.shape[0]):
        for i in range(3):
            at = i * GROUP * head + l * head
            gqkv[:, :, at : at + head] = qkv[l, :, :, i * head : (i + 1) * head].astype(F32)
    block = mlp.shape[3] // 3
    for l in range(CUBE):
        for i in range(2):
            at = (i * CUBE + l) * block
            ggu[:, :, at : at + block] = mlp[l, :, :, i * block : (i + 1) * block].astype(F32)
        gdown[:, :, l * block : (l + 1) * block] = mlp[l, :, :, 2 * block :].astype(F32)
    gout[...] = out[...]


def lay_out(qkv, out, mlp):
    _, hi, rows, w = mlp.shape
    ff = w // 3 * CUBE
    shapes = [(hi, rows, GROUP * qkv.shape[3]), out.shape, (hi, rows, 2 * ff), (hi, rows, ff)]
    return pl.pallas_call(
        lay_out_kernel,
        out_shape=tuple(jax.ShapeDtypeStruct(s, F32) for s in shapes),
        in_specs=vmem_spec(3),
        out_specs=tuple(vmem_spec(4)),
        compiler_params=local_params(),
    )(qkv, out, mlp)


def slot_layout(lengths_row, capacity):
    seq_count = lengths_row.shape[-1]
    seq_ends = jnp.cumsum(lengths_row, axis=-1)
    slot_index = jnp.arange(capacity, dtype=jnp.int32)
    segment = jnp.sum((slot_index[:, None] >= seq_ends[..., None, :]).astype(jnp.int32), axis=-1)
    seq_starts = seq_ends - lengths_row
    chosen = (segment[..., None] == jnp.arange(seq_count, dtype=jnp.int32)).astype(jnp.int32)
    start_of = jnp.sum(chosen * seq_starts[..., None, :], axis=-1)
    is_live = segment < seq_count
    segment = jnp.where(is_live, segment, seq_count + slot_index)
    position = jnp.where(is_live, slot_index - start_of, 0)
    return (segment, position)


def rope_tables(position, head_width):
    half_width = head_width // 2
    frequency = jnp.exp(
        jnp.arange(half_width, dtype=jnp.float32) * (-2.0 * math.log(10000.0) / head_width)
    )
    angles = position.astype(jnp.float32)[..., None] * frequency
    return (jnp.cos(angles), jnp.sin(angles))


def dot(a, b):
    return jnp.dot(a, b, preferred_element_type=F32)


def dot_t(a, b):
    return lax.dot_general(a, b, CONTRACT_LAST, preferred_element_type=F32)


def t_dot(a, b):
    return lax.dot_general(a, b, CONTRACT_FIRST, preferred_element_type=F32)


def shards(streams, cotangent, deal, lengths, mix_attn, mix_mlp, w_qkv, w_out, w_gu, w_down):
    tokens, stream_count, width = streams.shape
    shard_size = lax.axis_size("shard")
    hi = shard_size // GROUP
    hi_groups = [[h * GROUP + l for h in range(hi)] for l in range(GROUP)]
    shard = lax.axis_index("shard")
    my_hi = shard // GROUP
    bin_count = shard_size // 4
    my_bins = bin_count // hi
    per_bin = tokens // bin_count
    capacity = per_bin * shard_size
    ff = w_down.shape[1]

    def swap_hi(rows):
        if hi == 1:
            return rows
        return lax.all_to_all(rows, "shard", 0, 0, axis_index_groups=hi_groups, tiled=True)

    def to_bins(rows):
        return swap_hi(rows).reshape(hi, my_bins, per_bin, -1).swapaxes(0, 1).reshape(tokens, -1)

    def from_bins(rows):
        return swap_hi(rows.reshape(my_bins, hi, per_bin, -1).swapaxes(0, 1).reshape(tokens, -1))

    def gather_hi(rows):
        if hi == 1:
            return rows[None]
        return lax.all_gather(rows, "shard", axis_index_groups=hi_groups)

    def sum_hi(rows):
        if hi == 1:
            return rows[0]
        return lax.psum_scatter(rows, "shard", axis_index_groups=hi_groups)

    sorter = (jnp.arange(tokens, dtype=jnp.int32)[:, None] == deal[None, :]).astype(BF)

    hs, n1 = open_streams(mix_attn, sorter, streams)
    low_attn = to_bins(n1)

    bins = lax.axis_index("rep") * bin_count + my_hi * my_bins
    lengths_here = lax.dynamic_slice_in_dim(lengths, bins, my_bins, 0)
    segment, position = slot_layout(lengths_here, capacity)

    def local_order(x):
        return x.reshape(my_bins, hi, GROUP, per_bin).swapaxes(1, 2).reshape(my_bins, capacity)

    segment, position = local_order(segment), local_order(position)
    cosine, sine = rope_tables(position, HEAD_DIM)
    code = segment * CODE + position
    tables = (jnp.concatenate([cosine, sine], -1), code[:, :, None], code[:, None, :])

    raw_qkv, gs, n1g, dy2g, qkvs, outs, gus, dns, attn_rows = front(
        mix_mlp, low_attn, tables, sorter, cotangent,
        gather_hi(w_qkv), gather_hi(w_out).reshape(-1, width), gather_hi(w_gu), gather_hi(w_down), 1,
    )
    rows = w_qkv.shape[0]
    qkvs = qkvs.reshape(width, 3 * HEAD_DIM)
    outs = outs.reshape(2, GROUP, hi, rows, width).swapaxes(1, 2).reshape(width, width)
    gus = gus.reshape(width, 2 * ff // CUBE)
    dns = dns.reshape(width, ff // CUBE)
    attn_rows = from_bins(attn_rows)
    y1, n2 = middle(mix_attn, mix_mlp, hs, attn_rows, outs)
    y2_part, g_mlp, dx2, low_grad_attn, grad_attn, mlp_sums = mlp(
        mix_attn, mix_mlp, n2, dy2g, gus, dns, hs, gs, outs, y1, 4
    )

    attn_cols = attn_rows.reshape(tokens, 2, hi, GROUP, rows).swapaxes(2, 3).reshape(tokens, width)
    dn1, y2, g_out, g_qkv, g_mlp = back(
        to_bins(grad_attn), raw_qkv, qkvs, low_grad_attn, attn_cols, tables,
        n1g, y2_part, g_mlp, hi, 7,
    )
    weight_grads = lay_out(g_qkv, g_out.reshape(hi, rows, width), g_mlp)
    new_streams, d_streams, g_mix_attn, g_mix_mlp = close(
        mix_attn, mix_mlp, sorter, hs, gs, dx2, y1, y2, from_bins(dn1), mlp_sums, 8
    )
    if hi > 1:
        g_mix_attn, g_mix_mlp = lax.psum((g_mix_attn, g_mix_mlp), "shard", axis_index_groups=hi_groups)
    return (new_streams, d_streams, g_mix_attn, g_mix_mlp, *(sum_hi(g) for g in weight_grads))


def solution(mesh):
    both = ("rep", "shard")
    return jax.shard_map(
        shards,
        mesh=mesh,
        in_specs=(
            P(both, None, None),
            P(both, None, None),
            P(both),
            P(),
            P(),
            P(),
            P(both, None),
            P(both, None),
            P(both, None),
            P(both, None),
        ),
        out_specs=(
            P(both, None, None),
            P(both, None, None),
            P(),
            P(),
            P(both, None),
            P(both, None),
            P(both, None),
            P(both, None),
        ),
        check_vma=False,
    )
```

```python
import functools
import math

import jax
import jax.numpy as jnp
from jax import lax
from jax.experimental import pallas as pl
from jax.experimental.pallas import tpu as pltpu
from jax.sharding import PartitionSpec as P

HEADS = 16
HEAD_DIM = 128
GROUP = 16
CUBE = 8
EPSILON = 1e-05
MESH = pl.DeviceIdType.MESH
CONTRACT_LAST = (((1,), (1,)), ((), ()))
CONTRACT_FIRST = (((0,), (0,)), ((), ()))
MIB = 1 << 20
BF = jnp.bfloat16
F32 = jnp.float32


class Here:
    def __init__(self):
        self.rep = lax.axis_index("rep")
        shard = lax.axis_index("shard")
        self.lo = shard % GROUP
        self.base = shard - self.lo
        self.bits = [(self.lo // (1 << i)) % 2 for i in range(4)]
        one, two, three = (self.flip(m) - self.lo for m in (4, 8, 12))
        self.inner = self.bits[2] + self.bits[3] - 2 * self.bits[2] * self.bits[3]
        self.away = (
            0,
            one,
            self.inner * three + (1 - self.inner) * two,
            self.inner * two + (1 - self.inner) * three,
        )

    def flip(self, mask):
        out = self.lo
        for i in range(4):
            if mask & (1 << i):
                out = out + (1 << i) * (1 - 2 * self.bits[i])
        return out

    def dev(self, mask):
        return (self.rep, self.base + self.flip(mask))

    def partner(self):
        return (1 - self.rep, self.base + self.lo)


def barrier(here, masks, partner):
    sem = pltpu.get_barrier_semaphore()
    targets = [here.dev(m) for m in masks]
    if partner:
        targets.append(here.partner())
    for t in targets:
        pl.semaphore_signal(sem, inc=1, device_id=t, device_id_type=MESH)
    pl.semaphore_wait(sem, len(targets))


TREE = (1, 2, 4, 8, 12)
ALL = tuple(range(1, GROUP))


def rcopy(src, dst, send, recv, dev):
    return pltpu.make_async_remote_copy(
        src_ref=src, dst_ref=dst, send_sem=send, recv_sem=recv, device_id=dev, device_id_type=MESH
    )


class Gather:
    sems = (4, 7)

    def __init__(self, here, x, out, send, recv):
        self.here, self.x, self.out, self.send, self.recv = here, x, out, send, recv
        self.half = x.shape[0] // 2
        self.off = here.lo - here.lo % out.shape[0]
        self.far = (1, 3, 2) if out.shape[0] == GROUP else (1,)
        self.sent = []

    def block(self, mask):
        return self.here.flip(mask) - self.off

    def _go(self, block, part, j, slot, mask):
        ref = self.out.at[block, pl.ds(part * self.half, self.half)]
        c = rcopy(ref, ref, self.send.at[j, slot], self.recv.at[j, slot], self.here.dev(mask))
        c.start()
        self.sent.append(c)

    def _wait(self, j, slot, block, part):
        ref = self.out.at[block, pl.ds(part * self.half, self.half)]
        rcopy(ref, ref, self.send.at[j, slot], self.recv.at[j, slot], self.here.dev(1)).wait_recv()

    def begin(self, own_sem):
        own = pltpu.make_async_copy(self.x, self.out.at[self.block(0)], own_sem)
        own.start()
        for j in self.far:
            c = rcopy(self.x, self.out.at[self.block(0)], self.send.at[j, 6], self.recv.at[j, 6], self.here.dev(4 * j))
            c.start()
            self.sent.append(c)
        own.wait()
        self.spread(0)

    def spread(self, j):
        b = self.block(4 * j)
        if j:
            ref = self.out.at[b]
            rcopy(ref, ref, self.send.at[j, 6], self.recv.at[j, 6], self.here.dev(4)).wait_recv()
        self._go(b, 0, j, 0, 1)
        self._go(b, 1, j, 1, 2)
        self._go(b, 0, j, 2, 2)
        self._go(b, 1, j, 3, 1)

    def forward(self, j):
        m = 4 * j
        self._wait(j, 0, self.block(m ^ 1), 0)
        self._go(self.block(m ^ 1), 0, j, 4, 2)
        self._wait(j, 1, self.block(m ^ 2), 1)
        self._go(self.block(m ^ 2), 1, j, 5, 1)

    def settle(self, j):
        m = 4 * j
        self._wait(j, 2, self.block(m ^ 2), 0)
        self._wait(j, 3, self.block(m ^ 1), 1)
        self._wait(j, 4, self.block(m ^ 3), 0)
        self._wait(j, 5, self.block(m ^ 3), 1)

    def end(self):
        for c in self.sent:
            c.wait_send()


def rowwise(n, step, body):
    def at(i, carry):
        body(pl.ds(pl.multiple_of(i * step, step), step))
        return carry

    lax.fori_loop(0, n // step, at, 0)


class Scatter:
    sems = (5, 7)

    @staticmethod
    def scratch(rows, d, span=GROUP):
        h = rows // 2
        zs = span // 4
        return [
            pltpu.VMEM((zs, 4, h, d), BF),
            pltpu.VMEM((zs, 2, h, d), BF),
            pltpu.VMEM((5 if span == GROUP else 1, rows, d), BF),
            pltpu.SemaphoreType.DMA(Scatter.sems),
            pltpu.SemaphoreType.DMA(Scatter.sems),
        ]

    def __init__(self, here, part, scratch):
        self.here, self.part = here, part
        self.first, self.second, self.zin, self.send, self.recv = scratch
        self.rows = part.shape[1]
        self.half = self.rows // 2
        self.off = here.lo - here.lo % part.shape[0]
        self.line = part.shape[0] == GROUP
        self.sent = []

    def _copy(self, k, slot, src, dst, mask):
        return rcopy(src, dst, self.send.at[k, slot], self.recv.at[k, slot], self.here.dev(mask))

    def _go(self, *a):
        c = self._copy(*a)
        c.start()
        self.sent.append(c)

    def _block(self, k, q):
        return self.here.flip(q) + self.here.away[k] - self.off

    def _piece(self, k, q, part):
        return self.part.at[self._block(k, q), pl.ds(part * self.half, self.half)]

    def start(self, k):
        self._go(k, 1, self._piece(k, 3, 0), self.first.at[k, 1], 2)
        self._go(k, 3, self._piece(k, 3, 1), self.first.at[k, 3], 1)
        self._go(k, 0, self._piece(k, 2, 0), self.first.at[k, 0], 2)
        self._go(k, 2, self._piece(k, 1, 1), self.first.at[k, 2], 1)

    def cross(self, k):
        h = self.half
        for slot, q, part, to in ((1, 1, 0, 1), (3, 2, 1, 2)):
            self._copy(k, slot, self.first.at[k, slot], self.first.at[k, slot], 1).wait_recv()
            own = self._piece(k, q, part)

            def body(r, own=own, slot=slot):
                own[r] = (own[r].astype(F32) + self.first[k, slot, r].astype(F32)).astype(BF)

            rowwise(h, 16, body)
            self._go(k, 4 + part, own, self.second.at[k, part], to)

    def _reduce(self, k, boxes, out):
        h = self.half
        for part, slot in ((0, 0), (1, 2)):
            own = self._piece(k, 0, part)

            def body(r, own=own, part=part, slot=slot):
                total = own[r].astype(F32) + self.first[k, slot, r].astype(F32) + self.second[k, part, r].astype(F32)
                at = pl.ds(part * h + r.start, r.size)
                for b in boxes:
                    total = total + self.zin[b, at].astype(F32)
                if out is None:
                    own[r] = total.astype(BF)
                else:
                    out[at] = total.astype(out.dtype)

            rowwise(h, 16, body)

    def _box(self, b):
        return self.zin.at[b], self.recv.at[(1, 2, 3, 0, 4)[b], 6]

    def _pass(self, k, b, mask):
        box, full = self._box(b)
        return rcopy(self.part.at[self._block(k, 0)], box, self.send.at[k, 6], full, self.here.dev(mask))

    def _full(self, b):
        box, full = self._box(b)
        rcopy(box, box, self.send.at[0, 6], full, self.here.dev(4)).wait_recv()

    def finish(self, k, out=None):
        for part, slot in ((0, 0), (1, 2)):
            self._copy(k, slot, self.first.at[k, slot], self.first.at[k, slot], 1).wait_recv()
            self._copy(k, 4 + part, self.second.at[k, part], self.second.at[k, part], 1).wait_recv()
        if k == 0:
            self._full(0)
        if not self.line:
            self._reduce(k, () if k else (0,), out)
            if k:
                self._pass(k, 0, 4).start()
                self.sent.append(self._pass(k, 0, 4))
            return
        inner = self.here.inner

        @pl.when(inner == 0)
        def _():
            self._reduce(k, () if k else (0,), out)
            if k:
                self._pass(k, k - 1, 4).start()

        @pl.when(inner == 1)
        def _():
            boxes = ((0, 3), (4,), (1,), (2,))[k]
            for b in boxes:
                if b:
                    self._full(b)
            self._reduce(k, boxes, out)
            if k == 1:
                self._pass(k, 0, 4).start()
            elif k:
                self._pass(k, k + 1, 12).start()

        if k:
            self.sent.append(self._pass(k, 0, 4))

    def end(self):
        for c in self.sent:
            c.wait_send()


def any_spec(n):
    return [pl.BlockSpec(memory_space=pl.ANY)] * n


def vmem_spec(n):
    return [pl.BlockSpec(memory_space=pltpu.VMEM)] * n


def params(cid, mib=60):
    return pltpu.CompilerParams(collective_id=cid, has_side_effects=True, vmem_limit_bytes=mib * MIB)


def exchange_columns(here, src, dst, width, cols, span, send, recv, own_sem):
    copies = []
    own = []
    for i, c in enumerate(cols):
        for m in range(GROUP):
            peer = here.flip(m)
            at = src.at[:, :, pl.ds(pl.multiple_of(c + (peer % span) * width, 128), width)]
            to = dst.at[here.rep, :, here.lo, :, pl.ds(i * width, width)]
            if m == 0:
                cp = pltpu.make_async_copy(at, to, own_sem.at[i])
                cp.start()
                own.append(cp)
            else:
                cp = rcopy(at, to, send.at[i, m], recv.at[i, m], here.dev(m))
                cp.start()
                copies.append(cp)

    def arrive():
        for cp in own:
            cp.wait()
        for i, c in enumerate(cols):
            for m in ALL:
                to = dst.at[here.rep, :, here.flip(m), :, pl.ds(i * width, width)]
                rcopy(to, to, send.at[i, m], recv.at[i, m], here.dev(m)).wait_recv()

    def end():
        for cp in copies:
            cp.wait_send()

    return arrive, end


def rope_parts(rope):
    other = pltpu.roll(rope, HEAD_DIM // 2, 1)
    first = lax.broadcasted_iota(jnp.int32, rope.shape, 1) < HEAD_DIM // 2
    return jnp.where(first, rope, other), jnp.where(first, -other, rope)


def turned(x, cosine, sine):
    return x * cosine + pltpu.roll(x, HEAD_DIM // 2, 1) * sine


CODE = 4096


def head_of_bin(qkv, tables, b):
    rope, code_row, code_col = tables
    slots = qkv.shape[1] // rope.shape[0]
    rows = pl.ds(b * slots, slots)
    n = GROUP * slots

    def piece(i):
        return qkv[:, rows, i * HEAD_DIM : (i + 1) * HEAD_DIM].reshape(n, HEAD_DIM)

    cos, sin = rope_parts(rope[b])
    queries = turned(piece(0).astype(F32), cos, sin).astype(BF)
    keys = turned(piece(1).astype(F32), cos, sin).astype(BF)
    query_code, key_code = code_row[b], code_col[b]
    segment_code = query_code - jnp.bitwise_and(query_code, CODE - 1)
    seen = (key_code <= query_code) & (key_code >= segment_code)
    scores = jnp.where(seen, dot_t(queries, keys) * (1.0 / math.sqrt(HEAD_DIM)), -1e30)
    weights = jnp.exp(scores - jnp.max(scores, -1, keepdims=True))
    probability = weights / jnp.sum(weights, -1, keepdims=True)
    return queries, keys, piece(2), probability, rows, cos, sin


def attend(qkv, out, tables, b):
    _, _, values, probability, rows, _, _ = head_of_bin(qkv, tables, b)
    attended = dot(probability.astype(BF), values).astype(BF)
    out[:, rows] = attended.reshape(GROUP, rows.size, HEAD_DIM)


def front_kernel(
    mixm, n1, rope, code_row, code_col, sorter, g, wqkv, wout, wgu, wdn,
    raw, gs, n1g_out, dy2g, qkvs, outs, gus, dns, attn,
    n1g, wq, attended, plane, dy2,
    gsend, grecv, own, csend, crecv, cown, psend, precv, late, group_out, ssend, srecv, sown,
):
    here = Here()
    barrier(here, ALL, True)
    tables = (rope, code_row, code_col)
    tokens, width = n1.shape
    q = exchange_columns(here, wqkv, qkvs, 128, (0, 2048, 4096), GROUP, csend.at[0], crecv.at[0], cown.at[0])
    half = wgu.shape[2] // 2
    ga = Gather(here, n1, n1g, gsend.at[0], grecv.at[0])
    gb = Gather(here, dy2, dy2g, gsend.at[1], grecv.at[1])
    gc = Gather(here, wout, outs.at[here.rep], gsend.at[2], grecv.at[2])
    o = (0, 1, 3, 2)

    def hand_over(i, dst):
        cp = rcopy(dst.at[here.rep], dst.at[here.rep], psend.at[i], precv.at[i], here.partner())
        cp.start()
        return cp

    def other_core(i, dst):
        other = dst.at[1 - here.rep]
        rcopy(other, other, psend.at[i], precv.at[i], here.partner()).wait_recv()

    ga.begin(own.at[0])
    ga.spread(o[1])
    ga.forward(o[0])
    q[0]()
    q_pass = hand_over(0, qkvs)
    ga.spread(o[2])
    ga.forward(o[1])
    ga.spread(o[3])
    ga.forward(o[2])
    gc.begin(own.at[2])
    u = exchange_columns(here, wgu, gus, half // CUBE, (0, half), CUBE, csend.at[1], crecv.at[1], cown.at[1])
    d = exchange_columns(here, wdn, dns, half // CUBE, (0,), CUBE, csend.at[2], crecv.at[2], cown.at[2])
    ga.forward(o[3])
    sort_planes(sorter, g, gs, plane)
    p = read_mix(mixm)

    def to_branch(r):
        dy2[r] = mixed([p[j][5] for j in range(4)], [gs[j, r].astype(F32) for j in range(4)]).astype(BF)

    rowwise(tokens, 16, to_branch)
    other_core(0, qkvs)
    get = pltpu.make_async_copy(qkvs, wq, late)
    get.start()
    get.wait()
    copies = []
    for k, j in enumerate(o):
        ga.settle(j)
        blocks = pl.ds(here.flip(4 * j) - here.lo % 4, 4)
        x = n1g[blocks].reshape(4 * tokens, width)
        raw[blocks] = dot(x, wq[...].reshape(width, wq.shape[-1])).astype(BF).reshape(4, tokens, wq.shape[-1])
        c = pltpu.make_async_copy(n1g.at[blocks], n1g_out.at[blocks], group_out.at[k])
        c.start()
        copies.append(c)
    bins = rope.shape[0]
    for b in range(bins):
        attend(raw, attended, tables, b)
        if b < 3:
            gc.spread(o[b + 1])
            gc.forward(o[b])
    swaps = []
    at = pl.ds(pl.multiple_of(here.lo * HEAD_DIM, HEAD_DIM), HEAD_DIM)
    for m in ALL:
        c = rcopy(attended.at[here.flip(m)], attn.at[:, at], ssend.at[m], srecv.at[m], here.dev(m))
        c.start()
        swaps.append(c)
    mine = pltpu.make_async_copy(attended.at[here.lo], attn.at[:, at], sown)
    mine.start()
    gb.begin(own.at[1])
    gc.forward(o[3])
    gb.spread(1)
    gb.forward(0)
    for j in o:
        gc.settle(j)
    out_pass = hand_over(3, outs)
    gb.forward(1)
    u[0]()
    u_pass = hand_over(1, gus)
    d[0]()
    d_pass = hand_over(2, dns)
    gb.settle(0)
    gb.settle(1)
    mine.wait()
    for m in ALL:
        ref = attn.at[:, pl.ds(pl.multiple_of(here.flip(m) * HEAD_DIM, HEAD_DIM), HEAD_DIM)]
        rcopy(ref, ref, ssend.at[m], srecv.at[m], here.dev(m)).wait_recv()
    for i, dst in ((1, gus), (2, dns), (3, outs)):
        other_core(i, dst)
    for c in (q_pass, u_pass, d_pass, out_pass, *swaps):
        c.wait_send()
    for c in copies:
        c.wait()
    for g in (ga, gb, gc):
        g.end()
    for _, end in (q, u, d):
        end()


def front(mixm, n1, tables, sorter, g, wqkv, wout, wgu, wdn, cid):
    hi, rows, _ = wqkv.shape
    ff = wdn.shape[2]
    tokens = n1.shape[0]
    shape = lambda *s: jax.ShapeDtypeStruct(s, BF)
    out_rows = wout.shape[0]
    head = 3 * HEAD_DIM
    return pl.pallas_call(
        front_kernel,
        out_shape=(
            shape(GROUP, tokens, head),
            shape(g.shape[1], tokens, g.shape[2]),
            shape(GROUP, *n1.shape),
            shape(CUBE, *n1.shape),
            shape(2, hi, GROUP, rows, head),
            shape(2, GROUP, out_rows, wout.shape[1]),
            shape(2, hi, GROUP, rows, 2 * ff // CUBE),
            shape(2, hi, GROUP, rows, ff // CUBE),
            shape(tokens, GROUP * HEAD_DIM),
        ),
        in_specs=[*smem_spec(1), *vmem_spec(6), *any_spec(4)],
        out_specs=(*vmem_spec(2), *any_spec(7)),
        scratch_shapes=[
            pltpu.VMEM((GROUP, *n1.shape), BF),
            pltpu.VMEM((2, hi, GROUP, rows, head), BF),
            pltpu.VMEM((GROUP, tokens, HEAD_DIM), BF),
            pltpu.VMEM((g.shape[1], tokens, g.shape[2]), BF),
            pltpu.VMEM(n1.shape, BF),
            pltpu.SemaphoreType.DMA((3,) + Gather.sems),
            pltpu.SemaphoreType.DMA((3,) + Gather.sems),
            pltpu.SemaphoreType.DMA((3,)),
            pltpu.SemaphoreType.DMA((3, 3, GROUP)),
            pltpu.SemaphoreType.DMA((3, 3, GROUP)),
            pltpu.SemaphoreType.DMA((3, 3)),
            pltpu.SemaphoreType.DMA((4,)),
            pltpu.SemaphoreType.DMA((4,)),
            pltpu.SemaphoreType.DMA,
            pltpu.SemaphoreType.DMA((4,)),
            pltpu.SemaphoreType.DMA((GROUP,)),
            pltpu.SemaphoreType.DMA((GROUP,)),
            pltpu.SemaphoreType.DMA,
        ],
        compiler_params=params(cid, 62),
    )(mixm, n1, *tables, sorter, g, wqkv, wout, wgu, wdn)


def pair_add(here, g, inbox, send, recv):
    cp = rcopy(g.at[1 - here.rep], inbox, send, recv, here.partner())
    cp.start()
    cp.wait()

    def body(r):
        g[here.rep, r] = (g[here.rep, r].astype(F32) + inbox[r].astype(F32)).astype(BF)

    rowwise(inbox.shape[0], 16, body)


def send_home(here, total, out, send, recv, own):
    _, hi, rows, _ = out.shape

    def block(h, m):
        at = (h * GROUP + here.flip(m)) * rows
        return total.at[pl.ds(pl.multiple_of(at, rows), rows)]

    cps = []
    owns = []
    for h in range(hi):
        for m in ALL:
            c = rcopy(block(h, m), out.at[here.lo, h], send.at[h, m], recv.at[h, m], here.dev(m))
            c.start()
            cps.append(c)
        c = pltpu.make_async_copy(block(h, 0), out.at[here.lo, h], own.at[h])
        c.start()
        owns.append(c)

    def end():
        for c in owns:
            c.wait()
        for h in range(hi):
            for m in ALL:
                ref = out.at[here.flip(m), h]
                rcopy(ref, ref, send.at[h, m], recv.at[h, m], here.dev(m)).wait_recv()
        for c in cps:
            c.wait_send()

    return end


def home_sems(hi):
    return [
        pltpu.SemaphoreType.DMA((hi, GROUP)),
        pltpu.SemaphoreType.DMA((hi, GROUP)),
        pltpu.SemaphoreType.DMA((hi,)),
    ]


def mlp_kernel(
    mixa, mixm, n2, dy2g_in, wgu_in, wdn_in, hs, gs, wout, y1, y2p, grads_out, dx2, dy1, d_out, sums,
    n2g, dy2g, wgu, wdn, part, hidden, dgu, y2s, grads, inbox, dn2,
    gsend, grecv, own, load, y2sem, psend, precv, late, *scratch,
):
    here = Here()
    barrier(here, (1, 2, 4), True)
    g = Gather(here, n2, n2g, gsend, grecv)
    rs = Scatter(here, part, scratch)
    g.begin(own)
    loads = []
    for i, (src, dst) in enumerate(((wgu_in, wgu), (wdn_in, wdn), (dy2g_in, dy2g))):
        c = pltpu.make_async_copy(src, dst, load.at[i])
        c.start()
        loads.append(c)
    width, ff = wdn.shape
    tokens = n2.shape[0]
    group_rows = 4 * tokens
    step = 256
    y2copies = []

    def compute(j):
        first = here.flip(4 * j) - here.lo % 4 - g.off
        blocks = pl.ds(first, 4)
        if not y2copies:
            for c in loads:
                c.wait()

        def gates(k, carry):
            up_at = pl.ds(pl.multiple_of(k * step, step), step)
            gate_at = pl.ds(pl.multiple_of(ff + k * step, step), step)
            x = n2g[blocks].reshape(group_rows, width)
            up = dot(x, wgu[:, up_at])
            gate = dot(x, wgu[:, gate_at])
            dh = dot(dy2g[blocks].reshape(group_rows, width), wdn[:, up_at])
            small = jnp.exp(-jnp.abs(gate))
            sigmoid = jnp.where(gate >= 0.0, 1.0, small) / (1.0 + small)
            silu = gate * sigmoid
            hidden[blocks, :, up_at] = (silu * up).astype(BF).reshape(4, tokens, step)
            dgu[blocks, :, up_at] = (dh * silu).astype(BF).reshape(4, tokens, step)
            dgu[blocks, :, gate_at] = (
                (dh * up * sigmoid * (1.0 + gate * (1.0 - sigmoid))).astype(BF).reshape(4, tokens, step)
            )
            return carry

        lax.fori_loop(0, ff // step, gates, 0)
        if y2copies:
            y2copies[-1].wait()

        def outputs(k, carry):
            at = pl.ds(pl.multiple_of(k * step, step), step)
            h = hidden[blocks].reshape(group_rows, ff)
            y2s[:, :, at] = dot_t(h, wdn[at, :]).astype(BF).reshape(4, tokens, step)
            d = dgu[blocks].reshape(group_rows, 2 * ff)
            part[blocks, :, at] = dot_t(d, wgu[at, :]).astype(BF).reshape(4, tokens, step)
            return carry

        lax.fori_loop(0, width // step, outputs, 0)
        c = pltpu.make_async_copy(y2s, y2p.at[blocks], y2sem.at[len(y2copies)])
        c.start()
        y2copies.append(c)

    half = width // 2
    chunks = half // step

    def weight_grads(which, k):
        cols = pl.ds(pl.multiple_of(which * half + k * step, step), step)
        rows = pl.ds(pl.multiple_of(k * step, step), step)
        x = n2g[:, :, cols].reshape(CUBE * tokens, step)
        grads[which, rows, : 2 * ff] = t_dot(x, dgu[...].reshape(CUBE * tokens, 2 * ff)).astype(BF)
        x = dy2g[:, :, cols].reshape(CUBE * tokens, step)
        grads[which, rows, 2 * ff :] = t_dot(x, hidden[...].reshape(CUBE * tokens, ff)).astype(BF)

    def pass_chunk(k):
        rows = pl.ds(pl.multiple_of(k * step, step), step)
        return rcopy(grads.at[1 - here.rep, rows], inbox.at[rows], psend.at[k], precv.at[k], here.partner())

    g.spread(1)
    g.forward(0)
    g.settle(0)
    compute(0)
    rs.start(0)
    g.forward(1)
    rs.cross(0)
    g.settle(1)
    compute(1)
    rs.start(1)

    def other_half(k, carry):
        weight_grads(1 - here.rep, k)
        pass_chunk(k).start()
        return carry

    lax.fori_loop(0, chunks, other_half, 0)
    rs.cross(1)
    rs.finish(1)

    def own_half(k, carry):
        weight_grads(here.rep, k)
        return carry

    lax.fori_loop(0, chunks, own_half, 0)
    g.end()
    streams = hs.shape[0]
    loads = []
    for i, (src, dst) in enumerate(((hs, n2g.at[:streams]), (gs, n2g.at[streams : 2 * streams]), (wout, wgu))):
        c = pltpu.make_async_copy(src, dst, late.at[i])
        c.start()
        loads.append(c)

    def add(k, carry):
        pass_chunk(k).wait()

        def rows_add(i, carry):
            r = pl.ds(pl.multiple_of(k * step + i * 16, 16), 16)
            grads[here.rep, r] = (grads[here.rep, r].astype(F32) + inbox[r].astype(F32)).astype(BF)
            return carry

        return lax.fori_loop(0, step // 16, rows_add, carry)

    lax.fori_loop(0, chunks, add, 0)
    out = pltpu.make_async_copy(grads.at[here.rep], grads_out, late.at[3])
    out.start()
    rs.finish(0, dn2)
    for c in loads:
        c.wait()
    turn(read_mix(mixa), read_mix(mixm), n2g, y1, dn2, wgu, dx2, dy1, d_out, sums)
    out.wait()
    y2copies[-1].wait()
    rs.end()


def mlp(mixa, mixm, n2, dy2g, wgu, wdn, hs, gs, wout, y1, cid):
    tokens, width = n2.shape
    ff = wdn.shape[1]
    half = width // 2
    blocks = (CUBE, tokens)
    return pl.pallas_call(
        mlp_kernel,
        out_shape=(
            jax.ShapeDtypeStruct((*blocks, width), BF),
            jax.ShapeDtypeStruct((half, 3 * ff), BF),
            jax.ShapeDtypeStruct((tokens, width), F32),
            jax.ShapeDtypeStruct((tokens, width), BF),
            jax.ShapeDtypeStruct((tokens, width), BF),
            jax.ShapeDtypeStruct((24, 16, 128), F32),
        ),
        in_specs=[*smem_spec(2), *vmem_spec(1), *any_spec(6), *vmem_spec(1)],
        out_specs=(*any_spec(2), *vmem_spec(4)),
        scratch_shapes=[
            pltpu.VMEM((*blocks, width), BF),
            pltpu.VMEM((*blocks, width), BF),
            pltpu.VMEM(wgu.shape, BF),
            pltpu.VMEM(wdn.shape, BF),
            pltpu.VMEM((*blocks, width), BF),
            pltpu.VMEM((*blocks, ff), BF),
            pltpu.VMEM((*blocks, 2 * ff), BF),
            pltpu.VMEM((4, tokens, width), BF),
            pltpu.VMEM((2, half, 3 * ff), BF),
            pltpu.VMEM((half, 3 * ff), BF),
            pltpu.VMEM((tokens, width), F32),
            pltpu.SemaphoreType.DMA(Gather.sems),
            pltpu.SemaphoreType.DMA(Gather.sems),
            pltpu.SemaphoreType.DMA,
            pltpu.SemaphoreType.DMA((3,)),
            pltpu.SemaphoreType.DMA((4,)),
            pltpu.SemaphoreType.DMA((half // 256,)),
            pltpu.SemaphoreType.DMA((half // 256,)),
            pltpu.SemaphoreType.DMA((4,)),
            *Scatter.scratch(tokens, width, CUBE),
        ],
        compiler_params=params(cid, 63),
        cost_estimate=pl.CostEstimate(
            flops=2 * CUBE * tokens * width * ff * 9, bytes_accessed=60 * MIB, transcendentals=0
        ),
    )(mixa, mixm, n2, dy2g, wgu, wdn, hs, gs, wout, y1)


def attend_back(qkv, d_out, dqkv, tables, b):
    queries, keys, values, probability, rows, cos, sin = head_of_bin(qkv, tables, b)
    n, slots = queries.shape[0], rows.size
    scale = 1.0 / math.sqrt(HEAD_DIM)
    grad = d_out[:, rows].reshape(n, HEAD_DIM)
    grad_values = t_dot(probability.astype(BF), grad)
    grad_probs = dot_t(grad, values)
    shared = jnp.sum(grad_probs * probability, -1, keepdims=True)
    grad_scores = (probability * (grad_probs - shared)).astype(BF)
    grad_query = dot(grad_scores, keys) * scale
    grad_keys = t_dot(grad_scores, queries) * scale
    for i, v in enumerate((turned(grad_query, cos, -sin), turned(grad_keys, cos, -sin), grad_values)):
        dqkv[:, rows, i * HEAD_DIM : (i + 1) * HEAD_DIM] = v.astype(BF).reshape(GROUP, slots, HEAD_DIM)


class GradsHome:
    @staticmethod
    def scratch(hi, rows, w):
        return [
            pltpu.VMEM((hi, CUBE, rows, w), BF),
            pltpu.VMEM((hi, CUBE, rows, w), BF),
            *[pltpu.SemaphoreType.DMA((hi, CUBE))] * 6,
        ]

    def __init__(self, here, gmlp, out, scratch):
        self.here, self.out = here, out
        self.mine, self.box, self.zsend, self.zrecv, self.load, self.send, self.recv, self.own = scratch
        self.hi, _, self.rows, _ = self.mine.shape
        self.sent = []
        self.loads = {}
        self.gmlp = gmlp

    def begin(self, wave):
        here = self.here
        for h in range(self.hi):
            for m in wave:

                def block(mask, h=h):
                    at = (h * GROUP + here.flip(mask)) * self.rows
                    return self.gmlp.at[pl.ds(pl.multiple_of(at, self.rows), self.rows)]

                c = rcopy(block(m ^ 8), self.box.at[h, m], self.zsend.at[h, m], self.zrecv.at[h, m], here.dev(8))
                c.start()
                self.sent.append(c)
                c = pltpu.make_async_copy(block(m), self.mine.at[h, m], self.load.at[h, m])
                c.start()
                self.loads[h, m] = c

    def relay(self, m):
        here = self.here
        for h in range(self.hi):
            box, mine = self.box.at[h, m], self.mine.at[h, m]
            self.loads[h, m].wait()
            rcopy(box, box, self.zsend.at[h, m], self.zrecv.at[h, m], here.dev(8)).wait_recv()

            def body(r, box=box, mine=mine):
                mine[r] = (mine[r].astype(F32) + box[r].astype(F32)).astype(BF)

            rowwise(self.rows, 16, body)
            to = self.out.at[here.lo % CUBE, h]
            if m:
                c = rcopy(mine, to, self.send.at[h, m], self.recv.at[h, m], here.dev(m))
                self.sent.append(c)
            else:
                c = pltpu.make_async_copy(mine, to, self.own.at[h, 0])
                self.loads[h, 0] = c
            c.start()

    def end(self):
        here = self.here
        for h in range(self.hi):
            self.loads[h, 0].wait()
            for m in range(1, CUBE):
                ref = self.out.at[here.flip(m) % CUBE, h]
                rcopy(ref, ref, self.send.at[h, m], self.recv.at[h, m], here.dev(m)).wait_recv()
        for c in self.sent:
            c.wait_send()


def back_kernel(
    d_rows, qkv, qkvs, dy1, attn, rope, code_row, code_col, n1g, y2_in, gmlp,
    dn_out, y2_out, gout_out, gqkv_out, gmlp_out,
    d_out, dqkv, dn, y2, gout, stage, gqkv, tiles, obox, qbox,
    dsend, drecv, down, load, tile_sem, osend, orecv, qsend, qrecv, *scratch,
):
    here = Here()
    barrier(here, ALL, True)
    tables = (rope, code_row, code_col)
    bins = rope.shape[0]
    swaps = []
    for m in ALL:
        at = pl.ds(pl.multiple_of(here.flip(m) * HEAD_DIM, HEAD_DIM), HEAD_DIM)
        c = rcopy(d_rows.at[:, at], d_out.at[here.lo], dsend.at[m], drecv.at[m], here.dev(m))
        c.start()
        swaps.append(c)
    at = pl.ds(pl.multiple_of(here.lo * HEAD_DIM, HEAD_DIM), HEAD_DIM)
    mine = pltpu.make_async_copy(d_rows.at[:, at], d_out.at[here.lo], down)
    mine.start()
    y2_load = pltpu.make_async_copy(y2_in, y2, load)
    y2_load.start()
    _, tokens, width = dn.shape
    k = len(Scatter.scratch(16, 128))
    rs_dn = Scatter(here, dn, scratch[:k])
    rs_y2 = Scatter(here, y2, scratch[k : 2 * k])
    rs_go = Scatter(here, gout.reshape(GROUP, gout.shape[0] // GROUP, width), scratch[2 * k : 3 * k])
    qhome = scratch[3 * k : 3 * k + 3]
    gm = GradsHome(here, gmlp, gmlp_out, scratch[3 * k + 3 :])
    gm.begin((0, 1))
    order = (3, 2, 1, 0)
    y2_load.wait()
    rs_y2.start(1)
    rs_y2.start(0)
    gm.begin((2, 3))
    mine.wait()
    for m in ALL:
        ref = d_out.at[here.flip(m)]
        rcopy(ref, ref, dsend.at[m], drecv.at[m], here.dev(m)).wait_recv()

    half = width // 2
    step = 256
    chunks = half // step

    def out_grads(which, k):
        cols = pl.ds(pl.multiple_of(which * half + k * step, step), step)
        return t_dot(attn[:, cols], dy1[...]).astype(BF)

    def gout_pass(k):
        at = pl.ds(k * step, step)
        return rcopy(stage.at[k % 2], obox.at[at], osend.at[k], orecv.at[k], here.partner())

    gqkv_pair = rcopy(gqkv.at[1 - here.rep], qbox, qsend, qrecv, here.partner())

    for b in range(bins):
        attend_back(qkv, d_out, dqkv, tables, b)
        if b == 1:
            rs_y2.cross(1)
        elif b == 2:
            rs_y2.cross(0)
            rs_y2.finish(1)

    narrow = tiles.shape[3]

    def qkv_tile(k):
        cols = pl.ds(k * narrow, narrow)
        return pltpu.make_async_copy(n1g.at[:, :, cols], tiles.at[k % 2], tile_sem.at[k % 2])

    qkv_tile(0).start()
    for j in order:
        blocks = pl.ds(here.lo + here.away[j] - here.lo % 4, 4)

        def part(k, carry, blocks=blocks):
            at = pl.ds(pl.multiple_of(k * TILE, TILE), TILE)
            d = dqkv[blocks].reshape(4 * tokens, 3 * HEAD_DIM)
            dn[blocks, :, at] = dot_t(d, qkvs[at, :]).astype(BF).reshape(4, tokens, TILE)
            return carry

        lax.fori_loop(0, width // TILE, part, 0)
        rs_dn.start(j)
    count = width // narrow
    for k in range(count):
        if k + 1 < count:
            qkv_tile(k + 1).start()
        qkv_tile(k).wait()
        x = tiles[k % 2].reshape(GROUP * tokens, narrow)
        rows = pl.ds((k % (count // 2)) * narrow, narrow)
        gqkv[k // (count // 2), rows, :] = t_dot(x, dqkv[...].reshape(GROUP * tokens, 3 * HEAD_DIM)).astype(BF)
    gqkv_pair.start()
    gm.relay(0)
    gm.relay(1)
    gm.begin((4, 5))
    rs_y2.finish(0, y2_out)
    rs_dn.cross(order[0])
    for k in range(chunks):
        if k >= 2:
            gout_pass(k - 2).wait_send()
        stage[k % 2] = out_grads(1 - here.rep, k)
        gout_pass(k).start()
    rs_dn.cross(order[1])
    rs_dn.finish(order[0])
    for k in range(chunks):
        gout[k * step : (k + 1) * step, :] = out_grads(here.rep, k)

    def add(ref, box):
        def body(r):
            ref[r] = (ref[r].astype(F32) + box[r].astype(F32)).astype(BF)

        rowwise(box.shape[0], 16, body)

    gqkv_pair.wait()
    add(gqkv.at[here.rep], qbox)
    gm.relay(2)
    gm.begin((6,))
    end_qkv = send_home(here, gqkv.at[here.rep], gqkv_out, *qhome)
    rs_dn.cross(order[2])
    rs_dn.finish(order[1])
    gm.relay(3)
    gm.begin((7,))
    for k in range(chunks):
        gout_pass(k).wait_recv()
        if k >= chunks - 2:
            gout_pass(k).wait_send()
    add(gout, obox)
    for j in order:
        rs_go.start(j)
    rs_dn.cross(order[3])
    rs_dn.finish(order[2])
    rs_go.cross(order[0])
    gm.relay(4)
    rs_go.cross(order[1])
    rs_go.finish(order[0])
    gm.relay(5)
    gm.relay(6)
    gm.relay(7)
    rs_go.cross(order[2])
    rs_go.finish(order[1])
    rs_go.cross(order[3])
    rs_go.finish(order[2])
    rs_dn.finish(0, dn_out)
    rs_go.finish(0, gout_out)
    gm.end()
    end_qkv()
    for c in swaps:
        c.wait_send()
    for rs in (rs_dn, rs_y2, rs_go):
        rs.end()


def back(d_rows, qkv, qkvs, dy1, attn, tables, n1g, y2, gmlp, hi, cid):
    tokens, width = d_rows.shape
    half = width // 2
    w = qkv.shape[2]
    return pl.pallas_call(
        back_kernel,
        out_shape=(
            jax.ShapeDtypeStruct((tokens, width), F32),
            jax.ShapeDtypeStruct((tokens, width), F32),
            jax.ShapeDtypeStruct((half // GROUP, width), F32),
            jax.ShapeDtypeStruct((GROUP, hi, half // (hi * GROUP), w), BF),
            jax.ShapeDtypeStruct((CUBE, hi, half // (hi * GROUP), gmlp.shape[1]), BF),
        ),
        in_specs=[*vmem_spec(8), *any_spec(3)],
        out_specs=(*vmem_spec(3), *any_spec(2)),
        scratch_shapes=[
            pltpu.VMEM((GROUP, tokens, HEAD_DIM), BF),
            pltpu.VMEM((GROUP, tokens, w), BF),
            pltpu.VMEM((GROUP, tokens, width), BF),
            pltpu.VMEM((CUBE, tokens, width), BF),
            pltpu.VMEM((half, width), BF),
            pltpu.VMEM((2, 256, width), BF),
            pltpu.VMEM((2, half, w), BF),
            pltpu.VMEM((2, GROUP, tokens, TILE // 4), BF),
            pltpu.VMEM((half, width), BF),
            pltpu.VMEM((half, w), BF),
            pltpu.SemaphoreType.DMA((GROUP,)),
            pltpu.SemaphoreType.DMA((GROUP,)),
            pltpu.SemaphoreType.DMA,
            pltpu.SemaphoreType.DMA,
            pltpu.SemaphoreType.DMA((2,)),
            pltpu.SemaphoreType.DMA((half // 256,)),
            pltpu.SemaphoreType.DMA((half // 256,)),
            pltpu.SemaphoreType.DMA,
            pltpu.SemaphoreType.DMA,
            *Scatter.scratch(tokens, width),
            *Scatter.scratch(tokens, width, CUBE),
            *Scatter.scratch(half // GROUP, width),
            *home_sems(hi),
            *GradsHome.scratch(hi, half // (hi * GROUP), gmlp.shape[1]),
        ],
        compiler_params=params(cid, 63),
    )(d_rows, qkv, qkvs, dy1, attn, *tables, n1g, y2, gmlp)


def read_mix(ref):
    return [[ref[i, k] for k in range(6)] for i in range(4)]


def mixed(weights, planes):
    total = weights[0] * planes[0]
    for w, p in zip(weights[1:], planes[1:]):
        total = total + w * p
    return total


def moments(x):
    centred = x - jnp.mean(x, -1, keepdims=True)
    inverse = lax.rsqrt(jnp.mean(centred * centred, -1, keepdims=True) + EPSILON)
    return centred * inverse, inverse


def normalize_back(grad_out, normed, inverse):
    return inverse * (
        grad_out
        - jnp.mean(grad_out, -1, keepdims=True)
        - normed * jnp.mean(grad_out * normed, -1, keepdims=True)
    )


def lane_sums(x):
    total = x[:, :128]
    for c in range(128, x.shape[1], 128):
        total = total + x[:, c : c + 128]
    return total


def read_x2(m, p, h, y1):
    fold = [sum(p[s][0] * m[j][1 + s] for s in range(4)) for j in range(4)]
    return mixed(fold + [sum(p[s][0] * m[s][5] for s in range(4))], [*h, y1])


TILE = 512


def sort_planes(sorter, x, planes, plane):
    tokens, streams, width = x.shape

    def split(r):
        v = x[r].astype(F32)
        for i in range(streams):
            plane[i, r] = v[:, i, :].astype(BF)

    rowwise(tokens, 16, split)
    for i in range(streams):
        for c in range(0, width, TILE):
            at = slice(c, c + TILE)
            planes[i, :, at] = dot(sorter[...], plane[i, :, at]).astype(BF)


def open_kernel(mixa, sorter, x, hs, n1, plane):
    m = read_mix(mixa)
    sort_planes(sorter, x, hs, plane)

    def norm(r):
        x1 = mixed([m[j][0] for j in range(4)], [hs[j, r].astype(F32) for j in range(4)])
        n1[r] = moments(x1)[0].astype(BF)

    rowwise(x.shape[0], 16, norm)


def smem_spec(n):
    return [pl.BlockSpec(memory_space=pltpu.SMEM)] * n


def local_params(mib=60):
    return pltpu.CompilerParams(vmem_limit_bytes=mib * MIB)


def open_streams(mixa, sorter, x):
    tokens, streams, width = x.shape
    return pl.pallas_call(
        open_kernel,
        out_shape=(
            jax.ShapeDtypeStruct((streams, tokens, width), BF),
            jax.ShapeDtypeStruct((tokens, width), BF),
        ),
        in_specs=[*smem_spec(1), *vmem_spec(2)],
        out_specs=tuple(vmem_spec(2)),
        scratch_shapes=[pltpu.VMEM((streams, tokens, width), BF)],
        compiler_params=local_params(),
    )(mixa, sorter, x)


def middle_kernel(mixa, mixm, hs, attn, wout, y1, n2):
    m, p = read_mix(mixa), read_mix(mixm)
    tokens, width = attn.shape

    def tile(i, carry):
        at = pl.ds(pl.multiple_of(i * TILE, TILE), TILE)
        y1[:, at] = dot(attn[...], wout[:, at])
        return carry

    lax.fori_loop(0, width // TILE, tile, 0)

    def norm(r):
        x2 = read_x2(m, p, [hs[j, r].astype(F32) for j in range(4)], y1[r])
        n2[r] = moments(x2)[0].astype(BF)

    rowwise(tokens, 16, norm)


def middle(mixa, mixm, hs, attn, wout):
    tokens, width = attn.shape
    return pl.pallas_call(
        middle_kernel,
        out_shape=(
            jax.ShapeDtypeStruct((tokens, width), F32),
            jax.ShapeDtypeStruct((tokens, width), BF),
        ),
        in_specs=[*smem_spec(2), *vmem_spec(3)],
        out_specs=tuple(vmem_spec(2)),
        compiler_params=local_params(),
    )(mixa, mixm, hs, attn, wout)


def unsort(sorter, planes, out):
    streams, tokens, width = planes.shape
    for i in range(streams):

        def tile(k, carry, i=i):
            at = pl.ds(pl.multiple_of(k * TILE, TILE), TILE)
            v = planes[i, :, at]
            high = v.astype(BF)
            low = (v - high.astype(F32)).astype(BF)
            out[:, i, at] = t_dot(sorter[...], high) + t_dot(sorter[...], low)
            return carry

        lax.fori_loop(0, width // TILE, tile, 0)


def turn(m, p, planes, y1, dn2, wout, dx2, dy1, d_out, sums):
    tokens, width = y1.shape
    sums[...] = jnp.zeros_like(sums)

    def body(r):
        x2 = read_x2(m, p, [planes[j, r].astype(F32) for j in range(4)], y1[r])
        normed, inverse = moments(x2)
        dx2[r] = normalize_back(dn2[r], normed, inverse)
        for c in range(0, width, TILE):
            at = slice(c, c + TILE)
            h = [planes[j, r, at].astype(F32) for j in range(4)]
            y = y1[r, at]
            h1 = [mixed([*(m[j][1 + i] for j in range(4)), m[i][5]], [*h, y]) for i in range(4)]
            g = [planes[4 + j, r, at].astype(F32) for j in range(4)]
            dx = dx2[r, at]
            g1 = [mixed([*(p[j][1 + i] for i in range(4)), p[j][0]], [*g, dx]) for j in range(4)]
            dy1[r, at] = mixed([m[j][5] for j in range(4)], g1).astype(BF)
            for j in range(4):
                sums[j * 6] += lane_sums(h1[j] * dx)
                for i in range(4):
                    sums[j * 6 + 1 + i] += lane_sums(h1[j] * g[i])

    rowwise(tokens, 16, body)
    def tile(i, carry):
        at = pl.ds(pl.multiple_of(i * TILE, TILE), TILE)
        d_out[:, at] = dot_t(dy1[...], wout[at, :]).astype(BF)
        return carry

    lax.fori_loop(0, width // TILE, tile, 0)


def close_kernel(
    mixa, mixm, sorter, hs, gs, dx2, y1, y2, dn1, other, new, d_streams, mix_a, mix_m,
    sums, planes, fresh, mine, inbox, send, recv,
):
    here = Here()
    barrier(here, ALL, True)
    m, p = read_mix(mixa), read_mix(mixm)
    tokens, width = y1.shape
    sums[:24] = jnp.zeros((24, *sums.shape[1:]), F32)
    sums[24:] = other[...]

    def body(r):
        x1 = mixed([m[j][0] for j in range(4)], [hs[j, r].astype(F32) for j in range(4)])
        normed, inverse = moments(x1)
        planes[0, r] = normalize_back(dn1[r], normed, inverse)
        for c in range(0, width, TILE):
            at = slice(c, c + TILE)
            h = [hs[j, r, at].astype(F32) for j in range(4)]
            g = [gs[j, r, at].astype(F32) for j in range(4)]
            y = y1[r, at]
            dx = planes[0, r, at]
            dm = dx2[r, at]
            g1 = [mixed([*(p[j][1 + i] for i in range(4)), p[j][0]], [*g, dm]) for j in range(4)]
            for j in range(4):
                planes[j, r, at] = mixed([*(m[j][1 + i] for i in range(4)), m[j][0]], [*g1, dx])
                sums[j * 6] += lane_sums(h[j] * dx)
                for i in range(4):
                    sums[j * 6 + 1 + i] += lane_sums(h[j] * g1[i])
                sums[j * 6 + 5] += lane_sums(y * g1[j])
            h1 = [mixed([*(m[j][1 + i] for j in range(4)), m[i][5]], [*h, y]) for i in range(4)]
            y = y2[r, at]
            for i in range(4):
                fresh[i, r, at] = mixed([*(p[j][1 + i] for j in range(4)), p[i][5]], [*h1, y])
                sums[24 + i * 6 + 5] += lane_sums(y * g[i])

    rowwise(tokens, 16, body)
    mine[0] = jnp.sum(sums[...], axis=1)
    pair = rcopy(mine.at[0], inbox.at[0], send.at[0], recv.at[0], here.partner())
    pair.start()
    pair.wait()
    mine[1] = mine[0] + inbox[0]
    cps = []
    for k in ALL:
        c = rcopy(mine.at[1], inbox.at[k], send.at[k], recv.at[k], here.dev(k))
        c.start()
        cps.append(c)
    unsort(sorter, fresh, new)
    unsort(sorter, planes, d_streams)
    everyone = mine[1]
    for c in cps:
        c.wait()
    for k in ALL:
        everyone = everyone + inbox[k]
    everyone = jnp.sum(everyone, axis=1, keepdims=True)
    for n, out in enumerate((mix_a, mix_m)):
        row = lax.broadcasted_iota(jnp.int32, out.shape, 0)
        col = lax.broadcasted_iota(jnp.int32, out.shape, 1)
        value = jnp.zeros(out.shape, F32)
        for j in range(4):
            for c in range(6):
                k = n * 24 + j * 6 + c
                value = jnp.where((row == j) & (col == c), everyone[k : k + 1], value)
        out[...] = value


def close(mixa, mixm, sorter, hs, gs, dx2, y1, y2, dn1, other, cid):
    streams, tokens, width = hs.shape
    return pl.pallas_call(
        close_kernel,
        out_shape=(
            jax.ShapeDtypeStruct((tokens, streams, width), F32),
            jax.ShapeDtypeStruct((tokens, streams, width), F32),
            jax.ShapeDtypeStruct(mixa.shape, F32),
            jax.ShapeDtypeStruct(mixm.shape, F32),
        ),
        in_specs=[*smem_spec(2), *vmem_spec(8)],
        out_specs=tuple(vmem_spec(4)),
        scratch_shapes=[
            pltpu.VMEM((48, 16, 128), F32),
            pltpu.VMEM((streams, tokens, width), F32),
            pltpu.VMEM((streams, tokens, width), F32),
            pltpu.VMEM((2, 48, 128), F32),
            pltpu.VMEM((GROUP, 48, 128), F32),
            pltpu.SemaphoreType.DMA((GROUP,)),
            pltpu.SemaphoreType.DMA((GROUP,)),
        ],
        compiler_params=params(cid),
    )(mixa, mixm, sorter, hs, gs, dx2, y1, y2, dn1, other)


def lay_out_kernel(qkv, out, mlp, gqkv, gout, ggu, gdown):
    head = HEAD_DIM
    for l in range(qkv.shape[0]):
        for i in range(3):
            at = i * GROUP * head + l * head
            gqkv[:, :, at : at + head] = qkv[l, :, :, i * head : (i + 1) * head].astype(F32)
    block = mlp.shape[3] // 3
    for l in range(CUBE):
        for i in range(2):
            at = (i * CUBE + l) * block
            ggu[:, :, at : at + block] = mlp[l, :, :, i * block : (i + 1) * block].astype(F32)
        gdown[:, :, l * block : (l + 1) * block] = mlp[l, :, :, 2 * block :].astype(F32)
    gout[...] = out[...]


def lay_out(qkv, out, mlp):
    _, hi, rows, w = mlp.shape
    ff = w // 3 * CUBE
    shapes = [(hi, rows, GROUP * qkv.shape[3]), out.shape, (hi, rows, 2 * ff), (hi, rows, ff)]
    return pl.pallas_call(
        lay_out_kernel,
        out_shape=tuple(jax.ShapeDtypeStruct(s, F32) for s in shapes),
        in_specs=vmem_spec(3),
        out_specs=tuple(vmem_spec(4)),
        compiler_params=local_params(),
    )(qkv, out, mlp)


def slot_layout(lengths_row, capacity):
    seq_count = lengths_row.shape[-1]
    seq_ends = jnp.cumsum(lengths_row, axis=-1)
    slot_index = jnp.arange(capacity, dtype=jnp.int32)
    segment = jnp.sum((slot_index[:, None] >= seq_ends[..., None, :]).astype(jnp.int32), axis=-1)
    seq_starts = seq_ends - lengths_row
    chosen = (segment[..., None] == jnp.arange(seq_count, dtype=jnp.int32)).astype(jnp.int32)
    start_of = jnp.sum(chosen * seq_starts[..., None, :], axis=-1)
    is_live = segment < seq_count
    segment = jnp.where(is_live, segment, seq_count + slot_index)
    position = jnp.where(is_live, slot_index - start_of, 0)
    return (segment, position)


def rope_tables(position, head_width):
    half_width = head_width // 2
    frequency = jnp.exp(
        jnp.arange(half_width, dtype=jnp.float32) * (-2.0 * math.log(10000.0) / head_width)
    )
    angles = position.astype(jnp.float32)[..., None] * frequency
    return (jnp.cos(angles), jnp.sin(angles))


def dot(a, b):
    return jnp.dot(a, b, preferred_element_type=F32)


def dot_t(a, b):
    return lax.dot_general(a, b, CONTRACT_LAST, preferred_element_type=F32)


def t_dot(a, b):
    return lax.dot_general(a, b, CONTRACT_FIRST, preferred_element_type=F32)


def shards(streams, cotangent, deal, lengths, mix_attn, mix_mlp, w_qkv, w_out, w_gu, w_down):
    tokens, stream_count, width = streams.shape
    shard_size = lax.axis_size("shard")
    hi = shard_size // GROUP
    hi_groups = [[h * GROUP + l for h in range(hi)] for l in range(GROUP)]
    shard = lax.axis_index("shard")
    my_hi = shard // GROUP
    bin_count = shard_size // 4
    my_bins = bin_count // hi
    per_bin = tokens // bin_count
    capacity = per_bin * shard_size
    ff = w_down.shape[1]

    def swap_hi(rows):
        if hi == 1:
            return rows
        return lax.all_to_all(rows, "shard", 0, 0, axis_index_groups=hi_groups, tiled=True)

    def to_bins(rows):
        return swap_hi(rows).reshape(hi, my_bins, per_bin, -1).swapaxes(0, 1).reshape(tokens, -1)

    def from_bins(rows):
        return swap_hi(rows.reshape(my_bins, hi, per_bin, -1).swapaxes(0, 1).reshape(tokens, -1))

    def gather_hi(rows):
        if hi == 1:
            return rows[None]
        return lax.all_gather(rows, "shard", axis_index_groups=hi_groups)

    def sum_hi(rows):
        if hi == 1:
            return rows[0]
        return lax.psum_scatter(rows, "shard", axis_index_groups=hi_groups)

    sorter = (jnp.arange(tokens, dtype=jnp.int32)[:, None] == deal[None, :]).astype(BF)

    hs, n1 = open_streams(mix_attn, sorter, streams)
    low_attn = to_bins(n1)

    bins = lax.axis_index("rep") * bin_count + my_hi * my_bins
    lengths_here = lax.dynamic_slice_in_dim(lengths, bins, my_bins, 0)
    segment, position = slot_layout(lengths_here, capacity)

    def local_order(x):
        return x.reshape(my_bins, hi, GROUP, per_bin).swapaxes(1, 2).reshape(my_bins, capacity)

    segment, position = local_order(segment), local_order(position)
    cosine, sine = rope_tables(position, HEAD_DIM)
    code = segment * CODE + position
    tables = (jnp.concatenate([cosine, sine], -1), code[:, :, None], code[:, None, :])

    raw_qkv, gs, n1g, dy2g, qkvs, outs, gus, dns, attn_rows = front(
        mix_mlp, low_attn, tables, sorter, cotangent,
        gather_hi(w_qkv), gather_hi(w_out).reshape(-1, width), gather_hi(w_gu), gather_hi(w_down), 1,
    )
    rows = w_qkv.shape[0]
    qkvs = qkvs.reshape(width, 3 * HEAD_DIM)
    outs = outs.reshape(2, GROUP, hi, rows, width).swapaxes(1, 2).reshape(width, width)
    gus = gus.reshape(width, 2 * ff // CUBE)
    dns = dns.reshape(width, ff // CUBE)
    attn_rows = from_bins(attn_rows)
    y1, n2 = middle(mix_attn, mix_mlp, hs, attn_rows, outs)
    y2_part, g_mlp, dx2, low_grad_attn, grad_attn, mlp_sums = mlp(
        mix_attn, mix_mlp, n2, dy2g, gus, dns, hs, gs, outs, y1, 4
    )

    attn_cols = attn_rows.reshape(tokens, 2, hi, GROUP, rows).swapaxes(2, 3).reshape(tokens, width)
    dn1, y2, g_out, g_qkv, g_mlp = back(
        to_bins(grad_attn), raw_qkv, qkvs, low_grad_attn, attn_cols, tables,
        n1g, y2_part, g_mlp, hi, 7,
    )
    weight_grads = lay_out(g_qkv, g_out.reshape(hi, rows, width), g_mlp)
    new_streams, d_streams, g_mix_attn, g_mix_mlp = close(
        mix_attn, mix_mlp, sorter, hs, gs, dx2, y1, y2, from_bins(dn1), mlp_sums, 8
    )
    if hi > 1:
        g_mix_attn, g_mix_mlp = lax.psum((g_mix_attn, g_mix_mlp), "shard", axis_index_groups=hi_groups)
    return (new_streams, d_streams, g_mix_attn, g_mix_mlp, *(sum_hi(g) for g in weight_grads))


def solution(mesh):
    both = ("rep", "shard")
    return jax.shard_map(
        shards,
        mesh=mesh,
        in_specs=(
            P(both, None, None),
            P(both, None, None),
            P(both),
            P(),
            P(),
            P(),
            P(both, None),
            P(both, None),
            P(both, None),
            P(both, None),
        ),
        out_specs=(
            P(both, None, None),
            P(both, None, None),
            P(),
            P(),
            P(both, None),
            P(both, None),
            P(both, None),
            P(both, None),
        ),
        check_vma=False,
    )
```

```python
import functools
import math

import jax
import jax.numpy as jnp
from jax import lax
from jax.experimental import pallas as pl
from jax.experimental.pallas import tpu as pltpu
from jax.sharding import PartitionSpec as P

HEADS = 16
HEAD_DIM = 128
GROUP = 16
CUBE = 8
EPSILON = 1e-05
MESH = pl.DeviceIdType.MESH
CONTRACT_LAST = (((1,), (1,)), ((), ()))
CONTRACT_FIRST = (((0,), (0,)), ((), ()))
MIB = 1 << 20
BF = jnp.bfloat16
F32 = jnp.float32


class Here:
    def __init__(self):
        self.rep = lax.axis_index("rep")
        shard = lax.axis_index("shard")
        self.lo = shard % GROUP
        self.base = shard - self.lo
        self.bits = [(self.lo // (1 << i)) % 2 for i in range(4)]
        one, two, three = (self.flip(m) - self.lo for m in (4, 8, 12))
        self.inner = self.bits[2] + self.bits[3] - 2 * self.bits[2] * self.bits[3]
        self.away = (
            0,
            one,
            self.inner * three + (1 - self.inner) * two,
            self.inner * two + (1 - self.inner) * three,
        )

    def flip(self, mask):
        out = self.lo
        for i in range(4):
            if mask & (1 << i):
                out = out + (1 << i) * (1 - 2 * self.bits[i])
        return out

    def dev(self, mask):
        return (self.rep, self.base + self.flip(mask))

    def partner(self):
        return (1 - self.rep, self.base + self.lo)


def barrier(here, masks, partner):
    sem = pltpu.get_barrier_semaphore()
    targets = [here.dev(m) for m in masks]
    if partner:
        targets.append(here.partner())
    for t in targets:
        pl.semaphore_signal(sem, inc=1, device_id=t, device_id_type=MESH)
    pl.semaphore_wait(sem, len(targets))


TREE = (1, 2, 4, 8, 12)
ALL = tuple(range(1, GROUP))


def rcopy(src, dst, send, recv, dev):
    return pltpu.make_async_remote_copy(
        src_ref=src, dst_ref=dst, send_sem=send, recv_sem=recv, device_id=dev, device_id_type=MESH
    )


class Gather:
    sems = (4, 7)

    def __init__(self, here, x, out, send, recv):
        self.here, self.x, self.out, self.send, self.recv = here, x, out, send, recv
        self.half = x.shape[0] // 2
        self.off = here.lo - here.lo % out.shape[0]
        self.far = (1, 3, 2) if out.shape[0] == GROUP else (1,)
        self.sent = []

    def block(self, mask):
        return self.here.flip(mask) - self.off

    def _go(self, block, part, j, slot, mask):
        ref = self.out.at[block, pl.ds(part * self.half, self.half)]
        c = rcopy(ref, ref, self.send.at[j, slot], self.recv.at[j, slot], self.here.dev(mask))
        c.start()
        self.sent.append(c)

    def _wait(self, j, slot, block, part):
        ref = self.out.at[block, pl.ds(part * self.half, self.half)]
        rcopy(ref, ref, self.send.at[j, slot], self.recv.at[j, slot], self.here.dev(1)).wait_recv()

    def begin(self, own_sem):
        own = pltpu.make_async_copy(self.x, self.out.at[self.block(0)], own_sem)
        own.start()
        for j in self.far:
            c = rcopy(self.x, self.out.at[self.block(0)], self.send.at[j, 6], self.recv.at[j, 6], self.here.dev(4 * j))
            c.start()
            self.sent.append(c)
        own.wait()
        self.spread(0)

    def spread(self, j):
        b = self.block(4 * j)
        if j:
            ref = self.out.at[b]
            rcopy(ref, ref, self.send.at[j, 6], self.recv.at[j, 6], self.here.dev(4)).wait_recv()
        self._go(b, 0, j, 0, 1)
        self._go(b, 1, j, 1, 2)
        self._go(b, 0, j, 2, 2)
        self._go(b, 1, j, 3, 1)

    def forward(self, j):
        m = 4 * j
        self._wait(j, 0, self.block(m ^ 1), 0)
        self._go(self.block(m ^ 1), 0, j, 4, 2)
        self._wait(j, 1, self.block(m ^ 2), 1)
        self._go(self.block(m ^ 2), 1, j, 5, 1)

    def settle(self, j):
        m = 4 * j
        self._wait(j, 2, self.block(m ^ 2), 0)
        self._wait(j, 3, self.block(m ^ 1), 1)
        self._wait(j, 4, self.block(m ^ 3), 0)
        self._wait(j, 5, self.block(m ^ 3), 1)

    def end(self):
        for c in self.sent:
            c.wait_send()


def rowwise(n, step, body):
    def at(i, carry):
        body(pl.ds(pl.multiple_of(i * step, step), step))
        return carry

    lax.fori_loop(0, n // step, at, 0)


class Scatter:
    sems = (5, 7)

    @staticmethod
    def scratch(rows, d, span=GROUP):
        h = rows // 2
        zs = span // 4
        return [
            pltpu.VMEM((zs, 4, h, d), BF),
            pltpu.VMEM((zs, 2, h, d), BF),
            pltpu.VMEM((5 if span == GROUP else 1, rows, d), BF),
            pltpu.SemaphoreType.DMA(Scatter.sems),
            pltpu.SemaphoreType.DMA(Scatter.sems),
        ]

    def __init__(self, here, part, scratch):
        self.here, self.part = here, part
        self.first, self.second, self.zin, self.send, self.recv = scratch
        self.rows = part.shape[1]
        self.half = self.rows // 2
        self.off = here.lo - here.lo % part.shape[0]
        self.line = part.shape[0] == GROUP
        self.sent = []

    def _copy(self, k, slot, src, dst, mask):
        return rcopy(src, dst, self.send.at[k, slot], self.recv.at[k, slot], self.here.dev(mask))

    def _go(self, *a):
        c = self._copy(*a)
        c.start()
        self.sent.append(c)

    def _block(self, k, q):
        return self.here.flip(q) + self.here.away[k] - self.off

    def _piece(self, k, q, part):
        return self.part.at[self._block(k, q), pl.ds(part * self.half, self.half)]

    def start(self, k):
        self._go(k, 1, self._piece(k, 3, 0), self.first.at[k, 1], 2)
        self._go(k, 3, self._piece(k, 3, 1), self.first.at[k, 3], 1)
        self._go(k, 0, self._piece(k, 2, 0), self.first.at[k, 0], 2)
        self._go(k, 2, self._piece(k, 1, 1), self.first.at[k, 2], 1)

    def cross(self, k):
        h = self.half
        for slot, q, part, to in ((1, 1, 0, 1), (3, 2, 1, 2)):
            self._copy(k, slot, self.first.at[k, slot], self.first.at[k, slot], 1).wait_recv()
            own = self._piece(k, q, part)

            def body(r, own=own, slot=slot):
                own[r] = (own[r].astype(F32) + self.first[k, slot, r].astype(F32)).astype(BF)

            rowwise(h, 16, body)
            self._go(k, 4 + part, own, self.second.at[k, part], to)

    def _reduce(self, k, boxes, out):
        h = self.half
        for part, slot in ((0, 0), (1, 2)):
            own = self._piece(k, 0, part)

            def body(r, own=own, part=part, slot=slot):
                total = own[r].astype(F32) + self.first[k, slot, r].astype(F32) + self.second[k, part, r].astype(F32)
                at = pl.ds(part * h + r.start, r.size)
                for b in boxes:
                    total = total + self.zin[b, at].astype(F32)
                if out is None:
                    own[r] = total.astype(BF)
                else:
                    out[at] = total.astype(out.dtype)

            rowwise(h, 16, body)

    def _box(self, b):
        return self.zin.at[b], self.recv.at[(1, 2, 3, 0, 4)[b], 6]

    def _pass(self, k, b, mask):
        box, full = self._box(b)
        return rcopy(self.part.at[self._block(k, 0)], box, self.send.at[k, 6], full, self.here.dev(mask))

    def _full(self, b):
        box, full = self._box(b)
        rcopy(box, box, self.send.at[0, 6], full, self.here.dev(4)).wait_recv()

    def finish(self, k, out=None):
        for part, slot in ((0, 0), (1, 2)):
            self._copy(k, slot, self.first.at[k, slot], self.first.at[k, slot], 1).wait_recv()
            self._copy(k, 4 + part, self.second.at[k, part], self.second.at[k, part], 1).wait_recv()
        if k == 0:
            self._full(0)
        if not self.line:
            self._reduce(k, () if k else (0,), out)
            if k:
                self._pass(k, 0, 4).start()
                self.sent.append(self._pass(k, 0, 4))
            return
        inner = self.here.inner

        @pl.when(inner == 0)
        def _():
            self._reduce(k, () if k else (0,), out)
            if k:
                self._pass(k, k - 1, 4).start()

        @pl.when(inner == 1)
        def _():
            boxes = ((0, 3), (4,), (1,), (2,))[k]
            for b in boxes:
                if b:
                    self._full(b)
            self._reduce(k, boxes, out)
            if k == 1:
                self._pass(k, 0, 4).start()
            elif k:
                self._pass(k, k + 1, 12).start()

        if k:
            self.sent.append(self._pass(k, 0, 4))

    def end(self):
        for c in self.sent:
            c.wait_send()


def any_spec(n):
    return [pl.BlockSpec(memory_space=pl.ANY)] * n


def vmem_spec(n):
    return [pl.BlockSpec(memory_space=pltpu.VMEM)] * n


def params(cid, mib=60):
    return pltpu.CompilerParams(collective_id=cid, has_side_effects=True, vmem_limit_bytes=mib * MIB)


def exchange_columns(here, src, dst, width, cols, span, send, recv, own_sem):
    copies = []
    own = []
    for i, c in enumerate(cols):
        for m in range(GROUP):
            peer = here.flip(m)
            at = src.at[:, :, pl.ds(pl.multiple_of(c + (peer % span) * width, 128), width)]
            to = dst.at[here.rep, :, here.lo, :, pl.ds(i * width, width)]
            if m == 0:
                cp = pltpu.make_async_copy(at, to, own_sem.at[i])
                cp.start()
                own.append(cp)
            else:
                cp = rcopy(at, to, send.at[i, m], recv.at[i, m], here.dev(m))
                cp.start()
                copies.append(cp)

    def arrive():
        for cp in own:
            cp.wait()
        for i, c in enumerate(cols):
            for m in ALL:
                to = dst.at[here.rep, :, here.flip(m), :, pl.ds(i * width, width)]
                rcopy(to, to, send.at[i, m], recv.at[i, m], here.dev(m)).wait_recv()

    def end():
        for cp in copies:
            cp.wait_send()

    return arrive, end


def rope_parts(rope):
    other = pltpu.roll(rope, HEAD_DIM // 2, 1)
    first = lax.broadcasted_iota(jnp.int32, rope.shape, 1) < HEAD_DIM // 2
    return jnp.where(first, rope, other), jnp.where(first, -other, rope)


def turned(x, cosine, sine):
    return x * cosine + pltpu.roll(x, HEAD_DIM // 2, 1) * sine


CODE = 4096


def head_of_bin(qkv, tables, b):
    rope, code_row, code_col = tables
    slots = qkv.shape[1] // rope.shape[0]
    rows = pl.ds(b * slots, slots)
    n = GROUP * slots

    def piece(i):
        return qkv[:, rows, i * HEAD_DIM : (i + 1) * HEAD_DIM].reshape(n, HEAD_DIM)

    cos, sin = rope_parts(rope[b])
    queries = turned(piece(0).astype(F32), cos, sin).astype(BF)
    keys = turned(piece(1).astype(F32), cos, sin).astype(BF)
    query_code, key_code = code_row[b], code_col[b]
    segment_code = query_code - jnp.bitwise_and(query_code, CODE - 1)
    seen = (key_code <= query_code) & (key_code >= segment_code)
    scores = jnp.where(seen, dot_t(queries, keys) * (1.0 / math.sqrt(HEAD_DIM)), -1e30)
    weights = jnp.exp(scores - jnp.max(scores, -1, keepdims=True))
    probability = weights / jnp.sum(weights, -1, keepdims=True)
    return queries, keys, piece(2), probability, rows, cos, sin


def attend(qkv, out, tables, b):
    _, _, values, probability, rows, _, _ = head_of_bin(qkv, tables, b)
    attended = dot(probability.astype(BF), values).astype(BF)
    out[:, rows] = attended.reshape(GROUP, rows.size, HEAD_DIM)


def front_kernel(
    mixm, n1, rope, code_row, code_col, sorter, g, wqkv, wout, wgu, wdn,
    raw, gs, n1g_out, dy2g, qkvs, outs, gus, dns, attn,
    n1g, wq, attended, plane, dy2,
    gsend, grecv, own, csend, crecv, cown, psend, precv, late, group_out, ssend, srecv, sown,
):
    here = Here()
    barrier(here, ALL, True)
    tables = (rope, code_row, code_col)
    tokens, width = n1.shape
    q = exchange_columns(here, wqkv, qkvs, 128, (0, 2048, 4096), GROUP, csend.at[0], crecv.at[0], cown.at[0])
    half = wgu.shape[2] // 2
    ga = Gather(here, n1, n1g, gsend.at[0], grecv.at[0])
    gb = Gather(here, dy2, dy2g, gsend.at[1], grecv.at[1])
    gc = Gather(here, wout, outs.at[here.rep], gsend.at[2], grecv.at[2])
    o = (0, 1, 3, 2)

    def hand_over(i, dst):
        cp = rcopy(dst.at[here.rep], dst.at[here.rep], psend.at[i], precv.at[i], here.partner())
        cp.start()
        return cp

    def other_core(i, dst):
        other = dst.at[1 - here.rep]
        rcopy(other, other, psend.at[i], precv.at[i], here.partner()).wait_recv()

    ga.begin(own.at[0])
    ga.spread(o[1])
    ga.forward(o[0])
    q[0]()
    q_pass = hand_over(0, qkvs)
    ga.spread(o[2])
    ga.forward(o[1])
    ga.spread(o[3])
    ga.forward(o[2])
    gc.begin(own.at[2])
    u = exchange_columns(here, wgu, gus, half // CUBE, (0, half), CUBE, csend.at[1], crecv.at[1], cown.at[1])
    d = exchange_columns(here, wdn, dns, half // CUBE, (0,), CUBE, csend.at[2], crecv.at[2], cown.at[2])
    ga.forward(o[3])
    sort_planes(sorter, g, gs, plane)
    p = read_mix(mixm)

    def to_branch(r):
        dy2[r] = mixed([p[j][5] for j in range(4)], [gs[j, r].astype(F32) for j in range(4)]).astype(BF)

    rowwise(tokens, 16, to_branch)
    other_core(0, qkvs)
    get = pltpu.make_async_copy(qkvs, wq, late)
    get.start()
    get.wait()
    copies = []
    for k, j in enumerate(o):
        ga.settle(j)
        blocks = pl.ds(here.flip(4 * j) - here.lo % 4, 4)
        x = n1g[blocks].reshape(4 * tokens, width)
        raw[blocks] = dot(x, wq[...].reshape(width, wq.shape[-1])).astype(BF).reshape(4, tokens, wq.shape[-1])
        c = pltpu.make_async_copy(n1g.at[blocks], n1g_out.at[blocks], group_out.at[k])
        c.start()
        copies.append(c)
    bins = rope.shape[0]
    for b in range(bins):
        attend(raw, attended, tables, b)
        if b < 3:
            gc.spread(o[b + 1])
            gc.forward(o[b])
    swaps = []
    at = pl.ds(pl.multiple_of(here.lo * HEAD_DIM, HEAD_DIM), HEAD_DIM)
    for m in ALL:
        c = rcopy(attended.at[here.flip(m)], attn.at[:, at], ssend.at[m], srecv.at[m], here.dev(m))
        c.start()
        swaps.append(c)
    mine = pltpu.make_async_copy(attended.at[here.lo], attn.at[:, at], sown)
    mine.start()
    gb.begin(own.at[1])
    gc.forward(o[3])
    gb.spread(1)
    gb.forward(0)
    for j in o:
        gc.settle(j)
    out_pass = hand_over(3, outs)
    gb.forward(1)
    u[0]()
    u_pass = hand_over(1, gus)
    d[0]()
    d_pass = hand_over(2, dns)
    gb.settle(0)
    gb.settle(1)
    mine.wait()
    for m in ALL:
        ref = attn.at[:, pl.ds(pl.multiple_of(here.flip(m) * HEAD_DIM, HEAD_DIM), HEAD_DIM)]
        rcopy(ref, ref, ssend.at[m], srecv.at[m], here.dev(m)).wait_recv()
    for i, dst in ((1, gus), (2, dns), (3, outs)):
        other_core(i, dst)
    for c in (q_pass, u_pass, d_pass, out_pass, *swaps):
        c.wait_send()
    for c in copies:
        c.wait()
    for g in (ga, gb, gc):
        g.end()
    for _, end in (q, u, d):
        end()


def front(mixm, n1, tables, sorter, g, wqkv, wout, wgu, wdn, cid):
    hi, rows, _ = wqkv.shape
    ff = wdn.shape[2]
    tokens = n1.shape[0]
    shape = lambda *s: jax.ShapeDtypeStruct(s, BF)
    out_rows = wout.shape[0]
    head = 3 * HEAD_DIM
    return pl.pallas_call(
        front_kernel,
        out_shape=(
            shape(GROUP, tokens, head),
            shape(g.shape[1], tokens, g.shape[2]),
            shape(GROUP, *n1.shape),
            shape(CUBE, *n1.shape),
            shape(2, hi, GROUP, rows, head),
            shape(2, GROUP, out_rows, wout.shape[1]),
            shape(2, hi, GROUP, rows, 2 * ff // CUBE),
            shape(2, hi, GROUP, rows, ff // CUBE),
            shape(tokens, GROUP * HEAD_DIM),
        ),
        in_specs=[*smem_spec(1), *vmem_spec(6), *any_spec(4)],
        out_specs=(*vmem_spec(2), *any_spec(7)),
        scratch_shapes=[
            pltpu.VMEM((GROUP, *n1.shape), BF),
            pltpu.VMEM((2, hi, GROUP, rows, head), BF),
            pltpu.VMEM((GROUP, tokens, HEAD_DIM), BF),
            pltpu.VMEM((g.shape[1], tokens, g.shape[2]), BF),
            pltpu.VMEM(n1.shape, BF),
            pltpu.SemaphoreType.DMA((3,) + Gather.sems),
            pltpu.SemaphoreType.DMA((3,) + Gather.sems),
            pltpu.SemaphoreType.DMA((3,)),
            pltpu.SemaphoreType.DMA((3, 3, GROUP)),
            pltpu.SemaphoreType.DMA((3, 3, GROUP)),
            pltpu.SemaphoreType.DMA((3, 3)),
            pltpu.SemaphoreType.DMA((4,)),
            pltpu.SemaphoreType.DMA((4,)),
            pltpu.SemaphoreType.DMA,
            pltpu.SemaphoreType.DMA((4,)),
            pltpu.SemaphoreType.DMA((GROUP,)),
            pltpu.SemaphoreType.DMA((GROUP,)),
            pltpu.SemaphoreType.DMA,
        ],
        compiler_params=params(cid, 62),
    )(mixm, n1, *tables, sorter, g, wqkv, wout, wgu, wdn)


def pair_add(here, g, inbox, send, recv):
    cp = rcopy(g.at[1 - here.rep], inbox, send, recv, here.partner())
    cp.start()
    cp.wait()

    def body(r):
        g[here.rep, r] = (g[here.rep, r].astype(F32) + inbox[r].astype(F32)).astype(BF)

    rowwise(inbox.shape[0], 16, body)


def send_home(here, total, out, send, recv, own):
    _, hi, rows, _ = out.shape

    def block(h, m):
        at = (h * GROUP + here.flip(m)) * rows
        return total.at[pl.ds(pl.multiple_of(at, rows), rows)]

    cps = []
    owns = []
    for h in range(hi):
        for m in ALL:
            c = rcopy(block(h, m), out.at[here.lo, h], send.at[h, m], recv.at[h, m], here.dev(m))
            c.start()
            cps.append(c)
        c = pltpu.make_async_copy(block(h, 0), out.at[here.lo, h], own.at[h])
        c.start()
        owns.append(c)

    def end():
        for c in owns:
            c.wait()
        for h in range(hi):
            for m in ALL:
                ref = out.at[here.flip(m), h]
                rcopy(ref, ref, send.at[h, m], recv.at[h, m], here.dev(m)).wait_recv()
        for c in cps:
            c.wait_send()

    return end


def home_sems(hi):
    return [
        pltpu.SemaphoreType.DMA((hi, GROUP)),
        pltpu.SemaphoreType.DMA((hi, GROUP)),
        pltpu.SemaphoreType.DMA((hi,)),
    ]


def mlp_kernel(
    mixa, mixm, n2, dy2g_in, wgu_in, wdn_in, hs, gs, wout, y1, y2p, grads_out, dx2, dy1, d_out, sums,
    n2g, dy2g, wgu, wdn, part, hidden, dgu, y2s, grads, inbox, dn2,
    gsend, grecv, own, load, y2sem, psend, precv, late, *scratch,
):
    here = Here()
    barrier(here, (1, 2, 4), True)
    g = Gather(here, n2, n2g, gsend, grecv)
    rs = Scatter(here, part, scratch)
    g.begin(own)
    loads = []
    for i, (src, dst) in enumerate(((wgu_in, wgu), (wdn_in, wdn), (dy2g_in, dy2g))):
        c = pltpu.make_async_copy(src, dst, load.at[i])
        c.start()
        loads.append(c)
    width, ff = wdn.shape
    tokens = n2.shape[0]
    group_rows = 4 * tokens
    step = 256
    wide = 512
    y2copies = []

    def compute(j):
        first = here.flip(4 * j) - here.lo % 4 - g.off
        blocks = pl.ds(first, 4)
        if not y2copies:
            for c in loads:
                c.wait()

        def gates(k, carry):
            up_at = pl.ds(pl.multiple_of(k * step, step), step)
            gate_at = pl.ds(pl.multiple_of(ff + k * step, step), step)
            x = n2g[blocks].reshape(group_rows, width)
            up = dot(x, wgu[:, up_at])
            gate = dot(x, wgu[:, gate_at])
            dh = dot(dy2g[blocks].reshape(group_rows, width), wdn[:, up_at])
            small = jnp.exp(-jnp.abs(gate))
            sigmoid = jnp.where(gate >= 0.0, 1.0, small) / (1.0 + small)
            silu = gate * sigmoid
            hidden[blocks, :, up_at] = (silu * up).astype(BF).reshape(4, tokens, step)
            dgu[blocks, :, up_at] = (dh * silu).astype(BF).reshape(4, tokens, step)
            dgu[blocks, :, gate_at] = (
                (dh * up * sigmoid * (1.0 + gate * (1.0 - sigmoid))).astype(BF).reshape(4, tokens, step)
            )
            return carry

        lax.fori_loop(0, ff // step, gates, 0)
        if y2copies:
            y2copies[-1].wait()

        def outputs(k, carry):
            at = pl.ds(pl.multiple_of(k * wide, wide), wide)
            h = hidden[blocks].reshape(group_rows, ff)
            y2s[:, :, at] = dot_t(h, wdn[at, :]).astype(BF).reshape(4, tokens, wide)
            d = dgu[blocks].reshape(group_rows, 2 * ff)
            part[blocks, :, at] = dot_t(d, wgu[at, :]).astype(BF).reshape(4, tokens, wide)
            return carry

        lax.fori_loop(0, width // wide, outputs, 0)
        c = pltpu.make_async_copy(y2s, y2p.at[blocks], y2sem.at[len(y2copies)])
        c.start()
        y2copies.append(c)

    half = width // 2
    chunks = half // step

    def weight_grads(which, k):
        cols = pl.ds(pl.multiple_of(which * half + k * step, step), step)
        rows = pl.ds(pl.multiple_of(k * step, step), step)
        x = n2g[:, :, cols].reshape(CUBE * tokens, step)
        grads[which, rows, : 2 * ff] = t_dot(x, dgu[...].reshape(CUBE * tokens, 2 * ff)).astype(BF)
        x = dy2g[:, :, cols].reshape(CUBE * tokens, step)
        grads[which, rows, 2 * ff :] = t_dot(x, hidden[...].reshape(CUBE * tokens, ff)).astype(BF)

    def pass_chunk(k):
        rows = pl.ds(pl.multiple_of(k * step, step), step)
        return rcopy(grads.at[1 - here.rep, rows], inbox.at[rows], psend.at[k], precv.at[k], here.partner())

    g.spread(1)
    g.forward(0)
    g.settle(0)
    compute(0)
    rs.start(0)
    g.forward(1)
    rs.cross(0)
    g.settle(1)
    compute(1)
    rs.start(1)

    def other_half(k, carry):
        weight_grads(1 - here.rep, k)
        pass_chunk(k).start()
        return carry

    lax.fori_loop(0, chunks, other_half, 0)
    rs.cross(1)
    rs.finish(1)

    def own_half(k, carry):
        weight_grads(here.rep, k)
        return carry

    lax.fori_loop(0, chunks, own_half, 0)
    g.end()
    streams = hs.shape[0]
    loads = []
    for i, (src, dst) in enumerate(((hs, n2g.at[:streams]), (gs, n2g.at[streams : 2 * streams]), (wout, wgu))):
        c = pltpu.make_async_copy(src, dst, late.at[i])
        c.start()
        loads.append(c)

    def add(k, carry):
        pass_chunk(k).wait()

        def rows_add(i, carry):
            r = pl.ds(pl.multiple_of(k * step + i * 16, 16), 16)
            grads[here.rep, r] = (grads[here.rep, r].astype(F32) + inbox[r].astype(F32)).astype(BF)
            return carry

        return lax.fori_loop(0, step // 16, rows_add, carry)

    lax.fori_loop(0, chunks, add, 0)
    out = pltpu.make_async_copy(grads.at[here.rep], grads_out, late.at[3])
    out.start()
    rs.finish(0, dn2)
    for c in loads:
        c.wait()
    turn(read_mix(mixa), read_mix(mixm), n2g, y1, dn2, wgu, dx2, dy1, d_out, sums)
    out.wait()
    y2copies[-1].wait()
    rs.end()


def mlp(mixa, mixm, n2, dy2g, wgu, wdn, hs, gs, wout, y1, cid):
    tokens, width = n2.shape
    ff = wdn.shape[1]
    half = width // 2
    blocks = (CUBE, tokens)
    return pl.pallas_call(
        mlp_kernel,
        out_shape=(
            jax.ShapeDtypeStruct((*blocks, width), BF),
            jax.ShapeDtypeStruct((half, 3 * ff), BF),
            jax.ShapeDtypeStruct((tokens, width), F32),
            jax.ShapeDtypeStruct((tokens, width), BF),
            jax.ShapeDtypeStruct((tokens, width), BF),
            jax.ShapeDtypeStruct((24, 16, 128), F32),
        ),
        in_specs=[*smem_spec(2), *vmem_spec(1), *any_spec(6), *vmem_spec(1)],
        out_specs=(*any_spec(2), *vmem_spec(4)),
        scratch_shapes=[
            pltpu.VMEM((*blocks, width), BF),
            pltpu.VMEM((*blocks, width), BF),
            pltpu.VMEM(wgu.shape, BF),
            pltpu.VMEM(wdn.shape, BF),
            pltpu.VMEM((*blocks, width), BF),
            pltpu.VMEM((*blocks, ff), BF),
            pltpu.VMEM((*blocks, 2 * ff), BF),
            pltpu.VMEM((4, tokens, width), BF),
            pltpu.VMEM((2, half, 3 * ff), BF),
            pltpu.VMEM((half, 3 * ff), BF),
            pltpu.VMEM((tokens, width), F32),
            pltpu.SemaphoreType.DMA(Gather.sems),
            pltpu.SemaphoreType.DMA(Gather.sems),
            pltpu.SemaphoreType.DMA,
            pltpu.SemaphoreType.DMA((3,)),
            pltpu.SemaphoreType.DMA((4,)),
            pltpu.SemaphoreType.DMA((half // 256,)),
            pltpu.SemaphoreType.DMA((half // 256,)),
            pltpu.SemaphoreType.DMA((4,)),
            *Scatter.scratch(tokens, width, CUBE),
        ],
        compiler_params=params(cid, 63),
        cost_estimate=pl.CostEstimate(
            flops=2 * CUBE * tokens * width * ff * 9, bytes_accessed=60 * MIB, transcendentals=0
        ),
    )(mixa, mixm, n2, dy2g, wgu, wdn, hs, gs, wout, y1)


def attend_back(qkv, d_out, dqkv, tables, b):
    queries, keys, values, probability, rows, cos, sin = head_of_bin(qkv, tables, b)
    n, slots = queries.shape[0], rows.size
    scale = 1.0 / math.sqrt(HEAD_DIM)
    grad = d_out[:, rows].reshape(n, HEAD_DIM)
    grad_values = t_dot(probability.astype(BF), grad)
    grad_probs = dot_t(grad, values)
    shared = jnp.sum(grad_probs * probability, -1, keepdims=True)
    grad_scores = (probability * (grad_probs - shared)).astype(BF)
    grad_query = dot(grad_scores, keys) * scale
    grad_keys = t_dot(grad_scores, queries) * scale
    for i, v in enumerate((turned(grad_query, cos, -sin), turned(grad_keys, cos, -sin), grad_values)):
        dqkv[:, rows, i * HEAD_DIM : (i + 1) * HEAD_DIM] = v.astype(BF).reshape(GROUP, slots, HEAD_DIM)


class GradsHome:
    @staticmethod
    def scratch(hi, rows, w):
        return [
            pltpu.VMEM((hi, CUBE, rows, w), BF),
            pltpu.VMEM((hi, CUBE, rows, w), BF),
            *[pltpu.SemaphoreType.DMA((hi, CUBE))] * 6,
        ]

    def __init__(self, here, gmlp, out, scratch):
        self.here, self.out = here, out
        self.mine, self.box, self.zsend, self.zrecv, self.load, self.send, self.recv, self.own = scratch
        self.hi, _, self.rows, _ = self.mine.shape
        self.sent = []
        self.loads = {}
        self.gmlp = gmlp

    def begin(self, wave):
        here = self.here
        for h in range(self.hi):
            for m in wave:

                def block(mask, h=h):
                    at = (h * GROUP + here.flip(mask)) * self.rows
                    return self.gmlp.at[pl.ds(pl.multiple_of(at, self.rows), self.rows)]

                c = rcopy(block(m ^ 8), self.box.at[h, m], self.zsend.at[h, m], self.zrecv.at[h, m], here.dev(8))
                c.start()
                self.sent.append(c)
                c = pltpu.make_async_copy(block(m), self.mine.at[h, m], self.load.at[h, m])
                c.start()
                self.loads[h, m] = c

    def relay(self, m):
        here = self.here
        for h in range(self.hi):
            box, mine = self.box.at[h, m], self.mine.at[h, m]
            self.loads[h, m].wait()
            rcopy(box, box, self.zsend.at[h, m], self.zrecv.at[h, m], here.dev(8)).wait_recv()

            def body(r, box=box, mine=mine):
                mine[r] = (mine[r].astype(F32) + box[r].astype(F32)).astype(BF)

            rowwise(self.rows, 16, body)
            to = self.out.at[here.lo % CUBE, h]
            if m:
                c = rcopy(mine, to, self.send.at[h, m], self.recv.at[h, m], here.dev(m))
                self.sent.append(c)
            else:
                c = pltpu.make_async_copy(mine, to, self.own.at[h, 0])
                self.loads[h, 0] = c
            c.start()

    def end(self):
        here = self.here
        for h in range(self.hi):
            self.loads[h, 0].wait()
            for m in range(1, CUBE):
                ref = self.out.at[here.flip(m) % CUBE, h]
                rcopy(ref, ref, self.send.at[h, m], self.recv.at[h, m], here.dev(m)).wait_recv()
        for c in self.sent:
            c.wait_send()


def back_kernel(
    d_rows, qkv, qkvs, dy1, attn, rope, code_row, code_col, n1g, y2_in, gmlp,
    dn_out, y2_out, gout_out, gqkv_out, gmlp_out,
    d_out, dqkv, dn, y2, gout, stage, gqkv, tiles, obox, qbox,
    dsend, drecv, down, load, tile_sem, osend, orecv, qsend, qrecv, *scratch,
):
    here = Here()
    barrier(here, ALL, True)
    tables = (rope, code_row, code_col)
    bins = rope.shape[0]
    swaps = []
    for m in ALL:
        at = pl.ds(pl.multiple_of(here.flip(m) * HEAD_DIM, HEAD_DIM), HEAD_DIM)
        c = rcopy(d_rows.at[:, at], d_out.at[here.lo], dsend.at[m], drecv.at[m], here.dev(m))
        c.start()
        swaps.append(c)
    at = pl.ds(pl.multiple_of(here.lo * HEAD_DIM, HEAD_DIM), HEAD_DIM)
    mine = pltpu.make_async_copy(d_rows.at[:, at], d_out.at[here.lo], down)
    mine.start()
    y2_load = pltpu.make_async_copy(y2_in, y2, load)
    y2_load.start()
    _, tokens, width = dn.shape
    k = len(Scatter.scratch(16, 128))
    rs_dn = Scatter(here, dn, scratch[:k])
    rs_y2 = Scatter(here, y2, scratch[k : 2 * k])
    rs_go = Scatter(here, gout.reshape(GROUP, gout.shape[0] // GROUP, width), scratch[2 * k : 3 * k])
    qhome = scratch[3 * k : 3 * k + 3]
    gm = GradsHome(here, gmlp, gmlp_out, scratch[3 * k + 3 :])
    gm.begin((0, 1))
    order = (3, 2, 1, 0)
    y2_load.wait()
    rs_y2.start(1)
    rs_y2.start(0)
    gm.begin((2, 3))
    mine.wait()
    for m in ALL:
        ref = d_out.at[here.flip(m)]
        rcopy(ref, ref, dsend.at[m], drecv.at[m], here.dev(m)).wait_recv()

    half = width // 2
    step = 256
    chunks = half // step

    def out_grads(which, k):
        cols = pl.ds(pl.multiple_of(which * half + k * step, step), step)
        return t_dot(attn[:, cols], dy1[...]).astype(BF)

    def gout_pass(k):
        at = pl.ds(k * step, step)
        return rcopy(stage.at[k % 2], obox.at[at], osend.at[k], orecv.at[k], here.partner())

    gqkv_pair = rcopy(gqkv.at[1 - here.rep], qbox, qsend, qrecv, here.partner())

    for b in range(bins):
        attend_back(qkv, d_out, dqkv, tables, b)
        if b == 1:
            rs_y2.cross(1)
        elif b == 2:
            rs_y2.cross(0)
            rs_y2.finish(1)

    narrow = tiles.shape[3]

    def qkv_tile(k):
        cols = pl.ds(k * narrow, narrow)
        return pltpu.make_async_copy(n1g.at[:, :, cols], tiles.at[k % 2], tile_sem.at[k % 2])

    qkv_tile(0).start()
    for j in order:
        blocks = pl.ds(here.lo + here.away[j] - here.lo % 4, 4)

        def part(k, carry, blocks=blocks):
            at = pl.ds(pl.multiple_of(k * TILE, TILE), TILE)
            d = dqkv[blocks].reshape(4 * tokens, 3 * HEAD_DIM)
            dn[blocks, :, at] = dot_t(d, qkvs[at, :]).astype(BF).reshape(4, tokens, TILE)
            return carry

        lax.fori_loop(0, width // TILE, part, 0)
        rs_dn.start(j)
    count = width // narrow
    for k in range(count):
        if k + 1 < count:
            qkv_tile(k + 1).start()
        qkv_tile(k).wait()
        x = tiles[k % 2].reshape(GROUP * tokens, narrow)
        rows = pl.ds((k % (count // 2)) * narrow, narrow)
        gqkv[k // (count // 2), rows, :] = t_dot(x, dqkv[...].reshape(GROUP * tokens, 3 * HEAD_DIM)).astype(BF)
    gqkv_pair.start()
    gm.relay(0)
    gm.relay(1)
    gm.begin((4, 5))
    rs_y2.finish(0, y2_out)
    rs_dn.cross(order[0])
    for k in range(chunks):
        if k >= 2:
            gout_pass(k - 2).wait_send()
        stage[k % 2] = out_grads(1 - here.rep, k)
        gout_pass(k).start()
    rs_dn.cross(order[1])
    rs_dn.finish(order[0])
    for k in range(chunks):
        gout[k * step : (k + 1) * step, :] = out_grads(here.rep, k)

    def add(ref, box):
        def body(r):
            ref[r] = (ref[r].astype(F32) + box[r].astype(F32)).astype(BF)

        rowwise(box.shape[0], 16, body)

    gqkv_pair.wait()
    add(gqkv.at[here.rep], qbox)
    gm.relay(2)
    gm.begin((6,))
    end_qkv = send_home(here, gqkv.at[here.rep], gqkv_out, *qhome)
    rs_dn.cross(order[2])
    rs_dn.finish(order[1])
    gm.relay(3)
    gm.begin((7,))
    for k in range(chunks):
        gout_pass(k).wait_recv()
        if k >= chunks - 2:
            gout_pass(k).wait_send()
    add(gout, obox)
    for j in order:
        rs_go.start(j)
    rs_dn.cross(order[3])
    rs_dn.finish(order[2])
    rs_go.cross(order[0])
    gm.relay(4)
    rs_go.cross(order[1])
    rs_go.finish(order[0])
    gm.relay(5)
    gm.relay(6)
    gm.relay(7)
    rs_go.cross(order[2])
    rs_go.finish(order[1])
    rs_go.cross(order[3])
    rs_go.finish(order[2])
    rs_dn.finish(0, dn_out)
    rs_go.finish(0, gout_out)
    gm.end()
    end_qkv()
    for c in swaps:
        c.wait_send()
    for rs in (rs_dn, rs_y2, rs_go):
        rs.end()


def back(d_rows, qkv, qkvs, dy1, attn, tables, n1g, y2, gmlp, hi, cid):
    tokens, width = d_rows.shape
    half = width // 2
    w = qkv.shape[2]
    return pl.pallas_call(
        back_kernel,
        out_shape=(
            jax.ShapeDtypeStruct((tokens, width), F32),
            jax.ShapeDtypeStruct((tokens, width), F32),
            jax.ShapeDtypeStruct((half // GROUP, width), F32),
            jax.ShapeDtypeStruct((GROUP, hi, half // (hi * GROUP), w), BF),
            jax.ShapeDtypeStruct((CUBE, hi, half // (hi * GROUP), gmlp.shape[1]), BF),
        ),
        in_specs=[*vmem_spec(8), *any_spec(3)],
        out_specs=(*vmem_spec(3), *any_spec(2)),
        scratch_shapes=[
            pltpu.VMEM((GROUP, tokens, HEAD_DIM), BF),
            pltpu.VMEM((GROUP, tokens, w), BF),
            pltpu.VMEM((GROUP, tokens, width), BF),
            pltpu.VMEM((CUBE, tokens, width), BF),
            pltpu.VMEM((half, width), BF),
            pltpu.VMEM((2, 256, width), BF),
            pltpu.VMEM((2, half, w), BF),
            pltpu.VMEM((2, GROUP, tokens, TILE // 4), BF),
            pltpu.VMEM((half, width), BF),
            pltpu.VMEM((half, w), BF),
            pltpu.SemaphoreType.DMA((GROUP,)),
            pltpu.SemaphoreType.DMA((GROUP,)),
            pltpu.SemaphoreType.DMA,
            pltpu.SemaphoreType.DMA,
            pltpu.SemaphoreType.DMA((2,)),
            pltpu.SemaphoreType.DMA((half // 256,)),
            pltpu.SemaphoreType.DMA((half // 256,)),
            pltpu.SemaphoreType.DMA,
            pltpu.SemaphoreType.DMA,
            *Scatter.scratch(tokens, width),
            *Scatter.scratch(tokens, width, CUBE),
            *Scatter.scratch(half // GROUP, width),
            *home_sems(hi),
            *GradsHome.scratch(hi, half // (hi * GROUP), gmlp.shape[1]),
        ],
        compiler_params=params(cid, 63),
    )(d_rows, qkv, qkvs, dy1, attn, *tables, n1g, y2, gmlp)


def read_mix(ref):
    return [[ref[i, k] for k in range(6)] for i in range(4)]


def mixed(weights, planes):
    total = weights[0] * planes[0]
    for w, p in zip(weights[1:], planes[1:]):
        total = total + w * p
    return total


def moments(x):
    centred = x - jnp.mean(x, -1, keepdims=True)
    inverse = lax.rsqrt(jnp.mean(centred * centred, -1, keepdims=True) + EPSILON)
    return centred * inverse, inverse


def normalize_back(grad_out, normed, inverse):
    return inverse * (
        grad_out
        - jnp.mean(grad_out, -1, keepdims=True)
        - normed * jnp.mean(grad_out * normed, -1, keepdims=True)
    )


def lane_sums(x):
    total = x[:, :128]
    for c in range(128, x.shape[1], 128):
        total = total + x[:, c : c + 128]
    return total


def read_x2(m, p, h, y1):
    fold = [sum(p[s][0] * m[j][1 + s] for s in range(4)) for j in range(4)]
    return mixed(fold + [sum(p[s][0] * m[s][5] for s in range(4))], [*h, y1])


TILE = 512


def sort_planes(sorter, x, planes, plane):
    tokens, streams, width = x.shape

    def split(r):
        v = x[r].astype(F32)
        for i in range(streams):
            plane[i, r] = v[:, i, :].astype(BF)

    rowwise(tokens, 16, split)
    for i in range(streams):
        for c in range(0, width, TILE):
            at = slice(c, c + TILE)
            planes[i, :, at] = dot(sorter[...], plane[i, :, at]).astype(BF)


def open_kernel(mixa, sorter, x, hs, n1, plane):
    m = read_mix(mixa)
    sort_planes(sorter, x, hs, plane)

    def norm(r):
        x1 = mixed([m[j][0] for j in range(4)], [hs[j, r].astype(F32) for j in range(4)])
        n1[r] = moments(x1)[0].astype(BF)

    rowwise(x.shape[0], 16, norm)


def smem_spec(n):
    return [pl.BlockSpec(memory_space=pltpu.SMEM)] * n


def local_params(mib=60):
    return pltpu.CompilerParams(vmem_limit_bytes=mib * MIB)


def open_streams(mixa, sorter, x):
    tokens, streams, width = x.shape
    return pl.pallas_call(
        open_kernel,
        out_shape=(
            jax.ShapeDtypeStruct((streams, tokens, width), BF),
            jax.ShapeDtypeStruct((tokens, width), BF),
        ),
        in_specs=[*smem_spec(1), *vmem_spec(2)],
        out_specs=tuple(vmem_spec(2)),
        scratch_shapes=[pltpu.VMEM((streams, tokens, width), BF)],
        compiler_params=local_params(),
    )(mixa, sorter, x)


def middle_kernel(mixa, mixm, hs, attn, wout_in, y1, n2, wout, load):
    m, p = read_mix(mixa), read_mix(mixm)
    tokens, width = attn.shape

    copies = []
    for i in range(width // TILE):
        at = slice(i * TILE, (i + 1) * TILE)
        c = pltpu.make_async_copy(wout_in.at[:, at], wout.at[i], load.at[i])
        c.start()
        copies.append(c)
    for i, c in enumerate(copies):
        c.wait()
        y1[:, i * TILE : (i + 1) * TILE] = dot(attn[...], wout[i])

    def norm(r):
        x2 = read_x2(m, p, [hs[j, r].astype(F32) for j in range(4)], y1[r])
        n2[r] = moments(x2)[0].astype(BF)

    rowwise(tokens, 16, norm)


def middle(mixa, mixm, hs, attn, wout):
    tokens, width = attn.shape
    return pl.pallas_call(
        middle_kernel,
        out_shape=(
            jax.ShapeDtypeStruct((tokens, width), F32),
            jax.ShapeDtypeStruct((tokens, width), BF),
        ),
        in_specs=[*smem_spec(2), *vmem_spec(2), *any_spec(1)],
        out_specs=tuple(vmem_spec(2)),
        scratch_shapes=[
            pltpu.VMEM((width // TILE, width, TILE), BF),
            pltpu.SemaphoreType.DMA((width // TILE,)),
        ],
        compiler_params=local_params(),
    )(mixa, mixm, hs, attn, wout)


def unsort(sorter, planes, out):
    streams, tokens, width = planes.shape
    for i in range(streams):

        def tile(k, carry, i=i):
            at = pl.ds(pl.multiple_of(k * TILE, TILE), TILE)
            v = planes[i, :, at]
            high = v.astype(BF)
            low = (v - high.astype(F32)).astype(BF)
            out[:, i, at] = t_dot(sorter[...], high) + t_dot(sorter[...], low)
            return carry

        lax.fori_loop(0, width // TILE, tile, 0)


def turn(m, p, planes, y1, dn2, wout, dx2, dy1, d_out, sums):
    tokens, width = y1.shape
    sums[...] = jnp.zeros_like(sums)

    def body(r):
        x2 = read_x2(m, p, [planes[j, r].astype(F32) for j in range(4)], y1[r])
        normed, inverse = moments(x2)
        dx2[r] = normalize_back(dn2[r], normed, inverse)
        for c in range(0, width, TILE):
            at = slice(c, c + TILE)
            h = [planes[j, r, at].astype(F32) for j in range(4)]
            y = y1[r, at]
            h1 = [mixed([*(m[j][1 + i] for j in range(4)), m[i][5]], [*h, y]) for i in range(4)]
            g = [planes[4 + j, r, at].astype(F32) for j in range(4)]
            dx = dx2[r, at]
            g1 = [mixed([*(p[j][1 + i] for i in range(4)), p[j][0]], [*g, dx]) for j in range(4)]
            dy1[r, at] = mixed([m[j][5] for j in range(4)], g1).astype(BF)
            for j in range(4):
                sums[j * 6] += lane_sums(h1[j] * dx)
                for i in range(4):
                    sums[j * 6 + 1 + i] += lane_sums(h1[j] * g[i])

    rowwise(tokens, 16, body)
    def tile(i, carry):
        at = pl.ds(pl.multiple_of(i * TILE, TILE), TILE)
        d_out[:, at] = dot_t(dy1[...], wout[at, :]).astype(BF)
        return carry

    lax.fori_loop(0, width // TILE, tile, 0)


def close_kernel(
    mixa, mixm, sorter, hs, gs, dx2, y1, y2, dn1, other, new, d_streams, mix_a, mix_m,
    sums, planes, fresh, mine, inbox, send, recv,
):
    here = Here()
    barrier(here, ALL, True)
    m, p = read_mix(mixa), read_mix(mixm)
    tokens, width = y1.shape
    sums[:24] = jnp.zeros((24, *sums.shape[1:]), F32)
    sums[24:] = other[...]

    def body(r):
        x1 = mixed([m[j][0] for j in range(4)], [hs[j, r].astype(F32) for j in range(4)])
        normed, inverse = moments(x1)
        planes[0, r] = normalize_back(dn1[r], normed, inverse)
        for c in range(0, width, TILE):
            at = slice(c, c + TILE)
            h = [hs[j, r, at].astype(F32) for j in range(4)]
            g = [gs[j, r, at].astype(F32) for j in range(4)]
            y = y1[r, at]
            dx = planes[0, r, at]
            dm = dx2[r, at]
            g1 = [mixed([*(p[j][1 + i] for i in range(4)), p[j][0]], [*g, dm]) for j in range(4)]
            for j in range(4):
                planes[j, r, at] = mixed([*(m[j][1 + i] for i in range(4)), m[j][0]], [*g1, dx])
                sums[j * 6] += lane_sums(h[j] * dx)
                for i in range(4):
                    sums[j * 6 + 1 + i] += lane_sums(h[j] * g1[i])
                sums[j * 6 + 5] += lane_sums(y * g1[j])
            h1 = [mixed([*(m[j][1 + i] for j in range(4)), m[i][5]], [*h, y]) for i in range(4)]
            y = y2[r, at]
            for i in range(4):
                fresh[i, r, at] = mixed([*(p[j][1 + i] for j in range(4)), p[i][5]], [*h1, y])
                sums[24 + i * 6 + 5] += lane_sums(y * g[i])

    rowwise(tokens, 16, body)
    mine[0] = jnp.sum(sums[...], axis=1)
    pair = rcopy(mine.at[0], inbox.at[0], send.at[0], recv.at[0], here.partner())
    pair.start()
    pair.wait()
    mine[1] = mine[0] + inbox[0]
    cps = []
    for k in ALL:
        c = rcopy(mine.at[1], inbox.at[k], send.at[k], recv.at[k], here.dev(k))
        c.start()
        cps.append(c)
    unsort(sorter, fresh, new)
    unsort(sorter, planes, d_streams)
    everyone = mine[1]
    for c in cps:
        c.wait()
    for k in ALL:
        everyone = everyone + inbox[k]
    everyone = jnp.sum(everyone, axis=1, keepdims=True)
    for n, out in enumerate((mix_a, mix_m)):
        row = lax.broadcasted_iota(jnp.int32, out.shape, 0)
        col = lax.broadcasted_iota(jnp.int32, out.shape, 1)
        value = jnp.zeros(out.shape, F32)
        for j in range(4):
            for c in range(6):
                k = n * 24 + j * 6 + c
                value = jnp.where((row == j) & (col == c), everyone[k : k + 1], value)
        out[...] = value


def close(mixa, mixm, sorter, hs, gs, dx2, y1, y2, dn1, other, cid):
    streams, tokens, width = hs.shape
    return pl.pallas_call(
        close_kernel,
        out_shape=(
            jax.ShapeDtypeStruct((tokens, streams, width), F32),
            jax.ShapeDtypeStruct((tokens, streams, width), F32),
            jax.ShapeDtypeStruct(mixa.shape, F32),
            jax.ShapeDtypeStruct(mixm.shape, F32),
        ),
        in_specs=[*smem_spec(2), *vmem_spec(8)],
        out_specs=tuple(vmem_spec(4)),
        scratch_shapes=[
            pltpu.VMEM((48, 16, 128), F32),
            pltpu.VMEM((streams, tokens, width), F32),
            pltpu.VMEM((streams, tokens, width), F32),
            pltpu.VMEM((2, 48, 128), F32),
            pltpu.VMEM((GROUP, 48, 128), F32),
            pltpu.SemaphoreType.DMA((GROUP,)),
            pltpu.SemaphoreType.DMA((GROUP,)),
        ],
        compiler_params=params(cid),
    )(mixa, mixm, sorter, hs, gs, dx2, y1, y2, dn1, other)


def lay_out_kernel(qkv, out, mlp, gqkv, gout, ggu, gdown):
    head = HEAD_DIM
    for l in range(qkv.shape[0]):
        for i in range(3):
            at = i * GROUP * head + l * head
            gqkv[:, :, at : at + head] = qkv[l, :, :, i * head : (i + 1) * head].astype(F32)
    block = mlp.shape[3] // 3
    for l in range(CUBE):
        for i in range(2):
            at = (i * CUBE + l) * block
            ggu[:, :, at : at + block] = mlp[l, :, :, i * block : (i + 1) * block].astype(F32)
        gdown[:, :, l * block : (l + 1) * block] = mlp[l, :, :, 2 * block :].astype(F32)
    gout[...] = out[...]


def lay_out(qkv, out, mlp):
    _, hi, rows, w = mlp.shape
    ff = w // 3 * CUBE
    shapes = [(hi, rows, GROUP * qkv.shape[3]), out.shape, (hi, rows, 2 * ff), (hi, rows, ff)]
    return pl.pallas_call(
        lay_out_kernel,
        out_shape=tuple(jax.ShapeDtypeStruct(s, F32) for s in shapes),
        in_specs=vmem_spec(3),
        out_specs=tuple(vmem_spec(4)),
        compiler_params=local_params(),
    )(qkv, out, mlp)


def slot_layout(lengths_row, capacity):
    seq_count = lengths_row.shape[-1]
    seq_ends = jnp.cumsum(lengths_row, axis=-1)
    slot_index = jnp.arange(capacity, dtype=jnp.int32)
    segment = jnp.sum((slot_index[:, None] >= seq_ends[..., None, :]).astype(jnp.int32), axis=-1)
    seq_starts = seq_ends - lengths_row
    chosen = (segment[..., None] == jnp.arange(seq_count, dtype=jnp.int32)).astype(jnp.int32)
    start_of = jnp.sum(chosen * seq_starts[..., None, :], axis=-1)
    is_live = segment < seq_count
    segment = jnp.where(is_live, segment, seq_count + slot_index)
    position = jnp.where(is_live, slot_index - start_of, 0)
    return (segment, position)


def rope_tables(position, head_width):
    half_width = head_width // 2
    frequency = jnp.exp(
        jnp.arange(half_width, dtype=jnp.float32) * (-2.0 * math.log(10000.0) / head_width)
    )
    angles = position.astype(jnp.float32)[..., None] * frequency
    return (jnp.cos(angles), jnp.sin(angles))


def dot(a, b):
    return jnp.dot(a, b, preferred_element_type=F32)


def dot_t(a, b):
    return lax.dot_general(a, b, CONTRACT_LAST, preferred_element_type=F32)


def t_dot(a, b):
    return lax.dot_general(a, b, CONTRACT_FIRST, preferred_element_type=F32)


def shards(streams, cotangent, deal, lengths, mix_attn, mix_mlp, w_qkv, w_out, w_gu, w_down):
    tokens, stream_count, width = streams.shape
    shard_size = lax.axis_size("shard")
    hi = shard_size // GROUP
    hi_groups = [[h * GROUP + l for h in range(hi)] for l in range(GROUP)]
    shard = lax.axis_index("shard")
    my_hi = shard // GROUP
    bin_count = shard_size // 4
    my_bins = bin_count // hi
    per_bin = tokens // bin_count
    capacity = per_bin * shard_size
    ff = w_down.shape[1]

    def swap_hi(rows):
        if hi == 1:
            return rows
        return lax.all_to_all(rows, "shard", 0, 0, axis_index_groups=hi_groups, tiled=True)

    def to_bins(rows):
        return swap_hi(rows).reshape(hi, my_bins, per_bin, -1).swapaxes(0, 1).reshape(tokens, -1)

    def from_bins(rows):
        return swap_hi(rows.reshape(my_bins, hi, per_bin, -1).swapaxes(0, 1).reshape(tokens, -1))

    def gather_hi(rows):
        if hi == 1:
            return rows[None]
        return lax.all_gather(rows, "shard", axis_index_groups=hi_groups)

    def sum_hi(rows):
        if hi == 1:
            return rows[0]
        return lax.psum_scatter(rows, "shard", axis_index_groups=hi_groups)

    sorter = (jnp.arange(tokens, dtype=jnp.int32)[:, None] == deal[None, :]).astype(BF)

    hs, n1 = open_streams(mix_attn, sorter, streams)
    low_attn = to_bins(n1)

    bins = lax.axis_index("rep") * bin_count + my_hi * my_bins
    lengths_here = lax.dynamic_slice_in_dim(lengths, bins, my_bins, 0)
    segment, position = slot_layout(lengths_here, capacity)

    def local_order(x):
        return x.reshape(my_bins, hi, GROUP, per_bin).swapaxes(1, 2).reshape(my_bins, capacity)

    segment, position = local_order(segment), local_order(position)
    cosine, sine = rope_tables(position, HEAD_DIM)
    code = segment * CODE + position
    tables = (jnp.concatenate([cosine, sine], -1), code[:, :, None], code[:, None, :])

    raw_qkv, gs, n1g, dy2g, qkvs, outs, gus, dns, attn_rows = front(
        mix_mlp, low_attn, tables, sorter, cotangent,
        gather_hi(w_qkv), gather_hi(w_out).reshape(-1, width), gather_hi(w_gu), gather_hi(w_down), 1,
    )
    rows = w_qkv.shape[0]
    qkvs = qkvs.reshape(width, 3 * HEAD_DIM)
    outs = outs.reshape(2, GROUP, hi, rows, width).swapaxes(1, 2).reshape(width, width)
    gus = gus.reshape(width, 2 * ff // CUBE)
    dns = dns.reshape(width, ff // CUBE)
    attn_rows = from_bins(attn_rows)
    y1, n2 = middle(mix_attn, mix_mlp, hs, attn_rows, outs)
    y2_part, g_mlp, dx2, low_grad_attn, grad_attn, mlp_sums = mlp(
        mix_attn, mix_mlp, n2, dy2g, gus, dns, hs, gs, outs, y1, 4
    )

    attn_cols = attn_rows.reshape(tokens, 2, hi, GROUP, rows).swapaxes(2, 3).reshape(tokens, width)
    dn1, y2, g_out, g_qkv, g_mlp = back(
        to_bins(grad_attn), raw_qkv, qkvs, low_grad_attn, attn_cols, tables,
        n1g, y2_part, g_mlp, hi, 7,
    )
    weight_grads = lay_out(g_qkv, g_out.reshape(hi, rows, width), g_mlp)
    new_streams, d_streams, g_mix_attn, g_mix_mlp = close(
        mix_attn, mix_mlp, sorter, hs, gs, dx2, y1, y2, from_bins(dn1), mlp_sums, 8
    )
    if hi > 1:
        g_mix_attn, g_mix_mlp = lax.psum((g_mix_attn, g_mix_mlp), "shard", axis_index_groups=hi_groups)
    return (new_streams, d_streams, g_mix_attn, g_mix_mlp, *(sum_hi(g) for g in weight_grads))


def solution(mesh):
    both = ("rep", "shard")
    return jax.shard_map(
        shards,
        mesh=mesh,
        in_specs=(
            P(both, None, None),
            P(both, None, None),
            P(both),
            P(),
            P(),
            P(),
            P(both, None),
            P(both, None),
            P(both, None),
            P(both, None),
        ),
        out_specs=(
            P(both, None, None),
            P(both, None, None),
            P(),
            P(),
            P(both, None),
            P(both, None),
            P(both, None),
            P(both, None),
        ),
        check_vma=False,
    )
```
